32 devices in a mesh: slab: 8 (over z, y), pair: 4 (over x, core).
Axes of the slice: x: 2, y: 2, z: 4, core: 2. Of those that a mesh axis runs over, the one named last changes fastest.
Arguments:
- initial_warmth: float32 [128, 256, 512], P('slab', 'pair'), may hold values from 0.5 to 1.5
- heat_passing_coefficient: float32 [128, 256, 512], P('slab', 'pair'), may hold values from 0.2 to 2
- mirror_fraction: float32 [512, 128], P(('slab', 'pair')), may hold values from 0.3 to 0.9
- element_facing_site: int32 [512, 128], P(('slab', 'pair')), may hold values from 0 to 1023
- tile_block_couples: int32 [8192, 2], P(('slab', 'pair')), may hold values from 0 to 511, as said below
- active_slot_count: int32 [32], P(('slab', 'pair')), may hold values from 42 to 256, as said below
- view_factor_blocks: float32 [8192, 128, 128], P(('slab', 'pair')), as said below
Outputs:
- radiosity: float32 [512, 128], P(('slab', 'pair'))
- warmed_liner: float32 [128, 256, 512], P('slab', 'pair')
The draws below stay inside these ranges and needn't reach their ends.
Inputs may be any that keep to these rules, and one draw needn't show every extreme that they name: `tile_block_couples`: each row names two different blocks, and no unordered pair of blocks appears twice in the whole list. A device's slots from its active_slot_count on are not used; in every draw some device has all 256 slots live, and some other device has the fewest allowed. `view_factor_blocks`: entries are nonnegative.
All inputs are finite; a program needn't handle non-finite values.
Results may differ from the reference program's by a relative error of at most 0.0003.
Values sent between devices are 32-bit elements; how exact they have to be, the bound alone decides.
No kernel may reach another device: no remote copies, remote signals or barrier semaphores. Data moves between devices by JAX's collectives and lax.ppermute only.
A program may use at most 192 MiB of HBM per device.

```python
import math
import jax
import jax.numpy as jnp
from jax import lax

BLK = 128
BLK_DEV = 16
PAIR_DEV = 256
CX = 16
CY = 64
THICKNESS_COUNT = 512
SWEEPS = 2
STEPS = 4
NBLK = 512
TILES = 8192
AXIAL_COUNT = 128
RADIAL_COUNT = 256
N_PAIR = 4
DEVICES = 32


def draw_tile_block_couples(key, part):
    key = jax.random.fold_in(key, 11)
    half = NBLK // 2 - 1
    picks = jax.random.permutation(key, NBLK * half)[:TILES].astype(jnp.int32)
    first = picks // half
    second = (first + 1 + picks % half) % NBLK
    return jnp.stack([first, second], axis=1).astype(jnp.int32)


def draw_active_slot_count(key, part):
    key = jax.random.fold_in(key, 12)
    key_counts, key_full, key_least = jax.random.split(key, 3)
    fewest = max(1, PAIR_DEV // 6)
    counts = jax.random.randint(key_counts, (DEVICES,), fewest, PAIR_DEV // 2 + 1)
    fullest = jax.random.randint(key_full, (), 0, DEVICES)
    offset = jax.random.randint(key_least, (), 1, DEVICES)
    least = (fullest + offset) % DEVICES
    counts = counts.at[least].set(fewest)
    return counts.at[fullest].set(PAIR_DEV).astype(jnp.int32)


def log_scales(key, shape, reach):
    factor = reach / math.sinh(reach)
    return jnp.exp(jax.random.uniform(key, shape, jnp.float32, -reach, reach)) * factor


def draw_view_factor_blocks(key, part):
    key = jax.random.fold_in(key, 13)
    key_vals, key_rows, key_cols, key_tiles = jax.random.split(key, 4)
    hits = 2.0 * PAIR_DEV / (3.0 * BLK_DEV)
    top = 1.0 / (hits * BLK)
    row_reach = 1.6
    column_reach = 1.6
    values = jax.random.uniform(key_vals, (TILES, BLK, BLK), jnp.float32, 0.0, top)
    values = values * log_scales(key_rows, (TILES, BLK, 1), row_reach)
    values = values * log_scales(key_cols, (TILES, 1, BLK), column_reach)
    values = values * log_scales(key_tiles, (TILES, 1, 1), 1.15)
    return values.astype(jnp.float32)


def with_ends(array, own_key, low, top_value):
    place = [jax.random.randint(jax.random.fold_in(own_key, axis), (), 0, length) for axis, length in enumerate(array.shape)]
    widest = array.shape.index(max(array.shape))
    next_to = place[:widest] + [(place[widest] + 1) % array.shape[widest]] + place[widest + 1:]
    return array.at[tuple(place)].set(low).at[tuple(next_to)].set(top_value)


def shard_levels(stream_key, shape, cuts, low, high):
    loudness = 1.0
    for dim, parts in cuts:
        steps = jax.random.uniform(jax.random.fold_in(jax.random.fold_in(stream_key, 6), dim), (parts,), jnp.float32, low / len(cuts), high / len(cuts))
        loudness = loudness * jnp.repeat(jnp.exp(steps), shape[dim] // parts).reshape((-1,) + (1,) * (len(shape) - 1 - dim))
    return loudness


def setup_inputs(seed: int = 0) -> dict:
    key_of = jax.random.split(jax.random.key(seed), 8)
    initial_warmth = jnp.clip(0.5 + 1.0 * jax.random.uniform(key_of[0], (AXIAL_COUNT, RADIAL_COUNT, THICKNESS_COUNT), jnp.float32) ** shard_levels(key_of[0], (AXIAL_COUNT, RADIAL_COUNT, THICKNESS_COUNT), ((0, 8), (1, 4)), -0.2, 0.2), 0.5, 1.5)
    heat_passing_coefficient = jnp.clip(jnp.exp(math.log(2.0) - 2.3025851 * jax.random.uniform(key_of[1], (AXIAL_COUNT, RADIAL_COUNT, THICKNESS_COUNT), jnp.float32) ** shard_levels(key_of[1], (AXIAL_COUNT, RADIAL_COUNT, THICKNESS_COUNT), ((0, 8), (1, 4)), -0.2, 0.2)), 0.2, 2.0)
    mirror_fraction = jnp.clip(0.3 + 0.59999996 * jax.random.uniform(key_of[2], (NBLK, BLK), jnp.float32) ** shard_levels(key_of[2], (NBLK, BLK), ((0, 32),), -0.2, 0.2), 0.3, 0.9)
    element_facing_site = with_ends(jax.random.randint(key_of[3], (NBLK, BLK), 0, CX * CY), jax.random.fold_in(key_of[3], 1), 0, (CX * CY) - 1).astype(jnp.int32)
    tile_block_couples = draw_tile_block_couples(jax.random.fold_in(key_of[7], 71), 0)
    active_slot_count = draw_active_slot_count(jax.random.fold_in(key_of[7], 71), 0)
    view_factor_blocks = draw_view_factor_blocks(jax.random.fold_in(key_of[7], 71), 0)
    return {"initial_warmth": initial_warmth, "heat_passing_coefficient": heat_passing_coefficient, "mirror_fraction": mirror_fraction, "element_facing_site": element_facing_site, "tile_block_couples": tile_block_couples, "active_slot_count": active_slot_count, "view_factor_blocks": view_factor_blocks}


step_size = 0.07


def sides(padded):
    return [padded[2:, 1:-1, 1:-1], padded[:-2, 1:-1, 1:-1],
            padded[1:-1, 2:, 1:-1], padded[1:-1, :-2, 1:-1],
            padded[1:-1, 1:-1, 2:], padded[1:-1, 1:-1, :-2]]


def heat_flux(temp_pad, cond_pad, temp, cond):
    total = jnp.zeros_like(temp)
    for near_temp, near_cond in zip(sides(temp_pad), sides(cond_pad)):
        face_cond = jnp.where(near_cond > 0.0, 0.5 * (cond + near_cond), cond)
        total = total + face_cond * (near_temp - temp)
    return total


def incident_of(rad, tile_block_couples, view_factor_blocks, alive):
    first = rad[tile_block_couples[:, 0]]
    second = rad[tile_block_couples[:, 1]]
    to_first = jnp.einsum("tpq,tq->tp", view_factor_blocks, second, precision=lax.Precision.HIGHEST) * alive[:, None]
    to_second = jnp.einsum("tpq,tp->tq", view_factor_blocks, first, precision=lax.Precision.HIGHEST) * alive[:, None]
    total = jnp.zeros((NBLK, BLK), jnp.float32)
    total = total.at[tile_block_couples[:, 0]].add(to_first)
    return total.at[tile_block_couples[:, 1]].add(to_second)


def reference(initial_warmth, heat_passing_coefficient, mirror_fraction, element_facing_site, tile_block_couples, active_slot_count, view_factor_blocks):
    owner = (jnp.arange(NBLK) // BLK_DEV).astype(jnp.int32)
    horizontal_span_sum = (owner // N_PAIR)[:, None] * CX + element_facing_site // CY
    vertical_span_sum = (owner % N_PAIR)[:, None] * CY + element_facing_site % CY
    facing_sheet = initial_warmth[horizontal_span_sum, vertical_span_sum, 0]
    emitted = (1.0 - mirror_fraction) * jnp.square(jnp.square(facing_sheet))
    slots = jnp.arange(TILES).astype(jnp.int32)
    alive = ((slots % PAIR_DEV) < active_slot_count[slots // PAIR_DEV]).astype(jnp.float32)
    radiosity = emitted
    incident = jnp.zeros_like(emitted)
    for sweep in range(SWEEPS):
        incident = incident_of(radiosity, tile_block_couples, view_factor_blocks, alive)
        radiosity = emitted + mirror_fraction * incident
    absorbed = (1.0 - mirror_fraction) * incident - emitted
    weight = (CX * CY) / (BLK_DEV * BLK * 1.0)
    source = jnp.zeros((AXIAL_COUNT, RADIAL_COUNT), jnp.float32).at[horizontal_span_sum, vertical_span_sum].add(absorbed) * weight
    cond_pad = jnp.pad(heat_passing_coefficient, 1)
    warmed_liner = initial_warmth
    for step in range(STEPS):
        temp_pad = jnp.pad(warmed_liner, 1)
        warmed_liner = warmed_liner + step_size * heat_flux(temp_pad, cond_pad, warmed_liner, heat_passing_coefficient)
        warmed_liner = warmed_liner.at[:, :, 0].add(step_size * source)
    return radiosity, warmed_liner
```

```python
import jax
import jax.numpy as jnp
from jax import lax
from jax.sharding import PartitionSpec as P

BLK = 128
SWEEPS = 2
STEPS = 4


step_size = 0.07


def padded_2(block, sides, width):
    for axis, dim in sides:
        count = lax.axis_size(axis)
        forward = [(i, i + 1) for i in range(count - 1)]
        backward = [(target, source) for source, target in forward]
        low = lax.ppermute(
            lax.slice_in_dim(block, block.shape[dim] - width, None, axis=dim), axis, forward
        )
        high = lax.ppermute(lax.slice_in_dim(block, 0, width, axis=dim), axis, backward)
        block = jnp.concatenate([low, block, high], axis=dim)
    return block


def sides(padded):
    return [
        padded[2:, 1:-1, 1:-1],
        padded[:-2, 1:-1, 1:-1],
        padded[1:-1, 2:, 1:-1],
        padded[1:-1, :-2, 1:-1],
        padded[1:-1, 1:-1, 2:],
        padded[1:-1, 1:-1, :-2],
    ]


def heat_flux(temp_pad, cond_pad, temp, cond):
    total = jnp.zeros_like(temp)
    for near_temp, near_cond in zip(sides(temp_pad), sides(cond_pad)):
        face_cond = jnp.where(near_cond > 0.0, 0.5 * (cond + near_cond), cond)
        total = total + face_cond * (near_temp - temp)
    return total


def depth_pad(field):
    return jnp.pad(field, ((0, 0), (0, 0), (1, 1)))


def collect(radiosity):
    count = lax.axis_size("slab") * lax.axis_size("pair")
    copies = jnp.broadcast_to(radiosity[None], (count,) + radiosity.shape)
    copies = copies.reshape(count * radiosity.shape[0], radiosity.shape[1])
    return lax.all_to_all(copies, ("slab", "pair"), split_axis=0, concat_axis=0, tiled=True)


def spread_back(term):
    count = lax.axis_size("slab") * lax.axis_size("pair")
    parts = lax.all_to_all(term, ("slab", "pair"), split_axis=0, concat_axis=0, tiled=True)
    return parts.reshape(count, -1, term.shape[1]).sum(axis=0)


def tile_terms(whole, tile_block_couples, view_factor_blocks, live_now):
    count = view_factor_blocks.shape[0]
    alive = (jnp.arange(count) < live_now).astype(jnp.float32)
    first = whole[tile_block_couples[:, 0]]
    second = whole[tile_block_couples[:, 1]]
    to_first = (
        jnp.einsum("tpq,tq->tp", view_factor_blocks, second, precision=lax.Precision.HIGHEST)
        * alive[:, None]
    )
    to_second = (
        jnp.einsum("tpq,tp->tq", view_factor_blocks, first, precision=lax.Precision.HIGHEST)
        * alive[:, None]
    )
    total = jnp.zeros(whole.shape, jnp.float32)
    total = total.at[tile_block_couples[:, 0]].add(to_first)
    return total.at[tile_block_couples[:, 1]].add(to_second)


def shards(
    initial_warmth,
    heat_passing_coefficient,
    mirror_fraction,
    element_facing_site,
    tile_block_couples,
    active_slot_count,
    view_factor_blocks,
):
    owned_horizontals, owned_verticals, thickness_span = initial_warmth.shape
    blocks_here = mirror_fraction.shape[0]
    lowest_sheet = initial_warmth[:, :, 0].reshape(-1)
    facing_sheet = lowest_sheet[element_facing_site]
    emitted = (1.0 - mirror_fraction) * jnp.square(jnp.square(facing_sheet))
    radiosity = emitted
    incident = jnp.zeros_like(emitted)
    for sweep in range(SWEEPS):
        whole = collect(radiosity)
        term = tile_terms(whole, tile_block_couples, view_factor_blocks, active_slot_count[0])
        incident = spread_back(term)
        radiosity = emitted + mirror_fraction * incident
    absorbed = (1.0 - mirror_fraction) * incident - emitted
    weight = owned_horizontals * owned_verticals / (blocks_here * BLK * 1.0)
    summed = jax.ops.segment_sum(
        absorbed.reshape(-1), element_facing_site.reshape(-1), owned_horizontals * owned_verticals
    )
    source = summed.reshape(owned_horizontals, owned_verticals) * weight
    cond_pad = depth_pad(padded_2(heat_passing_coefficient, (("slab", 0), ("pair", 1)), 1))
    warmed_liner = initial_warmth
    for step in range(STEPS):
        temp_pad = depth_pad(padded_2(warmed_liner, (("slab", 0), ("pair", 1)), 1))
        warmed_liner = warmed_liner + step_size * heat_flux(
            temp_pad, cond_pad, warmed_liner, heat_passing_coefficient
        )
        warmed_liner = warmed_liner.at[:, :, 0].add(step_size * source)
    return (radiosity, warmed_liner)


def solution(mesh):
    return jax.shard_map(
        shards,
        mesh=mesh,
        in_specs=(
            P("slab", "pair", None),
            P("slab", "pair", None),
            P(("slab", "pair"), None),
            P(("slab", "pair"), None),
            P(("slab", "pair"), None),
            P(("slab", "pair")),
            P(("slab", "pair"), None, None),
        ),
        out_specs=(P(("slab", "pair"), None), P("slab", "pair", None)),
        check_vma=False,
    )
```

```python
import functools

import jax
import jax.numpy as jnp
from jax import lax
from jax.experimental import pallas as pl
from jax.experimental.pallas import tpu as pltpu
from jax.sharding import PartitionSpec as P

BLK = 128
SWEEPS = 2
STEPS = 4
HALO = STEPS
LANES = 128
CHUNK = 16

step_size = 0.07

NT = (((1,), (1,)), ((), ()))
NN = (((1,), (0,)), ((), ()))


def params(mib):
    return pltpu.CompilerParams(vmem_limit_bytes=mib * 1024 * 1024)


def cost(flops, nbytes):
    return pl.CostEstimate(flops=flops, bytes_accessed=nbytes, transcendentals=0)


def parts_of(x, count):
    out = []
    for _ in range(count - 1):
        part = x.astype(jnp.bfloat16)
        out.append(part)
        x = x - part.astype(jnp.float32)
    out.append(x.astype(jnp.bfloat16))
    return out


def emit_kernel(plane_ref, site_ref, mirror_ref, emitted_ref, copies_ref):
    sheets = plane_ref.shape[0]
    for half in range(site_ref.shape[0] // 8):
        rows = pl.ds(half * 8, 8)
        site = site_ref[rows, :]
        lane = site & (LANES - 1)
        sheet = site >> 7
        warmth = jnp.zeros(site.shape, jnp.float32)
        for r in range(sheets):
            line = jnp.broadcast_to(plane_ref[r : r + 1, :], site.shape)
            picked = jnp.take_along_axis(line, lane, axis=1)
            warmth = jnp.where(sheet == r, picked, warmth)
        square = warmth * warmth
        emitted = (1.0 - mirror_ref[rows, :]) * (square * square)
        emitted_ref[rows, :] = emitted
        for d in range(copies_ref.shape[0]):
            copies_ref[d, rows, :] = emitted


def emit(plane, site, mirror, count):
    shape = mirror.shape
    return pl.pallas_call(
        emit_kernel,
        out_shape=(
            jax.ShapeDtypeStruct(shape, jnp.float32),
            jax.ShapeDtypeStruct((count,) + shape, jnp.float32),
        ),
        compiler_params=params(8),
        cost_estimate=cost(10_000, 400_000),
        name="emit",
    )(plane, site, mirror)


def tiles_kernel(
    live_ref, pairs_ref, lanes_ref, whole_ref, tiles_ref, out_ref, held, terms, sems
):
    slots = held.shape[0]
    live = live_ref[0]
    chunks = (live + CHUNK - 1) // CHUNK

    def chunk_copy(c):
        span = pl.ds(c * CHUNK, CHUNK)
        return pltpu.make_async_copy(tiles_ref.at[span], held.at[span], sems.at[c])

    @pl.loop(0, chunks)
    def _(c):
        chunk_copy(c).start()

    top = lax.broadcasted_iota(jnp.int32, (8, BLK), 0) == 0

    def split_row(block):
        row = jnp.broadcast_to(whole_ref[pl.ds(block, 1), :], (8, BLK))
        high = row.astype(jnp.bfloat16).astype(jnp.float32)
        return jnp.where(top, high, row - high)

    def vectors(a, b):
        stacked = jnp.concatenate([split_row(a), split_row(b)], axis=0)
        stacked = stacked.astype(jnp.bfloat16)
        return jnp.concatenate([stacked, stacked], axis=1)

    @pl.loop(0, chunks)
    def _(c):
        chunk_copy(c).wait()
        for u in range(0, CHUNK, 2):
            t = c * CHUNK + u
            high_a, low_a = parts_of(held[t], 2)
            high_b, low_b = parts_of(held[t + 1], 2)
            both = jnp.concatenate(
                [
                    jnp.concatenate([high_a, high_b], axis=1),
                    jnp.concatenate([low_a, low_b], axis=1),
                ],
                axis=0,
            )
            second = lax.dot_general(
                vectors(pairs_ref[0, t], pairs_ref[0, t + 1]),
                both,
                NN,
                preferred_element_type=jnp.float32,
            )
            turned = jnp.concatenate(
                [
                    jnp.concatenate([high_a, low_a], axis=1),
                    jnp.concatenate([high_b, low_b], axis=1),
                ],
                axis=0,
            )
            first = lax.dot_general(
                vectors(pairs_ref[1, t], pairs_ref[1, t + 1]),
                turned,
                NT,
                preferred_element_type=jnp.float32,
            )
            for side, result in ((0, first), (1, second)):
                terms[side, pl.ds(t, 1), :] = result[0:1, :BLK] + result[1:2, :BLK]
                terms[side, pl.ds(t + 1, 1), :] = result[8:9, BLK:] + result[9:10, BLK:]

    used = lax.broadcasted_iota(jnp.int32, (slots, BLK), 0) < live
    used_lane = lax.broadcasted_iota(jnp.int32, (1, slots), 1) < live
    blocks = out_ref.shape[0]
    group = min(blocks, 512)
    split = []
    for side in range(2):
        masked = jnp.where(used, terms[side], 0.0)
        split.append(jnp.concatenate(parts_of(masked, 2), axis=1))
    for base in range(0, blocks, group):
        rows = lax.broadcasted_iota(jnp.int32, (group, slots), 0) + base
        total = jnp.zeros((group, 2 * BLK), jnp.float32)
        for side in range(2):
            target = jnp.where(used_lane, lanes_ref[side : side + 1, :], -1)
            choose = jnp.where(rows == target, 1.0, 0.0).astype(jnp.bfloat16)
            total = total + jnp.dot(choose, split[side], preferred_element_type=jnp.float32)
        out_ref[base : base + group, :] = total[:, :BLK] + total[:, BLK:]


def tile_terms(whole, couples, live, tiles):
    slots = tiles.shape[0]
    smem = pl.BlockSpec(memory_space=pltpu.SMEM)
    vmem = pl.BlockSpec(memory_space=pltpu.VMEM)
    return pl.pallas_call(
        tiles_kernel,
        out_shape=jax.ShapeDtypeStruct(whole.shape, jnp.float32),
        in_specs=[smem, smem, vmem, vmem, pl.BlockSpec(memory_space=pl.ANY)],
        out_specs=vmem,
        scratch_shapes=[
            pltpu.VMEM(tiles.shape, jnp.float32),
            pltpu.VMEM((2, slots, BLK), jnp.float32),
            pltpu.SemaphoreType.DMA((slots // CHUNK,)),
        ],
        compiler_params=params(36),
        cost_estimate=cost(slots * BLK * BLK * 32, slots * BLK * BLK * 4),
        name="tiles",
    )(live, couples, couples, whole, tiles)


def sum_parts(parts_ref, rows):
    total = parts_ref[0, rows, :]
    for d in range(1, parts_ref.shape[0]):
        total = total + parts_ref[d, rows, :]
    return total


def middle_kernel(parts_ref, emitted_ref, mirror_ref, copies_ref):
    for half in range(emitted_ref.shape[0] // 8):
        rows = pl.ds(half * 8, 8)
        incident = sum_parts(parts_ref, rows)
        radiosity = emitted_ref[rows, :] + mirror_ref[rows, :] * incident
        for d in range(copies_ref.shape[0]):
            copies_ref[d, rows, :] = radiosity


def middle(parts, emitted, mirror):
    return pl.pallas_call(
        middle_kernel,
        out_shape=jax.ShapeDtypeStruct(parts.shape, jnp.float32),
        compiler_params=params(8),
        cost_estimate=cost(100_000, 600_000),
        name="middle",
    )(parts, emitted, mirror)


def last_kernel(scale, parts_ref, emitted_ref, mirror_ref, site_ref, rad_ref, source_ref):
    blocks = emitted_ref.shape[0]
    incident = sum_parts(parts_ref, slice(None))
    emitted = emitted_ref[...]
    mirror = mirror_ref[...]
    rad_ref[...] = emitted + mirror * incident
    absorbed = ((1.0 - mirror) * incident - emitted) * scale
    site = site_ref[...]
    lane = site & (LANES - 1)
    sheet = site >> 7
    sheets = source_ref.shape[1]
    sheet_iota = lax.broadcasted_iota(jnp.int32, (sheets, BLK), 0)
    lane_iota = lax.broadcasted_iota(jnp.int32, (LANES, BLK), 0)
    left = []
    right = []
    for b in range(blocks):
        here = jnp.where(sheet_iota == sheet[b : b + 1, :], absorbed[b : b + 1, :], 0.0)
        left.append(here)
        pick = jnp.where(lane_iota == lane[b : b + 1, :], 1.0, 0.0)
        right.append(pick.astype(jnp.bfloat16))
    left = jnp.concatenate(left, axis=1)
    right = jnp.concatenate(right, axis=1)
    source = jnp.zeros((sheets, LANES), jnp.float32)
    for part in parts_of(left, 3):
        source = source + lax.dot_general(part, right, NT, preferred_element_type=jnp.float32)
    for d in range(source_ref.shape[0]):
        source_ref[d] = source


def last(parts, emitted, mirror, site, cells):
    count = parts.shape[0]
    weight = cells / (mirror.shape[0] * BLK * 1.0)
    return pl.pallas_call(
        functools.partial(last_kernel, step_size * weight),
        out_shape=(
            jax.ShapeDtypeStruct(mirror.shape, jnp.float32),
            jax.ShapeDtypeStruct((count, cells // LANES, LANES), jnp.float32),
        ),
        compiler_params=params(16),
        cost_estimate=cost(10_000_000, 600_000),
        name="last",
    )(parts, emitted, mirror, site)


def pack_x_kernel(t_low, k_low, t_high, k_high, low_ref, high_ref):
    low_ref[:HALO] = t_low[...]
    low_ref[HALO:] = k_low[...]
    high_ref[:HALO] = t_high[...]
    high_ref[HALO:] = k_high[...]


def pack_x(temp, cond):
    nx, ny, nz = temp.shape
    first = pl.BlockSpec((HALO, ny, nz), lambda i: (0, 0, 0))
    final = pl.BlockSpec((HALO, ny, nz), lambda i: (nx // HALO - 1, 0, 0))
    whole = pl.BlockSpec((2 * HALO, ny, nz), lambda i: (0, 0, 0))
    shape = jax.ShapeDtypeStruct((2 * HALO, ny, nz), jnp.float32)
    return pl.pallas_call(
        pack_x_kernel,
        grid=(1,),
        out_shape=(shape, shape),
        in_specs=[first, first, final, final],
        out_specs=(whole, whole),
        compiler_params=params(20),
        cost_estimate=cost(0, 4 * 2 * HALO * ny * nz * 4),
        name="pack_x",
    )(temp, cond, temp, cond)


def pack_y_kernel(nx, t0, k0, t7, k7, lo0, hi0, lo7, hi7, down_ref, up_ref):
    upper = lax.broadcasted_iota(jnp.int32, down_ref.shape[1:], 0) < HALO

    def put(x, t_first, k_first, t_final, k_final):
        down_ref[x] = jnp.where(upper, t_first, pltpu.roll(k_first, HALO, 0))
        up_ref[x] = jnp.where(upper, pltpu.roll(t_final, HALO, 0), k_final)

    for x in range(HALO):
        put(x, lo0[x], lo0[HALO + x], lo7[x], lo7[HALO + x])
        put(HALO + nx + x, hi0[x], hi0[HALO + x], hi7[x], hi7[HALO + x])
    for x in range(nx):
        put(HALO + x, t0[x], k0[x], t7[x], k7[x])


def pack_y(temp, cond, low, high):
    nx, ny, nz = temp.shape

    def edges(planes):
        return (
            pl.BlockSpec((planes, 8, nz), lambda i: (0, 0, 0)),
            pl.BlockSpec((planes, 8, nz), lambda i: (0, ny // 8 - 1, 0)),
        )

    first, final = edges(nx)
    halo_first, halo_final = edges(2 * HALO)
    tall = nx + 2 * HALO
    whole = pl.BlockSpec((tall, 8, nz), lambda i: (0, 0, 0))
    shape = jax.ShapeDtypeStruct((tall, 8, nz), jnp.float32)
    return pl.pallas_call(
        functools.partial(pack_y_kernel, nx),
        grid=(1,),
        out_shape=(shape, shape),
        in_specs=[first, first, final, final, halo_first, halo_first, halo_final, halo_final],
        out_specs=(whole, whole),
        compiler_params=params(20),
        cost_estimate=cost(0, 4 * tall * 8 * nz * 4),
        name="pack_y",
    )(temp, cond, temp, cond, low, high, low, high)


def coupling(a, b):
    return jnp.where(jnp.minimum(a, b) > 0.0, (0.5 * step_size) * (a + b), 0.0)


def heat_kernel(
    t_ref, k_ref, low_ref, high_ref, below_ref, above_ref, out_ref, thin_ref,
    field, cond, centre, cx, cy, cz,
):
    nx, ny, nz = t_ref.shape
    tall = nx + 2 * HALO
    wide = ny + 2 * HALO
    upper = lax.broadcasted_iota(jnp.int32, (8, nz), 0) < HALO

    field[0, :HALO, :ny] = low_ref[:HALO]
    field[0, HALO : HALO + nx, :ny] = t_ref[...]
    field[0, HALO + nx :, :ny] = high_ref[:HALO]
    cond[:HALO, :ny] = low_ref[HALO:]
    cond[HALO : HALO + nx, :ny] = k_ref[...]
    cond[HALO + nx :, :ny] = high_ref[HALO:]

    @pl.loop(0, tall)
    def _(x):
        down = above_ref[x]
        up = below_ref[x]
        field[0, x, ny:] = jnp.where(upper, down, pltpu.roll(up, HALO, 0))
        cond[x, ny:] = jnp.where(upper, pltpu.roll(down, HALO, 0), up)

    depth = lax.broadcasted_iota(jnp.int32, (wide, nz), 1)

    @pl.loop(0, tall)
    def _(x):
        here = cond[x]
        outer = here * 0.0
        total = 6.0 * here
        after = cond[jnp.minimum(x + 1, tall - 1)]
        before = cond[jnp.maximum(x - 1, 0)]
        cx[x] = coupling(here, after)
        y_after = pltpu.roll(here, wide - 1, 0)
        y_before = pltpu.roll(here, 1, 0)
        cy[x] = coupling(here, y_after)
        z_after = jnp.where(depth == nz - 1, outer, pltpu.roll(here, nz - 1, 1))
        z_before = jnp.where(depth == 0, outer, pltpu.roll(here, 1, 1))
        cz[x] = coupling(here, z_after)
        for near in (after, before, y_after, y_before, z_after, z_before):
            total = total + jnp.where(near > 0.0, near, here)
        centre[x] = 1.0 - (0.5 * step_size) * total

    def update(old, x):
        here = field[old, x]
        new = centre[x] * here
        new = new + (cx[x] * field[old, x + 1] + cx[x - 1] * field[old, x - 1])
        new = new + cy[x] * pltpu.roll(here, wide - 1, 0)
        new = new + pltpu.roll(cy[x] * here, 1, 0)
        new = new + cz[x] * pltpu.roll(here, nz - 1, 1)
        return new + pltpu.roll(cz[x] * here, 1, 1)

    @pl.loop(0, STEPS - 1)
    def _(step):
        old = step & 1

        @pl.loop(1 + step, tall - 1 - step)
        def _(x):
            field[1 - old, x] = update(old, x)

    @pl.loop(0, nx)
    def _(x):
        out_ref[x] = update((STEPS - 1) & 1, x + HALO)[:ny]

    lane = lax.broadcasted_iota(jnp.int32, (wide, LANES), 1)
    y_lane = lax.broadcasted_iota(jnp.int32, (8, LANES), 1)
    for base in range(0, tall, 16):
        planes = min(16, tall - base)
        gathered = jnp.zeros((wide, LANES), jnp.float32)
        for g in range(planes):
            piece = cond[base + g, :, :LANES]
            if g:
                piece = pltpu.roll(piece, 8 * g, 1)
            gathered = jnp.where((lane >> 3) == g, piece, gathered)
        square = jnp.concatenate(
            [gathered, jnp.zeros((LANES - wide, LANES), jnp.float32)], axis=0
        )
        turned = square.T
        for g in range(planes):
            rows = turned[8 * g : 8 * g + 8, :]
            moved = pltpu.roll(rows, LANES - wide, 1)
            thin_ref[base + g] = jnp.where(
                y_lane < ny + HALO, rows, jnp.where(y_lane >= LANES - HALO, moved, 0.0)
            )


def heat(temp, cond, low, high, below, above):
    nx, ny, nz = temp.shape
    tall, wide = nx + 2 * HALO, ny + 2 * HALO
    big = pltpu.VMEM((tall, wide, nz), jnp.float32)
    return pl.pallas_call(
        heat_kernel,
        out_shape=(
            jax.ShapeDtypeStruct(temp.shape, jnp.float32),
            jax.ShapeDtypeStruct((tall, 8, LANES), jnp.float32),
        ),
        scratch_shapes=[pltpu.VMEM((2, tall, wide, nz), jnp.float32)] + [big] * 5,
        compiler_params=params(48),
        cost_estimate=cost(tall * wide * nz * 100, 12 * nx * ny * nz * 4),
        name="heat",
    )(temp, cond, low, high, below, above)


def source_kernel(ny, near_ref, flag_ref, all_ref, thin_ref, base_ref, out_ref):
    tall = thin_ref.shape[0]
    nx = tall - 2 * HALO
    sheets = all_ref.shape[1]
    sub = lax.broadcasted_iota(jnp.int32, (8, LANES), 0)
    y_lane = lax.broadcasted_iota(jnp.int32, (8, LANES), 1)

    def sheet(k):
        return all_ref[near_ref[k]] * flag_ref[k].astype(jnp.float32)

    def rows_of(slab):
        low, own, high = (sheet(3 * slab + k) for k in range(3))
        out = []
        for half in range(2):
            if half == 0:
                own_at, high_at, low_at = own, pltpu.roll(high, ny, 1), pltpu.roll(low, ny, 1)
            else:
                own_at, high_at, low_at = pltpu.roll(own, ny, 1), high, low
            out.append(
                jnp.where(
                    y_lane < ny,
                    own_at,
                    jnp.where(
                        y_lane < ny + HALO,
                        high_at,
                        jnp.where(y_lane >= LANES - HALO, low_at, 0.0),
                    ),
                )
            )
        return out

    lines = [rows_of(s) for s in range(3)]
    source = []
    for x in range(-HALO, nx + HALO):
        which, local = (x + nx) // nx, x % nx
        row = lines[which][local % 2][local // 2 : local // 2 + 1, :]
        source.append(jnp.where(sub == 0, jnp.broadcast_to(row, (8, LANES)), 0.0))

    cond = [thin_ref[x] for x in range(tall)]
    cx, cy, cz, centre = [], [], [], []
    for x in range(tall):
        here = cond[x]
        after = cond[min(x + 1, tall - 1)]
        before = cond[max(x - 1, 0)]
        y_after = pltpu.roll(here, LANES - 1, 1)
        y_before = pltpu.roll(here, 1, 1)
        z_after = jnp.where(sub == 7, 0.0, pltpu.roll(here, 7, 0))
        z_before = jnp.where(sub == 0, 0.0, pltpu.roll(here, 1, 0))
        cx.append(coupling(here, after))
        cy.append(coupling(here, y_after))
        cz.append(coupling(here, z_after))
        total = 6.0 * here
        for near in (after, before, y_after, y_before, z_after, z_before):
            total = total + jnp.where(near > 0.0, near, here)
        centre.append(1.0 - (0.5 * step_size) * total)

    added = source
    for step in range(1, STEPS):
        new = list(added)
        for x in range(step, tall - step):
            here = added[x]
            total = source[x] + centre[x] * here
            total = total + (cx[x] * added[x + 1] + cx[x - 1] * added[x - 1])
            total = total + cy[x] * pltpu.roll(here, LANES - 1, 1)
            total = total + pltpu.roll(cy[x] * here, 1, 1)
            total = total + cz[x] * pltpu.roll(here, 7, 0)
            new[x] = total + pltpu.roll(cz[x] * here, 1, 0)
        added = new

    lane = lax.broadcasted_iota(jnp.int32, (ny, LANES), 1)
    turned = jnp.concatenate(added[HALO : HALO + nx], axis=0).T[:ny]
    for x in range(nx):
        piece = turned if x == 0 else pltpu.roll(turned, LANES - 8 * x, 1)
        out_ref[x] = base_ref[x] + jnp.where(lane < STEPS, piece, 0.0)


def add_source(near, flag, everything, thin, base):
    nx, ny, nz = base.shape
    smem = pl.BlockSpec(memory_space=pltpu.SMEM)
    block = pl.BlockSpec((nx, ny, LANES), lambda i: (0, 0, 0))
    return pl.pallas_call(
        functools.partial(source_kernel, ny),
        grid=(1,),
        out_shape=jax.ShapeDtypeStruct(base.shape, jnp.float32),
        in_specs=[
            smem,
            smem,
            pl.BlockSpec(everything.shape, lambda i: (0, 0, 0)),
            pl.BlockSpec(thin.shape, lambda i: (0, 0, 0)),
            block,
        ],
        out_specs=block,
        input_output_aliases={4: 0},
        compiler_params=params(16),
        cost_estimate=cost(1_000_000, 2 * nx * ny * LANES * 4),
        name="add_source",
    )(near, flag, everything, thin, base)


def exchange(copies):
    return lax.all_to_all(copies, ("slab", "pair"), split_axis=0, concat_axis=0, tiled=True)


def both_ways(low, high, axis):
    count = lax.axis_size(axis)
    forward = [(i, i + 1) for i in range(count - 1)]
    backward = [(target, source) for source, target in forward]
    from_low = lax.ppermute(high, axis, forward)
    from_high = lax.ppermute(low, axis, backward)
    return from_low, from_high


def shards(
    initial_warmth,
    heat_passing_coefficient,
    mirror_fraction,
    element_facing_site,
    tile_block_couples,
    active_slot_count,
    view_factor_blocks,
):
    nx, ny, _ = initial_warmth.shape
    slabs, pairs = lax.axis_size("slab"), lax.axis_size("pair")
    count = slabs * pairs
    blocks = mirror_fraction.shape[0]
    cells = nx * ny
    plane = initial_warmth[:, :, 0].reshape(cells // LANES, LANES)
    couples = tile_block_couples.T

    emitted, copies = emit(plane, element_facing_site, mirror_fraction, count)
    for sweep in range(SWEEPS):
        whole = exchange(copies).reshape(count * blocks, BLK)
        term = tile_terms(whole, couples, active_slot_count, view_factor_blocks)
        parts = exchange(term.reshape(count, blocks, BLK))
        if sweep + 1 < SWEEPS:
            copies = middle(parts, emitted, mirror_fraction)
    radiosity, source = last(parts, emitted, mirror_fraction, element_facing_site, cells)
    everything = exchange(source)

    send_low, send_high = pack_x(initial_warmth, heat_passing_coefficient)
    low, high = both_ways(send_low, send_high, "slab")
    send_down, send_up = pack_y(initial_warmth, heat_passing_coefficient, low, high)
    below, above = both_ways(send_down, send_up, "pair")
    base, thin = heat(initial_warmth, heat_passing_coefficient, low, high, below, above)

    slab, pair = lax.axis_index("slab"), lax.axis_index("pair")
    near, flag = [], []
    for ds in (-1, 0, 1):
        for dp in (-1, 0, 1):
            s, p = slab + ds, pair + dp
            inside = (s >= 0) & (s < slabs) & (p >= 0) & (p < pairs)
            near.append(jnp.where(inside, s * pairs + p, 0))
            flag.append(inside)
    near = jnp.stack(near).astype(jnp.int32)
    flag = jnp.stack(flag).astype(jnp.int32)
    warmed_liner = add_source(near, flag, everything, thin, base)
    return (radiosity, warmed_liner)


def solution(mesh):
    return jax.shard_map(
        shards,
        mesh=mesh,
        in_specs=(
            P("slab", "pair", None),
            P("slab", "pair", None),
            P(("slab", "pair"), None),
            P(("slab", "pair"), None),
            P(("slab", "pair"), None),
            P(("slab", "pair")),
            P(("slab", "pair"), None, None),
        ),
        out_specs=(P(("slab", "pair"), None), P("slab", "pair", None)),
        check_vma=False,
    )
```

```python
import functools

import jax
import jax.numpy as jnp
from jax import lax
from jax.experimental import pallas as pl
from jax.experimental.pallas import tpu as pltpu
from jax.sharding import PartitionSpec as P

BLK = 128
SWEEPS = 2
STEPS = 4
HALO = STEPS
DEPTH = STEPS // 2
ROWS = STEPS
LANES = 128
CHUNK = 16

step_size = 0.07

NT = (((1,), (1,)), ((), ()))
NN = (((1,), (0,)), ((), ()))


def params(mib):
    return pltpu.CompilerParams(vmem_limit_bytes=mib * 1024 * 1024)


def cost(flops, nbytes):
    return pl.CostEstimate(flops=flops, bytes_accessed=nbytes, transcendentals=0)


def parts_of(x, count):
    out = []
    for _ in range(count - 1):
        part = x.astype(jnp.bfloat16)
        out.append(part)
        x = x - part.astype(jnp.float32)
    out.append(x.astype(jnp.bfloat16))
    return out


def emit_kernel(temp_ref, site_ref, mirror_ref, emitted_ref, copies_ref):
    nx, ny, _ = temp_ref.shape
    sheets = nx * ny // LANES
    per = LANES // ny
    lanes = lax.broadcasted_iota(jnp.int32, (LANES, LANES), 1)
    gathered = jnp.zeros((LANES, LANES), jnp.float32)
    for r in range(sheets):
        piece = temp_ref[per * r : per * r + per].reshape(LANES, LANES)
        if r:
            piece = pltpu.roll(piece, r, 1)
        gathered = jnp.where(lanes == r, piece, gathered)
    plane = gathered.T[:sheets]
    for half in range(site_ref.shape[0] // 8):
        rows = pl.ds(half * 8, 8)
        site = site_ref[rows, :]
        lane = site & (LANES - 1)
        sheet = site >> 7
        warmth = jnp.zeros(site.shape, jnp.float32)
        for r in range(sheets):
            line = jnp.broadcast_to(plane[r : r + 1, :], site.shape)
            picked = jnp.take_along_axis(line, lane, axis=1)
            warmth = jnp.where(sheet == r, picked, warmth)
        square = warmth * warmth
        emitted = (1.0 - mirror_ref[rows, :]) * (square * square)
        emitted_ref[rows, :] = emitted
        for d in range(copies_ref.shape[0]):
            copies_ref[d, rows, :] = emitted


def emit(temp, site, mirror, count):
    shape = mirror.shape
    nx, ny, _ = temp.shape
    patch = pl.BlockSpec(shape, lambda i: (0, 0))
    return pl.pallas_call(
        emit_kernel,
        grid=(1,),
        out_shape=(
            jax.ShapeDtypeStruct(shape, jnp.float32),
            jax.ShapeDtypeStruct((count,) + shape, jnp.float32),
        ),
        in_specs=[pl.BlockSpec((nx, ny, LANES), lambda i: (0, 0, 0)), patch, patch],
        out_specs=(patch, pl.BlockSpec((count,) + shape, lambda i: (0, 0, 0))),
        compiler_params=params(56),
        cost_estimate=cost(10_000, 900_000),
        name="emit",
    )(temp, site, mirror)


def tiles_kernel(
    live_ref, pairs_ref, lanes_ref, whole_ref, tiles_ref, out_ref, held, terms, sems
):
    slots = held.shape[0]
    live = live_ref[0]
    chunks = (live + CHUNK - 1) // CHUNK

    def chunk_copy(c):
        span = pl.ds(c * CHUNK, CHUNK)
        return pltpu.make_async_copy(tiles_ref.at[span], held.at[span], sems.at[c])

    @pl.loop(0, chunks)
    def _(c):
        chunk_copy(c).start()

    top = lax.broadcasted_iota(jnp.int32, (8, BLK), 0) == 0

    def split_row(block):
        row = jnp.broadcast_to(whole_ref[pl.ds(block, 1), :], (8, BLK))
        high = row.astype(jnp.bfloat16).astype(jnp.float32)
        return jnp.where(top, high, row - high)

    def vectors(a, b):
        stacked = jnp.concatenate([split_row(a), split_row(b)], axis=0)
        stacked = stacked.astype(jnp.bfloat16)
        return jnp.concatenate([stacked, stacked], axis=1)

    @pl.loop(0, chunks)
    def _(c):
        chunk_copy(c).wait()
        for u in range(0, CHUNK, 2):
            t = c * CHUNK + u
            high_a, low_a = parts_of(held[t], 2)
            high_b, low_b = parts_of(held[t + 1], 2)
            both = jnp.concatenate(
                [
                    jnp.concatenate([high_a, high_b], axis=1),
                    jnp.concatenate([low_a, low_b], axis=1),
                ],
                axis=0,
            )
            second = lax.dot_general(
                vectors(pairs_ref[0, t], pairs_ref[0, t + 1]),
                both,
                NN,
                preferred_element_type=jnp.float32,
            )
            turned = jnp.concatenate(
                [
                    jnp.concatenate([high_a, low_a], axis=1),
                    jnp.concatenate([high_b, low_b], axis=1),
                ],
                axis=0,
            )
            first = lax.dot_general(
                vectors(pairs_ref[1, t], pairs_ref[1, t + 1]),
                turned,
                NT,
                preferred_element_type=jnp.float32,
            )
            for side, result in ((0, first), (1, second)):
                terms[side, pl.ds(t, 1), :] = result[0:1, :BLK] + result[1:2, :BLK]
                terms[side, pl.ds(t + 1, 1), :] = result[8:9, BLK:] + result[9:10, BLK:]

    used = lax.broadcasted_iota(jnp.int32, (slots, BLK), 0) < live
    used_lane = lax.broadcasted_iota(jnp.int32, (1, slots), 1) < live
    blocks = out_ref.shape[0]
    group = min(blocks, 512)
    split = []
    for side in range(2):
        masked = jnp.where(used, terms[side], 0.0)
        split.append(jnp.concatenate(parts_of(masked, 2), axis=1))
    for base in range(0, blocks, group):
        rows = lax.broadcasted_iota(jnp.int32, (group, slots), 0) + base
        total = jnp.zeros((group, 2 * BLK), jnp.float32)
        for side in range(2):
            target = jnp.where(used_lane, lanes_ref[side : side + 1, :], -1)
            choose = jnp.where(rows == target, 1.0, 0.0).astype(jnp.bfloat16)
            total = total + jnp.dot(choose, split[side], preferred_element_type=jnp.float32)
        out_ref[base : base + group, :] = total[:, :BLK] + total[:, BLK:]


def tile_terms(whole, couples, live, tiles):
    slots = tiles.shape[0]
    smem = pl.BlockSpec(memory_space=pltpu.SMEM)
    vmem = pl.BlockSpec(memory_space=pltpu.VMEM)
    return pl.pallas_call(
        tiles_kernel,
        out_shape=jax.ShapeDtypeStruct(whole.shape, jnp.float32),
        in_specs=[smem, smem, vmem, vmem, pl.BlockSpec(memory_space=pl.ANY)],
        out_specs=vmem,
        scratch_shapes=[
            pltpu.VMEM(tiles.shape, jnp.float32),
            pltpu.VMEM((2, slots, BLK), jnp.float32),
            pltpu.SemaphoreType.DMA((slots // CHUNK,)),
        ],
        compiler_params=params(56),
        cost_estimate=cost(slots * BLK * BLK * 32, slots * BLK * BLK * 4),
        name="tiles",
    )(live, couples, couples, whole, tiles)


def sum_parts(parts_ref, rows):
    total = parts_ref[0, rows, :]
    for d in range(1, parts_ref.shape[0]):
        total = total + parts_ref[d, rows, :]
    return total


def middle_kernel(parts_ref, emitted_ref, mirror_ref, copies_ref):
    for half in range(emitted_ref.shape[0] // 8):
        rows = pl.ds(half * 8, 8)
        incident = sum_parts(parts_ref, rows)
        radiosity = emitted_ref[rows, :] + mirror_ref[rows, :] * incident
        for d in range(copies_ref.shape[0]):
            copies_ref[d, rows, :] = radiosity


def middle(parts, emitted, mirror):
    return pl.pallas_call(
        middle_kernel,
        out_shape=jax.ShapeDtypeStruct(parts.shape, jnp.float32),
        compiler_params=params(8),
        cost_estimate=cost(100_000, 600_000),
        name="middle",
    )(parts, emitted, mirror)


def last_kernel(scale, parts_ref, emitted_ref, mirror_ref, site_ref, rad_ref, source_ref):
    blocks = emitted_ref.shape[0]
    incident = sum_parts(parts_ref, slice(None))
    emitted = emitted_ref[...]
    mirror = mirror_ref[...]
    rad_ref[...] = emitted + mirror * incident
    absorbed = ((1.0 - mirror) * incident - emitted) * scale
    site = site_ref[...]
    lane = site & (LANES - 1)
    sheet = site >> 7
    sheets = source_ref.shape[1]
    sheet_iota = lax.broadcasted_iota(jnp.int32, (sheets, BLK), 0)
    lane_iota = lax.broadcasted_iota(jnp.int32, (LANES, BLK), 0)
    left = []
    right = []
    for b in range(blocks):
        here = jnp.where(sheet_iota == sheet[b : b + 1, :], absorbed[b : b + 1, :], 0.0)
        left.append(here)
        pick = jnp.where(lane_iota == lane[b : b + 1, :], 1.0, 0.0)
        right.append(pick.astype(jnp.bfloat16))
    left = jnp.concatenate(left, axis=1)
    right = jnp.concatenate(right, axis=1)
    source = jnp.zeros((sheets, LANES), jnp.float32)
    for part in parts_of(left, 3):
        source = source + lax.dot_general(part, right, NT, preferred_element_type=jnp.float32)
    for d in range(source_ref.shape[0]):
        source_ref[d] = source


def last(parts, emitted, mirror, site, cells):
    count = parts.shape[0]
    weight = cells / (mirror.shape[0] * BLK * 1.0)
    return pl.pallas_call(
        functools.partial(last_kernel, step_size * weight),
        out_shape=(
            jax.ShapeDtypeStruct(mirror.shape, jnp.float32),
            jax.ShapeDtypeStruct((count, cells // LANES, LANES), jnp.float32),
        ),
        compiler_params=params(16),
        cost_estimate=cost(10_000_000, 600_000),
        name="last",
    )(parts, emitted, mirror, site)


def first_planes(depth, ny, nz):
    return pl.BlockSpec((depth, ny, nz), lambda i: (0, 0, 0))


def pack_x_kernel(t_low, k_low, k_low_thin, t_high, k_high, k_high_thin, low_ref, high_ref):
    ny, nz = t_low.shape[1:]
    tail = 2 * DEPTH * ny
    piece = ny * LANES // nz
    for send, temp, cond, thin, at in (
        (low_ref, t_low, k_low, k_low_thin, DEPTH),
        (high_ref, t_high, k_high, k_high_thin, k_high_thin.shape[0] - DEPTH - 1),
    ):
        for p in range(DEPTH):
            send[p * ny : p * ny + ny, :] = temp[p]
            send[(DEPTH + p) * ny : (DEPTH + p + 1) * ny, :] = cond[p]
        for j in range(nz // LANES):
            send[tail:, j * LANES : (j + 1) * LANES] = thin[at, j * piece : (j + 1) * piece, :]


def pack_x(temp, cond):
    nx, ny, nz = temp.shape
    ends = 2 * DEPTH
    rows = 2 * DEPTH * ny + ny * LANES // nz
    first = pl.BlockSpec((DEPTH, ny, nz), lambda i: (0, 0, 0))
    final = pl.BlockSpec((DEPTH, ny, nz), lambda i: (nx // DEPTH - 1, 0, 0))
    first_thin = pl.BlockSpec((ends, ny, LANES), lambda i: (0, 0, 0))
    final_thin = pl.BlockSpec((ends, ny, LANES), lambda i: (nx // ends - 1, 0, 0))
    whole = pl.BlockSpec((rows, nz), lambda i: (0, 0))
    shape = jax.ShapeDtypeStruct((rows, nz), jnp.float32)
    return pl.pallas_call(
        pack_x_kernel,
        grid=(1,),
        out_shape=(shape, shape),
        in_specs=[first, first, first_thin, final, final, final_thin],
        out_specs=(whole, whole),
        compiler_params=params(56),
        cost_estimate=cost(0, 4 * rows * nz * 4),
        name="pack_x",
    )(temp, cond, cond, temp, cond, cond)


def pack_y_kernel(nx, ny, t0, k0, t7, k7, low_ref, high_ref, down_ref, up_ref):
    upper = lax.broadcasted_iota(jnp.int32, down_ref.shape[1:], 0) < ROWS

    def put(x, t_first, k_first, t_final, k_final):
        down_ref[x] = jnp.where(upper, t_first, pltpu.roll(k_first, ROWS, 0))
        up_ref[x] = jnp.where(upper, pltpu.roll(t_final, ROWS, 0), k_final)

    for side, base in ((low_ref, 0), (high_ref, DEPTH + nx)):
        for p in range(DEPTH):
            t_at, k_at = p * ny, (DEPTH + p) * ny
            put(
                base + p,
                side[t_at : t_at + 8, :],
                side[k_at : k_at + 8, :],
                side[t_at + ny - 8 : t_at + ny, :],
                side[k_at + ny - 8 : k_at + ny, :],
            )
    for x in range(nx):
        put(DEPTH + x, t0[x], k0[x], t7[x], k7[x])


def pack_y(temp, cond, low, high):
    nx, ny, nz = temp.shape
    first = pl.BlockSpec((nx, 8, nz), lambda i: (0, 0, 0))
    final = pl.BlockSpec((nx, 8, nz), lambda i: (0, ny // 8 - 1, 0))
    halo = pl.BlockSpec(low.shape, lambda i: (0, 0))
    tall = nx + 2 * DEPTH
    whole = pl.BlockSpec((tall, 8, nz), lambda i: (0, 0, 0))
    shape = jax.ShapeDtypeStruct((tall, 8, nz), jnp.float32)
    return pl.pallas_call(
        functools.partial(pack_y_kernel, nx, ny),
        grid=(1,),
        out_shape=(shape, shape),
        in_specs=[first, first, final, final, halo, halo],
        out_specs=(whole, whole),
        compiler_params=params(56),
        cost_estimate=cost(0, 4 * tall * 8 * nz * 4),
        name="pack_y",
    )(temp, cond, temp, cond, low, high)


def coupling(a, b):
    return jnp.where(jnp.minimum(a, b) > 0.0, (0.5 * step_size) * (a + b), 0.0)


def neighbours():
    slab, pair = lax.axis_index("slab"), lax.axis_index("pair")
    return slab > 0, slab < lax.axis_size("slab") - 1, pair > 0, pair < lax.axis_size("pair") - 1


def lane_tiles(nz):
    return [slice(j * LANES, (j + 1) * LANES) for j in range(nz // LANES)]


def prepare(cond, gx, gy, gz, gb):
    tall, wide, nz = cond.shape
    tiles = wide // 8
    lane = lax.broadcasted_iota(jnp.int32, (8, LANES), 1)
    half = 0.5 * step_size

    @pl.loop(0, tall)
    def _(x):
        after = jnp.minimum(x + 1, tall - 1)
        for z in lane_tiles(nz):
            last = z.stop == nz
            for t in range(tiles):
                rows = slice(8 * t, 8 * t + 8)
                here = cond[x, rows, z]
                gx[x, rows, z] = half * (here + cond[after, rows, z])
                if t + 1 < tiles:
                    beside = cond[x, 8 * t + 8 : 8 * t + 16, z]
                else:
                    beside = pltpu.roll(cond[x, :8, z], 7, 0)
                gy[x, rows, z] = half * (here + beside)
                turned = pltpu.roll(here, LANES - 1, 1)
                if last:
                    deeper = here
                else:
                    deeper = pltpu.roll(cond[x, rows, z.stop : z.stop + LANES], LANES - 1, 1)
                gz[x, rows, z] = half * (here + jnp.where(lane < LANES - 1, turned, deeper))
                if z.start == 0:
                    gb[x, rows, :] = step_size * here


def one_step(field, old, begin, end, store, gx, gy, gz, gb, carried):
    wide, nz = field.shape[2:]
    tiles = wide // 8
    lane = lax.broadcasted_iota(jnp.int32, (8, LANES), 1)
    sub = lax.broadcasted_iota(jnp.int32, (8, LANES), 0)
    _, _, has_below, has_above = neighbours()
    keep_above = (sub < 7) | has_above
    keep_below = (sub < 7) | has_below

    carried[...] = gx[begin - 1] * (field[old, begin] - field[old, begin - 1])

    @pl.loop(begin, end)
    def _(x):
        here, across_y = {}, {}
        spans = lane_tiles(nz)
        count = len(spans)

        def tile(t, j):
            if (t, j) not in here:
                here[t, j] = field[old, x, 8 * t : 8 * t + 8, spans[j]]
            return here[t, j]

        def y_flux(t, j):
            if (t, j) not in across_y:
                if t + 1 < tiles:
                    beside = tile(t + 1, j)
                else:
                    beside = pltpu.roll(tile(0, j), 7, 0)
                across_y[t, j] = gy[x, 8 * t : 8 * t + 8, spans[j]] * (beside - tile(t, j))
            return across_y[t, j]

        for t in range(tiles):
            rows = slice(8 * t, 8 * t + 8)
            turned = [pltpu.roll(tile(t, j), LANES - 1, 1) for j in range(count)]
            flux = []
            for j in range(count):
                deeper = turned[j + 1] if j + 1 < count else 0.0
                deeper = jnp.where(lane < LANES - 1, turned[j], deeper)
                flux.append(gz[x, rows, spans[j]] * (deeper - tile(t, j)))
            back = [pltpu.roll(f, 1, 1) for f in flux]
            for j in range(count):
                now = tile(t, j)
                low_z = back[j - 1] if j else gb[x, rows, :] * now
                low_z = jnp.where(lane > 0, back[j], low_z)
                x_flux = gx[x, rows, spans[j]] * (field[old, x + 1, rows, spans[j]] - now)
                low_x = carried[rows, spans[j]]
                carried[rows, spans[j]] = x_flux
                low_y = y_flux(t - 1, j) if t else pltpu.roll(y_flux(tiles - 1, j), 1, 0)
                new = now + (x_flux - low_x) + (y_flux(t, j) - low_y) + (flux[j] - low_z)
                if t:
                    new = jnp.where(keep_above if t <= ROWS else keep_below, new, 0.0)
                store(x, t, spans[j], new)


def thin_planes(cond, ny, thin_ref, base_plane):
    tall, _, wide, _ = cond.shape
    lane = lax.broadcasted_iota(jnp.int32, (wide, LANES), 1)
    y_lane = lax.broadcasted_iota(jnp.int32, (8, LANES), 1)
    for base in range(0, tall, 16):
        planes = min(16, tall - base)
        gathered = jnp.zeros((wide, LANES), jnp.float32)
        for g in range(planes):
            piece = cond[base + g, 0]
            if g:
                piece = pltpu.roll(piece, 8 * g, 1)
            gathered = jnp.where((lane >> 3) == g, piece, gathered)
        turned = jnp.concatenate(
            [gathered, jnp.zeros((LANES - wide, LANES), jnp.float32)], axis=0
        ).T
        for g in range(planes):
            rows = turned[8 * g : 8 * g + 8, :]
            moved = pltpu.roll(rows, LANES - wide, 1)
            thin_ref[base_plane + base + g] = jnp.where(
                y_lane < ny + ROWS, rows, jnp.where(y_lane >= LANES - ROWS, moved, 0.0)
            )


def first_round_kernel(
    t_ref, k_ref, low_ref, high_ref, below_ref, above_ref,
    out_ref, low_out, high_out, cond_out, thin_ref,
    loaded, field, gx, gy, gz, gb, carried, sems,
):
    nx, ny, nz = t_ref.shape
    tall, wide = nx + 2 * DEPTH, ny + 2 * ROWS
    tiles = wide // 8
    raw_t, raw_k = loaded.at[0], loaded.at[1]
    spans = lane_tiles(nz)
    copies = [
        pltpu.make_async_copy(
            ref.at[:, :, pl.ds(z.start, LANES)],
            loaded.at[which, pl.ds(DEPTH, nx), j, pl.ds(0, ny)],
            sems.at[which, j],
        )
        for which, ref in ((1, k_ref), (0, t_ref))
        for j, z in enumerate(spans)
    ]
    for copy in copies:
        copy.start()
    has_low, has_high, has_below, has_above = neighbours()
    upper = lax.broadcasted_iota(jnp.int32, (8, LANES), 0) < ROWS
    for side, base in ((low_ref, 0), (high_ref, DEPTH + nx)):
        for p in range(DEPTH):
            for j, z in enumerate(spans):
                raw_t[base + p, j, :ny] = side[p * ny : p * ny + ny, z]
                raw_k[base + p, j, :ny] = side[(DEPTH + p) * ny : (DEPTH + p + 1) * ny, z]

    @pl.loop(0, tall)
    def _(x):
        for j, z in enumerate(spans):
            down, up = above_ref[x, :, z], below_ref[x, :, z]
            raw_t[x, j, ny:] = jnp.where(upper, down, pltpu.roll(up, ROWS, 0))
            raw_k[x, j, ny:] = jnp.where(upper, pltpu.roll(down, ROWS, 0), up)

    for copy in copies:
        copy.wait()

    piece = ny * LANES // nz
    tail = 2 * DEPTH * ny
    thin_planes(raw_k, ny, thin_ref, HALO - DEPTH)
    for side, at in ((low_ref, HALO - DEPTH - 1), (high_ref, HALO + nx + DEPTH)):
        edge = [side[tail:, z] for z in lane_tiles(nz)]
        edge.append(jnp.zeros((LANES - ny, LANES), jnp.float32))
        turned = jnp.concatenate(edge, axis=0).T
        thin_ref[at] = turned[:8]
    for at in [*range(HALO - DEPTH - 1), *range(HALO + nx + DEPTH + 1, nx + 2 * HALO)]:
        thin_ref[at] = jnp.zeros((8, LANES), jnp.float32)

    @pl.loop(0, tall)
    def _(x):
        missing = (upper & jnp.logical_not(has_above)) | (
            jnp.logical_not(upper) & jnp.logical_not(has_below)
        )
        for j in range(len(spans)):
            edge = raw_k[x, j, ny:]
            last = jnp.broadcast_to(raw_k[x, j, ny - 1 : ny, :], edge.shape)
            first = jnp.broadcast_to(raw_k[x, j, 0:1, :], edge.shape)
            raw_k[x, j, ny:] = jnp.where(missing, jnp.where(upper, last, first), edge)

    @pl.when(jnp.logical_not(has_low))
    def _():
        for p in range(DEPTH):
            raw_k[p] = raw_k[DEPTH]

    @pl.when(jnp.logical_not(has_high))
    def _():
        for p in range(DEPTH):
            raw_k[DEPTH + nx + p] = raw_k[DEPTH + nx - 1]

    @pl.loop(0, tall)
    def _(x):
        for t in range(tiles):
            rows = pl.ds(t, 8, stride=tiles)
            for j, z in enumerate(spans):
                field[0, x, 8 * t : 8 * t + 8, z] = loaded[0, x, j, rows, :]
                cond_out[x, 8 * t : 8 * t + 8, z] = loaded[1, x, j, rows, :]

    prepare(cond_out, gx, gy, gz, gb)
    two_steps(field, gx, gy, gz, gb, carried, lambda x, t, z, new: out_ref.__setitem__(
        (x - DEPTH, slice(8 * t, 8 * t + 8), z), new))
    low_out[...] = out_ref[:DEPTH]
    high_out[...] = out_ref[nx - DEPTH :]


def two_steps(field, gx, gy, gz, gb, carried, store):
    tall = field.shape[1]
    has_low, has_high, _, _ = neighbours()
    for x in (1, tall - 2):
        field[1, x] = jnp.zeros(field.shape[2:], jnp.float32)

    def keep(x, t, z, new):
        field[1, x, 8 * t : 8 * t + 8, z] = new

    begin = jnp.where(has_low, 1, DEPTH)
    end = jnp.where(has_high, tall - 1, tall - DEPTH)
    one_step(field, 0, begin, end, keep, gx, gy, gz, gb, carried)
    one_step(field, 1, DEPTH, tall - DEPTH, store, gx, gy, gz, gb, carried)


def heat_scratch(tall, wide, nz):
    big = pltpu.VMEM((tall, wide, nz), jnp.float32)
    return [
        pltpu.VMEM((2, tall, wide, nz), jnp.float32),
        big,
        big,
        big,
        pltpu.VMEM((tall, wide, LANES), jnp.float32),
        pltpu.VMEM((wide, nz), jnp.float32),
    ]


def first_round(temp, cond, low, high, below, above):
    nx, ny, nz = temp.shape
    tall, wide = nx + 2 * DEPTH, ny + 2 * ROWS
    hbm = pl.BlockSpec(memory_space=pl.ANY)
    vmem = pl.BlockSpec(memory_space=pltpu.VMEM)
    plane = jax.ShapeDtypeStruct((DEPTH, wide, nz), jnp.float32)
    return pl.pallas_call(
        first_round_kernel,
        out_shape=(
            jax.ShapeDtypeStruct((nx, wide, nz), jnp.float32),
            plane,
            plane,
            jax.ShapeDtypeStruct((tall, wide, nz), jnp.float32),
            jax.ShapeDtypeStruct((nx + 2 * HALO, 8, LANES), jnp.float32),
        ),
        in_specs=[hbm, hbm] + [vmem] * 4,
        scratch_shapes=[pltpu.VMEM((2, tall, nz // LANES, wide, LANES), jnp.float32)]
        + heat_scratch(tall, wide, nz)
        + [pltpu.SemaphoreType.DMA((2, nz // LANES))],
        compiler_params=params(56),
        cost_estimate=cost(tall * wide * nz * 100, 12 * nx * ny * nz * 4),
        name="first_round",
    )(temp, cond, low, high, below, above)


def second_round_kernel(
    t_ref, low_ref, high_ref, k_ref, out_ref,
    cond, field, gx, gy, gz, gb, carried, placed, sems,
):
    nx, wide, nz = t_ref.shape
    ny = out_ref.shape[1]
    tiles = wide // 8
    copies = [
        pltpu.make_async_copy(k_ref, cond, sems.at[0]),
        pltpu.make_async_copy(t_ref, field.at[0, pl.ds(DEPTH, nx)], sems.at[1]),
        pltpu.make_async_copy(low_ref, field.at[0, pl.ds(0, DEPTH)], sems.at[2]),
        pltpu.make_async_copy(high_ref, field.at[0, pl.ds(DEPTH + nx, DEPTH)], sems.at[3]),
    ]
    for copy in copies:
        copy.start()
    copies[0].wait()
    prepare(cond, gx, gy, gz, gb)
    for copy in copies[1:]:
        copy.wait()

    def store(x, t, z, new):
        placed[x - DEPTH, z.start // LANES, pl.ds(t, 8, stride=tiles), :] = new

    two_steps(field, gx, gy, gz, gb, carried, store)

    @pl.loop(0, nx)
    def _(x):
        for j, z in enumerate(lane_tiles(out_ref.shape[2])):
            out_ref[x, :, z] = placed[x, j, :ny, :]


def second_round(temp, low, high, cond, shape):
    nx, wide, nz = temp.shape
    tall = cond.shape[0]
    hbm = pl.BlockSpec(memory_space=pl.ANY)
    return pl.pallas_call(
        second_round_kernel,
        out_shape=jax.ShapeDtypeStruct(shape, jnp.float32),
        in_specs=[hbm] * 4,
        scratch_shapes=[pltpu.VMEM((tall, wide, nz), jnp.float32)]
        + heat_scratch(tall, wide, nz)
        + [
            pltpu.VMEM((nx, nz // LANES, wide, LANES), jnp.float32),
            pltpu.SemaphoreType.DMA((4,)),
        ],
        compiler_params=params(56),
        cost_estimate=cost(tall * wide * nz * 60, 8 * nx * wide * nz * 4),
        name="second_round",
    )(temp, low, high, cond)


def source_kernel(ny, near_ref, flag_ref, all_ref, thin_ref, base_ref, out_ref):
    tall = thin_ref.shape[0]
    nx = tall - 2 * HALO
    sheets = all_ref.shape[1]
    sub = lax.broadcasted_iota(jnp.int32, (8, LANES), 0)
    y_lane = lax.broadcasted_iota(jnp.int32, (8, LANES), 1)

    def sheet(k):
        return all_ref[near_ref[k]] * flag_ref[k].astype(jnp.float32)

    def rows_of(slab):
        low, own, high = (sheet(3 * slab + k) for k in range(3))
        out = []
        for half in range(2):
            if half == 0:
                own_at, high_at, low_at = own, pltpu.roll(high, ny, 1), pltpu.roll(low, ny, 1)
            else:
                own_at, high_at, low_at = pltpu.roll(own, ny, 1), high, low
            out.append(
                jnp.where(
                    y_lane < ny,
                    own_at,
                    jnp.where(
                        y_lane < ny + HALO,
                        high_at,
                        jnp.where(y_lane >= LANES - HALO, low_at, 0.0),
                    ),
                )
            )
        return out

    lines = [rows_of(s) for s in range(3)]
    source = []
    for x in range(-HALO, nx + HALO):
        which, local = (x + nx) // nx, x % nx
        row = lines[which][local % 2][local // 2 : local // 2 + 1, :]
        source.append(jnp.where(sub == 0, jnp.broadcast_to(row, (8, LANES)), 0.0))

    cond = [thin_ref[x] for x in range(tall)]
    cx, cy, cz, centre = [], [], [], []
    for x in range(tall):
        here = cond[x]
        after = cond[min(x + 1, tall - 1)]
        before = cond[max(x - 1, 0)]
        y_after = pltpu.roll(here, LANES - 1, 1)
        y_before = pltpu.roll(here, 1, 1)
        z_after = jnp.where(sub == 7, 0.0, pltpu.roll(here, 7, 0))
        z_before = jnp.where(sub == 0, 0.0, pltpu.roll(here, 1, 0))
        cx.append(coupling(here, after))
        cy.append(coupling(here, y_after))
        cz.append(coupling(here, z_after))
        total = 6.0 * here
        for near in (after, before, y_after, y_before, z_after, z_before):
            total = total + jnp.where(near > 0.0, near, here)
        centre.append(1.0 - (0.5 * step_size) * total)

    added = source
    for step in range(1, STEPS):
        new = list(added)
        for x in range(step, tall - step):
            here = added[x]
            total = source[x] + centre[x] * here
            total = total + (cx[x] * added[x + 1] + cx[x - 1] * added[x - 1])
            total = total + cy[x] * pltpu.roll(here, LANES - 1, 1)
            total = total + pltpu.roll(cy[x] * here, 1, 1)
            total = total + cz[x] * pltpu.roll(here, 7, 0)
            new[x] = total + pltpu.roll(cz[x] * here, 1, 0)
        added = new

    lane = lax.broadcasted_iota(jnp.int32, (ny, LANES), 1)
    turned = jnp.concatenate(added[HALO : HALO + nx], axis=0).T[:ny]
    for x in range(nx):
        piece = turned if x == 0 else pltpu.roll(turned, LANES - 8 * x, 1)
        out_ref[x] = base_ref[x] + jnp.where(lane < STEPS, piece, 0.0)


def add_source(near, flag, everything, thin, base):
    nx, ny, nz = base.shape
    smem = pl.BlockSpec(memory_space=pltpu.SMEM)
    block = pl.BlockSpec((nx, ny, LANES), lambda i: (0, 0, 0))
    return pl.pallas_call(
        functools.partial(source_kernel, ny),
        grid=(1,),
        out_shape=jax.ShapeDtypeStruct(base.shape, jnp.float32),
        in_specs=[
            smem,
            smem,
            pl.BlockSpec(everything.shape, lambda i: (0, 0, 0)),
            pl.BlockSpec(thin.shape, lambda i: (0, 0, 0)),
            block,
        ],
        out_specs=block,
        input_output_aliases={4: 0},
        compiler_params=params(16),
        cost_estimate=cost(1_000_000, 2 * nx * ny * LANES * 4),
        name="add_source",
    )(near, flag, everything, thin, base)


def exchange(copies):
    return lax.all_to_all(copies, ("slab", "pair"), split_axis=0, concat_axis=0, tiled=True)


def both_ways(low, high, axis):
    count = lax.axis_size(axis)
    forward = [(i, i + 1) for i in range(count - 1)]
    backward = [(target, source) for source, target in forward]
    from_low = lax.ppermute(high, axis, forward)
    from_high = lax.ppermute(low, axis, backward)
    return from_low, from_high


def shards(
    initial_warmth,
    heat_passing_coefficient,
    mirror_fraction,
    element_facing_site,
    tile_block_couples,
    active_slot_count,
    view_factor_blocks,
):
    nx, ny, _ = initial_warmth.shape
    slabs, pairs = lax.axis_size("slab"), lax.axis_size("pair")
    count = slabs * pairs
    blocks = mirror_fraction.shape[0]
    couples = tile_block_couples.T

    emitted, copies = emit(initial_warmth, element_facing_site, mirror_fraction, count)
    send_low, send_high = pack_x(initial_warmth, heat_passing_coefficient)
    low, high = both_ways(send_low, send_high, "slab")
    for sweep in range(SWEEPS):
        whole = exchange(copies).reshape(count * blocks, BLK)
        term = tile_terms(whole, couples, active_slot_count, view_factor_blocks)
        parts = exchange(term.reshape(count, blocks, BLK))
        if sweep + 1 < SWEEPS:
            copies = middle(parts, emitted, mirror_fraction)
    radiosity, source = last(parts, emitted, mirror_fraction, element_facing_site, nx * ny)
    everything = exchange(source)

    send_down, send_up = pack_y(initial_warmth, heat_passing_coefficient, low, high)
    below, above = both_ways(send_down, send_up, "pair")
    temp, send_low, send_high, cond, thin = first_round(
        initial_warmth, heat_passing_coefficient, low, high, below, above
    )
    low, high = both_ways(send_low, send_high, "slab")
    base = second_round(temp, low, high, cond, initial_warmth.shape)

    slab, pair = lax.axis_index("slab"), lax.axis_index("pair")
    near, flag = [], []
    for ds in (-1, 0, 1):
        for dp in (-1, 0, 1):
            s, p = slab + ds, pair + dp
            inside = (s >= 0) & (s < slabs) & (p >= 0) & (p < pairs)
            near.append(jnp.where(inside, s * pairs + p, 0))
            flag.append(inside)
    near = jnp.stack(near).astype(jnp.int32)
    flag = jnp.stack(flag).astype(jnp.int32)
    warmed_liner = add_source(near, flag, everything, thin, base)
    return (radiosity, warmed_liner)


def solution(mesh):
    return jax.shard_map(
        shards,
        mesh=mesh,
        in_specs=(
            P("slab", "pair", None),
            P("slab", "pair", None),
            P(("slab", "pair"), None),
            P(("slab", "pair"), None),
            P(("slab", "pair"), None),
            P(("slab", "pair")),
            P(("slab", "pair"), None, None),
        ),
        out_specs=(P(("slab", "pair"), None), P("slab", "pair", None)),
        check_vma=False,
    )
```

```python
import functools

import jax
import jax.numpy as jnp
from jax import lax
from jax.experimental import pallas as pl
from jax.experimental.pallas import tpu as pltpu
from jax.sharding import PartitionSpec as P

BLK = 128
SWEEPS = 2
STEPS = 4
HALO = STEPS
DEPTH = STEPS // 2
ROWS = STEPS
LANES = 128
CHUNK = 16

step_size = 0.07

NT = (((1,), (1,)), ((), ()))
NN = (((1,), (0,)), ((), ()))


def params(mib):
    return pltpu.CompilerParams(vmem_limit_bytes=mib * 1024 * 1024)


def cost(flops, nbytes):
    return pl.CostEstimate(flops=flops, bytes_accessed=nbytes, transcendentals=0)


def parts_of(x, count):
    out = []
    for _ in range(count - 1):
        part = x.astype(jnp.bfloat16)
        out.append(part)
        x = x - part.astype(jnp.float32)
    out.append(x.astype(jnp.bfloat16))
    return out


def emit_kernel(temp_ref, site_ref, mirror_ref, emitted_ref, copies_ref):
    nx, ny, _ = temp_ref.shape
    sheets = nx * ny // LANES
    per = LANES // ny
    lanes = lax.broadcasted_iota(jnp.int32, (LANES, LANES), 1)
    gathered = jnp.zeros((LANES, LANES), jnp.float32)
    for r in range(sheets):
        piece = temp_ref[per * r : per * r + per].reshape(LANES, LANES)
        if r:
            piece = pltpu.roll(piece, r, 1)
        gathered = jnp.where(lanes == r, piece, gathered)
    plane = gathered.T[:sheets]
    for half in range(site_ref.shape[0] // 8):
        rows = pl.ds(half * 8, 8)
        site = site_ref[rows, :]
        lane = site & (LANES - 1)
        sheet = site >> 7
        warmth = jnp.zeros(site.shape, jnp.float32)
        for r in range(sheets):
            line = jnp.broadcast_to(plane[r : r + 1, :], site.shape)
            picked = jnp.take_along_axis(line, lane, axis=1)
            warmth = jnp.where(sheet == r, picked, warmth)
        square = warmth * warmth
        emitted = (1.0 - mirror_ref[rows, :]) * (square * square)
        emitted_ref[rows, :] = emitted
        for d in range(copies_ref.shape[0]):
            copies_ref[d, rows, :] = emitted


def emit(temp, site, mirror, count):
    shape = mirror.shape
    nx, ny, _ = temp.shape
    patch = pl.BlockSpec(shape, lambda i: (0, 0))
    return pl.pallas_call(
        emit_kernel,
        grid=(1,),
        out_shape=(
            jax.ShapeDtypeStruct(shape, jnp.float32),
            jax.ShapeDtypeStruct((count,) + shape, jnp.float32),
        ),
        in_specs=[pl.BlockSpec((nx, ny, LANES), lambda i: (0, 0, 0)), patch, patch],
        out_specs=(patch, pl.BlockSpec((count,) + shape, lambda i: (0, 0, 0))),
        compiler_params=params(64),
        cost_estimate=cost(10_000, 900_000),
        name="emit",
    )(temp, site, mirror)


def tiles_kernel(
    live_ref, pairs_ref, lanes_ref, whole_ref, tiles_ref, out_ref, held, terms, sems
):
    slots = held.shape[0]
    live = live_ref[0]
    chunks = (live + CHUNK - 1) // CHUNK

    def chunk_copy(c):
        span = pl.ds(c * CHUNK, CHUNK)
        return pltpu.make_async_copy(tiles_ref.at[span], held.at[span], sems.at[c])

    @pl.loop(0, chunks)
    def _(c):
        chunk_copy(c).start()

    top = lax.broadcasted_iota(jnp.int32, (8, BLK), 0) == 0

    def split_row(block):
        row = jnp.broadcast_to(whole_ref[pl.ds(block, 1), :], (8, BLK))
        high = row.astype(jnp.bfloat16).astype(jnp.float32)
        return jnp.where(top, high, row - high)

    def vectors(a, b):
        stacked = jnp.concatenate([split_row(a), split_row(b)], axis=0)
        stacked = stacked.astype(jnp.bfloat16)
        return jnp.concatenate([stacked, stacked], axis=1)

    @pl.loop(0, chunks)
    def _(c):
        chunk_copy(c).wait()
        for u in range(0, CHUNK, 2):
            t = c * CHUNK + u
            high_a, low_a = parts_of(held[t], 2)
            high_b, low_b = parts_of(held[t + 1], 2)
            both = jnp.concatenate(
                [
                    jnp.concatenate([high_a, high_b], axis=1),
                    jnp.concatenate([low_a, low_b], axis=1),
                ],
                axis=0,
            )
            second = lax.dot_general(
                vectors(pairs_ref[0, t], pairs_ref[0, t + 1]),
                both,
                NN,
                preferred_element_type=jnp.float32,
            )
            turned = jnp.concatenate(
                [
                    jnp.concatenate([high_a, low_a], axis=1),
                    jnp.concatenate([high_b, low_b], axis=1),
                ],
                axis=0,
            )
            first = lax.dot_general(
                vectors(pairs_ref[1, t], pairs_ref[1, t + 1]),
                turned,
                NT,
                preferred_element_type=jnp.float32,
            )
            for side, result in ((0, first), (1, second)):
                terms[side, pl.ds(t, 1), :] = result[0:1, :BLK] + result[1:2, :BLK]
                terms[side, pl.ds(t + 1, 1), :] = result[8:9, BLK:] + result[9:10, BLK:]

    used = lax.broadcasted_iota(jnp.int32, (slots, BLK), 0) < live
    used_lane = lax.broadcasted_iota(jnp.int32, (1, slots), 1) < live
    blocks = out_ref.shape[0]
    group = min(blocks, 512)
    split = []
    for side in range(2):
        masked = jnp.where(used, terms[side], 0.0)
        split.append(jnp.concatenate(parts_of(masked, 2), axis=1))
    for base in range(0, blocks, group):
        rows = lax.broadcasted_iota(jnp.int32, (group, slots), 0) + base
        total = jnp.zeros((group, 2 * BLK), jnp.float32)
        for side in range(2):
            target = jnp.where(used_lane, lanes_ref[side : side + 1, :], -1)
            choose = jnp.where(rows == target, 1.0, 0.0).astype(jnp.bfloat16)
            total = total + jnp.dot(choose, split[side], preferred_element_type=jnp.float32)
        out_ref[base : base + group, :] = total[:, :BLK] + total[:, BLK:]


def tile_terms(whole, couples, live, tiles):
    slots = tiles.shape[0]
    smem = pl.BlockSpec(memory_space=pltpu.SMEM)
    vmem = pl.BlockSpec(memory_space=pltpu.VMEM)
    return pl.pallas_call(
        tiles_kernel,
        out_shape=jax.ShapeDtypeStruct(whole.shape, jnp.float32),
        in_specs=[smem, smem, vmem, vmem, pl.BlockSpec(memory_space=pl.ANY)],
        out_specs=vmem,
        scratch_shapes=[
            pltpu.VMEM(tiles.shape, jnp.float32),
            pltpu.VMEM((2, slots, BLK), jnp.float32),
            pltpu.SemaphoreType.DMA((slots // CHUNK,)),
        ],
        compiler_params=params(64),
        cost_estimate=cost(slots * BLK * BLK * 32, slots * BLK * BLK * 4),
        name="tiles",
    )(live, couples, couples, whole, tiles)


def sum_parts(parts_ref, rows):
    total = parts_ref[0, rows, :]
    for d in range(1, parts_ref.shape[0]):
        total = total + parts_ref[d, rows, :]
    return total


def middle_kernel(parts_ref, emitted_ref, mirror_ref, copies_ref):
    for half in range(emitted_ref.shape[0] // 8):
        rows = pl.ds(half * 8, 8)
        incident = sum_parts(parts_ref, rows)
        radiosity = emitted_ref[rows, :] + mirror_ref[rows, :] * incident
        for d in range(copies_ref.shape[0]):
            copies_ref[d, rows, :] = radiosity


def middle(parts, emitted, mirror):
    return pl.pallas_call(
        middle_kernel,
        out_shape=jax.ShapeDtypeStruct(parts.shape, jnp.float32),
        compiler_params=params(64),
        cost_estimate=cost(100_000, 600_000),
        name="middle",
    )(parts, emitted, mirror)


def last_kernel(scale, parts_ref, emitted_ref, mirror_ref, site_ref, rad_ref, source_ref):
    blocks = emitted_ref.shape[0]
    incident = sum_parts(parts_ref, slice(None))
    emitted = emitted_ref[...]
    mirror = mirror_ref[...]
    rad_ref[...] = emitted + mirror * incident
    absorbed = ((1.0 - mirror) * incident - emitted) * scale
    site = site_ref[...]
    lane = site & (LANES - 1)
    sheet = site >> 7
    sheets = source_ref.shape[1]
    sheet_iota = lax.broadcasted_iota(jnp.int32, (sheets, BLK), 0)
    lane_iota = lax.broadcasted_iota(jnp.int32, (LANES, BLK), 0)
    left = []
    right = []
    for b in range(blocks):
        here = jnp.where(sheet_iota == sheet[b : b + 1, :], absorbed[b : b + 1, :], 0.0)
        left.append(here)
        pick = jnp.where(lane_iota == lane[b : b + 1, :], 1.0, 0.0)
        right.append(pick.astype(jnp.bfloat16))
    left = jnp.concatenate(left, axis=1)
    right = jnp.concatenate(right, axis=1)
    source = jnp.zeros((sheets, LANES), jnp.float32)
    for part in parts_of(left, 3):
        source = source + lax.dot_general(part, right, NT, preferred_element_type=jnp.float32)
    for d in range(source_ref.shape[0]):
        source_ref[d] = source


def last(parts, emitted, mirror, site, cells):
    count = parts.shape[0]
    weight = cells / (mirror.shape[0] * BLK * 1.0)
    return pl.pallas_call(
        functools.partial(last_kernel, step_size * weight),
        out_shape=(
            jax.ShapeDtypeStruct(mirror.shape, jnp.float32),
            jax.ShapeDtypeStruct((count, cells // LANES, LANES), jnp.float32),
        ),
        compiler_params=params(64),
        cost_estimate=cost(10_000_000, 600_000),
        name="last",
    )(parts, emitted, mirror, site)


def first_planes(depth, ny, nz):
    return pl.BlockSpec((depth, ny, nz), lambda i: (0, 0, 0))


def pack_x_kernel(t_low, k_low, k_low_thin, t_high, k_high, k_high_thin, low_ref, high_ref):
    ny, nz = t_low.shape[1:]
    tail = 2 * DEPTH * ny
    piece = ny * LANES // nz
    for send, temp, cond, thin, at in (
        (low_ref, t_low, k_low, k_low_thin, DEPTH),
        (high_ref, t_high, k_high, k_high_thin, k_high_thin.shape[0] - DEPTH - 1),
    ):
        for p in range(DEPTH):
            send[p * ny : p * ny + ny, :] = temp[p]
            send[(DEPTH + p) * ny : (DEPTH + p + 1) * ny, :] = cond[p]
        for j in range(nz // LANES):
            send[tail:, j * LANES : (j + 1) * LANES] = thin[at, j * piece : (j + 1) * piece, :]


def pack_x(temp, cond):
    nx, ny, nz = temp.shape
    ends = 2 * DEPTH
    rows = 2 * DEPTH * ny + ny * LANES // nz
    first = pl.BlockSpec((DEPTH, ny, nz), lambda i: (0, 0, 0))
    final = pl.BlockSpec((DEPTH, ny, nz), lambda i: (nx // DEPTH - 1, 0, 0))
    first_thin = pl.BlockSpec((ends, ny, LANES), lambda i: (0, 0, 0))
    final_thin = pl.BlockSpec((ends, ny, LANES), lambda i: (nx // ends - 1, 0, 0))
    whole = pl.BlockSpec((rows, nz), lambda i: (0, 0))
    shape = jax.ShapeDtypeStruct((rows, nz), jnp.float32)
    return pl.pallas_call(
        pack_x_kernel,
        grid=(1,),
        out_shape=(shape, shape),
        in_specs=[first, first, first_thin, final, final, final_thin],
        out_specs=(whole, whole),
        compiler_params=params(64),
        cost_estimate=cost(0, 4 * rows * nz * 4),
        name="pack_x",
    )(temp, cond, cond, temp, cond, cond)


def pack_y_kernel(nx, ny, t0, k0, t7, k7, low_ref, high_ref, down_ref, up_ref):
    upper = lax.broadcasted_iota(jnp.int32, down_ref.shape[1:], 0) < ROWS

    def put(x, t_first, k_first, t_final, k_final):
        down_ref[x] = jnp.where(upper, t_first, pltpu.roll(k_first, ROWS, 0))
        up_ref[x] = jnp.where(upper, pltpu.roll(t_final, ROWS, 0), k_final)

    for side, base in ((low_ref, 0), (high_ref, DEPTH + nx)):
        for p in range(DEPTH):
            t_at, k_at = p * ny, (DEPTH + p) * ny
            put(
                base + p,
                side[t_at : t_at + 8, :],
                side[k_at : k_at + 8, :],
                side[t_at + ny - 8 : t_at + ny, :],
                side[k_at + ny - 8 : k_at + ny, :],
            )
    for x in range(nx):
        put(DEPTH + x, t0[x], k0[x], t7[x], k7[x])


def pack_y(temp, cond, low, high):
    nx, ny, nz = temp.shape
    first = pl.BlockSpec((nx, 8, nz), lambda i: (0, 0, 0))
    final = pl.BlockSpec((nx, 8, nz), lambda i: (0, ny // 8 - 1, 0))
    halo = pl.BlockSpec(low.shape, lambda i: (0, 0))
    tall = nx + 2 * DEPTH
    whole = pl.BlockSpec((tall, 8, nz), lambda i: (0, 0, 0))
    shape = jax.ShapeDtypeStruct((tall, 8, nz), jnp.float32)
    return pl.pallas_call(
        functools.partial(pack_y_kernel, nx, ny),
        grid=(1,),
        out_shape=(shape, shape),
        in_specs=[first, first, final, final, halo, halo],
        out_specs=(whole, whole),
        compiler_params=params(64),
        cost_estimate=cost(0, 4 * tall * 8 * nz * 4),
        name="pack_y",
    )(temp, cond, temp, cond, low, high)


def coupling(a, b):
    return jnp.where(jnp.minimum(a, b) > 0.0, (0.5 * step_size) * (a + b), 0.0)


def neighbours():
    slab, pair = lax.axis_index("slab"), lax.axis_index("pair")
    return slab > 0, slab < lax.axis_size("slab") - 1, pair > 0, pair < lax.axis_size("pair") - 1


def lane_tiles(nz):
    return [slice(j * LANES, (j + 1) * LANES) for j in range(nz // LANES)]


class Lagging:
    def __init__(self, depth):
        self.depth = depth
        self.waiting = []

    def add(self, store):
        self.waiting.append(store)
        if len(self.waiting) > self.depth:
            self.waiting.pop(0)()

    def finish(self):
        for store in self.waiting:
            store()
        self.waiting = []


def put(ref, index, value):
    return lambda: ref.__setitem__(index, value)


def prepare(cond, gx, gy, gz, gb):
    tall, wide, nz = cond.shape
    tiles = wide // 8
    lane = lax.broadcasted_iota(jnp.int32, (8, LANES), 1)
    half = 0.5 * step_size

    @pl.loop(0, tall)
    def _(x):
        after = jnp.minimum(x + 1, tall - 1)
        stores = Lagging(16)
        for z in lane_tiles(nz):
            last = z.stop == nz
            for t in range(tiles):
                rows = slice(8 * t, 8 * t + 8)
                here = cond[x, rows, z]
                stores.add(put(gx, (x, rows, z), half * (here + cond[after, rows, z])))
                if t + 1 < tiles:
                    beside = cond[x, 8 * t + 8 : 8 * t + 16, z]
                else:
                    beside = pltpu.roll(cond[x, :8, z], 7, 0)
                stores.add(put(gy, (x, rows, z), half * (here + beside)))
                turned = pltpu.roll(here, LANES - 1, 1)
                if last:
                    deeper = here
                else:
                    deeper = pltpu.roll(cond[x, rows, z.stop : z.stop + LANES], LANES - 1, 1)
                deeper = jnp.where(lane < LANES - 1, turned, deeper)
                stores.add(put(gz, (x, rows, z), half * (here + deeper)))
                if z.start == 0:
                    stores.add(put(gb, (x, rows), step_size * here))
        stores.finish()


def one_step(field, begin, end, target, gx, gy, gz, gb, carried):
    wide, nz = field.shape[1:]
    tiles = wide // 8
    lane = lax.broadcasted_iota(jnp.int32, (8, LANES), 1)
    sub = lax.broadcasted_iota(jnp.int32, (8, LANES), 0)
    _, _, has_below, has_above = neighbours()
    keep_above = (sub < 7) | has_above
    keep_below = (sub < 7) | has_below

    carried[...] = gx[begin - 1] * (field[begin] - field[begin - 1])

    @pl.loop(begin, end)
    def _(x):
        here, across_y = {}, {}
        stores = Lagging(16)
        spans = lane_tiles(nz)
        count = len(spans)

        def tile(t, j):
            if (t, j) not in here:
                here[t, j] = field[x, 8 * t : 8 * t + 8, spans[j]]
            return here[t, j]

        def y_flux(t, j):
            if (t, j) not in across_y:
                if t + 1 < tiles:
                    beside = tile(t + 1, j)
                else:
                    beside = pltpu.roll(tile(0, j), 7, 0)
                across_y[t, j] = gy[x, 8 * t : 8 * t + 8, spans[j]] * (beside - tile(t, j))
            return across_y[t, j]

        for t in range(tiles):
            rows = slice(8 * t, 8 * t + 8)
            turned = [pltpu.roll(tile(t, j), LANES - 1, 1) for j in range(count)]
            flux = []
            for j in range(count):
                deeper = turned[j + 1] if j + 1 < count else 0.0
                deeper = jnp.where(lane < LANES - 1, turned[j], deeper)
                flux.append(gz[x, rows, spans[j]] * (deeper - tile(t, j)))
            back = [pltpu.roll(f, 1, 1) for f in flux]
            for j in range(count):
                now = tile(t, j)
                low_z = back[j - 1] if j else gb[x, rows, :] * now
                low_z = jnp.where(lane > 0, back[j], low_z)
                x_flux = gx[x, rows, spans[j]] * (field[x + 1, rows, spans[j]] - now)
                low_x = carried[rows, spans[j]]
                stores.add(put(carried, (rows, spans[j]), x_flux))
                low_y = y_flux(t - 1, j) if t else pltpu.roll(y_flux(tiles - 1, j), 1, 0)
                new = now + (x_flux - low_x) + (y_flux(t, j) - low_y) + (flux[j] - low_z)
                if t:
                    new = jnp.where(keep_above if t <= ROWS else keep_below, new, 0.0)
                stores.add(put(*target(x, t, spans[j]), new))
        stores.finish()


def thin_planes(cond, ny, thin_ref, base_plane):
    tall, _, wide, _ = cond.shape
    lane = lax.broadcasted_iota(jnp.int32, (wide, LANES), 1)
    y_lane = lax.broadcasted_iota(jnp.int32, (8, LANES), 1)
    for base in range(0, tall, 16):
        planes = min(16, tall - base)
        gathered = jnp.zeros((wide, LANES), jnp.float32)
        for g in range(planes):
            piece = cond[base + g, 0]
            if g:
                piece = pltpu.roll(piece, 8 * g, 1)
            gathered = jnp.where((lane >> 3) == g, piece, gathered)
        turned = jnp.concatenate(
            [gathered, jnp.zeros((LANES - wide, LANES), jnp.float32)], axis=0
        ).T
        for g in range(planes):
            rows = turned[8 * g : 8 * g + 8, :]
            moved = pltpu.roll(rows, LANES - wide, 1)
            thin_ref[base_plane + base + g] = jnp.where(
                y_lane < ny + ROWS, rows, jnp.where(y_lane >= LANES - ROWS, moved, 0.0)
            )


def first_round_kernel(
    t_ref, k_ref, low_ref, high_ref, below_ref, above_ref,
    out_ref, low_out, high_out, cond_out, thin_ref,
    loaded, field, between, gx, gy, gz, gb, carried, sems,
):
    nx, ny, nz = t_ref.shape
    tall, wide = nx + 2 * DEPTH, ny + 2 * ROWS
    tiles = wide // 8
    raw_t, raw_k = loaded.at[0], loaded.at[1]
    spans = lane_tiles(nz)
    copies = [
        pltpu.make_async_copy(
            ref.at[:, :, pl.ds(z.start, LANES)],
            loaded.at[which, pl.ds(DEPTH, nx), j, pl.ds(0, ny)],
            sems.at[which, j],
        )
        for which, ref in ((1, k_ref), (0, t_ref))
        for j, z in enumerate(spans)
    ]
    for copy in copies:
        copy.start()
    has_low, has_high, has_below, has_above = neighbours()
    upper = lax.broadcasted_iota(jnp.int32, (8, LANES), 0) < ROWS
    for side, base in ((low_ref, 0), (high_ref, DEPTH + nx)):
        for p in range(DEPTH):
            for j, z in enumerate(spans):
                raw_t[base + p, j, :ny] = side[p * ny : p * ny + ny, z]
                raw_k[base + p, j, :ny] = side[(DEPTH + p) * ny : (DEPTH + p + 1) * ny, z]

    @pl.loop(0, tall)
    def _(x):
        for j, z in enumerate(spans):
            down, up = above_ref[x, :, z], below_ref[x, :, z]
            raw_t[x, j, ny:] = jnp.where(upper, down, pltpu.roll(up, ROWS, 0))
            raw_k[x, j, ny:] = jnp.where(upper, pltpu.roll(down, ROWS, 0), up)

    for copy in copies:
        copy.wait()

    piece = ny * LANES // nz
    tail = 2 * DEPTH * ny
    thin_planes(raw_k, ny, thin_ref, HALO - DEPTH)
    for side, at in ((low_ref, HALO - DEPTH - 1), (high_ref, HALO + nx + DEPTH)):
        edge = [side[tail:, z] for z in lane_tiles(nz)]
        edge.append(jnp.zeros((LANES - ny, LANES), jnp.float32))
        turned = jnp.concatenate(edge, axis=0).T
        thin_ref[at] = turned[:8]
    for at in [*range(HALO - DEPTH - 1), *range(HALO + nx + DEPTH + 1, nx + 2 * HALO)]:
        thin_ref[at] = jnp.zeros((8, LANES), jnp.float32)

    @pl.loop(0, tall)
    def _(x):
        missing = (upper & jnp.logical_not(has_above)) | (
            jnp.logical_not(upper) & jnp.logical_not(has_below)
        )
        for j in range(len(spans)):
            edge = raw_k[x, j, ny:]
            last = jnp.broadcast_to(raw_k[x, j, ny - 1 : ny, :], edge.shape)
            first = jnp.broadcast_to(raw_k[x, j, 0:1, :], edge.shape)
            raw_k[x, j, ny:] = jnp.where(missing, jnp.where(upper, last, first), edge)

    @pl.when(jnp.logical_not(has_low))
    def _():
        for p in range(DEPTH):
            raw_k[p] = raw_k[DEPTH]

    @pl.when(jnp.logical_not(has_high))
    def _():
        for p in range(DEPTH):
            raw_k[DEPTH + nx + p] = raw_k[DEPTH + nx - 1]

    @pl.loop(0, tall)
    def _(x):
        stores = Lagging(16)
        for t in range(tiles):
            rows = pl.ds(t, 8, stride=tiles)
            for j, z in enumerate(spans):
                stores.add(put(field, (x, slice(8 * t, 8 * t + 8), z), loaded[0, x, j, rows, :]))
                stores.add(put(cond_out, (x, slice(8 * t, 8 * t + 8), z), loaded[1, x, j, rows, :]))
        stores.finish()

    prepare(cond_out, gx, gy, gz, gb)

    def target(x, t, z):
        return out_ref, (x - DEPTH, slice(8 * t, 8 * t + 8), z)

    two_steps(field, between, gx, gy, gz, gb, carried, target)
    low_out[...] = out_ref[:DEPTH]
    high_out[...] = out_ref[nx - DEPTH :]


def two_steps(field, between, gx, gy, gz, gb, carried, target):
    tall = field.shape[0]
    has_low, has_high, _, _ = neighbours()
    for x in (1, tall - 2):
        between[x] = jnp.zeros(field.shape[1:], jnp.float32)

    def inner(x, t, z):
        return between, (x, slice(8 * t, 8 * t + 8), z)

    begin = jnp.where(has_low, 1, DEPTH)
    end = jnp.where(has_high, tall - 1, tall - DEPTH)
    one_step(field, begin, end, inner, gx, gy, gz, gb, carried)
    one_step(between, DEPTH, tall - DEPTH, target, gx, gy, gz, gb, carried)


def heat_scratch(tall, wide, nz):
    big = pltpu.VMEM((tall, wide, nz), jnp.float32)
    return [
        big,
        big,
        big,
        big,
        big,
        pltpu.VMEM((tall, wide, LANES), jnp.float32),
        pltpu.VMEM((wide, nz), jnp.float32),
    ]


def first_round(temp, cond, low, high, below, above):
    nx, ny, nz = temp.shape
    tall, wide = nx + 2 * DEPTH, ny + 2 * ROWS
    hbm = pl.BlockSpec(memory_space=pl.ANY)
    vmem = pl.BlockSpec(memory_space=pltpu.VMEM)
    plane = jax.ShapeDtypeStruct((DEPTH, wide, nz), jnp.float32)
    return pl.pallas_call(
        first_round_kernel,
        out_shape=(
            jax.ShapeDtypeStruct((nx, wide, nz), jnp.float32),
            plane,
            plane,
            jax.ShapeDtypeStruct((tall, wide, nz), jnp.float32),
            jax.ShapeDtypeStruct((nx + 2 * HALO, 8, LANES), jnp.float32),
        ),
        in_specs=[hbm, hbm] + [vmem] * 4,
        scratch_shapes=[pltpu.VMEM((2, tall, nz // LANES, wide, LANES), jnp.float32)]
        + heat_scratch(tall, wide, nz)
        + [pltpu.SemaphoreType.DMA((2, nz // LANES))],
        compiler_params=params(64),
        cost_estimate=cost(tall * wide * nz * 100, 12 * nx * ny * nz * 4),
        name="first_round",
    )(temp, cond, low, high, below, above)


def second_round_kernel(
    t_ref, low_ref, high_ref, k_ref, out_ref,
    cond, field, between, gx, gy, gz, gb, carried, placed, sems,
):
    nx, wide, nz = t_ref.shape
    ny = out_ref.shape[1]
    tiles = wide // 8
    copies = [
        pltpu.make_async_copy(k_ref, cond, sems.at[0]),
        pltpu.make_async_copy(t_ref, field.at[pl.ds(DEPTH, nx)], sems.at[1]),
        pltpu.make_async_copy(low_ref, field.at[pl.ds(0, DEPTH)], sems.at[2]),
        pltpu.make_async_copy(high_ref, field.at[pl.ds(DEPTH + nx, DEPTH)], sems.at[3]),
    ]
    for copy in copies:
        copy.start()
    copies[0].wait()
    prepare(cond, gx, gy, gz, gb)
    for copy in copies[1:]:
        copy.wait()

    def target(x, t, z):
        return placed, (x - DEPTH, z.start // LANES, pl.ds(t, 8, stride=tiles))

    two_steps(field, between, gx, gy, gz, gb, carried, target)

    @pl.loop(0, nx)
    def _(x):
        for j, z in enumerate(lane_tiles(out_ref.shape[2])):
            out_ref[x, :, z] = placed[x, j, :ny, :]


def second_round(temp, low, high, cond, shape):
    nx, wide, nz = temp.shape
    tall = cond.shape[0]
    hbm = pl.BlockSpec(memory_space=pl.ANY)
    return pl.pallas_call(
        second_round_kernel,
        out_shape=jax.ShapeDtypeStruct(shape, jnp.float32),
        in_specs=[hbm] * 4,
        scratch_shapes=[pltpu.VMEM((tall, wide, nz), jnp.float32)]
        + heat_scratch(tall, wide, nz)
        + [
            pltpu.VMEM((nx, nz // LANES, wide, LANES), jnp.float32),
            pltpu.SemaphoreType.DMA((4,)),
        ],
        compiler_params=params(64),
        cost_estimate=cost(tall * wide * nz * 60, 8 * nx * wide * nz * 4),
        name="second_round",
    )(temp, low, high, cond)


def source_kernel(ny, near_ref, flag_ref, all_ref, thin_ref, base_ref, out_ref):
    tall = thin_ref.shape[0]
    nx = tall - 2 * HALO
    sheets = all_ref.shape[1]
    sub = lax.broadcasted_iota(jnp.int32, (8, LANES), 0)
    y_lane = lax.broadcasted_iota(jnp.int32, (8, LANES), 1)

    def sheet(k):
        return all_ref[near_ref[k]] * flag_ref[k].astype(jnp.float32)

    def rows_of(slab):
        low, own, high = (sheet(3 * slab + k) for k in range(3))
        out = []
        for half in range(2):
            if half == 0:
                own_at, high_at, low_at = own, pltpu.roll(high, ny, 1), pltpu.roll(low, ny, 1)
            else:
                own_at, high_at, low_at = pltpu.roll(own, ny, 1), high, low
            out.append(
                jnp.where(
                    y_lane < ny,
                    own_at,
                    jnp.where(
                        y_lane < ny + HALO,
                        high_at,
                        jnp.where(y_lane >= LANES - HALO, low_at, 0.0),
                    ),
                )
            )
        return out

    lines = [rows_of(s) for s in range(3)]
    source = []
    for x in range(-HALO, nx + HALO):
        which, local = (x + nx) // nx, x % nx
        row = lines[which][local % 2][local // 2 : local // 2 + 1, :]
        source.append(jnp.where(sub == 0, jnp.broadcast_to(row, (8, LANES)), 0.0))

    cond = [thin_ref[x] for x in range(tall)]
    cx, cy, cz, centre = [], [], [], []
    for x in range(tall):
        here = cond[x]
        after = cond[min(x + 1, tall - 1)]
        before = cond[max(x - 1, 0)]
        y_after = pltpu.roll(here, LANES - 1, 1)
        y_before = pltpu.roll(here, 1, 1)
        z_after = jnp.where(sub == 7, 0.0, pltpu.roll(here, 7, 0))
        z_before = jnp.where(sub == 0, 0.0, pltpu.roll(here, 1, 0))
        cx.append(coupling(here, after))
        cy.append(coupling(here, y_after))
        cz.append(coupling(here, z_after))
        total = 6.0 * here
        for near in (after, before, y_after, y_before, z_after, z_before):
            total = total + jnp.where(near > 0.0, near, here)
        centre.append(1.0 - (0.5 * step_size) * total)

    added = source
    for step in range(1, STEPS):
        new = list(added)
        for x in range(step, tall - step):
            here = added[x]
            total = source[x] + centre[x] * here
            total = total + (cx[x] * added[x + 1] + cx[x - 1] * added[x - 1])
            total = total + cy[x] * pltpu.roll(here, LANES - 1, 1)
            total = total + pltpu.roll(cy[x] * here, 1, 1)
            total = total + cz[x] * pltpu.roll(here, 7, 0)
            new[x] = total + pltpu.roll(cz[x] * here, 1, 0)
        added = new

    lane = lax.broadcasted_iota(jnp.int32, (ny, LANES), 1)
    turned = jnp.concatenate(added[HALO : HALO + nx], axis=0).T[:ny]
    for x in range(nx):
        piece = turned if x == 0 else pltpu.roll(turned, LANES - 8 * x, 1)
        out_ref[x] = base_ref[x] + jnp.where(lane < STEPS, piece, 0.0)


def add_source(near, flag, everything, thin, base):
    nx, ny, nz = base.shape
    smem = pl.BlockSpec(memory_space=pltpu.SMEM)
    block = pl.BlockSpec((nx, ny, LANES), lambda i: (0, 0, 0))
    return pl.pallas_call(
        functools.partial(source_kernel, ny),
        grid=(1,),
        out_shape=jax.ShapeDtypeStruct(base.shape, jnp.float32),
        in_specs=[
            smem,
            smem,
            pl.BlockSpec(everything.shape, lambda i: (0, 0, 0)),
            pl.BlockSpec(thin.shape, lambda i: (0, 0, 0)),
            block,
        ],
        out_specs=block,
        input_output_aliases={4: 0},
        compiler_params=params(64),
        cost_estimate=cost(1_000_000, 2 * nx * ny * LANES * 4),
        name="add_source",
    )(near, flag, everything, thin, base)


def exchange(copies):
    return lax.all_to_all(copies, ("slab", "pair"), split_axis=0, concat_axis=0, tiled=True)


def together(*arrays):
    return lax.optimization_barrier(arrays)


def both_ways(low, high, axis):
    count = lax.axis_size(axis)
    forward = [(i, i + 1) for i in range(count - 1)]
    backward = [(target, source) for source, target in forward]
    from_low = lax.ppermute(high, axis, forward)
    from_high = lax.ppermute(low, axis, backward)
    return from_low, from_high


def shards(
    initial_warmth,
    heat_passing_coefficient,
    mirror_fraction,
    element_facing_site,
    tile_block_couples,
    active_slot_count,
    view_factor_blocks,
):
    nx, ny, _ = initial_warmth.shape
    slabs, pairs = lax.axis_size("slab"), lax.axis_size("pair")
    count = slabs * pairs
    blocks = mirror_fraction.shape[0]
    couples = tile_block_couples.T

    temp, cond = initial_warmth, heat_passing_coefficient
    emitted, copies = emit(temp, element_facing_site, mirror_fraction, count)
    temp, copies = together(temp, copies)

    def sweep_terms(whole):
        whole = whole.reshape(count * blocks, BLK)
        term = tile_terms(whole, couples, active_slot_count, view_factor_blocks)
        return term.reshape(count, blocks, BLK)

    whole = exchange(copies)
    send_low, send_high = pack_x(temp, cond)
    whole, send_low, send_high = together(whole, send_low, send_high)
    low, high = both_ways(send_low, send_high, "slab")
    parts = exchange(sweep_terms(whole))
    send_down, send_up = pack_y(temp, cond, low, high)
    parts, send_down, send_up = together(parts, send_down, send_up)
    below, above = both_ways(send_down, send_up, "pair")
    whole = exchange(middle(parts, emitted, mirror_fraction))
    middle_temp, send_low, send_high, strided_cond, thin = first_round(
        temp, cond, low, high, below, above
    )
    whole, send_low, send_high = together(whole, send_low, send_high)
    low, high = both_ways(send_low, send_high, "slab")
    parts = exchange(sweep_terms(whole))
    parts, low, high = together(parts, low, high)
    radiosity, source = last(parts, emitted, mirror_fraction, element_facing_site, nx * ny)
    everything = exchange(source)
    base = second_round(middle_temp, low, high, strided_cond, temp.shape)

    slab, pair = lax.axis_index("slab"), lax.axis_index("pair")
    near, flag = [], []
    for ds in (-1, 0, 1):
        for dp in (-1, 0, 1):
            s, p = slab + ds, pair + dp
            inside = (s >= 0) & (s < slabs) & (p >= 0) & (p < pairs)
            near.append(jnp.where(inside, s * pairs + p, 0))
            flag.append(inside)
    near = jnp.stack(near).astype(jnp.int32)
    flag = jnp.stack(flag).astype(jnp.int32)
    warmed_liner = add_source(near, flag, everything, thin, base)
    return (radiosity, warmed_liner)


def solution(mesh):
    return jax.shard_map(
        shards,
        mesh=mesh,
        in_specs=(
            P("slab", "pair", None),
            P("slab", "pair", None),
            P(("slab", "pair"), None),
            P(("slab", "pair"), None),
            P(("slab", "pair"), None),
            P(("slab", "pair")),
            P(("slab", "pair"), None, None),
        ),
        out_specs=(P(("slab", "pair"), None), P("slab", "pair", None)),
        check_vma=False,
    )
```

```python
import functools

import jax
import jax.numpy as jnp
from jax import lax
from jax.experimental import pallas as pl
from jax.experimental.pallas import tpu as pltpu
from jax.sharding import PartitionSpec as P

BLK = 128
SWEEPS = 2
STEPS = 4
HALO = STEPS
DEPTH = STEPS // 2
ROWS = STEPS
LANES = 128
CHUNK = 16
LAG = 40

step_size = 0.07

NT = (((1,), (1,)), ((), ()))
NN = (((1,), (0,)), ((), ()))


def params(mib):
    return pltpu.CompilerParams(vmem_limit_bytes=mib * 1024 * 1024)


def cost(flops, nbytes):
    return pl.CostEstimate(flops=flops, bytes_accessed=nbytes, transcendentals=0)


def parts_of(x, count):
    out = []
    for _ in range(count - 1):
        part = x.astype(jnp.bfloat16)
        out.append(part)
        x = x - part.astype(jnp.float32)
    out.append(x.astype(jnp.bfloat16))
    return out


class Lagging:
    def __init__(self, depth):
        self.depth = depth
        self.waiting = []

    def add(self, store):
        self.waiting.append(store)
        if len(self.waiting) > self.depth:
            self.waiting.pop(0)()

    def finish(self):
        for store in self.waiting:
            store()
        self.waiting = []


def put(ref, index, value):
    return lambda: ref.__setitem__(index, value)


def unrolled(begin, end, most):
    return max(u for u in range(1, most + 1) if (end - begin) % u == 0)


def emit_kernel(temp_ref, site_ref, mirror_ref, emitted_ref, copies_ref):
    nx, ny, _ = temp_ref.shape
    sheets = nx * ny // LANES
    per = LANES // ny
    lanes = lax.broadcasted_iota(jnp.int32, (LANES, LANES), 1)
    gathered = jnp.zeros((LANES, LANES), jnp.float32)
    for r in range(sheets):
        piece = temp_ref[per * r : per * r + per].reshape(LANES, LANES)
        if r:
            piece = pltpu.roll(piece, r, 1)
        gathered = jnp.where(lanes == r, piece, gathered)
    plane = gathered.T[:sheets]
    for half in range(site_ref.shape[0] // 8):
        rows = pl.ds(half * 8, 8)
        site = site_ref[rows, :]
        lane = site & (LANES - 1)
        sheet = site >> 7
        warmth = jnp.zeros(site.shape, jnp.float32)
        for r in range(sheets):
            line = jnp.broadcast_to(plane[r : r + 1, :], site.shape)
            picked = jnp.take_along_axis(line, lane, axis=1)
            warmth = jnp.where(sheet == r, picked, warmth)
        square = warmth * warmth
        emitted = (1.0 - mirror_ref[rows, :]) * (square * square)
        emitted_ref[rows, :] = emitted
        for d in range(copies_ref.shape[0]):
            copies_ref[d, rows, :] = emitted


def emit(temp, site, mirror, count):
    shape = mirror.shape
    nx, ny, _ = temp.shape
    patch = pl.BlockSpec(shape, lambda i: (0, 0))
    return pl.pallas_call(
        emit_kernel,
        grid=(1,),
        out_shape=(
            jax.ShapeDtypeStruct(shape, jnp.float32),
            jax.ShapeDtypeStruct((count,) + shape, jnp.float32),
        ),
        in_specs=[pl.BlockSpec((nx, ny, LANES), lambda i: (0, 0, 0)), patch, patch],
        out_specs=(patch, pl.BlockSpec((count,) + shape, lambda i: (0, 0, 0))),
        compiler_params=params(64),
        cost_estimate=cost(10_000, 900_000),
        name="emit",
    )(temp, site, mirror)


def tiles_kernel(
    live_ref, pairs_ref, lanes_ref, whole_ref, tiles_ref, out_ref, held, terms, sems
):
    slots = held.shape[0]
    live = live_ref[0]
    chunks = (live + CHUNK - 1) // CHUNK

    def chunk_copy(c):
        span = pl.ds(c * CHUNK, CHUNK)
        return pltpu.make_async_copy(tiles_ref.at[span], held.at[span], sems.at[c])

    @pl.loop(0, chunks)
    def _(c):
        chunk_copy(c).start()

    top = lax.broadcasted_iota(jnp.int32, (8, BLK), 0) == 0

    def split_row(block):
        row = jnp.broadcast_to(whole_ref[pl.ds(block, 1), :], (8, BLK))
        high = row.astype(jnp.bfloat16).astype(jnp.float32)
        return jnp.where(top, high, row - high)

    def vectors(a, b):
        stacked = jnp.concatenate([split_row(a), split_row(b)], axis=0)
        stacked = stacked.astype(jnp.bfloat16)
        return jnp.concatenate([stacked, stacked], axis=1)

    @pl.loop(0, chunks)
    def _(c):
        chunk_copy(c).wait()
        stores = Lagging(4 * CHUNK)
        for u in range(0, CHUNK, 2):
            t = c * CHUNK + u
            high_a, low_a = parts_of(held[t], 2)
            high_b, low_b = parts_of(held[t + 1], 2)
            both = jnp.concatenate(
                [
                    jnp.concatenate([high_a, high_b], axis=1),
                    jnp.concatenate([low_a, low_b], axis=1),
                ],
                axis=0,
            )
            second = lax.dot_general(
                vectors(pairs_ref[0, t], pairs_ref[0, t + 1]),
                both,
                NN,
                preferred_element_type=jnp.float32,
            )
            turned = jnp.concatenate(
                [
                    jnp.concatenate([high_a, low_a], axis=1),
                    jnp.concatenate([high_b, low_b], axis=1),
                ],
                axis=0,
            )
            first = lax.dot_general(
                vectors(pairs_ref[1, t], pairs_ref[1, t + 1]),
                turned,
                NT,
                preferred_element_type=jnp.float32,
            )
            for side, result in ((0, first), (1, second)):
                for v, (top_row, cols) in enumerate(((0, slice(0, BLK)), (8, slice(BLK, 2 * BLK)))):
                    row = result[top_row : top_row + 1, cols] + result[top_row + 1 : top_row + 2, cols]
                    stores.add(put(terms, (side, pl.ds(t + v, 1)), row))
        stores.finish()

    used = lax.broadcasted_iota(jnp.int32, (slots, BLK), 0) < live
    used_lane = lax.broadcasted_iota(jnp.int32, (1, slots), 1) < live
    blocks = out_ref.shape[0]
    group = min(blocks, 512)
    split = []
    for side in range(2):
        masked = jnp.where(used, terms[side], 0.0)
        split.append(jnp.concatenate(parts_of(masked, 2), axis=1))
    for base in range(0, blocks, group):
        rows = lax.broadcasted_iota(jnp.int32, (group, slots), 0) + base
        total = jnp.zeros((group, 2 * BLK), jnp.float32)
        for side in range(2):
            target = jnp.where(used_lane, lanes_ref[side : side + 1, :], -1)
            choose = jnp.where(rows == target, 1.0, 0.0).astype(jnp.bfloat16)
            total = total + jnp.dot(choose, split[side], preferred_element_type=jnp.float32)
        out_ref[base : base + group, :] = total[:, :BLK] + total[:, BLK:]


def tile_terms(whole, couples, live, tiles):
    slots = tiles.shape[0]
    smem = pl.BlockSpec(memory_space=pltpu.SMEM)
    vmem = pl.BlockSpec(memory_space=pltpu.VMEM)
    return pl.pallas_call(
        tiles_kernel,
        out_shape=jax.ShapeDtypeStruct(whole.shape, jnp.float32),
        in_specs=[smem, smem, vmem, vmem, pl.BlockSpec(memory_space=pl.ANY)],
        out_specs=vmem,
        scratch_shapes=[
            pltpu.VMEM(tiles.shape, jnp.float32),
            pltpu.VMEM((2, slots, BLK), jnp.float32),
            pltpu.SemaphoreType.DMA((slots // CHUNK,)),
        ],
        compiler_params=params(50),
        cost_estimate=cost(slots * BLK * BLK * 32, slots * BLK * BLK * 4),
        name="tiles",
    )(live, couples, couples, whole, tiles)


def sum_parts(parts_ref, rows):
    total = parts_ref[0, rows, :]
    for d in range(1, parts_ref.shape[0]):
        total = total + parts_ref[d, rows, :]
    return total


def middle_kernel(parts_ref, emitted_ref, mirror_ref, copies_ref):
    for half in range(emitted_ref.shape[0] // 8):
        rows = pl.ds(half * 8, 8)
        incident = sum_parts(parts_ref, rows)
        radiosity = emitted_ref[rows, :] + mirror_ref[rows, :] * incident
        for d in range(copies_ref.shape[0]):
            copies_ref[d, rows, :] = radiosity


def middle(parts, emitted, mirror):
    return pl.pallas_call(
        middle_kernel,
        out_shape=jax.ShapeDtypeStruct(parts.shape, jnp.float32),
        compiler_params=params(32),
        cost_estimate=cost(100_000, 600_000),
        name="middle",
    )(parts, emitted, mirror)


def last_kernel(scale, parts_ref, emitted_ref, mirror_ref, site_ref, rad_ref, source_ref):
    blocks = emitted_ref.shape[0]
    incident = sum_parts(parts_ref, slice(None))
    emitted = emitted_ref[...]
    mirror = mirror_ref[...]
    rad_ref[...] = emitted + mirror * incident
    absorbed = ((1.0 - mirror) * incident - emitted) * scale
    site = site_ref[...]
    lane = site & (LANES - 1)
    sheet = site >> 7
    sheets = source_ref.shape[1]
    sheet_iota = lax.broadcasted_iota(jnp.int32, (sheets, BLK), 0)
    lane_iota = lax.broadcasted_iota(jnp.int32, (LANES, BLK), 0)
    left = []
    right = []
    for b in range(blocks):
        here = jnp.where(sheet_iota == sheet[b : b + 1, :], absorbed[b : b + 1, :], 0.0)
        left.append(here)
        pick = jnp.where(lane_iota == lane[b : b + 1, :], 1.0, 0.0)
        right.append(pick.astype(jnp.bfloat16))
    left = jnp.concatenate(left, axis=1)
    right = jnp.concatenate(right, axis=1)
    source = jnp.zeros((sheets, LANES), jnp.float32)
    for part in parts_of(left, 3):
        source = source + lax.dot_general(part, right, NT, preferred_element_type=jnp.float32)
    for d in range(source_ref.shape[0]):
        source_ref[d] = source


def last(parts, emitted, mirror, site, cells):
    count = parts.shape[0]
    weight = cells / (mirror.shape[0] * BLK * 1.0)
    return pl.pallas_call(
        functools.partial(last_kernel, step_size * weight),
        out_shape=(
            jax.ShapeDtypeStruct(mirror.shape, jnp.float32),
            jax.ShapeDtypeStruct((count, cells // LANES, LANES), jnp.float32),
        ),
        compiler_params=params(32),
        cost_estimate=cost(10_000_000, 600_000),
        name="last",
    )(parts, emitted, mirror, site)


def first_planes(depth, ny, nz):
    return pl.BlockSpec((depth, ny, nz), lambda i: (0, 0, 0))


def pack_x_kernel(t_low, k_low, k_low_thin, t_high, k_high, k_high_thin, low_ref, high_ref):
    ny, nz = t_low.shape[1:]
    tail = 2 * DEPTH * ny
    piece = ny * LANES // nz
    for send, temp, cond, thin, at in (
        (low_ref, t_low, k_low, k_low_thin, DEPTH),
        (high_ref, t_high, k_high, k_high_thin, k_high_thin.shape[0] - DEPTH - 1),
    ):
        for p in range(DEPTH):
            send[p * ny : p * ny + ny, :] = temp[p]
            send[(DEPTH + p) * ny : (DEPTH + p + 1) * ny, :] = cond[p]
        for j in range(nz // LANES):
            send[tail:, j * LANES : (j + 1) * LANES] = thin[at, j * piece : (j + 1) * piece, :]


def pack_x(temp, cond):
    nx, ny, nz = temp.shape
    ends = 2 * DEPTH
    rows = 2 * DEPTH * ny + ny * LANES // nz
    first = pl.BlockSpec((DEPTH, ny, nz), lambda i: (0, 0, 0))
    final = pl.BlockSpec((DEPTH, ny, nz), lambda i: (nx // DEPTH - 1, 0, 0))
    first_thin = pl.BlockSpec((ends, ny, LANES), lambda i: (0, 0, 0))
    final_thin = pl.BlockSpec((ends, ny, LANES), lambda i: (nx // ends - 1, 0, 0))
    whole = pl.BlockSpec((rows, nz), lambda i: (0, 0))
    shape = jax.ShapeDtypeStruct((rows, nz), jnp.float32)
    return pl.pallas_call(
        pack_x_kernel,
        grid=(1,),
        out_shape=(shape, shape),
        in_specs=[first, first, first_thin, final, final, final_thin],
        out_specs=(whole, whole),
        compiler_params=params(64),
        cost_estimate=cost(0, 4 * rows * nz * 4),
        name="pack_x",
    )(temp, cond, cond, temp, cond, cond)


def pack_y_kernel(nx, ny, t0, k0, t7, k7, low_ref, high_ref, down_ref, up_ref):
    upper = lax.broadcasted_iota(jnp.int32, down_ref.shape[1:], 0) < ROWS

    def edge(x, t_first, k_first, t_final, k_final):
        down_ref[x] = jnp.where(upper, t_first, pltpu.roll(k_first, ROWS, 0))
        up_ref[x] = jnp.where(upper, pltpu.roll(t_final, ROWS, 0), k_final)

    for side, base in ((low_ref, 0), (high_ref, DEPTH + nx)):
        for p in range(DEPTH):
            t_at, k_at = p * ny, (DEPTH + p) * ny
            edge(
                base + p,
                side[t_at : t_at + 8, :],
                side[k_at : k_at + 8, :],
                side[t_at + ny - 8 : t_at + ny, :],
                side[k_at + ny - 8 : k_at + ny, :],
            )
    for x in range(nx):
        edge(DEPTH + x, t0[x], k0[x], t7[x], k7[x])


def pack_y(temp, cond, low, high):
    nx, ny, nz = temp.shape
    first = pl.BlockSpec((nx, 8, nz), lambda i: (0, 0, 0))
    final = pl.BlockSpec((nx, 8, nz), lambda i: (0, ny // 8 - 1, 0))
    halo = pl.BlockSpec(low.shape, lambda i: (0, 0))
    tall = nx + 2 * DEPTH
    whole = pl.BlockSpec((tall, 8, nz), lambda i: (0, 0, 0))
    shape = jax.ShapeDtypeStruct((tall, 8, nz), jnp.float32)
    return pl.pallas_call(
        functools.partial(pack_y_kernel, nx, ny),
        grid=(1,),
        out_shape=(shape, shape),
        in_specs=[first, first, final, final, halo, halo],
        out_specs=(whole, whole),
        compiler_params=params(64),
        cost_estimate=cost(0, 4 * tall * 8 * nz * 4),
        name="pack_y",
    )(temp, cond, temp, cond, low, high)


def coupling(a, b):
    return jnp.where(jnp.minimum(a, b) > 0.0, (0.5 * step_size) * (a + b), 0.0)


def neighbours():
    slab, pair = lax.axis_index("slab"), lax.axis_index("pair")
    return slab > 0, slab < lax.axis_size("slab") - 1, pair > 0, pair < lax.axis_size("pair") - 1


def lane_tiles(nz):
    return [slice(j * LANES, (j + 1) * LANES) for j in range(nz // LANES)]


def prepare(cond, gx, gy, gz, gb):
    tall, wide, nz = cond.shape
    tiles = wide // 8
    lane = lax.broadcasted_iota(jnp.int32, (8, LANES), 1)
    half = 0.5 * step_size

    together_planes = unrolled(0, tall, 2)

    @pl.loop(0, tall, step=together_planes)
    def _(base):
        stores = Lagging(LAG)
        for p in range(together_planes):
            x = base + p
            after = jnp.minimum(x + 1, tall - 1)
            for z in lane_tiles(nz):
                last = z.stop == nz
                for t in range(tiles):
                    rows = slice(8 * t, 8 * t + 8)
                    here = cond[x, rows, z]
                    stores.add(put(gx, (x, rows, z), half * (here + cond[after, rows, z])))
                    if t + 1 < tiles:
                        beside = cond[x, 8 * t + 8 : 8 * t + 16, z]
                    else:
                        beside = pltpu.roll(cond[x, :8, z], 7, 0)
                    stores.add(put(gy, (x, rows, z), half * (here + beside)))
                    turned = pltpu.roll(here, LANES - 1, 1)
                    if last:
                        deeper = here
                    else:
                        deeper = pltpu.roll(cond[x, rows, z.stop : z.stop + LANES], LANES - 1, 1)
                    deeper = jnp.where(lane < LANES - 1, turned, deeper)
                    stores.add(put(gz, (x, rows, z), half * (here + deeper)))
                    if z.start == 0:
                        stores.add(put(gb, (x, rows), step_size * here))
        stores.finish()


def one_step(field, begin, end, target, gx, gy, gz, gb):
    wide, nz = field.shape[1:]
    tiles = wide // 8
    lane = lax.broadcasted_iota(jnp.int32, (8, LANES), 1)
    sub = lax.broadcasted_iota(jnp.int32, (8, LANES), 0)
    _, _, has_below, has_above = neighbours()
    keep_above = (sub < 7) | has_above
    keep_below = (sub < 7) | has_below

    spans = lane_tiles(nz)
    count = len(spans)
    together_planes = unrolled(begin, end, 4)

    def plane_step(x, stores):
        here, across_y = {}, {}

        def tile(t, j):
            if (t, j) not in here:
                here[t, j] = field[x, 8 * t : 8 * t + 8, spans[j]]
            return here[t, j]

        def y_flux(t, j):
            if (t, j) not in across_y:
                if t + 1 < tiles:
                    beside = tile(t + 1, j)
                else:
                    beside = pltpu.roll(tile(0, j), 7, 0)
                across_y[t, j] = gy[x, 8 * t : 8 * t + 8, spans[j]] * (beside - tile(t, j))
            return across_y[t, j]

        for t in range(tiles):
            rows = slice(8 * t, 8 * t + 8)
            turned = [pltpu.roll(tile(t, j), LANES - 1, 1) for j in range(count)]
            flux = []
            for j in range(count):
                deeper = turned[j + 1] if j + 1 < count else 0.0
                deeper = jnp.where(lane < LANES - 1, turned[j], deeper)
                flux.append(gz[x, rows, spans[j]] * (deeper - tile(t, j)))
            back = [pltpu.roll(f, 1, 1) for f in flux]
            for j in range(count):
                now = tile(t, j)
                low_z = back[j - 1] if j else gb[x, rows, :] * now
                low_z = jnp.where(lane > 0, back[j], low_z)
                x_flux = gx[x, rows, spans[j]] * (field[x + 1, rows, spans[j]] - now)
                low_x = gx[x - 1, rows, spans[j]] * (now - field[x - 1, rows, spans[j]])
                low_y = y_flux(t - 1, j) if t else pltpu.roll(y_flux(tiles - 1, j), 1, 0)
                new = now + (x_flux - low_x) + (y_flux(t, j) - low_y) + (flux[j] - low_z)
                if t:
                    new = jnp.where(keep_above if t <= ROWS else keep_below, new, 0.0)
                stores.add(put(*target(x, t, spans[j]), new))

    @pl.loop(begin, end, step=together_planes)
    def _(base):
        stores = Lagging(LAG)
        for p in range(together_planes):
            plane_step(base + p, stores)
        stores.finish()


def thin_planes(cond, ny, thin_ref, base_plane):
    tall, _, wide, _ = cond.shape
    lane = lax.broadcasted_iota(jnp.int32, (wide, LANES), 1)
    y_lane = lax.broadcasted_iota(jnp.int32, (8, LANES), 1)
    for base in range(0, tall, 16):
        planes = min(16, tall - base)
        gathered = jnp.zeros((wide, LANES), jnp.float32)
        for g in range(planes):
            piece = cond[base + g, 0]
            if g:
                piece = pltpu.roll(piece, 8 * g, 1)
            gathered = jnp.where((lane >> 3) == g, piece, gathered)
        turned = jnp.concatenate(
            [gathered, jnp.zeros((LANES - wide, LANES), jnp.float32)], axis=0
        ).T
        for g in range(planes):
            rows = turned[8 * g : 8 * g + 8, :]
            moved = pltpu.roll(rows, LANES - wide, 1)
            thin_ref[base_plane + base + g] = jnp.where(
                y_lane < ny + ROWS, rows, jnp.where(y_lane >= LANES - ROWS, moved, 0.0)
            )


def first_round_kernel(
    t_ref, k_ref, low_ref, high_ref, below_ref, above_ref,
    out_ref, low_out, high_out, cond_out, thin_ref,
    loaded, field, between, gx, gy, gz, gb, sems,
):
    nx, ny, nz = t_ref.shape
    tall, wide = nx + 2 * DEPTH, ny + 2 * ROWS
    tiles = wide // 8
    raw_t, raw_k = loaded.at[0], loaded.at[1]
    spans = lane_tiles(nz)
    copies = [
        pltpu.make_async_copy(
            ref.at[:, :, pl.ds(z.start, LANES)],
            loaded.at[which, pl.ds(DEPTH, nx), j, pl.ds(0, ny)],
            sems.at[which, j],
        )
        for which, ref in ((1, k_ref), (0, t_ref))
        for j, z in enumerate(spans)
    ]
    for copy in copies:
        copy.start()
    has_low, has_high, has_below, has_above = neighbours()
    upper = lax.broadcasted_iota(jnp.int32, (8, LANES), 0) < ROWS
    for side, base in ((low_ref, 0), (high_ref, DEPTH + nx)):
        for p in range(DEPTH):
            for j, z in enumerate(spans):
                raw_t[base + p, j, :ny] = side[p * ny : p * ny + ny, z]
                raw_k[base + p, j, :ny] = side[(DEPTH + p) * ny : (DEPTH + p + 1) * ny, z]

    @pl.loop(0, tall)
    def _(x):
        for j, z in enumerate(spans):
            down, up = above_ref[x, :, z], below_ref[x, :, z]
            raw_t[x, j, ny:] = jnp.where(upper, down, pltpu.roll(up, ROWS, 0))
            raw_k[x, j, ny:] = jnp.where(upper, pltpu.roll(down, ROWS, 0), up)

    for copy in copies:
        copy.wait()

    piece = ny * LANES // nz
    tail = 2 * DEPTH * ny
    thin_planes(raw_k, ny, thin_ref, HALO - DEPTH)
    for side, at in ((low_ref, HALO - DEPTH - 1), (high_ref, HALO + nx + DEPTH)):
        edge = [side[tail:, z] for z in lane_tiles(nz)]
        edge.append(jnp.zeros((LANES - ny, LANES), jnp.float32))
        turned = jnp.concatenate(edge, axis=0).T
        thin_ref[at] = turned[:8]
    for at in [*range(HALO - DEPTH - 1), *range(HALO + nx + DEPTH + 1, nx + 2 * HALO)]:
        thin_ref[at] = jnp.zeros((8, LANES), jnp.float32)

    @pl.loop(0, tall)
    def _(x):
        missing = (upper & jnp.logical_not(has_above)) | (
            jnp.logical_not(upper) & jnp.logical_not(has_below)
        )
        for j in range(len(spans)):
            edge = raw_k[x, j, ny:]
            last = jnp.broadcast_to(raw_k[x, j, ny - 1 : ny, :], edge.shape)
            first = jnp.broadcast_to(raw_k[x, j, 0:1, :], edge.shape)
            raw_k[x, j, ny:] = jnp.where(missing, jnp.where(upper, last, first), edge)

    @pl.when(jnp.logical_not(has_low))
    def _():
        for p in range(DEPTH):
            raw_k[p] = raw_k[DEPTH]

    @pl.when(jnp.logical_not(has_high))
    def _():
        for p in range(DEPTH):
            raw_k[DEPTH + nx + p] = raw_k[DEPTH + nx - 1]

    @pl.loop(0, tall)
    def _(x):
        stores = Lagging(LAG)
        for t in range(tiles):
            rows = pl.ds(t, 8, stride=tiles)
            for j, z in enumerate(spans):
                stores.add(put(field, (x, slice(8 * t, 8 * t + 8), z), loaded[0, x, j, rows, :]))
                stores.add(put(cond_out, (x, slice(8 * t, 8 * t + 8), z), loaded[1, x, j, rows, :]))
        stores.finish()

    prepare(cond_out, gx, gy, gz, gb)

    def target(x, t, z):
        return out_ref, (x - DEPTH, slice(8 * t, 8 * t + 8), z)

    two_steps(field, between, gx, gy, gz, gb, target)
    low_out[...] = out_ref[:DEPTH]
    high_out[...] = out_ref[nx - DEPTH :]


def two_steps(field, between, gx, gy, gz, gb, target):
    tall = field.shape[0]
    has_low, has_high, _, _ = neighbours()
    def inner(x, t, z):
        return between, (x, slice(8 * t, 8 * t + 8), z)

    one_step(field, 1, tall - 1, inner, gx, gy, gz, gb)
    for x, inside in ((1, has_low), (tall - 2, has_high)):

        @pl.when(jnp.logical_not(inside))
        def _():
            between[x] = jnp.zeros(field.shape[1:], jnp.float32)

    one_step(between, DEPTH, tall - DEPTH, target, gx, gy, gz, gb)


def heat_scratch(tall, wide, nz):
    big = pltpu.VMEM((tall, wide, nz), jnp.float32)
    return [
        big,
        big,
        big,
        big,
        big,
        pltpu.VMEM((tall, wide, LANES), jnp.float32),
    ]


def first_round(temp, cond, low, high, below, above):
    nx, ny, nz = temp.shape
    tall, wide = nx + 2 * DEPTH, ny + 2 * ROWS
    hbm = pl.BlockSpec(memory_space=pl.ANY)
    vmem = pl.BlockSpec(memory_space=pltpu.VMEM)
    plane = jax.ShapeDtypeStruct((DEPTH, wide, nz), jnp.float32)
    return pl.pallas_call(
        first_round_kernel,
        out_shape=(
            jax.ShapeDtypeStruct((nx, wide, nz), jnp.float32),
            plane,
            plane,
            jax.ShapeDtypeStruct((tall, wide, nz), jnp.float32),
            jax.ShapeDtypeStruct((nx + 2 * HALO, 8, LANES), jnp.float32),
        ),
        in_specs=[hbm, hbm] + [vmem] * 4,
        scratch_shapes=[pltpu.VMEM((2, tall, nz // LANES, wide, LANES), jnp.float32)]
        + heat_scratch(tall, wide, nz)
        + [pltpu.SemaphoreType.DMA((2, nz // LANES))],
        compiler_params=params(64),
        cost_estimate=cost(tall * wide * nz * 100, 12 * nx * ny * nz * 4),
        name="first_round",
    )(temp, cond, low, high, below, above)


def second_round_kernel(
    t_ref, low_ref, high_ref, k_ref, out_ref,
    cond, field, between, gx, gy, gz, gb, placed, sems,
):
    nx, wide, nz = t_ref.shape
    ny = out_ref.shape[1]
    tiles = wide // 8
    copies = [
        pltpu.make_async_copy(k_ref, cond, sems.at[0]),
        pltpu.make_async_copy(t_ref, field.at[pl.ds(DEPTH, nx)], sems.at[1]),
        pltpu.make_async_copy(low_ref, field.at[pl.ds(0, DEPTH)], sems.at[2]),
        pltpu.make_async_copy(high_ref, field.at[pl.ds(DEPTH + nx, DEPTH)], sems.at[3]),
    ]
    for copy in copies:
        copy.start()
    copies[0].wait()
    prepare(cond, gx, gy, gz, gb)
    for copy in copies[1:]:
        copy.wait()

    def target(x, t, z):
        return placed, (x - DEPTH, z.start // LANES, pl.ds(t, 8, stride=tiles))

    two_steps(field, between, gx, gy, gz, gb, target)

    @pl.loop(0, nx)
    def _(x):
        for j, z in enumerate(lane_tiles(out_ref.shape[2])):
            out_ref[x, :, z] = placed[x, j, :ny, :]


def second_round(temp, low, high, cond, shape):
    nx, wide, nz = temp.shape
    tall = cond.shape[0]
    hbm = pl.BlockSpec(memory_space=pl.ANY)
    return pl.pallas_call(
        second_round_kernel,
        out_shape=jax.ShapeDtypeStruct(shape, jnp.float32),
        in_specs=[hbm] * 4,
        scratch_shapes=[pltpu.VMEM((tall, wide, nz), jnp.float32)]
        + heat_scratch(tall, wide, nz)
        + [
            pltpu.VMEM((nx, nz // LANES, wide, LANES), jnp.float32),
            pltpu.SemaphoreType.DMA((4,)),
        ],
        compiler_params=params(64),
        cost_estimate=cost(tall * wide * nz * 60, 8 * nx * wide * nz * 4),
        name="second_round",
    )(temp, low, high, cond)


def source_kernel(ny, near_ref, flag_ref, all_ref, thin_ref, base_ref, out_ref):
    tall = thin_ref.shape[0]
    nx = tall - 2 * HALO
    sheets = all_ref.shape[1]
    sub = lax.broadcasted_iota(jnp.int32, (8, LANES), 0)
    y_lane = lax.broadcasted_iota(jnp.int32, (8, LANES), 1)

    def sheet(k):
        return all_ref[near_ref[k]] * flag_ref[k].astype(jnp.float32)

    def rows_of(slab):
        low, own, high = (sheet(3 * slab + k) for k in range(3))
        out = []
        for half in range(2):
            if half == 0:
                own_at, high_at, low_at = own, pltpu.roll(high, ny, 1), pltpu.roll(low, ny, 1)
            else:
                own_at, high_at, low_at = pltpu.roll(own, ny, 1), high, low
            out.append(
                jnp.where(
                    y_lane < ny,
                    own_at,
                    jnp.where(
                        y_lane < ny + HALO,
                        high_at,
                        jnp.where(y_lane >= LANES - HALO, low_at, 0.0),
                    ),
                )
            )
        return out

    lines = [rows_of(s) for s in range(3)]
    source = []
    for x in range(-HALO, nx + HALO):
        which, local = (x + nx) // nx, x % nx
        row = lines[which][local % 2][local // 2 : local // 2 + 1, :]
        source.append(jnp.where(sub == 0, jnp.broadcast_to(row, (8, LANES)), 0.0))

    cond = [thin_ref[x] for x in range(tall)]
    cx, cy, cz, centre = [], [], [], []
    for x in range(tall):
        here = cond[x]
        after = cond[min(x + 1, tall - 1)]
        before = cond[max(x - 1, 0)]
        y_after = pltpu.roll(here, LANES - 1, 1)
        y_before = pltpu.roll(here, 1, 1)
        z_after = jnp.where(sub == 7, 0.0, pltpu.roll(here, 7, 0))
        z_before = jnp.where(sub == 0, 0.0, pltpu.roll(here, 1, 0))
        cx.append(coupling(here, after))
        cy.append(coupling(here, y_after))
        cz.append(coupling(here, z_after))
        total = 6.0 * here
        for near in (after, before, y_after, y_before, z_after, z_before):
            total = total + jnp.where(near > 0.0, near, here)
        centre.append(1.0 - (0.5 * step_size) * total)

    added = source
    for step in range(1, STEPS):
        new = list(added)
        for x in range(step, tall - step):
            here = added[x]
            total = source[x] + centre[x] * here
            total = total + (cx[x] * added[x + 1] + cx[x - 1] * added[x - 1])
            total = total + cy[x] * pltpu.roll(here, LANES - 1, 1)
            total = total + pltpu.roll(cy[x] * here, 1, 1)
            total = total + cz[x] * pltpu.roll(here, 7, 0)
            new[x] = total + pltpu.roll(cz[x] * here, 1, 0)
        added = new

    lane = lax.broadcasted_iota(jnp.int32, (ny, LANES), 1)
    turned = jnp.concatenate(added[HALO : HALO + nx], axis=0).T[:ny]
    for x in range(nx):
        piece = turned if x == 0 else pltpu.roll(turned, LANES - 8 * x, 1)
        out_ref[x] = base_ref[x] + jnp.where(lane < STEPS, piece, 0.0)


def add_source(near, flag, everything, thin, base):
    nx, ny, nz = base.shape
    smem = pl.BlockSpec(memory_space=pltpu.SMEM)
    block = pl.BlockSpec((nx, ny, LANES), lambda i: (0, 0, 0))
    return pl.pallas_call(
        functools.partial(source_kernel, ny),
        grid=(1,),
        out_shape=jax.ShapeDtypeStruct(base.shape, jnp.float32),
        in_specs=[
            smem,
            smem,
            pl.BlockSpec(everything.shape, lambda i: (0, 0, 0)),
            pl.BlockSpec(thin.shape, lambda i: (0, 0, 0)),
            block,
        ],
        out_specs=block,
        input_output_aliases={4: 0},
        compiler_params=params(64),
        cost_estimate=cost(1_000_000, 2 * nx * ny * LANES * 4),
        name="add_source",
    )(near, flag, everything, thin, base)


def exchange(copies):
    return lax.all_to_all(copies, ("slab", "pair"), split_axis=0, concat_axis=0, tiled=True)


def together(*arrays):
    return lax.optimization_barrier(arrays)


def both_ways(low, high, axis):
    count = lax.axis_size(axis)
    forward = [(i, i + 1) for i in range(count - 1)]
    backward = [(target, source) for source, target in forward]
    from_low = lax.ppermute(high, axis, forward)
    from_high = lax.ppermute(low, axis, backward)
    return from_low, from_high


def shards(
    initial_warmth,
    heat_passing_coefficient,
    mirror_fraction,
    element_facing_site,
    tile_block_couples,
    active_slot_count,
    view_factor_blocks,
):
    nx, ny, _ = initial_warmth.shape
    slabs, pairs = lax.axis_size("slab"), lax.axis_size("pair")
    count = slabs * pairs
    blocks = mirror_fraction.shape[0]
    couples = tile_block_couples.T

    temp, cond = initial_warmth, heat_passing_coefficient
    emitted, copies = emit(temp, element_facing_site, mirror_fraction, count)
    temp, copies = together(temp, copies)

    def sweep_terms(whole):
        whole = whole.reshape(count * blocks, BLK)
        term = tile_terms(whole, couples, active_slot_count, view_factor_blocks)
        return term.reshape(count, blocks, BLK)

    whole = exchange(copies)
    send_low, send_high = pack_x(temp, cond)
    low, high = both_ways(send_low, send_high, "slab")
    whole = together(whole, send_low, send_high)[0]
    parts = exchange(sweep_terms(whole))
    send_down, send_up = pack_y(temp, cond, low, high)
    parts = together(parts, send_down, send_up)[0]
    below, above = both_ways(send_down, send_up, "pair")
    whole = exchange(middle(parts, emitted, mirror_fraction))
    middle_temp, send_low, send_high, strided_cond, thin = first_round(
        temp, cond, low, high, below, above
    )
    low, high = both_ways(send_low, send_high, "slab")
    whole = together(whole, send_low, send_high)[0]
    term, low, high = together(sweep_terms(whole), low, high)
    parts = exchange(term)
    radiosity, source = last(parts, emitted, mirror_fraction, element_facing_site, nx * ny)
    everything = exchange(source)
    base = second_round(middle_temp, low, high, strided_cond, temp.shape)

    slab, pair = lax.axis_index("slab"), lax.axis_index("pair")
    near, flag = [], []
    for ds in (-1, 0, 1):
        for dp in (-1, 0, 1):
            s, p = slab + ds, pair + dp
            inside = (s >= 0) & (s < slabs) & (p >= 0) & (p < pairs)
            near.append(jnp.where(inside, s * pairs + p, 0))
            flag.append(inside)
    near = jnp.stack(near).astype(jnp.int32)
    flag = jnp.stack(flag).astype(jnp.int32)
    warmed_liner = add_source(near, flag, everything, thin, base)
    return (radiosity, warmed_liner)


def solution(mesh):
    return jax.shard_map(
        shards,
        mesh=mesh,
        in_specs=(
            P("slab", "pair", None),
            P("slab", "pair", None),
            P(("slab", "pair"), None),
            P(("slab", "pair"), None),
            P(("slab", "pair"), None),
            P(("slab", "pair")),
            P(("slab", "pair"), None, None),
        ),
        out_specs=(P(("slab", "pair"), None), P("slab", "pair", None)),
        check_vma=False,
    )
```

```python
import functools

import jax
import jax.numpy as jnp
from jax import lax
from jax.experimental import pallas as pl
from jax.experimental.pallas import tpu as pltpu
from jax.sharding import PartitionSpec as P

BLK = 128
SWEEPS = 2
STEPS = 4
HALO = STEPS
DEPTH = STEPS // 2
ROWS = STEPS
LANES = 128
CHUNK = 16
LAG = 12

step_size = 0.07

NT = (((1,), (1,)), ((), ()))
NN = (((1,), (0,)), ((), ()))


def params(mib):
    return pltpu.CompilerParams(vmem_limit_bytes=mib * 1024 * 1024)


def cost(flops, nbytes):
    return pl.CostEstimate(flops=flops, bytes_accessed=nbytes, transcendentals=0)


def parts_of(x, count):
    out = []
    for _ in range(count - 1):
        part = x.astype(jnp.bfloat16)
        out.append(part)
        x = x - part.astype(jnp.float32)
    out.append(x.astype(jnp.bfloat16))
    return out


class Lagging:
    def __init__(self, depth):
        self.depth = depth
        self.waiting = []

    def add(self, store):
        self.waiting.append(store)
        if len(self.waiting) > self.depth:
            self.waiting.pop(0)()

    def finish(self):
        for store in self.waiting:
            store()
        self.waiting = []


def put(ref, index, value):
    return lambda: ref.__setitem__(index, value)


def emit_kernel(temp_ref, site_ref, mirror_ref, emitted_ref, copies_ref):
    nx, ny, _ = temp_ref.shape
    sheets = nx * ny // LANES
    per = LANES // ny
    lanes = lax.broadcasted_iota(jnp.int32, (LANES, LANES), 1)
    gathered = jnp.zeros((LANES, LANES), jnp.float32)
    for r in range(sheets):
        piece = temp_ref[per * r : per * r + per].reshape(LANES, LANES)
        if r:
            piece = pltpu.roll(piece, r, 1)
        gathered = jnp.where(lanes == r, piece, gathered)
    plane = gathered.T[:sheets]
    for half in range(site_ref.shape[0] // 8):
        rows = pl.ds(half * 8, 8)
        site = site_ref[rows, :]
        lane = site & (LANES - 1)
        sheet = site >> 7
        warmth = jnp.zeros(site.shape, jnp.float32)
        for r in range(sheets):
            line = jnp.broadcast_to(plane[r : r + 1, :], site.shape)
            picked = jnp.take_along_axis(line, lane, axis=1)
            warmth = jnp.where(sheet == r, picked, warmth)
        square = warmth * warmth
        emitted = (1.0 - mirror_ref[rows, :]) * (square * square)
        emitted_ref[rows, :] = emitted
        for d in range(copies_ref.shape[0]):
            copies_ref[d, rows, :] = emitted


def emit(temp, site, mirror, count):
    shape = mirror.shape
    nx, ny, _ = temp.shape
    patch = pl.BlockSpec(shape, lambda i: (0, 0))
    return pl.pallas_call(
        emit_kernel,
        grid=(1,),
        out_shape=(
            jax.ShapeDtypeStruct(shape, jnp.float32),
            jax.ShapeDtypeStruct((count,) + shape, jnp.float32),
        ),
        in_specs=[pl.BlockSpec((nx, ny, LANES), lambda i: (0, 0, 0)), patch, patch],
        out_specs=(patch, pl.BlockSpec((count,) + shape, lambda i: (0, 0, 0))),
        compiler_params=params(64),
        cost_estimate=cost(10_000, 900_000),
        name="emit",
    )(temp, site, mirror)


def tiles_kernel(
    live_ref, pairs_ref, lanes_ref, whole_ref, tiles_ref, out_ref, held, terms, sems
):
    slots = held.shape[0]
    live = live_ref[0]
    chunks = (live + CHUNK - 1) // CHUNK

    def chunk_copy(c):
        span = pl.ds(c * CHUNK, CHUNK)
        return pltpu.make_async_copy(tiles_ref.at[span], held.at[span], sems.at[c])

    @pl.loop(0, chunks)
    def _(c):
        chunk_copy(c).start()

    top = lax.broadcasted_iota(jnp.int32, (8, BLK), 0) == 0

    def split_row(block):
        row = jnp.broadcast_to(whole_ref[pl.ds(block, 1), :], (8, BLK))
        high = row.astype(jnp.bfloat16).astype(jnp.float32)
        return jnp.where(top, high, row - high)

    def vectors(a, b):
        stacked = jnp.concatenate([split_row(a), split_row(b)], axis=0)
        stacked = stacked.astype(jnp.bfloat16)
        return jnp.concatenate([stacked, stacked], axis=1)

    @pl.loop(0, chunks)
    def _(c):
        chunk_copy(c).wait()
        stores = Lagging(4 * CHUNK)
        for u in range(0, CHUNK, 2):
            t = c * CHUNK + u
            high_a, low_a = parts_of(held[t], 2)
            high_b, low_b = parts_of(held[t + 1], 2)
            both = jnp.concatenate(
                [
                    jnp.concatenate([high_a, high_b], axis=1),
                    jnp.concatenate([low_a, low_b], axis=1),
                ],
                axis=0,
            )
            second = lax.dot_general(
                vectors(pairs_ref[0, t], pairs_ref[0, t + 1]),
                both,
                NN,
                preferred_element_type=jnp.float32,
            )
            turned = jnp.concatenate(
                [
                    jnp.concatenate([high_a, low_a], axis=1),
                    jnp.concatenate([high_b, low_b], axis=1),
                ],
                axis=0,
            )
            first = lax.dot_general(
                vectors(pairs_ref[1, t], pairs_ref[1, t + 1]),
                turned,
                NT,
                preferred_element_type=jnp.float32,
            )
            for side, result in ((0, first), (1, second)):
                for v, (top_row, cols) in enumerate(((0, slice(0, BLK)), (8, slice(BLK, 2 * BLK)))):
                    row = result[top_row : top_row + 1, cols] + result[top_row + 1 : top_row + 2, cols]
                    stores.add(put(terms, (side, pl.ds(t + v, 1)), row))
        stores.finish()

    used = lax.broadcasted_iota(jnp.int32, (slots, BLK), 0) < live
    used_lane = lax.broadcasted_iota(jnp.int32, (1, slots), 1) < live
    blocks = out_ref.shape[0]
    group = min(blocks, 512)
    split = []
    for side in range(2):
        masked = jnp.where(used, terms[side], 0.0)
        split.append(jnp.concatenate(parts_of(masked, 2), axis=1))
    for base in range(0, blocks, group):
        rows = lax.broadcasted_iota(jnp.int32, (group, slots), 0) + base
        total = jnp.zeros((group, 2 * BLK), jnp.float32)
        for side in range(2):
            target = jnp.where(used_lane, lanes_ref[side : side + 1, :], -1)
            choose = jnp.where(rows == target, 1.0, 0.0).astype(jnp.bfloat16)
            total = total + jnp.dot(choose, split[side], preferred_element_type=jnp.float32)
        out_ref[base : base + group, :] = total[:, :BLK] + total[:, BLK:]


def tile_terms(whole, couples, live, tiles):
    slots = tiles.shape[0]
    smem = pl.BlockSpec(memory_space=pltpu.SMEM)
    vmem = pl.BlockSpec(memory_space=pltpu.VMEM)
    return pl.pallas_call(
        tiles_kernel,
        out_shape=jax.ShapeDtypeStruct(whole.shape, jnp.float32),
        in_specs=[smem, smem, vmem, vmem, pl.BlockSpec(memory_space=pl.ANY)],
        out_specs=vmem,
        scratch_shapes=[
            pltpu.VMEM(tiles.shape, jnp.float32),
            pltpu.VMEM((2, slots, BLK), jnp.float32),
            pltpu.SemaphoreType.DMA((slots // CHUNK,)),
        ],
        compiler_params=params(50),
        cost_estimate=cost(slots * BLK * BLK * 32, slots * BLK * BLK * 4),
        name="tiles",
    )(live, couples, couples, whole, tiles)


def sum_parts(parts_ref, rows):
    total = parts_ref[0, rows, :]
    for d in range(1, parts_ref.shape[0]):
        total = total + parts_ref[d, rows, :]
    return total


def middle_kernel(parts_ref, emitted_ref, mirror_ref, copies_ref):
    for half in range(emitted_ref.shape[0] // 8):
        rows = pl.ds(half * 8, 8)
        incident = sum_parts(parts_ref, rows)
        radiosity = emitted_ref[rows, :] + mirror_ref[rows, :] * incident
        for d in range(copies_ref.shape[0]):
            copies_ref[d, rows, :] = radiosity


def middle(parts, emitted, mirror):
    return pl.pallas_call(
        middle_kernel,
        out_shape=jax.ShapeDtypeStruct(parts.shape, jnp.float32),
        compiler_params=params(32),
        cost_estimate=cost(100_000, 600_000),
        name="middle",
    )(parts, emitted, mirror)


def last_kernel(scale, parts_ref, emitted_ref, mirror_ref, site_ref, rad_ref, source_ref):
    blocks = emitted_ref.shape[0]
    incident = sum_parts(parts_ref, slice(None))
    emitted = emitted_ref[...]
    mirror = mirror_ref[...]
    rad_ref[...] = emitted + mirror * incident
    absorbed = ((1.0 - mirror) * incident - emitted) * scale
    site = site_ref[...]
    lane = site & (LANES - 1)
    sheet = site >> 7
    sheets = source_ref.shape[1]
    sheet_iota = lax.broadcasted_iota(jnp.int32, (sheets, BLK), 0)
    lane_iota = lax.broadcasted_iota(jnp.int32, (LANES, BLK), 0)
    left = []
    right = []
    for b in range(blocks):
        here = jnp.where(sheet_iota == sheet[b : b + 1, :], absorbed[b : b + 1, :], 0.0)
        left.append(here)
        pick = jnp.where(lane_iota == lane[b : b + 1, :], 1.0, 0.0)
        right.append(pick.astype(jnp.bfloat16))
    left = jnp.concatenate(left, axis=1)
    right = jnp.concatenate(right, axis=1)
    source = jnp.zeros((sheets, LANES), jnp.float32)
    for part in parts_of(left, 3):
        source = source + lax.dot_general(part, right, NT, preferred_element_type=jnp.float32)
    for d in range(source_ref.shape[0]):
        source_ref[d] = source


def last(parts, emitted, mirror, site, cells, count):
    weight = cells / (mirror.shape[0] * BLK * 1.0)
    return pl.pallas_call(
        functools.partial(last_kernel, step_size * weight),
        out_shape=(
            jax.ShapeDtypeStruct(mirror.shape, jnp.float32),
            jax.ShapeDtypeStruct((count, cells // LANES, LANES), jnp.float32),
        ),
        compiler_params=params(32),
        cost_estimate=cost(10_000_000, 600_000),
        name="last",
    )(parts, emitted, mirror, site)


def first_planes(depth, ny, nz):
    return pl.BlockSpec((depth, ny, nz), lambda i: (0, 0, 0))


def pack_x_kernel(t_low, k_low, k_low_thin, t_high, k_high, k_high_thin, low_ref, high_ref):
    ny, nz = t_low.shape[1:]
    tail = 2 * DEPTH * ny
    piece = ny * LANES // nz
    for send, temp, cond, thin, at in (
        (low_ref, t_low, k_low, k_low_thin, DEPTH),
        (high_ref, t_high, k_high, k_high_thin, k_high_thin.shape[0] - DEPTH - 1),
    ):
        for p in range(DEPTH):
            send[p * ny : p * ny + ny, :] = temp[p]
            send[(DEPTH + p) * ny : (DEPTH + p + 1) * ny, :] = cond[p]
        for j in range(nz // LANES):
            send[tail:, j * LANES : (j + 1) * LANES] = thin[at, j * piece : (j + 1) * piece, :]


def pack_x(temp, cond):
    nx, ny, nz = temp.shape
    ends = 2 * DEPTH
    rows = 2 * DEPTH * ny + ny * LANES // nz
    first = pl.BlockSpec((DEPTH, ny, nz), lambda i: (0, 0, 0))
    final = pl.BlockSpec((DEPTH, ny, nz), lambda i: (nx // DEPTH - 1, 0, 0))
    first_thin = pl.BlockSpec((ends, ny, LANES), lambda i: (0, 0, 0))
    final_thin = pl.BlockSpec((ends, ny, LANES), lambda i: (nx // ends - 1, 0, 0))
    whole = pl.BlockSpec((rows, nz), lambda i: (0, 0))
    shape = jax.ShapeDtypeStruct((rows, nz), jnp.float32)
    return pl.pallas_call(
        pack_x_kernel,
        grid=(1,),
        out_shape=(shape, shape),
        in_specs=[first, first, first_thin, final, final, final_thin],
        out_specs=(whole, whole),
        compiler_params=params(64),
        cost_estimate=cost(0, 4 * rows * nz * 4),
        name="pack_x",
    )(temp, cond, cond, temp, cond, cond)


def pack_y_kernel(nx, ny, t0, k0, t7, k7, low_ref, high_ref, down_ref, up_ref):
    upper = lax.broadcasted_iota(jnp.int32, down_ref.shape[1:], 0) < ROWS

    def edge(x, t_first, k_first, t_final, k_final):
        down_ref[x] = jnp.where(upper, t_first, pltpu.roll(k_first, ROWS, 0))
        up_ref[x] = jnp.where(upper, pltpu.roll(t_final, ROWS, 0), k_final)

    for side, base in ((low_ref, 0), (high_ref, DEPTH + nx)):
        for p in range(DEPTH):
            t_at, k_at = p * ny, (DEPTH + p) * ny
            edge(
                base + p,
                side[t_at : t_at + 8, :],
                side[k_at : k_at + 8, :],
                side[t_at + ny - 8 : t_at + ny, :],
                side[k_at + ny - 8 : k_at + ny, :],
            )
    for x in range(nx):
        edge(DEPTH + x, t0[x], k0[x], t7[x], k7[x])


def pack_y(temp, cond, low, high):
    nx, ny, nz = temp.shape
    first = pl.BlockSpec((nx, 8, nz), lambda i: (0, 0, 0))
    final = pl.BlockSpec((nx, 8, nz), lambda i: (0, ny // 8 - 1, 0))
    halo = pl.BlockSpec(low.shape, lambda i: (0, 0))
    tall = nx + 2 * DEPTH
    whole = pl.BlockSpec((tall, 8, nz), lambda i: (0, 0, 0))
    shape = jax.ShapeDtypeStruct((tall, 8, nz), jnp.float32)
    return pl.pallas_call(
        functools.partial(pack_y_kernel, nx, ny),
        grid=(1,),
        out_shape=(shape, shape),
        in_specs=[first, first, final, final, halo, halo],
        out_specs=(whole, whole),
        compiler_params=params(64),
        cost_estimate=cost(0, 4 * tall * 8 * nz * 4),
        name="pack_y",
    )(temp, cond, temp, cond, low, high)


def coupling(a, b):
    return jnp.where(jnp.minimum(a, b) > 0.0, (0.5 * step_size) * (a + b), 0.0)


def neighbours():
    slab, pair = lax.axis_index("slab"), lax.axis_index("pair")
    return slab > 0, slab < lax.axis_size("slab") - 1, pair > 0, pair < lax.axis_size("pair") - 1


def lane_tiles(nz):
    return [slice(j * LANES, (j + 1) * LANES) for j in range(nz // LANES)]


def prepare(cond, gx, gy, gz, gb):
    tall, wide, nz = cond.shape
    tiles = wide // 8
    lane = lax.broadcasted_iota(jnp.int32, (8, LANES), 1)
    half = 0.5 * step_size

    @pl.loop(0, tall)
    def _(x):
        after = jnp.minimum(x + 1, tall - 1)
        stores = Lagging(LAG)
        for z in lane_tiles(nz):
            last = z.stop == nz
            for t in range(tiles):
                rows = slice(8 * t, 8 * t + 8)
                here = cond[x, rows, z]
                stores.add(put(gx, (x, rows, z), half * (here + cond[after, rows, z])))
                if t + 1 < tiles:
                    beside = cond[x, 8 * t + 8 : 8 * t + 16, z]
                else:
                    beside = pltpu.roll(cond[x, :8, z], 7, 0)
                stores.add(put(gy, (x, rows, z), half * (here + beside)))
                turned = pltpu.roll(here, LANES - 1, 1)
                if last:
                    deeper = here
                else:
                    deeper = pltpu.roll(cond[x, rows, z.stop : z.stop + LANES], LANES - 1, 1)
                deeper = jnp.where(lane < LANES - 1, turned, deeper)
                stores.add(put(gz, (x, rows, z), half * (here + deeper)))
                if z.start == 0:
                    stores.add(put(gb, (x, rows), step_size * here))
        stores.finish()


def one_step(field, begin, end, target, gx, gy, gz, gb, carried):
    wide, nz = field.shape[1:]
    tiles = wide // 8
    lane = lax.broadcasted_iota(jnp.int32, (8, LANES), 1)
    sub = lax.broadcasted_iota(jnp.int32, (8, LANES), 0)
    _, _, has_below, has_above = neighbours()
    keep_above = (sub < 7) | has_above
    keep_below = (sub < 7) | has_below

    carried[...] = gx[begin - 1] * (field[begin] - field[begin - 1])

    @pl.loop(begin, end)
    def _(x):
        here, across_y = {}, {}
        stores = Lagging(LAG)
        spans = lane_tiles(nz)
        count = len(spans)

        def tile(t, j):
            if (t, j) not in here:
                here[t, j] = field[x, 8 * t : 8 * t + 8, spans[j]]
            return here[t, j]

        def y_flux(t, j):
            if (t, j) not in across_y:
                if t + 1 < tiles:
                    beside = tile(t + 1, j)
                else:
                    beside = pltpu.roll(tile(0, j), 7, 0)
                across_y[t, j] = gy[x, 8 * t : 8 * t + 8, spans[j]] * (beside - tile(t, j))
            return across_y[t, j]

        for t in range(tiles):
            rows = slice(8 * t, 8 * t + 8)
            turned = [pltpu.roll(tile(t, j), LANES - 1, 1) for j in range(count)]
            flux = []
            for j in range(count):
                deeper = turned[j + 1] if j + 1 < count else 0.0
                deeper = jnp.where(lane < LANES - 1, turned[j], deeper)
                flux.append(gz[x, rows, spans[j]] * (deeper - tile(t, j)))
            back = [pltpu.roll(f, 1, 1) for f in flux]
            for j in range(count):
                now = tile(t, j)
                low_z = back[j - 1] if j else gb[x, rows, :] * now
                low_z = jnp.where(lane > 0, back[j], low_z)
                x_flux = gx[x, rows, spans[j]] * (field[x + 1, rows, spans[j]] - now)
                low_x = carried[rows, spans[j]]
                stores.add(put(carried, (rows, spans[j]), x_flux))
                low_y = y_flux(t - 1, j) if t else pltpu.roll(y_flux(tiles - 1, j), 1, 0)
                new = now + (x_flux - low_x) + (y_flux(t, j) - low_y) + (flux[j] - low_z)
                if t:
                    new = jnp.where(keep_above if t <= ROWS else keep_below, new, 0.0)
                stores.add(put(*target(x, t, spans[j]), new))
        stores.finish()


def thin_planes(cond, ny, thin_ref, base_plane):
    tall, _, wide, _ = cond.shape
    lane = lax.broadcasted_iota(jnp.int32, (wide, LANES), 1)
    y_lane = lax.broadcasted_iota(jnp.int32, (8, LANES), 1)
    for base in range(0, tall, 16):
        planes = min(16, tall - base)
        gathered = jnp.zeros((wide, LANES), jnp.float32)
        for g in range(planes):
            piece = cond[base + g, 0]
            if g:
                piece = pltpu.roll(piece, 8 * g, 1)
            gathered = jnp.where((lane >> 3) == g, piece, gathered)
        turned = jnp.concatenate(
            [gathered, jnp.zeros((LANES - wide, LANES), jnp.float32)], axis=0
        ).T
        for g in range(planes):
            rows = turned[8 * g : 8 * g + 8, :]
            moved = pltpu.roll(rows, LANES - wide, 1)
            thin_ref[base_plane + base + g] = jnp.where(
                y_lane < ny + ROWS, rows, jnp.where(y_lane >= LANES - ROWS, moved, 0.0)
            )


def first_round_kernel(
    t_ref, k_ref, low_ref, high_ref, below_ref, above_ref,
    out_ref, low_out, high_out, cond_out, thin_ref,
    loaded, field, between, gx, gy, gz, gb, carried, sems,
):
    nx, ny, nz = t_ref.shape
    tall, wide = nx + 2 * DEPTH, ny + 2 * ROWS
    tiles = wide // 8
    raw_t, raw_k = loaded.at[0], loaded.at[1]
    spans = lane_tiles(nz)
    copies = [
        pltpu.make_async_copy(
            ref.at[:, :, pl.ds(z.start, LANES)],
            loaded.at[which, pl.ds(DEPTH, nx), j, pl.ds(0, ny)],
            sems.at[which, j],
        )
        for which, ref in ((1, k_ref), (0, t_ref))
        for j, z in enumerate(spans)
    ]
    for copy in copies:
        copy.start()
    has_low, has_high, has_below, has_above = neighbours()
    upper = lax.broadcasted_iota(jnp.int32, (8, LANES), 0) < ROWS
    for side, base in ((low_ref, 0), (high_ref, DEPTH + nx)):
        for p in range(DEPTH):
            for j, z in enumerate(spans):
                raw_t[base + p, j, :ny] = side[p * ny : p * ny + ny, z]
                raw_k[base + p, j, :ny] = side[(DEPTH + p) * ny : (DEPTH + p + 1) * ny, z]

    @pl.loop(0, tall)
    def _(x):
        for j, z in enumerate(spans):
            down, up = above_ref[x, :, z], below_ref[x, :, z]
            raw_t[x, j, ny:] = jnp.where(upper, down, pltpu.roll(up, ROWS, 0))
            raw_k[x, j, ny:] = jnp.where(upper, pltpu.roll(down, ROWS, 0), up)

    for copy in copies:
        copy.wait()

    piece = ny * LANES // nz
    tail = 2 * DEPTH * ny
    thin_planes(raw_k, ny, thin_ref, HALO - DEPTH)
    for side, at in ((low_ref, HALO - DEPTH - 1), (high_ref, HALO + nx + DEPTH)):
        edge = [side[tail:, z] for z in lane_tiles(nz)]
        edge.append(jnp.zeros((LANES - ny, LANES), jnp.float32))
        turned = jnp.concatenate(edge, axis=0).T
        thin_ref[at] = turned[:8]
    for at in [*range(HALO - DEPTH - 1), *range(HALO + nx + DEPTH + 1, nx + 2 * HALO)]:
        thin_ref[at] = jnp.zeros((8, LANES), jnp.float32)

    @pl.loop(0, tall)
    def _(x):
        missing = (upper & jnp.logical_not(has_above)) | (
            jnp.logical_not(upper) & jnp.logical_not(has_below)
        )
        for j in range(len(spans)):
            edge = raw_k[x, j, ny:]
            last = jnp.broadcast_to(raw_k[x, j, ny - 1 : ny, :], edge.shape)
            first = jnp.broadcast_to(raw_k[x, j, 0:1, :], edge.shape)
            raw_k[x, j, ny:] = jnp.where(missing, jnp.where(upper, last, first), edge)

    @pl.when(jnp.logical_not(has_low))
    def _():
        for p in range(DEPTH):
            raw_k[p] = raw_k[DEPTH]

    @pl.when(jnp.logical_not(has_high))
    def _():
        for p in range(DEPTH):
            raw_k[DEPTH + nx + p] = raw_k[DEPTH + nx - 1]

    @pl.loop(0, tall)
    def _(x):
        stores = Lagging(LAG)
        for t in range(tiles):
            rows = pl.ds(t, 8, stride=tiles)
            for j, z in enumerate(spans):
                stores.add(put(field, (x, slice(8 * t, 8 * t + 8), z), loaded[0, x, j, rows, :]))
                stores.add(put(cond_out, (x, slice(8 * t, 8 * t + 8), z), loaded[1, x, j, rows, :]))
        stores.finish()

    prepare(cond_out, gx, gy, gz, gb)

    def target(x, t, z):
        return out_ref, (x - DEPTH, slice(8 * t, 8 * t + 8), z)

    two_steps(field, between, gx, gy, gz, gb, carried, target)
    low_out[...] = out_ref[:DEPTH]
    high_out[...] = out_ref[nx - DEPTH :]


def two_steps(field, between, gx, gy, gz, gb, carried, target):
    tall = field.shape[0]
    has_low, has_high, _, _ = neighbours()
    for x in (1, tall - 2):
        between[x] = jnp.zeros(field.shape[1:], jnp.float32)

    def inner(x, t, z):
        return between, (x, slice(8 * t, 8 * t + 8), z)

    begin = jnp.where(has_low, 1, DEPTH)
    end = jnp.where(has_high, tall - 1, tall - DEPTH)
    one_step(field, begin, end, inner, gx, gy, gz, gb, carried)
    one_step(between, DEPTH, tall - DEPTH, target, gx, gy, gz, gb, carried)


def heat_scratch(tall, wide, nz):
    big = pltpu.VMEM((tall, wide, nz), jnp.float32)
    return [
        big,
        big,
        big,
        big,
        big,
        pltpu.VMEM((tall, wide, LANES), jnp.float32),
        pltpu.VMEM((wide, nz), jnp.float32),
    ]


def first_round(temp, cond, low, high, below, above):
    nx, ny, nz = temp.shape
    tall, wide = nx + 2 * DEPTH, ny + 2 * ROWS
    hbm = pl.BlockSpec(memory_space=pl.ANY)
    vmem = pl.BlockSpec(memory_space=pltpu.VMEM)
    plane = jax.ShapeDtypeStruct((DEPTH, wide, nz), jnp.float32)
    return pl.pallas_call(
        first_round_kernel,
        out_shape=(
            jax.ShapeDtypeStruct((nx, wide, nz), jnp.float32),
            plane,
            plane,
            jax.ShapeDtypeStruct((tall, wide, nz), jnp.float32),
            jax.ShapeDtypeStruct((nx + 2 * HALO, 8, LANES), jnp.float32),
        ),
        in_specs=[hbm, hbm] + [vmem] * 4,
        scratch_shapes=[pltpu.VMEM((2, tall, nz // LANES, wide, LANES), jnp.float32)]
        + heat_scratch(tall, wide, nz)
        + [pltpu.SemaphoreType.DMA((2, nz // LANES))],
        compiler_params=params(64),
        cost_estimate=cost(tall * wide * nz * 100, 12 * nx * ny * nz * 4),
        name="first_round",
    )(temp, cond, low, high, below, above)


def second_round_kernel(
    t_ref, low_ref, high_ref, k_ref, out_ref,
    cond, field, between, gx, gy, gz, gb, carried, placed, sems,
):
    nx, wide, nz = t_ref.shape
    ny = out_ref.shape[1]
    tiles = wide // 8
    copies = [
        pltpu.make_async_copy(k_ref, cond, sems.at[0]),
        pltpu.make_async_copy(t_ref, field.at[pl.ds(DEPTH, nx)], sems.at[1]),
        pltpu.make_async_copy(low_ref, field.at[pl.ds(0, DEPTH)], sems.at[2]),
        pltpu.make_async_copy(high_ref, field.at[pl.ds(DEPTH + nx, DEPTH)], sems.at[3]),
    ]
    for copy in copies:
        copy.start()
    copies[0].wait()
    prepare(cond, gx, gy, gz, gb)
    for copy in copies[1:]:
        copy.wait()

    def target(x, t, z):
        return placed, (x - DEPTH, z.start // LANES, pl.ds(t, 8, stride=tiles))

    two_steps(field, between, gx, gy, gz, gb, carried, target)

    @pl.loop(0, nx)
    def _(x):
        for j, z in enumerate(lane_tiles(out_ref.shape[2])):
            out_ref[x, :, z] = placed[x, j, :ny, :]


def second_round(temp, low, high, cond, shape):
    nx, wide, nz = temp.shape
    tall = cond.shape[0]
    hbm = pl.BlockSpec(memory_space=pl.ANY)
    return pl.pallas_call(
        second_round_kernel,
        out_shape=jax.ShapeDtypeStruct(shape, jnp.float32),
        in_specs=[hbm] * 4,
        scratch_shapes=[pltpu.VMEM((tall, wide, nz), jnp.float32)]
        + heat_scratch(tall, wide, nz)
        + [
            pltpu.VMEM((nx, nz // LANES, wide, LANES), jnp.float32),
            pltpu.SemaphoreType.DMA((4,)),
        ],
        compiler_params=params(64),
        cost_estimate=cost(tall * wide * nz * 60, 8 * nx * wide * nz * 4),
        name="second_round",
    )(temp, low, high, cond)


def source_kernel(ny, all_ref, thin_ref, base_ref, out_ref):
    tall = thin_ref.shape[0]
    nx = tall - 2 * HALO
    sheets = all_ref.shape[1]
    sub = lax.broadcasted_iota(jnp.int32, (8, LANES), 0)
    y_lane = lax.broadcasted_iota(jnp.int32, (8, LANES), 1)

    slabs, pairs = lax.axis_size("slab"), lax.axis_size("pair")

    def sheet(down, across):
        slab = lax.axis_index("slab") + down
        pair = lax.axis_index("pair") + across
        inside = (slab >= 0) & (slab < slabs) & (pair >= 0) & (pair < pairs)
        found = all_ref[jnp.where(inside, slab * pairs + pair, 0)]
        return jnp.where(inside, found, 0.0)

    def rows_of(down):
        low, own, high = (sheet(down, across) for across in (-1, 0, 1))
        out = []
        for half in range(2):
            if half == 0:
                own_at, high_at, low_at = own, pltpu.roll(high, ny, 1), pltpu.roll(low, ny, 1)
            else:
                own_at, high_at, low_at = pltpu.roll(own, ny, 1), high, low
            out.append(
                jnp.where(
                    y_lane < ny,
                    own_at,
                    jnp.where(
                        y_lane < ny + HALO,
                        high_at,
                        jnp.where(y_lane >= LANES - HALO, low_at, 0.0),
                    ),
                )
            )
        return out

    lines = [rows_of(down) for down in (-1, 0, 1)]
    source = []
    for x in range(-HALO, nx + HALO):
        which, local = (x + nx) // nx, x % nx
        row = lines[which][local % 2][local // 2 : local // 2 + 1, :]
        source.append(jnp.where(sub == 0, jnp.broadcast_to(row, (8, LANES)), 0.0))

    cond = [thin_ref[x] for x in range(tall)]
    cx, cy, cz, centre = [], [], [], []
    for x in range(tall):
        here = cond[x]
        after = cond[min(x + 1, tall - 1)]
        before = cond[max(x - 1, 0)]
        y_after = pltpu.roll(here, LANES - 1, 1)
        y_before = pltpu.roll(here, 1, 1)
        z_after = jnp.where(sub == 7, 0.0, pltpu.roll(here, 7, 0))
        z_before = jnp.where(sub == 0, 0.0, pltpu.roll(here, 1, 0))
        cx.append(coupling(here, after))
        cy.append(coupling(here, y_after))
        cz.append(coupling(here, z_after))
        total = 6.0 * here
        for near in (after, before, y_after, y_before, z_after, z_before):
            total = total + jnp.where(near > 0.0, near, here)
        centre.append(1.0 - (0.5 * step_size) * total)

    added = source
    for step in range(1, STEPS):
        new = list(added)
        for x in range(step, tall - step):
            here = added[x]
            total = source[x] + centre[x] * here
            total = total + (cx[x] * added[x + 1] + cx[x - 1] * added[x - 1])
            total = total + cy[x] * pltpu.roll(here, LANES - 1, 1)
            total = total + pltpu.roll(cy[x] * here, 1, 1)
            total = total + cz[x] * pltpu.roll(here, 7, 0)
            new[x] = total + pltpu.roll(cz[x] * here, 1, 0)
        added = new

    lane = lax.broadcasted_iota(jnp.int32, (ny, LANES), 1)
    turned = jnp.concatenate(added[HALO : HALO + nx], axis=0).T[:ny]
    for x in range(nx):
        piece = turned if x == 0 else pltpu.roll(turned, LANES - 8 * x, 1)
        out_ref[x] = base_ref[x] + jnp.where(lane < STEPS, piece, 0.0)


def add_source(everything, thin, base):
    nx, ny, nz = base.shape
    block = pl.BlockSpec((nx, ny, LANES), lambda i: (0, 0, 0))
    return pl.pallas_call(
        functools.partial(source_kernel, ny),
        grid=(1,),
        out_shape=jax.ShapeDtypeStruct(base.shape, jnp.float32),
        in_specs=[
            pl.BlockSpec(everything.shape, lambda i: (0, 0, 0)),
            pl.BlockSpec(thin.shape, lambda i: (0, 0, 0)),
            block,
        ],
        out_specs=block,
        input_output_aliases={2: 0},
        compiler_params=params(64),
        cost_estimate=cost(1_000_000, 2 * nx * ny * LANES * 4),
        name="add_source",
    )(everything, thin, base)


def swap(rows, axis):
    return lax.all_to_all(rows, axis, split_axis=0, concat_axis=0, tiled=True)


def gather(copies):
    column = swap(copies, "slab")
    pairs = lax.axis_size("pair")
    everyone = jnp.broadcast_to(column[None], (pairs,) + column.shape)
    return swap(everyone, "pair")


def reduce_pairs(term):
    pairs, slabs = lax.axis_size("pair"), lax.axis_size("slab")
    parts = swap(term, "pair").reshape(pairs, slabs, -1, BLK)
    return swap(parts.sum(axis=0), "slab")


def together(*arrays):
    return lax.optimization_barrier(arrays)


def both_ways(low, high, axis):
    count = lax.axis_size(axis)
    forward = [(i, i + 1) for i in range(count - 1)]
    backward = [(target, source) for source, target in forward]
    from_low = lax.ppermute(high, axis, forward)
    from_high = lax.ppermute(low, axis, backward)
    return from_low, from_high


def shards(
    initial_warmth,
    heat_passing_coefficient,
    mirror_fraction,
    element_facing_site,
    tile_block_couples,
    active_slot_count,
    view_factor_blocks,
):
    nx, ny, _ = initial_warmth.shape
    slabs, pairs = lax.axis_size("slab"), lax.axis_size("pair")
    count = slabs * pairs
    blocks = mirror_fraction.shape[0]
    couples = tile_block_couples.T
    owner, local = couples // blocks, couples % blocks
    couples = ((owner % pairs) * slabs + owner // pairs) * blocks + local

    temp, cond = initial_warmth, heat_passing_coefficient
    emitted, copies = emit(temp, element_facing_site, mirror_fraction, slabs)
    temp, copies = together(temp, copies)

    def sweep_terms(whole):
        whole = whole.reshape(count * blocks, BLK)
        term = tile_terms(whole, couples, active_slot_count, view_factor_blocks)
        return term.reshape(pairs, slabs * blocks, BLK)

    whole = gather(copies)
    send_low, send_high = pack_x(temp, cond)
    low, high = both_ways(send_low, send_high, "slab")
    whole = together(whole, send_low, send_high)[0]
    parts = reduce_pairs(sweep_terms(whole))
    send_down, send_up = pack_y(temp, cond, low, high)
    parts = together(parts, send_down, send_up)[0]
    below, above = both_ways(send_down, send_up, "pair")
    whole = gather(middle(parts, emitted, mirror_fraction))
    middle_temp, send_low, send_high, strided_cond, thin = first_round(
        temp, cond, low, high, below, above
    )
    low, high = both_ways(send_low, send_high, "slab")
    whole = together(whole, send_low, send_high)[0]
    term, low, high = together(sweep_terms(whole), low, high)
    parts = reduce_pairs(term)
    base = second_round(middle_temp, low, high, strided_cond, temp.shape)
    parts = together(parts, base)[0]
    radiosity, source = last(parts, emitted, mirror_fraction, element_facing_site, nx * ny, count)
    everything = lax.all_to_all(
        source, ("slab", "pair"), split_axis=0, concat_axis=0, tiled=True
    )

    warmed_liner = add_source(everything, thin, base)
    return (radiosity, warmed_liner)


def solution(mesh):
    return jax.shard_map(
        shards,
        mesh=mesh,
        in_specs=(
            P("slab", "pair", None),
            P("slab", "pair", None),
            P(("slab", "pair"), None),
            P(("slab", "pair"), None),
            P(("slab", "pair"), None),
            P(("slab", "pair")),
            P(("slab", "pair"), None, None),
        ),
        out_specs=(P(("slab", "pair"), None), P("slab", "pair", None)),
        check_vma=False,
    )
```

```python
import functools

import jax
import jax.numpy as jnp
from jax import lax
from jax.experimental import pallas as pl
from jax.experimental.pallas import tpu as pltpu
from jax.sharding import PartitionSpec as P

BLK = 128
SWEEPS = 2
STEPS = 4
HALO = STEPS
DEPTH = STEPS // 2
ROWS = STEPS
LANES = 128
CHUNK = 16
LAG = 12

step_size = 0.07

NT = (((1,), (1,)), ((), ()))
NN = (((1,), (0,)), ((), ()))


def params(mib):
    return pltpu.CompilerParams(vmem_limit_bytes=mib * 1024 * 1024)


def cost(flops, nbytes):
    return pl.CostEstimate(flops=flops, bytes_accessed=nbytes, transcendentals=0)


def parts_of(x, count):
    out = []
    for _ in range(count - 1):
        part = x.astype(jnp.bfloat16)
        out.append(part)
        x = x - part.astype(jnp.float32)
    out.append(x.astype(jnp.bfloat16))
    return out


class Lagging:
    def __init__(self, depth):
        self.depth = depth
        self.waiting = []

    def add(self, store):
        self.waiting.append(store)
        if len(self.waiting) > self.depth:
            self.waiting.pop(0)()

    def finish(self):
        for store in self.waiting:
            store()
        self.waiting = []


def put(ref, index, value):
    return lambda: ref.__setitem__(index, value)


def emit_kernel(temp_ref, site_ref, mirror_ref, emitted_ref, copies_ref):
    nx, ny, _ = temp_ref.shape
    sheets = nx * ny // LANES
    per = LANES // ny
    lanes = lax.broadcasted_iota(jnp.int32, (LANES, LANES), 1)
    gathered = jnp.zeros((LANES, LANES), jnp.float32)
    for r in range(sheets):
        piece = temp_ref[per * r : per * r + per].reshape(LANES, LANES)
        if r:
            piece = pltpu.roll(piece, r, 1)
        gathered = jnp.where(lanes == r, piece, gathered)
    plane = gathered.T[:sheets]
    for half in range(site_ref.shape[0] // 8):
        rows = pl.ds(half * 8, 8)
        site = site_ref[rows, :]
        lane = site & (LANES - 1)
        sheet = site >> 7
        warmth = jnp.zeros(site.shape, jnp.float32)
        for r in range(sheets):
            line = jnp.broadcast_to(plane[r : r + 1, :], site.shape)
            picked = jnp.take_along_axis(line, lane, axis=1)
            warmth = jnp.where(sheet == r, picked, warmth)
        square = warmth * warmth
        emitted = (1.0 - mirror_ref[rows, :]) * (square * square)
        emitted_ref[rows, :] = emitted
        for d in range(copies_ref.shape[0]):
            copies_ref[d, rows, :] = emitted


def emit(temp, site, mirror, count):
    shape = mirror.shape
    nx, ny, _ = temp.shape
    patch = pl.BlockSpec(shape, lambda i: (0, 0))
    return pl.pallas_call(
        emit_kernel,
        grid=(1,),
        out_shape=(
            jax.ShapeDtypeStruct(shape, jnp.float32),
            jax.ShapeDtypeStruct((count,) + shape, jnp.float32),
        ),
        in_specs=[pl.BlockSpec((nx, ny, LANES), lambda i: (0, 0, 0)), patch, patch],
        out_specs=(patch, pl.BlockSpec((count,) + shape, lambda i: (0, 0, 0))),
        compiler_params=params(64),
        cost_estimate=cost(10_000, 900_000),
        name="emit",
    )(temp, site, mirror)


def tiles_kernel(
    live_ref, pairs_ref, lanes_ref, whole_ref, tiles_ref, out_ref, held, terms, sems
):
    slots = held.shape[0]
    live = live_ref[0]
    chunks = (live + CHUNK - 1) // CHUNK

    def chunk_copy(c):
        span = pl.ds(c * CHUNK, CHUNK)
        return pltpu.make_async_copy(tiles_ref.at[span], held.at[span], sems.at[c])

    @pl.loop(0, chunks)
    def _(c):
        chunk_copy(c).start()

    top = lax.broadcasted_iota(jnp.int32, (8, BLK), 0) == 0

    def split_row(block):
        row = jnp.broadcast_to(whole_ref[pl.ds(block, 1), :], (8, BLK))
        high = row.astype(jnp.bfloat16).astype(jnp.float32)
        return jnp.where(top, high, row - high)

    def vectors(a, b):
        stacked = jnp.concatenate([split_row(a), split_row(b)], axis=0)
        stacked = stacked.astype(jnp.bfloat16)
        return jnp.concatenate([stacked, stacked], axis=1)

    @pl.loop(0, chunks)
    def _(c):
        chunk_copy(c).wait()
        stores = Lagging(4 * CHUNK)
        for u in range(0, CHUNK, 2):
            t = c * CHUNK + u
            high_a, low_a = parts_of(held[t], 2)
            high_b, low_b = parts_of(held[t + 1], 2)
            both = jnp.concatenate(
                [
                    jnp.concatenate([high_a, high_b], axis=1),
                    jnp.concatenate([low_a, low_b], axis=1),
                ],
                axis=0,
            )
            second = lax.dot_general(
                vectors(pairs_ref[0, t], pairs_ref[0, t + 1]),
                both,
                NN,
                preferred_element_type=jnp.float32,
            )
            turned = jnp.concatenate(
                [
                    jnp.concatenate([high_a, low_a], axis=1),
                    jnp.concatenate([high_b, low_b], axis=1),
                ],
                axis=0,
            )
            first = lax.dot_general(
                vectors(pairs_ref[1, t], pairs_ref[1, t + 1]),
                turned,
                NT,
                preferred_element_type=jnp.float32,
            )
            for side, result in ((0, first), (1, second)):
                for v, (top_row, cols) in enumerate(((0, slice(0, BLK)), (8, slice(BLK, 2 * BLK)))):
                    row = result[top_row : top_row + 1, cols] + result[top_row + 1 : top_row + 2, cols]
                    stores.add(put(terms, (side, pl.ds(t + v, 1)), row))
        stores.finish()

    used = lax.broadcasted_iota(jnp.int32, (slots, BLK), 0) < live
    used_lane = lax.broadcasted_iota(jnp.int32, (1, slots), 1) < live
    blocks = out_ref.shape[0]
    group = min(blocks, 512)
    split = []
    for side in range(2):
        masked = jnp.where(used, terms[side], 0.0)
        split.append(jnp.concatenate(parts_of(masked, 2), axis=1))
    for base in range(0, blocks, group):
        rows = lax.broadcasted_iota(jnp.int32, (group, slots), 0) + base
        total = jnp.zeros((group, 2 * BLK), jnp.float32)
        for side in range(2):
            target = jnp.where(used_lane, lanes_ref[side : side + 1, :], -1)
            choose = jnp.where(rows == target, 1.0, 0.0).astype(jnp.bfloat16)
            total = total + jnp.dot(choose, split[side], preferred_element_type=jnp.float32)
        out_ref[base : base + group, :] = total[:, :BLK] + total[:, BLK:]


def tile_terms(whole, couples, live, tiles):
    slots = tiles.shape[0]
    smem = pl.BlockSpec(memory_space=pltpu.SMEM)
    vmem = pl.BlockSpec(memory_space=pltpu.VMEM)
    return pl.pallas_call(
        tiles_kernel,
        out_shape=jax.ShapeDtypeStruct(whole.shape, jnp.float32),
        in_specs=[smem, smem, vmem, vmem, pl.BlockSpec(memory_space=pl.ANY)],
        out_specs=vmem,
        scratch_shapes=[
            pltpu.VMEM(tiles.shape, jnp.float32),
            pltpu.VMEM((2, slots, BLK), jnp.float32),
            pltpu.SemaphoreType.DMA((slots // CHUNK,)),
        ],
        compiler_params=params(50),
        cost_estimate=cost(slots * BLK * BLK * 32, slots * BLK * BLK * 4),
        name="tiles",
    )(live, couples, couples, whole, tiles)


def sum_parts(parts_ref, rows):
    total = parts_ref[0, rows, :]
    for d in range(1, parts_ref.shape[0]):
        total = total + parts_ref[d, rows, :]
    return total


def middle_kernel(parts_ref, emitted_ref, mirror_ref, copies_ref):
    for half in range(emitted_ref.shape[0] // 8):
        rows = pl.ds(half * 8, 8)
        incident = sum_parts(parts_ref, rows)
        radiosity = emitted_ref[rows, :] + mirror_ref[rows, :] * incident
        for d in range(copies_ref.shape[0]):
            copies_ref[d, rows, :] = radiosity


def middle(parts, emitted, mirror):
    return pl.pallas_call(
        middle_kernel,
        out_shape=jax.ShapeDtypeStruct(parts.shape, jnp.float32),
        compiler_params=params(32),
        cost_estimate=cost(100_000, 600_000),
        name="middle",
    )(parts, emitted, mirror)


def last_kernel(scale, parts_ref, emitted_ref, mirror_ref, site_ref, rad_ref, source_ref):
    blocks = emitted_ref.shape[0]
    incident = sum_parts(parts_ref, slice(None))
    emitted = emitted_ref[...]
    mirror = mirror_ref[...]
    rad_ref[...] = emitted + mirror * incident
    absorbed = ((1.0 - mirror) * incident - emitted) * scale
    site = site_ref[...]
    lane = site & (LANES - 1)
    sheet = site >> 7
    sheets = source_ref.shape[1]
    sheet_iota = lax.broadcasted_iota(jnp.int32, (sheets, BLK), 0)
    lane_iota = lax.broadcasted_iota(jnp.int32, (LANES, BLK), 0)
    left = []
    right = []
    for b in range(blocks):
        here = jnp.where(sheet_iota == sheet[b : b + 1, :], absorbed[b : b + 1, :], 0.0)
        left.append(here)
        pick = jnp.where(lane_iota == lane[b : b + 1, :], 1.0, 0.0)
        right.append(pick.astype(jnp.bfloat16))
    left = jnp.concatenate(left, axis=1)
    right = jnp.concatenate(right, axis=1)
    source = jnp.zeros((sheets, LANES), jnp.float32)
    for part in parts_of(left, 3):
        source = source + lax.dot_general(part, right, NT, preferred_element_type=jnp.float32)
    for d in range(source_ref.shape[0]):
        source_ref[d] = source


def last(parts, emitted, mirror, site, cells, count):
    weight = cells / (mirror.shape[0] * BLK * 1.0)
    return pl.pallas_call(
        functools.partial(last_kernel, step_size * weight),
        out_shape=(
            jax.ShapeDtypeStruct(mirror.shape, jnp.float32),
            jax.ShapeDtypeStruct((count, cells // LANES, LANES), jnp.float32),
        ),
        compiler_params=params(32),
        cost_estimate=cost(10_000_000, 600_000),
        name="last",
    )(parts, emitted, mirror, site)


def first_planes(depth, ny, nz):
    return pl.BlockSpec((depth, ny, nz), lambda i: (0, 0, 0))


def pack_x_kernel(t_low, k_low, k_low_thin, t_high, k_high, k_high_thin, low_ref, high_ref):
    ny, nz = t_low.shape[1:]
    tail = 2 * DEPTH * ny
    piece = ny * LANES // nz
    for send, temp, cond, thin, at in (
        (low_ref, t_low, k_low, k_low_thin, DEPTH),
        (high_ref, t_high, k_high, k_high_thin, k_high_thin.shape[0] - DEPTH - 1),
    ):
        for p in range(DEPTH):
            send[p * ny : p * ny + ny, :] = temp[p]
            send[(DEPTH + p) * ny : (DEPTH + p + 1) * ny, :] = cond[p]
        for j in range(nz // LANES):
            send[tail:, j * LANES : (j + 1) * LANES] = thin[at, j * piece : (j + 1) * piece, :]


def pack_x(temp, cond):
    nx, ny, nz = temp.shape
    ends = 2 * DEPTH
    rows = 2 * DEPTH * ny + ny * LANES // nz
    first = pl.BlockSpec((DEPTH, ny, nz), lambda i: (0, 0, 0))
    final = pl.BlockSpec((DEPTH, ny, nz), lambda i: (nx // DEPTH - 1, 0, 0))
    first_thin = pl.BlockSpec((ends, ny, LANES), lambda i: (0, 0, 0))
    final_thin = pl.BlockSpec((ends, ny, LANES), lambda i: (nx // ends - 1, 0, 0))
    whole = pl.BlockSpec((rows, nz), lambda i: (0, 0))
    shape = jax.ShapeDtypeStruct((rows, nz), jnp.float32)
    return pl.pallas_call(
        pack_x_kernel,
        grid=(1,),
        out_shape=(shape, shape),
        in_specs=[first, first, first_thin, final, final, final_thin],
        out_specs=(whole, whole),
        compiler_params=params(64),
        cost_estimate=cost(0, 4 * rows * nz * 4),
        name="pack_x",
    )(temp, cond, cond, temp, cond, cond)


def pack_y_kernel(nx, ny, t0, k0, t7, k7, low_ref, high_ref, down_ref, up_ref):
    upper = lax.broadcasted_iota(jnp.int32, down_ref.shape[1:], 0) < ROWS

    def edge(x, t_first, k_first, t_final, k_final):
        down_ref[x] = jnp.where(upper, t_first, pltpu.roll(k_first, ROWS, 0))
        up_ref[x] = jnp.where(upper, pltpu.roll(t_final, ROWS, 0), k_final)

    for side, base in ((low_ref, 0), (high_ref, DEPTH + nx)):
        for p in range(DEPTH):
            t_at, k_at = p * ny, (DEPTH + p) * ny
            edge(
                base + p,
                side[t_at : t_at + 8, :],
                side[k_at : k_at + 8, :],
                side[t_at + ny - 8 : t_at + ny, :],
                side[k_at + ny - 8 : k_at + ny, :],
            )
    for x in range(nx):
        edge(DEPTH + x, t0[x], k0[x], t7[x], k7[x])


def pack_y(temp, cond, low, high):
    nx, ny, nz = temp.shape
    first = pl.BlockSpec((nx, 8, nz), lambda i: (0, 0, 0))
    final = pl.BlockSpec((nx, 8, nz), lambda i: (0, ny // 8 - 1, 0))
    halo = pl.BlockSpec(low.shape, lambda i: (0, 0))
    tall = nx + 2 * DEPTH
    whole = pl.BlockSpec((tall, 8, nz), lambda i: (0, 0, 0))
    shape = jax.ShapeDtypeStruct((tall, 8, nz), jnp.float32)
    return pl.pallas_call(
        functools.partial(pack_y_kernel, nx, ny),
        grid=(1,),
        out_shape=(shape, shape),
        in_specs=[first, first, final, final, halo, halo],
        out_specs=(whole, whole),
        compiler_params=params(64),
        cost_estimate=cost(0, 4 * tall * 8 * nz * 4),
        name="pack_y",
    )(temp, cond, temp, cond, low, high)


def coupling(a, b):
    return jnp.where(jnp.minimum(a, b) > 0.0, (0.5 * step_size) * (a + b), 0.0)


def neighbours():
    slab, pair = lax.axis_index("slab"), lax.axis_index("pair")
    return slab > 0, slab < lax.axis_size("slab") - 1, pair > 0, pair < lax.axis_size("pair") - 1


def lane_tiles(nz):
    return [slice(j * LANES, (j + 1) * LANES) for j in range(nz // LANES)]


def prepare(cond, gx, gy, gz, gb):
    tall, wide, nz = cond.shape
    tiles = wide // 8
    lane = lax.broadcasted_iota(jnp.int32, (8, LANES), 1)
    half = 0.5 * step_size

    @pl.loop(0, tall)
    def _(x):
        after = jnp.minimum(x + 1, tall - 1)
        stores = Lagging(LAG)
        for z in lane_tiles(nz):
            last = z.stop == nz
            for t in range(tiles):
                rows = slice(8 * t, 8 * t + 8)
                here = cond[x, rows, z]
                stores.add(put(gx, (x, rows, z), half * (here + cond[after, rows, z])))
                if t + 1 < tiles:
                    beside = cond[x, 8 * t + 8 : 8 * t + 16, z]
                else:
                    beside = pltpu.roll(cond[x, :8, z], 7, 0)
                stores.add(put(gy, (x, rows, z), half * (here + beside)))
                turned = pltpu.roll(here, LANES - 1, 1)
                if last:
                    deeper = here
                else:
                    deeper = pltpu.roll(cond[x, rows, z.stop : z.stop + LANES], LANES - 1, 1)
                deeper = jnp.where(lane < LANES - 1, turned, deeper)
                stores.add(put(gz, (x, rows, z), half * (here + deeper)))
                if z.start == 0:
                    stores.add(put(gb, (x, rows), step_size * here))
        stores.finish()


def one_step(field, begin, end, target, gx, gy, gz, gb, carried):
    wide, nz = field.shape[1:]
    tiles = wide // 8
    lane = lax.broadcasted_iota(jnp.int32, (8, LANES), 1)
    sub = lax.broadcasted_iota(jnp.int32, (8, LANES), 0)
    _, _, has_below, has_above = neighbours()
    keep_above = (sub < 7) | has_above
    keep_below = (sub < 7) | has_below

    carried[...] = gx[begin - 1] * (field[begin] - field[begin - 1])

    @pl.loop(begin, end)
    def _(x):
        here, across_y = {}, {}
        stores = Lagging(LAG)
        spans = lane_tiles(nz)
        count = len(spans)

        def tile(t, j):
            if (t, j) not in here:
                here[t, j] = field[x, 8 * t : 8 * t + 8, spans[j]]
            return here[t, j]

        def y_flux(t, j):
            if (t, j) not in across_y:
                if t + 1 < tiles:
                    beside = tile(t + 1, j)
                else:
                    beside = pltpu.roll(tile(0, j), 7, 0)
                across_y[t, j] = gy[x, 8 * t : 8 * t + 8, spans[j]] * (beside - tile(t, j))
            return across_y[t, j]

        for t in range(tiles):
            rows = slice(8 * t, 8 * t + 8)
            turned = [pltpu.roll(tile(t, j), LANES - 1, 1) for j in range(count)]
            flux = []
            for j in range(count):
                deeper = turned[j + 1] if j + 1 < count else 0.0
                deeper = jnp.where(lane < LANES - 1, turned[j], deeper)
                flux.append(gz[x, rows, spans[j]] * (deeper - tile(t, j)))
            back = [pltpu.roll(f, 1, 1) for f in flux]
            for j in range(count):
                now = tile(t, j)
                low_z = back[j - 1] if j else gb[x, rows, :] * now
                low_z = jnp.where(lane > 0, back[j], low_z)
                x_flux = gx[x, rows, spans[j]] * (field[x + 1, rows, spans[j]] - now)
                low_x = carried[rows, spans[j]]
                stores.add(put(carried, (rows, spans[j]), x_flux))
                low_y = y_flux(t - 1, j) if t else pltpu.roll(y_flux(tiles - 1, j), 1, 0)
                new = now + (x_flux - low_x) + (y_flux(t, j) - low_y) + (flux[j] - low_z)
                if t:
                    new = jnp.where(keep_above if t <= ROWS else keep_below, new, 0.0)
                stores.add(put(*target(x, t, spans[j]), new))
        stores.finish()


def thin_planes(cond, ny, thin_ref, base_plane):
    tall, _, wide, _ = cond.shape
    lane = lax.broadcasted_iota(jnp.int32, (wide, LANES), 1)
    y_lane = lax.broadcasted_iota(jnp.int32, (8, LANES), 1)
    for base in range(0, tall, 16):
        planes = min(16, tall - base)
        gathered = jnp.zeros((wide, LANES), jnp.float32)
        for g in range(planes):
            piece = cond[base + g, 0]
            if g:
                piece = pltpu.roll(piece, 8 * g, 1)
            gathered = jnp.where((lane >> 3) == g, piece, gathered)
        turned = jnp.concatenate(
            [gathered, jnp.zeros((LANES - wide, LANES), jnp.float32)], axis=0
        ).T
        for g in range(planes):
            rows = turned[8 * g : 8 * g + 8, :]
            moved = pltpu.roll(rows, LANES - wide, 1)
            thin_ref[base_plane + base + g] = jnp.where(
                y_lane < ny + ROWS, rows, jnp.where(y_lane >= LANES - ROWS, moved, 0.0)
            )


def first_round_kernel(
    t_ref, k_ref, low_ref, high_ref, below_ref, above_ref,
    out_ref, low_out, high_out, cond_out, thin_ref,
    loaded, field, between, gx, gy, gz, gb, carried, sems,
):
    nx, ny, nz = t_ref.shape
    tall, wide = nx + 2 * DEPTH, ny + 2 * ROWS
    tiles = wide // 8
    raw_t, raw_k = loaded.at[0], loaded.at[1]
    spans = lane_tiles(nz)
    copies = [
        pltpu.make_async_copy(
            ref.at[:, :, pl.ds(z.start, LANES)],
            loaded.at[which, pl.ds(DEPTH, nx), j, pl.ds(0, ny)],
            sems.at[which, j],
        )
        for which, ref in ((1, k_ref), (0, t_ref))
        for j, z in enumerate(spans)
    ]
    for copy in copies:
        copy.start()
    has_low, has_high, has_below, has_above = neighbours()
    upper = lax.broadcasted_iota(jnp.int32, (8, LANES), 0) < ROWS
    for side, base in ((low_ref, 0), (high_ref, DEPTH + nx)):
        for p in range(DEPTH):
            for j, z in enumerate(spans):
                raw_t[base + p, j, :ny] = side[p * ny : p * ny + ny, z]
                raw_k[base + p, j, :ny] = side[(DEPTH + p) * ny : (DEPTH + p + 1) * ny, z]

    @pl.loop(0, tall)
    def _(x):
        for j, z in enumerate(spans):
            down, up = above_ref[x, :, z], below_ref[x, :, z]
            raw_t[x, j, ny:] = jnp.where(upper, down, pltpu.roll(up, ROWS, 0))
            raw_k[x, j, ny:] = jnp.where(upper, pltpu.roll(down, ROWS, 0), up)

    for copy in copies:
        copy.wait()

    piece = ny * LANES // nz
    tail = 2 * DEPTH * ny
    thin_planes(raw_k, ny, thin_ref, HALO - DEPTH)
    for side, at in ((low_ref, HALO - DEPTH - 1), (high_ref, HALO + nx + DEPTH)):
        edge = [side[tail:, z] for z in lane_tiles(nz)]
        edge.append(jnp.zeros((LANES - ny, LANES), jnp.float32))
        turned = jnp.concatenate(edge, axis=0).T
        thin_ref[at] = turned[:8]
    for at in [*range(HALO - DEPTH - 1), *range(HALO + nx + DEPTH + 1, nx + 2 * HALO)]:
        thin_ref[at] = jnp.zeros((8, LANES), jnp.float32)

    @pl.loop(0, tall)
    def _(x):
        missing = (upper & jnp.logical_not(has_above)) | (
            jnp.logical_not(upper) & jnp.logical_not(has_below)
        )
        for j in range(len(spans)):
            edge = raw_k[x, j, ny:]
            last = jnp.broadcast_to(raw_k[x, j, ny - 1 : ny, :], edge.shape)
            first = jnp.broadcast_to(raw_k[x, j, 0:1, :], edge.shape)
            raw_k[x, j, ny:] = jnp.where(missing, jnp.where(upper, last, first), edge)

    @pl.when(jnp.logical_not(has_low))
    def _():
        for p in range(DEPTH):
            raw_k[p] = raw_k[DEPTH]

    @pl.when(jnp.logical_not(has_high))
    def _():
        for p in range(DEPTH):
            raw_k[DEPTH + nx + p] = raw_k[DEPTH + nx - 1]

    @pl.loop(0, tall)
    def _(x):
        stores = Lagging(LAG)
        for t in range(tiles):
            rows = pl.ds(t, 8, stride=tiles)
            for j, z in enumerate(spans):
                stores.add(put(field, (x, slice(8 * t, 8 * t + 8), z), loaded[0, x, j, rows, :]))
                stores.add(put(cond_out, (x, slice(8 * t, 8 * t + 8), z), loaded[1, x, j, rows, :]))
        stores.finish()

    prepare(cond_out, gx, gy, gz, gb)

    def target(x, t, z):
        return out_ref, (x - DEPTH, slice(8 * t, 8 * t + 8), z)

    two_steps(field, between, gx, gy, gz, gb, carried, target)
    low_out[...] = out_ref[:DEPTH]
    high_out[...] = out_ref[nx - DEPTH :]


def two_steps(field, between, gx, gy, gz, gb, carried, target):
    tall = field.shape[0]
    has_low, has_high, _, _ = neighbours()
    for x in (1, tall - 2):
        between[x] = jnp.zeros(field.shape[1:], jnp.float32)

    def inner(x, t, z):
        return between, (x, slice(8 * t, 8 * t + 8), z)

    begin = jnp.where(has_low, 1, DEPTH)
    end = jnp.where(has_high, tall - 1, tall - DEPTH)
    one_step(field, begin, end, inner, gx, gy, gz, gb, carried)
    one_step(between, DEPTH, tall - DEPTH, target, gx, gy, gz, gb, carried)


def heat_scratch(tall, wide, nz):
    big = pltpu.VMEM((tall, wide, nz), jnp.float32)
    return [
        big,
        big,
        big,
        big,
        big,
        pltpu.VMEM((tall, wide, LANES), jnp.float32),
        pltpu.VMEM((wide, nz), jnp.float32),
    ]


def first_round(temp, cond, low, high, below, above):
    nx, ny, nz = temp.shape
    tall, wide = nx + 2 * DEPTH, ny + 2 * ROWS
    hbm = pl.BlockSpec(memory_space=pl.ANY)
    vmem = pl.BlockSpec(memory_space=pltpu.VMEM)
    plane = jax.ShapeDtypeStruct((DEPTH, wide, nz), jnp.float32)
    return pl.pallas_call(
        first_round_kernel,
        out_shape=(
            jax.ShapeDtypeStruct((nx, wide, nz), jnp.float32),
            plane,
            plane,
            jax.ShapeDtypeStruct((tall, wide, nz), jnp.float32),
            jax.ShapeDtypeStruct((nx + 2 * HALO, 8, LANES), jnp.float32),
        ),
        in_specs=[hbm, hbm] + [vmem] * 4,
        scratch_shapes=[pltpu.VMEM((2, tall, nz // LANES, wide, LANES), jnp.float32)]
        + heat_scratch(tall, wide, nz)
        + [pltpu.SemaphoreType.DMA((2, nz // LANES))],
        compiler_params=params(64),
        cost_estimate=cost(tall * wide * nz * 100, 12 * nx * ny * nz * 4),
        name="first_round",
    )(temp, cond, low, high, below, above)


def second_round_kernel(
    t_ref, low_ref, high_ref, k_ref, out_ref,
    cond, field, between, gx, gy, gz, gb, carried, placed, sems,
):
    nx, wide, nz = t_ref.shape
    ny = out_ref.shape[1]
    tiles = wide // 8
    copies = [
        pltpu.make_async_copy(k_ref, cond, sems.at[0]),
        pltpu.make_async_copy(t_ref, field.at[pl.ds(DEPTH, nx)], sems.at[1]),
        pltpu.make_async_copy(low_ref, field.at[pl.ds(0, DEPTH)], sems.at[2]),
        pltpu.make_async_copy(high_ref, field.at[pl.ds(DEPTH + nx, DEPTH)], sems.at[3]),
    ]
    for copy in copies:
        copy.start()
    copies[0].wait()
    prepare(cond, gx, gy, gz, gb)
    for copy in copies[1:]:
        copy.wait()

    def target(x, t, z):
        return placed, (x - DEPTH, z.start // LANES, pl.ds(t, 8, stride=tiles))

    two_steps(field, between, gx, gy, gz, gb, carried, target)

    @pl.loop(0, nx)
    def _(x):
        for j, z in enumerate(lane_tiles(out_ref.shape[2])):
            out_ref[x, :, z] = placed[x, j, :ny, :]


def second_round(temp, low, high, cond, shape):
    nx, wide, nz = temp.shape
    tall = cond.shape[0]
    hbm = pl.BlockSpec(memory_space=pl.ANY)
    return pl.pallas_call(
        second_round_kernel,
        out_shape=jax.ShapeDtypeStruct(shape, jnp.float32),
        in_specs=[hbm] * 4,
        scratch_shapes=[pltpu.VMEM((tall, wide, nz), jnp.float32)]
        + heat_scratch(tall, wide, nz)
        + [
            pltpu.VMEM((nx, nz // LANES, wide, LANES), jnp.float32),
            pltpu.SemaphoreType.DMA((4,)),
        ],
        compiler_params=params(64),
        cost_estimate=cost(tall * wide * nz * 60, 8 * nx * wide * nz * 4),
        name="second_round",
    )(temp, low, high, cond)


def source_kernel(ny, all_ref, thin_ref, base_ref, out_ref):
    tall = thin_ref.shape[0]
    nx = tall - 2 * HALO
    sheets = all_ref.shape[1]
    sub = lax.broadcasted_iota(jnp.int32, (8, LANES), 0)
    y_lane = lax.broadcasted_iota(jnp.int32, (8, LANES), 1)

    slabs, pairs = lax.axis_size("slab"), lax.axis_size("pair")

    def sheet(down, across):
        slab = lax.axis_index("slab") + down
        pair = lax.axis_index("pair") + across
        inside = (slab >= 0) & (slab < slabs) & (pair >= 0) & (pair < pairs)
        found = all_ref[jnp.where(inside, slab * pairs + pair, 0)]
        return jnp.where(inside, found, 0.0)

    def rows_of(down):
        low, own, high = (sheet(down, across) for across in (-1, 0, 1))
        out = []
        for half in range(2):
            if half == 0:
                own_at, high_at, low_at = own, pltpu.roll(high, ny, 1), pltpu.roll(low, ny, 1)
            else:
                own_at, high_at, low_at = pltpu.roll(own, ny, 1), high, low
            out.append(
                jnp.where(
                    y_lane < ny,
                    own_at,
                    jnp.where(
                        y_lane < ny + HALO,
                        high_at,
                        jnp.where(y_lane >= LANES - HALO, low_at, 0.0),
                    ),
                )
            )
        return out

    lines = [rows_of(down) for down in (-1, 0, 1)]
    source = []
    for x in range(-HALO, nx + HALO):
        which, local = (x + nx) // nx, x % nx
        row = lines[which][local % 2][local // 2 : local // 2 + 1, :]
        source.append(jnp.where(sub == 0, jnp.broadcast_to(row, (8, LANES)), 0.0))

    cond = [thin_ref[x] for x in range(tall)]
    cx, cy, cz, centre = [], [], [], []
    for x in range(tall):
        here = cond[x]
        after = cond[min(x + 1, tall - 1)]
        before = cond[max(x - 1, 0)]
        y_after = pltpu.roll(here, LANES - 1, 1)
        y_before = pltpu.roll(here, 1, 1)
        z_after = jnp.where(sub == 7, 0.0, pltpu.roll(here, 7, 0))
        z_before = jnp.where(sub == 0, 0.0, pltpu.roll(here, 1, 0))
        cx.append(coupling(here, after))
        cy.append(coupling(here, y_after))
        cz.append(coupling(here, z_after))
        total = 6.0 * here
        for near in (after, before, y_after, y_before, z_after, z_before):
            total = total + jnp.where(near > 0.0, near, here)
        centre.append(1.0 - (0.5 * step_size) * total)

    added = source
    for step in range(1, STEPS):
        new = list(added)
        for x in range(step, tall - step):
            here = added[x]
            total = source[x] + centre[x] * here
            total = total + (cx[x] * added[x + 1] + cx[x - 1] * added[x - 1])
            total = total + cy[x] * pltpu.roll(here, LANES - 1, 1)
            total = total + pltpu.roll(cy[x] * here, 1, 1)
            total = total + cz[x] * pltpu.roll(here, 7, 0)
            new[x] = total + pltpu.roll(cz[x] * here, 1, 0)
        added = new

    lane = lax.broadcasted_iota(jnp.int32, (ny, LANES), 1)
    turned = jnp.concatenate(added[HALO : HALO + nx], axis=0).T[:ny]
    for x in range(nx):
        piece = turned if x == 0 else pltpu.roll(turned, LANES - 8 * x, 1)
        out_ref[x] = base_ref[x] + jnp.where(lane < STEPS, piece, 0.0)


def add_source(everything, thin, base):
    nx, ny, nz = base.shape
    block = pl.BlockSpec((nx, ny, LANES), lambda i: (0, 0, 0))
    return pl.pallas_call(
        functools.partial(source_kernel, ny),
        grid=(1,),
        out_shape=jax.ShapeDtypeStruct(base.shape, jnp.float32),
        in_specs=[
            pl.BlockSpec(everything.shape, lambda i: (0, 0, 0)),
            pl.BlockSpec(thin.shape, lambda i: (0, 0, 0)),
            block,
        ],
        out_specs=block,
        input_output_aliases={2: 0},
        compiler_params=params(64),
        cost_estimate=cost(1_000_000, 2 * nx * ny * LANES * 4),
        name="add_source",
    )(everything, thin, base)


def exchange(rows):
    return lax.all_to_all(rows, ("slab", "pair"), split_axis=0, concat_axis=0, tiled=True)


def together(*arrays):
    return lax.optimization_barrier(arrays)


def both_ways(low, high, axis):
    count = lax.axis_size(axis)
    forward = [(i, i + 1) for i in range(count - 1)]
    backward = [(target, source) for source, target in forward]
    from_low = lax.ppermute(high, axis, forward)
    from_high = lax.ppermute(low, axis, backward)
    return from_low, from_high


def shards(
    initial_warmth,
    heat_passing_coefficient,
    mirror_fraction,
    element_facing_site,
    tile_block_couples,
    active_slot_count,
    view_factor_blocks,
):
    nx, ny, _ = initial_warmth.shape
    slabs, pairs = lax.axis_size("slab"), lax.axis_size("pair")
    count = slabs * pairs
    blocks = mirror_fraction.shape[0]
    couples = tile_block_couples.T

    temp, cond = initial_warmth, heat_passing_coefficient
    emitted, copies = emit(temp, element_facing_site, mirror_fraction, count)
    temp, copies = together(temp, copies)

    def sweep_terms(whole):
        whole = whole.reshape(count * blocks, BLK)
        term = tile_terms(whole, couples, active_slot_count, view_factor_blocks)
        return term.reshape(count, blocks, BLK)

    whole = exchange(copies)
    send_low, send_high = pack_x(temp, cond)
    low, high = both_ways(send_low, send_high, "slab")
    whole = together(whole, send_low, send_high)[0]
    parts = exchange(sweep_terms(whole))
    copies, low, high = together(middle(parts, emitted, mirror_fraction), low, high)
    whole = exchange(copies)
    send_down, send_up = pack_y(temp, cond, low, high)
    below, above = both_ways(send_down, send_up, "pair")
    middle_temp, send_low, send_high, strided_cond, thin = first_round(
        temp, cond, low, high, below, above
    )
    low, high = both_ways(send_low, send_high, "slab")
    whole = together(whole, send_low, send_high)[0]
    term, low, high = together(sweep_terms(whole), low, high)
    parts = exchange(term)
    base = second_round(middle_temp, low, high, strided_cond, temp.shape)
    parts = together(parts, base)[0]
    radiosity, source = last(parts, emitted, mirror_fraction, element_facing_site, nx * ny, count)
    everything = exchange(source)

    warmed_liner = add_source(everything, thin, base)
    return (radiosity, warmed_liner)


def solution(mesh):
    return jax.shard_map(
        shards,
        mesh=mesh,
        in_specs=(
            P("slab", "pair", None),
            P("slab", "pair", None),
            P(("slab", "pair"), None),
            P(("slab", "pair"), None),
            P(("slab", "pair"), None),
            P(("slab", "pair")),
            P(("slab", "pair"), None, None),
        ),
        out_specs=(P(("slab", "pair"), None), P("slab", "pair", None)),
        check_vma=False,
    )
```

```python
import functools

import jax
import jax.numpy as jnp
from jax import lax
from jax.experimental import pallas as pl
from jax.experimental.pallas import tpu as pltpu
from jax.sharding import PartitionSpec as P

BLK = 128
SWEEPS = 2
STEPS = 4
HALO = STEPS
ROWS = STEPS
LANES = 128
CHUNK = 16
LAG = 12

step_size = 0.07

NT = (((1,), (1,)), ((), ()))
NN = (((1,), (0,)), ((), ()))


def params(mib):
    return pltpu.CompilerParams(vmem_limit_bytes=mib * 1024 * 1024)


def cost(flops, nbytes):
    return pl.CostEstimate(flops=flops, bytes_accessed=nbytes, transcendentals=0)


def parts_of(x, count):
    out = []
    for _ in range(count - 1):
        part = x.astype(jnp.bfloat16)
        out.append(part)
        x = x - part.astype(jnp.float32)
    out.append(x.astype(jnp.bfloat16))
    return out


class Lagging:
    def __init__(self, depth):
        self.depth = depth
        self.waiting = []

    def add(self, store):
        self.waiting.append(store)
        if len(self.waiting) > self.depth:
            self.waiting.pop(0)()

    def finish(self):
        for store in self.waiting:
            store()
        self.waiting = []


def put(ref, index, value):
    return lambda: ref.__setitem__(index, value)


def emit_kernel(temp_ref, site_ref, mirror_ref, emitted_ref, copies_ref):
    nx, ny, _ = temp_ref.shape
    sheets = nx * ny // LANES
    per = LANES // ny
    lanes = lax.broadcasted_iota(jnp.int32, (LANES, LANES), 1)
    gathered = jnp.zeros((LANES, LANES), jnp.float32)
    for r in range(sheets):
        piece = temp_ref[per * r : per * r + per].reshape(LANES, LANES)
        if r:
            piece = pltpu.roll(piece, r, 1)
        gathered = jnp.where(lanes == r, piece, gathered)
    plane = gathered.T[:sheets]
    for half in range(site_ref.shape[0] // 8):
        rows = pl.ds(half * 8, 8)
        site = site_ref[rows, :]
        lane = site & (LANES - 1)
        sheet = site >> 7
        warmth = jnp.zeros(site.shape, jnp.float32)
        for r in range(sheets):
            line = jnp.broadcast_to(plane[r : r + 1, :], site.shape)
            picked = jnp.take_along_axis(line, lane, axis=1)
            warmth = jnp.where(sheet == r, picked, warmth)
        square = warmth * warmth
        emitted = (1.0 - mirror_ref[rows, :]) * (square * square)
        emitted_ref[rows, :] = emitted
        for d in range(copies_ref.shape[0]):
            copies_ref[d, rows, :] = emitted


def emit(temp, site, mirror, count):
    shape = mirror.shape
    nx, ny, _ = temp.shape
    patch = pl.BlockSpec(shape, lambda i: (0, 0))
    return pl.pallas_call(
        emit_kernel,
        grid=(1,),
        out_shape=(
            jax.ShapeDtypeStruct(shape, jnp.float32),
            jax.ShapeDtypeStruct((count,) + shape, jnp.float32),
        ),
        in_specs=[pl.BlockSpec((nx, ny, LANES), lambda i: (0, 0, 0)), patch, patch],
        out_specs=(patch, pl.BlockSpec((count,) + shape, lambda i: (0, 0, 0))),
        compiler_params=params(64),
        cost_estimate=cost(10_000, 900_000),
        name="emit",
    )(temp, site, mirror)


def tiles_kernel(
    live_ref, pairs_ref, lanes_ref, whole_ref, tiles_ref, out_ref, held, terms, sems
):
    slots = held.shape[0]
    live = live_ref[0]
    chunks = (live + CHUNK - 1) // CHUNK

    def chunk_copy(c):
        span = pl.ds(c * CHUNK, CHUNK)
        return pltpu.make_async_copy(tiles_ref.at[span], held.at[span], sems.at[c])

    @pl.loop(0, chunks)
    def _(c):
        chunk_copy(c).start()

    top = lax.broadcasted_iota(jnp.int32, (8, BLK), 0) == 0

    def split_row(block):
        row = jnp.broadcast_to(whole_ref[pl.ds(block, 1), :], (8, BLK))
        high = row.astype(jnp.bfloat16).astype(jnp.float32)
        return jnp.where(top, high, row - high)

    def vectors(a, b):
        stacked = jnp.concatenate([split_row(a), split_row(b)], axis=0)
        stacked = stacked.astype(jnp.bfloat16)
        return jnp.concatenate([stacked, stacked], axis=1)

    @pl.loop(0, chunks)
    def _(c):
        chunk_copy(c).wait()
        stores = Lagging(4 * CHUNK)
        for u in range(0, CHUNK, 2):
            t = c * CHUNK + u
            high_a, low_a = parts_of(held[t], 2)
            high_b, low_b = parts_of(held[t + 1], 2)
            both = jnp.concatenate(
                [
                    jnp.concatenate([high_a, high_b], axis=1),
                    jnp.concatenate([low_a, low_b], axis=1),
                ],
                axis=0,
            )
            second = lax.dot_general(
                vectors(pairs_ref[0, t], pairs_ref[0, t + 1]),
                both,
                NN,
                preferred_element_type=jnp.float32,
            )
            turned = jnp.concatenate(
                [
                    jnp.concatenate([high_a, low_a], axis=1),
                    jnp.concatenate([high_b, low_b], axis=1),
                ],
                axis=0,
            )
            first = lax.dot_general(
                vectors(pairs_ref[1, t], pairs_ref[1, t + 1]),
                turned,
                NT,
                preferred_element_type=jnp.float32,
            )
            for side, result in ((0, first), (1, second)):
                for v, (top_row, cols) in enumerate(((0, slice(0, BLK)), (8, slice(BLK, 2 * BLK)))):
                    row = result[top_row : top_row + 1, cols] + result[top_row + 1 : top_row + 2, cols]
                    stores.add(put(terms, (side, pl.ds(t + v, 1)), row))
        stores.finish()

    used = lax.broadcasted_iota(jnp.int32, (slots, BLK), 0) < live
    used_lane = lax.broadcasted_iota(jnp.int32, (1, slots), 1) < live
    blocks = out_ref.shape[0]
    group = min(blocks, 512)
    split = []
    for side in range(2):
        masked = jnp.where(used, terms[side], 0.0)
        split.append(jnp.concatenate(parts_of(masked, 2), axis=1))
    for base in range(0, blocks, group):
        rows = lax.broadcasted_iota(jnp.int32, (group, slots), 0) + base
        total = jnp.zeros((group, 2 * BLK), jnp.float32)
        for side in range(2):
            target = jnp.where(used_lane, lanes_ref[side : side + 1, :], -1)
            choose = jnp.where(rows == target, 1.0, 0.0).astype(jnp.bfloat16)
            total = total + jnp.dot(choose, split[side], preferred_element_type=jnp.float32)
        out_ref[base : base + group, :] = total[:, :BLK] + total[:, BLK:]


def tile_terms(whole, couples, live, tiles):
    slots = tiles.shape[0]
    smem = pl.BlockSpec(memory_space=pltpu.SMEM)
    vmem = pl.BlockSpec(memory_space=pltpu.VMEM)
    return pl.pallas_call(
        tiles_kernel,
        out_shape=jax.ShapeDtypeStruct(whole.shape, jnp.float32),
        in_specs=[smem, smem, vmem, vmem, pl.BlockSpec(memory_space=pl.ANY)],
        out_specs=vmem,
        scratch_shapes=[
            pltpu.VMEM(tiles.shape, jnp.float32),
            pltpu.VMEM((2, slots, BLK), jnp.float32),
            pltpu.SemaphoreType.DMA((slots // CHUNK,)),
        ],
        compiler_params=params(64),
        cost_estimate=cost(slots * BLK * BLK * 32, slots * BLK * BLK * 4),
        name="tiles",
    )(live, couples, couples, whole, tiles)


def sum_parts(parts_ref, rows):
    total = parts_ref[0, rows, :]
    for d in range(1, parts_ref.shape[0]):
        total = total + parts_ref[d, rows, :]
    return total


def middle_kernel(parts_ref, emitted_ref, mirror_ref, copies_ref):
    for half in range(emitted_ref.shape[0] // 8):
        rows = pl.ds(half * 8, 8)
        incident = sum_parts(parts_ref, rows)
        radiosity = emitted_ref[rows, :] + mirror_ref[rows, :] * incident
        for d in range(copies_ref.shape[0]):
            copies_ref[d, rows, :] = radiosity


def middle(parts, emitted, mirror):
    return pl.pallas_call(
        middle_kernel,
        out_shape=jax.ShapeDtypeStruct(parts.shape, jnp.float32),
        compiler_params=params(64),
        cost_estimate=cost(100_000, 600_000),
        name="middle",
    )(parts, emitted, mirror)


def last_kernel(scale, parts_ref, emitted_ref, mirror_ref, site_ref, rad_ref, source_ref):
    blocks = emitted_ref.shape[0]
    incident = sum_parts(parts_ref, slice(None))
    emitted = emitted_ref[...]
    mirror = mirror_ref[...]
    rad_ref[...] = emitted + mirror * incident
    absorbed = ((1.0 - mirror) * incident - emitted) * scale
    site = site_ref[...]
    lane = site & (LANES - 1)
    sheet = site >> 7
    sheets = source_ref.shape[1]
    sheet_iota = lax.broadcasted_iota(jnp.int32, (sheets, BLK), 0)
    lane_iota = lax.broadcasted_iota(jnp.int32, (LANES, BLK), 0)
    left = []
    right = []
    for b in range(blocks):
        here = jnp.where(sheet_iota == sheet[b : b + 1, :], absorbed[b : b + 1, :], 0.0)
        left.append(here)
        pick = jnp.where(lane_iota == lane[b : b + 1, :], 1.0, 0.0)
        right.append(pick.astype(jnp.bfloat16))
    left = jnp.concatenate(left, axis=1)
    right = jnp.concatenate(right, axis=1)
    source = jnp.zeros((sheets, LANES), jnp.float32)
    for part in parts_of(left, 3):
        source = source + lax.dot_general(part, right, NT, preferred_element_type=jnp.float32)
    for d in range(source_ref.shape[0]):
        source_ref[d] = source


def last(parts, emitted, mirror, site, cells, count):
    weight = cells / (mirror.shape[0] * BLK * 1.0)
    return pl.pallas_call(
        functools.partial(last_kernel, step_size * weight),
        out_shape=(
            jax.ShapeDtypeStruct(mirror.shape, jnp.float32),
            jax.ShapeDtypeStruct((count, cells // LANES, LANES), jnp.float32),
        ),
        compiler_params=params(64),
        cost_estimate=cost(10_000_000, 600_000),
        name="last",
    )(parts, emitted, mirror, site)


def pack_y_kernel(t0, k0, t7, k7, down_ref, up_ref):
    upper = lax.broadcasted_iota(jnp.int32, down_ref.shape[1:], 0) < ROWS
    for x in range(down_ref.shape[0]):
        down_ref[x] = jnp.where(upper, t0[x], pltpu.roll(k0[x], ROWS, 0))
        up_ref[x] = jnp.where(upper, pltpu.roll(t7[x], ROWS, 0), k7[x])


def pack_y(temp, cond):
    nx, ny, nz = temp.shape
    first = pl.BlockSpec((nx, 8, nz), lambda i: (0, 0, 0))
    final = pl.BlockSpec((nx, 8, nz), lambda i: (0, ny // 8 - 1, 0))
    shape = jax.ShapeDtypeStruct((nx, 8, nz), jnp.float32)
    return pl.pallas_call(
        pack_y_kernel,
        grid=(1,),
        out_shape=(shape, shape),
        in_specs=[first, first, final, final],
        out_specs=(first, first),
        compiler_params=params(64),
        cost_estimate=cost(0, 4 * nx * 8 * nz * 4),
        name="pack_y",
    )(temp, cond, temp, cond)


def pack_x_kernel(first, final, below0, above0, below1, above1, low_ref, high_ref):
    ny, nz = first.shape[1:]
    upper = lax.broadcasted_iota(jnp.int32, (8, nz), 0) < ROWS
    for send, temp, below, above in (
        (low_ref, first, below0, above0),
        (high_ref, final, below1, above1),
    ):
        for p in range(HALO):
            send[p, :ny] = temp[p]
            send[p, ny : ny + 8] = jnp.where(upper, above[p], pltpu.roll(below[p], ROWS, 0))
            send[p, ny + 8 :] = jnp.where(upper, pltpu.roll(above[p], ROWS, 0), below[p])


def pack_x(temp, below, above):
    nx, ny, nz = temp.shape

    def ends(rows):
        return (
            pl.BlockSpec((HALO, rows, nz), lambda i: (0, 0, 0)),
            pl.BlockSpec((HALO, rows, nz), lambda i: (nx // HALO - 1, 0, 0)),
        )

    first, final = ends(ny)
    first_rows, final_rows = ends(8)
    whole = pl.BlockSpec((HALO, ny + 16, nz), lambda i: (0, 0, 0))
    shape = jax.ShapeDtypeStruct((HALO, ny + 16, nz), jnp.float32)
    return pl.pallas_call(
        pack_x_kernel,
        grid=(1,),
        out_shape=(shape, shape),
        in_specs=[first, final, first_rows, first_rows, final_rows, final_rows],
        out_specs=(whole, whole),
        compiler_params=params(64),
        cost_estimate=cost(0, 4 * HALO * (ny + 16) * nz * 4),
        name="pack_x",
    )(temp, temp, below, above, below, above)


def coupling(a, b):
    return jnp.where(jnp.minimum(a, b) > 0.0, (0.5 * step_size) * (a + b), 0.0)


def neighbours():
    slab, pair = lax.axis_index("slab"), lax.axis_index("pair")
    return slab > 0, slab < lax.axis_size("slab") - 1, pair > 0, pair < lax.axis_size("pair") - 1


def lane_tiles(nz):
    return [slice(j * LANES, (j + 1) * LANES) for j in range(nz // LANES)]


def prepare(cond, gx, gy, gz, gb):
    tall, wide, nz = cond.shape
    tiles = wide // 8
    lane = lax.broadcasted_iota(jnp.int32, (8, LANES), 1)
    half = 0.5 * step_size

    @pl.loop(0, tall)
    def _(x):
        after = jnp.minimum(x + 1, tall - 1)
        stores = Lagging(LAG)
        for z in lane_tiles(nz):
            last = z.stop == nz
            for t in range(tiles):
                rows = slice(8 * t, 8 * t + 8)
                here = cond[x, rows, z]
                stores.add(put(gx, (x, rows, z), half * (here + cond[after, rows, z])))
                if t + 1 < tiles:
                    beside = cond[x, 8 * t + 8 : 8 * t + 16, z]
                else:
                    beside = pltpu.roll(cond[x, :8, z], 7, 0)
                stores.add(put(gy, (x, rows, z), half * (here + beside)))
                turned = pltpu.roll(here, LANES - 1, 1)
                if last:
                    deeper = here
                else:
                    deeper = pltpu.roll(cond[x, rows, z.stop : z.stop + LANES], LANES - 1, 1)
                deeper = jnp.where(lane < LANES - 1, turned, deeper)
                stores.add(put(gz, (x, rows, z), half * (here + deeper)))
                if z.start == 0:
                    stores.add(put(gb, (x, rows), step_size * here))
        stores.finish()


def one_step(field, begin, end, target, gx, gy, gz, gb, carried):
    wide, nz = field.shape[1:]
    tiles = wide // 8
    lane = lax.broadcasted_iota(jnp.int32, (8, LANES), 1)
    sub = lax.broadcasted_iota(jnp.int32, (8, LANES), 0)
    _, _, has_below, has_above = neighbours()
    keep_above = (sub < 7) | has_above
    keep_below = (sub < 7) | has_below

    carried[...] = gx[begin - 1] * (field[begin] - field[begin - 1])

    @pl.loop(begin, end)
    def _(x):
        here, across_y = {}, {}
        stores = Lagging(LAG)
        spans = lane_tiles(nz)
        count = len(spans)

        def tile(t, j):
            if (t, j) not in here:
                here[t, j] = field[x, 8 * t : 8 * t + 8, spans[j]]
            return here[t, j]

        def y_flux(t, j):
            if (t, j) not in across_y:
                if t + 1 < tiles:
                    beside = tile(t + 1, j)
                else:
                    beside = pltpu.roll(tile(0, j), 7, 0)
                across_y[t, j] = gy[x, 8 * t : 8 * t + 8, spans[j]] * (beside - tile(t, j))
            return across_y[t, j]

        for t in range(tiles):
            rows = slice(8 * t, 8 * t + 8)
            turned = [pltpu.roll(tile(t, j), LANES - 1, 1) for j in range(count)]
            flux = []
            for j in range(count):
                deeper = turned[j + 1] if j + 1 < count else 0.0
                deeper = jnp.where(lane < LANES - 1, turned[j], deeper)
                flux.append(gz[x, rows, spans[j]] * (deeper - tile(t, j)))
            back = [pltpu.roll(f, 1, 1) for f in flux]
            for j in range(count):
                now = tile(t, j)
                low_z = back[j - 1] if j else gb[x, rows, :] * now
                low_z = jnp.where(lane > 0, back[j], low_z)
                x_flux = gx[x, rows, spans[j]] * (field[x + 1, rows, spans[j]] - now)
                low_x = carried[rows, spans[j]]
                stores.add(put(carried, (rows, spans[j]), x_flux))
                low_y = y_flux(t - 1, j) if t else pltpu.roll(y_flux(tiles - 1, j), 1, 0)
                new = now + (x_flux - low_x) + (y_flux(t, j) - low_y) + (flux[j] - low_z)
                if t:
                    new = jnp.where(keep_above if t <= ROWS else keep_below, new, 0.0)
                stores.add(put(*target(x, t, spans[j]), new))
        stores.finish()


def thin_planes(cond, ny, thin_ref):
    tall, _, wide, _ = cond.shape
    lane = lax.broadcasted_iota(jnp.int32, (wide, LANES), 1)
    y_lane = lax.broadcasted_iota(jnp.int32, (8, LANES), 1)
    for base in range(0, tall, 16):
        planes = min(16, tall - base)
        gathered = jnp.zeros((wide, LANES), jnp.float32)
        for g in range(planes):
            piece = cond[base + g, 0]
            if g:
                piece = pltpu.roll(piece, 8 * g, 1)
            gathered = jnp.where((lane >> 3) == g, piece, gathered)
        turned = jnp.concatenate(
            [gathered, jnp.zeros((LANES - wide, LANES), jnp.float32)], axis=0
        ).T
        for g in range(planes):
            rows = turned[8 * g : 8 * g + 8, :]
            moved = pltpu.roll(rows, LANES - wide, 1)
            thin_ref[base + g] = jnp.where(
                y_lane < ny + ROWS, rows, jnp.where(y_lane >= LANES - ROWS, moved, 0.0)
            )


def heat_kernel(
    t_ref, k_ref, k_low, k_high, t_low, t_high, below_ref, above_ref, out_ref, thin_ref,
    loaded, field, between, gx, gy, gz, gb, carried, placed, sems,
):
    nx, ny, nz = t_ref.shape
    tall, wide = nx + 2 * HALO, ny + 2 * ROWS
    tiles = wide // 8
    raw_t, raw_k = loaded.at[0], loaded.at[1]
    spans = lane_tiles(nz)
    ends = (0, HALO + nx)

    def fetch(which, k, ref, source_row, planes, at, row, rows):
        return [
            pltpu.make_async_copy(
                ref.at[:, pl.ds(source_row, rows), pl.ds(z.start, LANES)],
                loaded.at[which, pl.ds(at, planes), j, pl.ds(row, rows)],
                sems.at[which, k, j],
            )
            for j, z in enumerate(spans)
        ]

    k_copies = fetch(1, 0, k_ref, 0, nx, HALO, 0, ny)
    t_copies = fetch(0, 0, t_ref, 0, nx, HALO, 0, ny)
    for k, (at, k_side, t_side) in enumerate(zip(ends, (k_low, k_high), (t_low, t_high))):
        k_copies += fetch(1, 1 + k, k_side, 0, HALO, at, 0, ny)
        k_copies += fetch(1, 3 + k, t_side, ny + 8, HALO, at, ny, 8)
        t_copies += fetch(0, 1 + k, t_side, 0, HALO, at, 0, ny + 8)
    for copy in k_copies + t_copies:
        copy.start()
    has_low, has_high, has_below, has_above = neighbours()
    upper = lax.broadcasted_iota(jnp.int32, (8, LANES), 0) < ROWS

    @pl.loop(0, nx)
    def _(x):
        for j, z in enumerate(spans):
            down, up = above_ref[x, :, z], below_ref[x, :, z]
            raw_t[HALO + x, j, ny:] = jnp.where(upper, down, pltpu.roll(up, ROWS, 0))
            raw_k[HALO + x, j, ny:] = jnp.where(upper, pltpu.roll(down, ROWS, 0), up)

    for copy in k_copies:
        copy.wait()

    thin_planes(raw_k, ny, thin_ref)

    @pl.when(jnp.logical_not(has_above & has_below))
    def _():
        missing = (upper & jnp.logical_not(has_above)) | (
            jnp.logical_not(upper) & jnp.logical_not(has_below)
        )

        @pl.loop(0, tall)
        def _(x):
            for j in range(len(spans)):
                edge = raw_k[x, j, ny:]
                last = jnp.broadcast_to(raw_k[x, j, ny - 1 : ny, :], edge.shape)
                first = jnp.broadcast_to(raw_k[x, j, 0:1, :], edge.shape)
                raw_k[x, j, ny:] = jnp.where(missing, jnp.where(upper, last, first), edge)

    @pl.when(jnp.logical_not(has_low))
    def _():
        raw_k[HALO - 1] = raw_k[HALO]

    @pl.when(jnp.logical_not(has_high))
    def _():
        raw_k[HALO + nx] = raw_k[HALO + nx - 1]

    def spread(which, target):
        @pl.loop(0, tall)
        def _(x):
            for t in range(tiles):
                rows = pl.ds(t, 8, stride=tiles)
                for j, z in enumerate(spans):
                    target[x, 8 * t : 8 * t + 8, z] = loaded[which, x, j, rows, :]

    spread(1, between)
    prepare(between, gx, gy, gz, gb)
    for copy in t_copies:
        copy.wait()
    spread(0, field)

    for x in (HALO - 1, HALO + nx):
        between[x] = jnp.zeros((wide, nz), jnp.float32)

    def inside(target):
        return lambda x, t, z: (target, (x, slice(8 * t, 8 * t + 8), z))

    def outside(x, t, z):
        return placed, (x - HALO, z.start // LANES, pl.ds(t, 8, stride=tiles))

    old, new = field, between
    for step in range(1, STEPS):
        begin = jnp.where(has_low, step, HALO)
        end = jnp.where(has_high, tall - step, tall - HALO)
        one_step(old, begin, end, inside(new), gx, gy, gz, gb, carried)
        old, new = new, old
    one_step(old, HALO, tall - HALO, outside, gx, gy, gz, gb, carried)

    @pl.loop(0, nx)
    def _(x):
        for j, z in enumerate(spans):
            out_ref[x, :, z] = placed[x, j, :ny, :]


def heat(temp, cond, k_low, k_high, t_low, t_high, below, above):
    nx, ny, nz = temp.shape
    tall, wide = nx + 2 * HALO, ny + 2 * ROWS
    hbm = pl.BlockSpec(memory_space=pl.ANY)
    vmem = pl.BlockSpec(memory_space=pltpu.VMEM)
    big = pltpu.VMEM((tall, wide, nz), jnp.float32)
    return pl.pallas_call(
        heat_kernel,
        out_shape=(
            jax.ShapeDtypeStruct(temp.shape, jnp.float32),
            jax.ShapeDtypeStruct((tall, 8, LANES), jnp.float32),
        ),
        in_specs=[hbm] * 6 + [vmem] * 2,
        scratch_shapes=[pltpu.VMEM((2, tall, nz // LANES, wide, LANES), jnp.float32)]
        + [big] * 5
        + [
            pltpu.VMEM((tall, wide, LANES), jnp.float32),
            pltpu.VMEM((wide, nz), jnp.float32),
            pltpu.VMEM((nx, nz // LANES, wide, LANES), jnp.float32),
            pltpu.SemaphoreType.DMA((2, 5, nz // LANES)),
        ],
        compiler_params=params(64),
        cost_estimate=cost(tall * wide * nz * 100, 12 * nx * ny * nz * 4),
        name="heat",
    )(temp, cond, k_low, k_high, t_low, t_high, below, above)


def source_kernel(ny, all_ref, thin_ref, base_ref, out_ref):
    tall = thin_ref.shape[0]
    nx = tall - 2 * HALO
    sheets = all_ref.shape[1]
    sub = lax.broadcasted_iota(jnp.int32, (8, LANES), 0)
    y_lane = lax.broadcasted_iota(jnp.int32, (8, LANES), 1)

    slabs, pairs = lax.axis_size("slab"), lax.axis_size("pair")

    def sheet(down, across):
        slab = lax.axis_index("slab") + down
        pair = lax.axis_index("pair") + across
        inside = (slab >= 0) & (slab < slabs) & (pair >= 0) & (pair < pairs)
        found = all_ref[jnp.where(inside, slab * pairs + pair, 0)]
        return jnp.where(inside, found, 0.0)

    def rows_of(down):
        low, own, high = (sheet(down, across) for across in (-1, 0, 1))
        out = []
        for half in range(2):
            if half == 0:
                own_at, high_at, low_at = own, pltpu.roll(high, ny, 1), pltpu.roll(low, ny, 1)
            else:
                own_at, high_at, low_at = pltpu.roll(own, ny, 1), high, low
            out.append(
                jnp.where(
                    y_lane < ny,
                    own_at,
                    jnp.where(
                        y_lane < ny + HALO,
                        high_at,
                        jnp.where(y_lane >= LANES - HALO, low_at, 0.0),
                    ),
                )
            )
        return out

    lines = [rows_of(down) for down in (-1, 0, 1)]
    source = []
    for x in range(-HALO, nx + HALO):
        which, local = (x + nx) // nx, x % nx
        row = lines[which][local % 2][local // 2 : local // 2 + 1, :]
        source.append(jnp.where(sub == 0, jnp.broadcast_to(row, (8, LANES)), 0.0))

    cond = [thin_ref[x] for x in range(tall)]
    cx, cy, cz, centre = [], [], [], []
    for x in range(tall):
        here = cond[x]
        after = cond[min(x + 1, tall - 1)]
        before = cond[max(x - 1, 0)]
        y_after = pltpu.roll(here, LANES - 1, 1)
        y_before = pltpu.roll(here, 1, 1)
        z_after = jnp.where(sub == 7, 0.0, pltpu.roll(here, 7, 0))
        z_before = jnp.where(sub == 0, 0.0, pltpu.roll(here, 1, 0))
        cx.append(coupling(here, after))
        cy.append(coupling(here, y_after))
        cz.append(coupling(here, z_after))
        total = 6.0 * here
        for near in (after, before, y_after, y_before, z_after, z_before):
            total = total + jnp.where(near > 0.0, near, here)
        centre.append(1.0 - (0.5 * step_size) * total)

    added = source
    for step in range(1, STEPS):
        new = list(added)
        for x in range(step, tall - step):
            here = added[x]
            total = source[x] + centre[x] * here
            total = total + (cx[x] * added[x + 1] + cx[x - 1] * added[x - 1])
            total = total + cy[x] * pltpu.roll(here, LANES - 1, 1)
            total = total + pltpu.roll(cy[x] * here, 1, 1)
            total = total + cz[x] * pltpu.roll(here, 7, 0)
            new[x] = total + pltpu.roll(cz[x] * here, 1, 0)
        added = new

    lane = lax.broadcasted_iota(jnp.int32, (ny, LANES), 1)
    turned = jnp.concatenate(added[HALO : HALO + nx], axis=0).T[:ny]
    for x in range(nx):
        piece = turned if x == 0 else pltpu.roll(turned, LANES - 8 * x, 1)
        out_ref[x] = base_ref[x] + jnp.where(lane < STEPS, piece, 0.0)


def add_source(everything, thin, base):
    nx, ny, nz = base.shape
    block = pl.BlockSpec((nx, ny, LANES), lambda i: (0, 0, 0))
    return pl.pallas_call(
        functools.partial(source_kernel, ny),
        grid=(1,),
        out_shape=jax.ShapeDtypeStruct(base.shape, jnp.float32),
        in_specs=[
            pl.BlockSpec(everything.shape, lambda i: (0, 0, 0)),
            pl.BlockSpec(thin.shape, lambda i: (0, 0, 0)),
            block,
        ],
        out_specs=block,
        input_output_aliases={2: 0},
        compiler_params=params(64),
        cost_estimate=cost(1_000_000, 2 * nx * ny * LANES * 4),
        name="add_source",
    )(everything, thin, base)


def exchange(rows):
    return lax.all_to_all(rows, ("slab", "pair"), split_axis=0, concat_axis=0, tiled=True)


def together(*arrays):
    return lax.optimization_barrier(arrays)


def both_ways(low, high, axis):
    count = lax.axis_size(axis)
    forward = [(i, i + 1) for i in range(count - 1)]
    backward = [(target, source) for source, target in forward]
    from_low = lax.ppermute(high, axis, forward)
    from_high = lax.ppermute(low, axis, backward)
    return from_low, from_high


def shards(
    initial_warmth,
    heat_passing_coefficient,
    mirror_fraction,
    element_facing_site,
    tile_block_couples,
    active_slot_count,
    view_factor_blocks,
):
    nx, ny, _ = initial_warmth.shape
    slabs, pairs = lax.axis_size("slab"), lax.axis_size("pair")
    count = slabs * pairs
    blocks = mirror_fraction.shape[0]
    couples = tile_block_couples.T

    temp, cond = initial_warmth, heat_passing_coefficient
    emitted, copies = emit(temp, element_facing_site, mirror_fraction, count)
    temp, copies = together(temp, copies)

    def sweep_terms(whole):
        whole = whole.reshape(count * blocks, BLK)
        term = tile_terms(whole, couples, active_slot_count, view_factor_blocks)
        return term.reshape(count, blocks, BLK)

    whole = exchange(copies)
    cond, copies = together(cond, copies)
    send_low, send_high = cond[:HALO], cond[nx - HALO :]
    k_low, k_high = both_ways(send_low, send_high, "slab")
    whole = together(whole, send_low, send_high)[0]
    temp, cond, term = together(temp, cond, sweep_terms(whole))
    parts = exchange(term)
    below, above = both_ways(*pack_y(temp, cond), "pair")
    parts, below, above = together(parts, below, above)
    copies, below, above = together(middle(parts, emitted, mirror_fraction), below, above)
    whole = exchange(copies)
    send_low, send_high = pack_x(temp, below, above)
    t_low, t_high = both_ways(send_low, send_high, "slab")
    whole = together(whole, send_low, send_high)[0]
    parts = exchange(sweep_terms(whole))
    parts, t_low, t_high = together(parts, t_low, t_high)
    radiosity, source = last(parts, emitted, mirror_fraction, element_facing_site, nx * ny, count)
    everything = exchange(source)
    below, source = together(below, source)
    base, thin = heat(temp, cond, k_low, k_high, t_low, t_high, below, above)

    warmed_liner = add_source(everything, thin, base)
    return (radiosity, warmed_liner)


def solution(mesh):
    return jax.shard_map(
        shards,
        mesh=mesh,
        in_specs=(
            P("slab", "pair", None),
            P("slab", "pair", None),
            P(("slab", "pair"), None),
            P(("slab", "pair"), None),
            P(("slab", "pair"), None),
            P(("slab", "pair")),
            P(("slab", "pair"), None, None),
        ),
        out_specs=(P(("slab", "pair"), None), P("slab", "pair", None)),
        check_vma=False,
    )
```

```python
import functools

import jax
import jax.numpy as jnp
from jax import lax
from jax.experimental import pallas as pl
from jax.experimental.pallas import tpu as pltpu
from jax.sharding import PartitionSpec as P

BLK = 128
SWEEPS = 2
STEPS = 4
HALO = STEPS
ROWS = STEPS
LANES = 128
CHUNK = 16
LAG = 12

step_size = 0.07

NT = (((1,), (1,)), ((), ()))
NN = (((1,), (0,)), ((), ()))


def params(mib):
    return pltpu.CompilerParams(vmem_limit_bytes=mib * 1024 * 1024)


def cost(flops, nbytes):
    return pl.CostEstimate(flops=flops, bytes_accessed=nbytes, transcendentals=0)


def parts_of(x, count):
    out = []
    for _ in range(count - 1):
        part = x.astype(jnp.bfloat16)
        out.append(part)
        x = x - part.astype(jnp.float32)
    out.append(x.astype(jnp.bfloat16))
    return out


class Lagging:
    def __init__(self, depth):
        self.depth = depth
        self.waiting = []

    def add(self, store):
        self.waiting.append(store)
        if len(self.waiting) > self.depth:
            self.waiting.pop(0)()

    def finish(self):
        for store in self.waiting:
            store()
        self.waiting = []


def put(ref, index, value):
    return lambda: ref.__setitem__(index, value)


def emit_kernel(temp_ref, site_ref, mirror_ref, emitted_ref, copies_ref):
    nx, ny, _ = temp_ref.shape
    sheets = nx * ny // LANES
    per = LANES // ny
    lanes = lax.broadcasted_iota(jnp.int32, (LANES, LANES), 1)
    gathered = jnp.zeros((LANES, LANES), jnp.float32)
    for r in range(sheets):
        piece = temp_ref[per * r : per * r + per].reshape(LANES, LANES)
        if r:
            piece = pltpu.roll(piece, r, 1)
        gathered = jnp.where(lanes == r, piece, gathered)
    plane = gathered.T[:sheets]
    for half in range(site_ref.shape[0] // 8):
        rows = pl.ds(half * 8, 8)
        site = site_ref[rows, :]
        lane = site & (LANES - 1)
        sheet = site >> 7
        warmth = jnp.zeros(site.shape, jnp.float32)
        for r in range(sheets):
            line = jnp.broadcast_to(plane[r : r + 1, :], site.shape)
            picked = jnp.take_along_axis(line, lane, axis=1)
            warmth = jnp.where(sheet == r, picked, warmth)
        square = warmth * warmth
        emitted = (1.0 - mirror_ref[rows, :]) * (square * square)
        emitted_ref[rows, :] = emitted
        for d in range(copies_ref.shape[0]):
            copies_ref[d, rows, :] = emitted


def emit(temp, site, mirror, count):
    shape = mirror.shape
    nx, ny, _ = temp.shape
    patch = pl.BlockSpec(shape, lambda i: (0, 0))
    return pl.pallas_call(
        emit_kernel,
        grid=(1,),
        out_shape=(
            jax.ShapeDtypeStruct(shape, jnp.float32),
            jax.ShapeDtypeStruct((count,) + shape, jnp.float32),
        ),
        in_specs=[pl.BlockSpec((nx, ny, LANES), lambda i: (0, 0, 0)), patch, patch],
        out_specs=(patch, pl.BlockSpec((count,) + shape, lambda i: (0, 0, 0))),
        compiler_params=params(64),
        cost_estimate=cost(10_000, 900_000),
        name="emit",
    )(temp, site, mirror)


def tiles_kernel(
    live_ref, pairs_ref, lanes_ref, whole_ref, tiles_ref, out_ref, held, terms, sems
):
    slots = held.shape[0]
    live = live_ref[0]
    chunks = (live + CHUNK - 1) // CHUNK

    def chunk_copy(c):
        span = pl.ds(c * CHUNK, CHUNK)
        return pltpu.make_async_copy(tiles_ref.at[span], held.at[span], sems.at[c])

    @pl.loop(0, chunks)
    def _(c):
        chunk_copy(c).start()

    top = lax.broadcasted_iota(jnp.int32, (8, BLK), 0) == 0

    def split_row(block):
        row = jnp.broadcast_to(whole_ref[pl.ds(block, 1), :], (8, BLK))
        high = row.astype(jnp.bfloat16).astype(jnp.float32)
        return jnp.where(top, high, row - high)

    def vectors(a, b):
        stacked = jnp.concatenate([split_row(a), split_row(b)], axis=0)
        stacked = stacked.astype(jnp.bfloat16)
        return jnp.concatenate([stacked, stacked], axis=1)

    @pl.loop(0, chunks)
    def _(c):
        chunk_copy(c).wait()
        stores = Lagging(4 * CHUNK)
        for u in range(0, CHUNK, 2):
            t = c * CHUNK + u
            high_a, low_a = parts_of(held[t], 2)
            high_b, low_b = parts_of(held[t + 1], 2)
            both = jnp.concatenate(
                [
                    jnp.concatenate([high_a, high_b], axis=1),
                    jnp.concatenate([low_a, low_b], axis=1),
                ],
                axis=0,
            )
            second = lax.dot_general(
                vectors(pairs_ref[0, t], pairs_ref[0, t + 1]),
                both,
                NN,
                preferred_element_type=jnp.float32,
            )
            turned = jnp.concatenate(
                [
                    jnp.concatenate([high_a, low_a], axis=1),
                    jnp.concatenate([high_b, low_b], axis=1),
                ],
                axis=0,
            )
            first = lax.dot_general(
                vectors(pairs_ref[1, t], pairs_ref[1, t + 1]),
                turned,
                NT,
                preferred_element_type=jnp.float32,
            )
            for side, result in ((0, first), (1, second)):
                for v, (top_row, cols) in enumerate(((0, slice(0, BLK)), (8, slice(BLK, 2 * BLK)))):
                    row = result[top_row : top_row + 1, cols] + result[top_row + 1 : top_row + 2, cols]
                    stores.add(put(terms, (side, pl.ds(t + v, 1)), row))
        stores.finish()

    used = lax.broadcasted_iota(jnp.int32, (slots, BLK), 0) < live
    used_lane = lax.broadcasted_iota(jnp.int32, (1, slots), 1) < live
    blocks = out_ref.shape[0]
    group = min(blocks, 512)
    split = []
    for side in range(2):
        masked = jnp.where(used, terms[side], 0.0)
        split.append(jnp.concatenate(parts_of(masked, 2), axis=1))
    for base in range(0, blocks, group):
        rows = lax.broadcasted_iota(jnp.int32, (group, slots), 0) + base
        total = jnp.zeros((group, 2 * BLK), jnp.float32)
        for side in range(2):
            target = jnp.where(used_lane, lanes_ref[side : side + 1, :], -1)
            choose = jnp.where(rows == target, 1.0, 0.0).astype(jnp.bfloat16)
            total = total + jnp.dot(choose, split[side], preferred_element_type=jnp.float32)
        out_ref[base : base + group, :] = total[:, :BLK] + total[:, BLK:]


def tile_terms(whole, couples, live, tiles):
    slots = tiles.shape[0]
    smem = pl.BlockSpec(memory_space=pltpu.SMEM)
    vmem = pl.BlockSpec(memory_space=pltpu.VMEM)
    return pl.pallas_call(
        tiles_kernel,
        out_shape=jax.ShapeDtypeStruct(whole.shape, jnp.float32),
        in_specs=[smem, smem, vmem, vmem, pl.BlockSpec(memory_space=pl.ANY)],
        out_specs=vmem,
        scratch_shapes=[
            pltpu.VMEM(tiles.shape, jnp.float32),
            pltpu.VMEM((2, slots, BLK), jnp.float32),
            pltpu.SemaphoreType.DMA((slots // CHUNK,)),
        ],
        compiler_params=params(64),
        cost_estimate=cost(slots * BLK * BLK * 32, slots * BLK * BLK * 4),
        name="tiles",
    )(live, couples, couples, whole, tiles)


def sum_parts(parts_ref, rows):
    total = parts_ref[0, rows, :]
    for d in range(1, parts_ref.shape[0]):
        total = total + parts_ref[d, rows, :]
    return total


def middle_kernel(parts_ref, emitted_ref, mirror_ref, copies_ref):
    for half in range(emitted_ref.shape[0] // 8):
        rows = pl.ds(half * 8, 8)
        incident = sum_parts(parts_ref, rows)
        radiosity = emitted_ref[rows, :] + mirror_ref[rows, :] * incident
        for d in range(copies_ref.shape[0]):
            copies_ref[d, rows, :] = radiosity


def middle(parts, emitted, mirror):
    return pl.pallas_call(
        middle_kernel,
        out_shape=jax.ShapeDtypeStruct(parts.shape, jnp.float32),
        compiler_params=params(64),
        cost_estimate=cost(100_000, 600_000),
        name="middle",
    )(parts, emitted, mirror)


def last_kernel(scale, parts_ref, emitted_ref, mirror_ref, site_ref, rad_ref, source_ref):
    blocks = emitted_ref.shape[0]
    incident = sum_parts(parts_ref, slice(None))
    emitted = emitted_ref[...]
    mirror = mirror_ref[...]
    rad_ref[...] = emitted + mirror * incident
    absorbed = ((1.0 - mirror) * incident - emitted) * scale
    site = site_ref[...]
    lane = site & (LANES - 1)
    sheet = site >> 7
    sheets = source_ref.shape[1]
    sheet_iota = lax.broadcasted_iota(jnp.int32, (sheets, BLK), 0)
    lane_iota = lax.broadcasted_iota(jnp.int32, (LANES, BLK), 0)
    left = []
    right = []
    for b in range(blocks):
        here = jnp.where(sheet_iota == sheet[b : b + 1, :], absorbed[b : b + 1, :], 0.0)
        left.append(here)
        pick = jnp.where(lane_iota == lane[b : b + 1, :], 1.0, 0.0)
        right.append(pick.astype(jnp.bfloat16))
    left = jnp.concatenate(left, axis=1)
    right = jnp.concatenate(right, axis=1)
    source = jnp.zeros((sheets, LANES), jnp.float32)
    for part in parts_of(left, 3):
        source = source + lax.dot_general(part, right, NT, preferred_element_type=jnp.float32)
    for d in range(source_ref.shape[0]):
        source_ref[d] = source


def last(parts, emitted, mirror, site, cells, count):
    weight = cells / (mirror.shape[0] * BLK * 1.0)
    return pl.pallas_call(
        functools.partial(last_kernel, step_size * weight),
        out_shape=(
            jax.ShapeDtypeStruct(mirror.shape, jnp.float32),
            jax.ShapeDtypeStruct((count, cells // LANES, LANES), jnp.float32),
        ),
        compiler_params=params(64),
        cost_estimate=cost(10_000_000, 600_000),
        name="last",
    )(parts, emitted, mirror, site)


def pack_y_kernel(t0, k0, t7, k7, down_ref, up_ref):
    upper = lax.broadcasted_iota(jnp.int32, down_ref.shape[1:], 0) < ROWS
    for x in range(down_ref.shape[0]):
        down_ref[x] = jnp.where(upper, t0[x], pltpu.roll(k0[x], ROWS, 0))
        up_ref[x] = jnp.where(upper, pltpu.roll(t7[x], ROWS, 0), k7[x])


def pack_y(temp, cond):
    nx, ny, nz = temp.shape
    first = pl.BlockSpec((nx, 8, nz), lambda i: (0, 0, 0))
    final = pl.BlockSpec((nx, 8, nz), lambda i: (0, ny // 8 - 1, 0))
    shape = jax.ShapeDtypeStruct((nx, 8, nz), jnp.float32)
    return pl.pallas_call(
        pack_y_kernel,
        grid=(1,),
        out_shape=(shape, shape),
        in_specs=[first, first, final, final],
        out_specs=(first, first),
        compiler_params=params(64),
        cost_estimate=cost(0, 4 * nx * 8 * nz * 4),
        name="pack_y",
    )(temp, cond, temp, cond)


def pack_x_kernel(first, final, below0, above0, below1, above1, low_ref, high_ref):
    ny, nz = first.shape[1:]
    upper = lax.broadcasted_iota(jnp.int32, (8, nz), 0) < ROWS
    for send, temp, below, above in (
        (low_ref, first, below0, above0),
        (high_ref, final, below1, above1),
    ):
        for p in range(HALO):
            send[p, :ny] = temp[p]
            send[p, ny : ny + 8] = jnp.where(upper, above[p], pltpu.roll(below[p], ROWS, 0))
            send[p, ny + 8 :] = jnp.where(upper, pltpu.roll(above[p], ROWS, 0), below[p])


def pack_x(temp, below, above):
    nx, ny, nz = temp.shape

    def ends(rows):
        return (
            pl.BlockSpec((HALO, rows, nz), lambda i: (0, 0, 0)),
            pl.BlockSpec((HALO, rows, nz), lambda i: (nx // HALO - 1, 0, 0)),
        )

    first, final = ends(ny)
    first_rows, final_rows = ends(8)
    whole = pl.BlockSpec((HALO, ny + 16, nz), lambda i: (0, 0, 0))
    shape = jax.ShapeDtypeStruct((HALO, ny + 16, nz), jnp.float32)
    return pl.pallas_call(
        pack_x_kernel,
        grid=(1,),
        out_shape=(shape, shape),
        in_specs=[first, final, first_rows, first_rows, final_rows, final_rows],
        out_specs=(whole, whole),
        compiler_params=params(64),
        cost_estimate=cost(0, 4 * HALO * (ny + 16) * nz * 4),
        name="pack_x",
    )(temp, temp, below, above, below, above)


def coupling(a, b):
    return jnp.where(jnp.minimum(a, b) > 0.0, (0.5 * step_size) * (a + b), 0.0)


def neighbours():
    slab, pair = lax.axis_index("slab"), lax.axis_index("pair")
    return slab > 0, slab < lax.axis_size("slab") - 1, pair > 0, pair < lax.axis_size("pair") - 1


def lane_tiles(nz):
    return [slice(j * LANES, (j + 1) * LANES) for j in range(nz // LANES)]


def prepare(cond, gx, gy, gz, gb):
    tall, wide, nz = cond.shape
    tiles = wide // 8
    lane = lax.broadcasted_iota(jnp.int32, (8, LANES), 1)
    half = 0.5 * step_size

    @pl.loop(0, tall)
    def _(x):
        after = jnp.minimum(x + 1, tall - 1)
        stores = Lagging(LAG)
        for z in lane_tiles(nz):
            last = z.stop == nz
            for t in range(tiles):
                rows = slice(8 * t, 8 * t + 8)
                here = cond[x, rows, z]
                stores.add(put(gx, (x, rows, z), half * (here + cond[after, rows, z])))
                if t + 1 < tiles:
                    beside = cond[x, 8 * t + 8 : 8 * t + 16, z]
                else:
                    beside = pltpu.roll(cond[x, :8, z], 7, 0)
                stores.add(put(gy, (x, rows, z), half * (here + beside)))
                turned = pltpu.roll(here, LANES - 1, 1)
                if last:
                    deeper = here
                else:
                    deeper = pltpu.roll(cond[x, rows, z.stop : z.stop + LANES], LANES - 1, 1)
                deeper = jnp.where(lane < LANES - 1, turned, deeper)
                stores.add(put(gz, (x, rows, z), half * (here + deeper)))
                if z.start == 0:
                    stores.add(put(gb, (x, rows), step_size * here))
        stores.finish()


def one_step(field, begin, end, target, gx, gy, gz, gb, carried):
    wide, nz = field.shape[1:]
    tiles = wide // 8
    lane = lax.broadcasted_iota(jnp.int32, (8, LANES), 1)
    sub = lax.broadcasted_iota(jnp.int32, (8, LANES), 0)
    _, _, has_below, has_above = neighbours()
    keep_above = (sub < 7) | has_above
    keep_below = (sub < 7) | has_below

    carried[...] = gx[begin - 1] * (field[begin] - field[begin - 1])

    @pl.loop(begin, end)
    def _(x):
        here, across_y = {}, {}
        stores = Lagging(LAG)
        spans = lane_tiles(nz)
        count = len(spans)

        def tile(t, j):
            if (t, j) not in here:
                here[t, j] = field[x, 8 * t : 8 * t + 8, spans[j]]
            return here[t, j]

        def y_flux(t, j):
            if (t, j) not in across_y:
                if t + 1 < tiles:
                    beside = tile(t + 1, j)
                else:
                    beside = pltpu.roll(tile(0, j), 7, 0)
                across_y[t, j] = gy[x, 8 * t : 8 * t + 8, spans[j]] * (beside - tile(t, j))
            return across_y[t, j]

        for t in range(tiles):
            rows = slice(8 * t, 8 * t + 8)
            turned = [pltpu.roll(tile(t, j), LANES - 1, 1) for j in range(count)]
            flux = []
            for j in range(count):
                deeper = turned[j + 1] if j + 1 < count else 0.0
                deeper = jnp.where(lane < LANES - 1, turned[j], deeper)
                flux.append(gz[x, rows, spans[j]] * (deeper - tile(t, j)))
            back = [pltpu.roll(f, 1, 1) for f in flux]
            for j in range(count):
                now = tile(t, j)
                low_z = back[j - 1] if j else gb[x, rows, :] * now
                low_z = jnp.where(lane > 0, back[j], low_z)
                x_flux = gx[x, rows, spans[j]] * (field[x + 1, rows, spans[j]] - now)
                low_x = carried[rows, spans[j]]
                stores.add(put(carried, (rows, spans[j]), x_flux))
                low_y = y_flux(t - 1, j) if t else pltpu.roll(y_flux(tiles - 1, j), 1, 0)
                new = now + (x_flux - low_x) + (y_flux(t, j) - low_y) + (flux[j] - low_z)
                if t:
                    new = jnp.where(keep_above if t <= ROWS else keep_below, new, 0.0)
                stores.add(put(*target(x, t, spans[j]), new))
        stores.finish()


def thin_planes(cond, ny, thin_ref):
    tall, _, wide, _ = cond.shape
    lane = lax.broadcasted_iota(jnp.int32, (wide, LANES), 1)
    y_lane = lax.broadcasted_iota(jnp.int32, (8, LANES), 1)
    for base in range(0, tall, 16):
        planes = min(16, tall - base)
        gathered = jnp.zeros((wide, LANES), jnp.float32)
        for g in range(planes):
            piece = cond[base + g, 0]
            if g:
                piece = pltpu.roll(piece, 8 * g, 1)
            gathered = jnp.where((lane >> 3) == g, piece, gathered)
        turned = jnp.concatenate(
            [gathered, jnp.zeros((LANES - wide, LANES), jnp.float32)], axis=0
        ).T
        for g in range(planes):
            rows = turned[8 * g : 8 * g + 8, :]
            moved = pltpu.roll(rows, LANES - wide, 1)
            thin_ref[base + g] = jnp.where(
                y_lane < ny + ROWS, rows, jnp.where(y_lane >= LANES - ROWS, moved, 0.0)
            )


def heat_kernel(
    t_ref, k_ref, k_low, k_high, t_low, t_high, below_ref, above_ref, out_ref, thin_ref,
    loaded, field, between, gx, gy, gz, gb, carried, placed, sems,
):
    nx, ny, nz = t_ref.shape
    tall, wide = nx + 2 * HALO, ny + 2 * ROWS
    tiles = wide // 8
    raw_t, raw_k = loaded.at[0], loaded.at[1]
    spans = lane_tiles(nz)
    ends = (0, HALO + nx)

    def fetch(which, k, ref, source_row, planes, at, row, rows):
        return [
            pltpu.make_async_copy(
                ref.at[:, pl.ds(source_row, rows), pl.ds(z.start, LANES)],
                loaded.at[which, pl.ds(at, planes), j, pl.ds(row, rows)],
                sems.at[which, k, j],
            )
            for j, z in enumerate(spans)
        ]

    k_copies = fetch(1, 0, k_ref, 0, nx, HALO, 0, ny)
    t_copies = fetch(0, 0, t_ref, 0, nx, HALO, 0, ny)
    for k, (at, k_side, t_side) in enumerate(zip(ends, (k_low, k_high), (t_low, t_high))):
        k_copies += fetch(1, 1 + k, k_side, 0, HALO, at, 0, ny)
        k_copies += fetch(1, 3 + k, t_side, ny + 8, HALO, at, ny, 8)
        t_copies += fetch(0, 1 + k, t_side, 0, HALO, at, 0, ny + 8)
    for copy in k_copies + t_copies:
        copy.start()
    has_low, has_high, has_below, has_above = neighbours()
    upper = lax.broadcasted_iota(jnp.int32, (8, LANES), 0) < ROWS

    @pl.loop(0, nx)
    def _(x):
        for j, z in enumerate(spans):
            down, up = above_ref[x, :, z], below_ref[x, :, z]
            raw_t[HALO + x, j, ny:] = jnp.where(upper, down, pltpu.roll(up, ROWS, 0))
            raw_k[HALO + x, j, ny:] = jnp.where(upper, pltpu.roll(down, ROWS, 0), up)

    for copy in k_copies:
        copy.wait()

    thin_planes(raw_k, ny, thin_ref)

    @pl.when(jnp.logical_not(has_above & has_below))
    def _():
        missing = (upper & jnp.logical_not(has_above)) | (
            jnp.logical_not(upper) & jnp.logical_not(has_below)
        )

        @pl.loop(0, tall)
        def _(x):
            for j in range(len(spans)):
                edge = raw_k[x, j, ny:]
                last = jnp.broadcast_to(raw_k[x, j, ny - 1 : ny, :], edge.shape)
                first = jnp.broadcast_to(raw_k[x, j, 0:1, :], edge.shape)
                raw_k[x, j, ny:] = jnp.where(missing, jnp.where(upper, last, first), edge)

    @pl.when(jnp.logical_not(has_low))
    def _():
        raw_k[HALO - 1] = raw_k[HALO]

    @pl.when(jnp.logical_not(has_high))
    def _():
        raw_k[HALO + nx] = raw_k[HALO + nx - 1]

    def spread(which, target):
        @pl.loop(0, tall)
        def _(x):
            for t in range(tiles):
                rows = pl.ds(t, 8, stride=tiles)
                for j, z in enumerate(spans):
                    target[x, 8 * t : 8 * t + 8, z] = loaded[which, x, j, rows, :]

    spread(1, between)
    prepare(between, gx, gy, gz, gb)
    for copy in t_copies:
        copy.wait()
    spread(0, field)

    for x in (HALO - 1, HALO + nx):
        between[x] = jnp.zeros((wide, nz), jnp.float32)

    def inside(target):
        return lambda x, t, z: (target, (x, slice(8 * t, 8 * t + 8), z))

    def outside(x, t, z):
        return placed, (x - HALO, z.start // LANES, pl.ds(t, 8, stride=tiles))

    old, new = field, between
    for step in range(1, STEPS):
        begin = jnp.where(has_low, step, HALO)
        end = jnp.where(has_high, tall - step, tall - HALO)
        one_step(old, begin, end, inside(new), gx, gy, gz, gb, carried)
        old, new = new, old
    one_step(old, HALO, tall - HALO, outside, gx, gy, gz, gb, carried)

    @pl.loop(0, nx)
    def _(x):
        for j, z in enumerate(spans):
            out_ref[x, :, z] = placed[x, j, :ny, :]


def heat(temp, cond, k_low, k_high, t_low, t_high, below, above):
    nx, ny, nz = temp.shape
    tall, wide = nx + 2 * HALO, ny + 2 * ROWS
    hbm = pl.BlockSpec(memory_space=pl.ANY)
    vmem = pl.BlockSpec(memory_space=pltpu.VMEM)
    big = pltpu.VMEM((tall, wide, nz), jnp.float32)
    return pl.pallas_call(
        heat_kernel,
        out_shape=(
            jax.ShapeDtypeStruct(temp.shape, jnp.float32),
            jax.ShapeDtypeStruct((tall, 8, LANES), jnp.float32),
        ),
        in_specs=[hbm] * 6 + [vmem] * 2,
        scratch_shapes=[pltpu.VMEM((2, tall, nz // LANES, wide, LANES), jnp.float32)]
        + [big] * 5
        + [
            pltpu.VMEM((tall, wide, LANES), jnp.float32),
            pltpu.VMEM((wide, nz), jnp.float32),
            pltpu.VMEM((nx, nz // LANES, wide, LANES), jnp.float32),
            pltpu.SemaphoreType.DMA((2, 5, nz // LANES)),
        ],
        compiler_params=params(64),
        cost_estimate=cost(tall * wide * nz * 100, 12 * nx * ny * nz * 4),
        name="heat",
    )(temp, cond, k_low, k_high, t_low, t_high, below, above)


def source_kernel(ny, all_ref, thin_ref, base_ref, out_ref):
    tall = thin_ref.shape[0]
    nx = tall - 2 * HALO
    sheets = all_ref.shape[1]
    sub = lax.broadcasted_iota(jnp.int32, (8, LANES), 0)
    y_lane = lax.broadcasted_iota(jnp.int32, (8, LANES), 1)

    slabs, pairs = lax.axis_size("slab"), lax.axis_size("pair")

    def sheet(down, across):
        slab = lax.axis_index("slab") + down
        pair = lax.axis_index("pair") + across
        inside = (slab >= 0) & (slab < slabs) & (pair >= 0) & (pair < pairs)
        found = all_ref[jnp.where(inside, slab * pairs + pair, 0)]
        return jnp.where(inside, found, 0.0)

    def rows_of(down):
        low, own, high = (sheet(down, across) for across in (-1, 0, 1))
        out = []
        for half in range(2):
            if half == 0:
                own_at, high_at, low_at = own, pltpu.roll(high, ny, 1), pltpu.roll(low, ny, 1)
            else:
                own_at, high_at, low_at = pltpu.roll(own, ny, 1), high, low
            out.append(
                jnp.where(
                    y_lane < ny,
                    own_at,
                    jnp.where(
                        y_lane < ny + HALO,
                        high_at,
                        jnp.where(y_lane >= LANES - HALO, low_at, 0.0),
                    ),
                )
            )
        return out

    lines = [rows_of(down) for down in (-1, 0, 1)]
    source = []
    for x in range(-HALO, nx + HALO):
        which, local = (x + nx) // nx, x % nx
        row = lines[which][local % 2][local // 2 : local // 2 + 1, :]
        source.append(jnp.where(sub == 0, jnp.broadcast_to(row, (8, LANES)), 0.0))

    cond = [thin_ref[x] for x in range(tall)]
    cx, cy, cz, centre = [], [], [], []
    for x in range(tall):
        here = cond[x]
        after = cond[min(x + 1, tall - 1)]
        before = cond[max(x - 1, 0)]
        y_after = pltpu.roll(here, LANES - 1, 1)
        y_before = pltpu.roll(here, 1, 1)
        z_after = jnp.where(sub == 7, 0.0, pltpu.roll(here, 7, 0))
        z_before = jnp.where(sub == 0, 0.0, pltpu.roll(here, 1, 0))
        cx.append(coupling(here, after))
        cy.append(coupling(here, y_after))
        cz.append(coupling(here, z_after))
        total = 6.0 * here
        for near in (after, before, y_after, y_before, z_after, z_before):
            total = total + jnp.where(near > 0.0, near, here)
        centre.append(1.0 - (0.5 * step_size) * total)

    added = source
    for step in range(1, STEPS):
        new = list(added)
        for x in range(step, tall - step):
            here = added[x]
            total = source[x] + centre[x] * here
            total = total + (cx[x] * added[x + 1] + cx[x - 1] * added[x - 1])
            total = total + cy[x] * pltpu.roll(here, LANES - 1, 1)
            total = total + pltpu.roll(cy[x] * here, 1, 1)
            total = total + cz[x] * pltpu.roll(here, 7, 0)
            new[x] = total + pltpu.roll(cz[x] * here, 1, 0)
        added = new

    lane = lax.broadcasted_iota(jnp.int32, (ny, LANES), 1)
    turned = jnp.concatenate(added[HALO : HALO + nx], axis=0).T[:ny]
    for x in range(nx):
        piece = turned if x == 0 else pltpu.roll(turned, LANES - 8 * x, 1)
        out_ref[x] = base_ref[x] + jnp.where(lane < STEPS, piece, 0.0)


def add_source(everything, thin, base):
    nx, ny, nz = base.shape
    block = pl.BlockSpec((nx, ny, LANES), lambda i: (0, 0, 0))
    return pl.pallas_call(
        functools.partial(source_kernel, ny),
        grid=(1,),
        out_shape=jax.ShapeDtypeStruct(base.shape, jnp.float32),
        in_specs=[
            pl.BlockSpec(everything.shape, lambda i: (0, 0, 0)),
            pl.BlockSpec(thin.shape, lambda i: (0, 0, 0)),
            block,
        ],
        out_specs=block,
        input_output_aliases={2: 0},
        compiler_params=params(64),
        cost_estimate=cost(1_000_000, 2 * nx * ny * LANES * 4),
        name="add_source",
    )(everything, thin, base)


def exchange(rows):
    return lax.all_to_all(rows, ("slab", "pair"), split_axis=0, concat_axis=0, tiled=True)


def together(*arrays):
    return lax.optimization_barrier(arrays)


def both_ways(low, high, axis):
    count = lax.axis_size(axis)
    forward = [(i, i + 1) for i in range(count - 1)]
    backward = [(target, source) for source, target in forward]
    from_low = lax.ppermute(high, axis, forward)
    from_high = lax.ppermute(low, axis, backward)
    return from_low, from_high


def shards(
    initial_warmth,
    heat_passing_coefficient,
    mirror_fraction,
    element_facing_site,
    tile_block_couples,
    active_slot_count,
    view_factor_blocks,
):
    nx, ny, _ = initial_warmth.shape
    slabs, pairs = lax.axis_size("slab"), lax.axis_size("pair")
    count = slabs * pairs
    blocks = mirror_fraction.shape[0]
    couples = tile_block_couples.T

    temp, cond = initial_warmth, heat_passing_coefficient
    emitted, copies = emit(temp, element_facing_site, mirror_fraction, count)
    temp, copies = together(temp, copies)

    def sweep_terms(whole):
        whole = whole.reshape(count * blocks, BLK)
        term = tile_terms(whole, couples, active_slot_count, view_factor_blocks)
        return term.reshape(count, blocks, BLK)

    whole = exchange(copies)
    cond, copies = together(cond, copies)
    send_low, send_high = cond[:HALO], cond[nx - HALO :]
    k_low, k_high = both_ways(send_low, send_high, "slab")
    whole = together(whole, send_low, send_high)[0]
    temp, cond, term = together(temp, cond, sweep_terms(whole))
    parts = exchange(term)
    below, above = both_ways(*pack_y(temp, cond), "pair")
    parts, below, above, k_low, k_high = together(parts, below, above, k_low, k_high)
    copies, below, above = together(middle(parts, emitted, mirror_fraction), below, above)
    whole = exchange(copies)
    send_low, send_high = pack_x(temp, below, above)
    t_low, t_high = both_ways(send_low, send_high, "slab")
    whole = together(whole, send_low, send_high)[0]
    parts = exchange(sweep_terms(whole))
    parts, t_low, t_high = together(parts, t_low, t_high)
    radiosity, source = last(parts, emitted, mirror_fraction, element_facing_site, nx * ny, count)
    everything = exchange(source)
    below, source = together(below, source)
    base, thin = heat(temp, cond, k_low, k_high, t_low, t_high, below, above)

    warmed_liner = add_source(everything, thin, base)
    return (radiosity, warmed_liner)


def solution(mesh):
    return jax.shard_map(
        shards,
        mesh=mesh,
        in_specs=(
            P("slab", "pair", None),
            P("slab", "pair", None),
            P(("slab", "pair"), None),
            P(("slab", "pair"), None),
            P(("slab", "pair"), None),
            P(("slab", "pair")),
            P(("slab", "pair"), None, None),
        ),
        out_specs=(P(("slab", "pair"), None), P("slab", "pair", None)),
        check_vma=False,
    )
```

```python
import functools

import jax
import jax.numpy as jnp
from jax import lax
from jax.experimental import pallas as pl
from jax.experimental.pallas import tpu as pltpu
from jax.sharding import PartitionSpec as P

BLK = 128
SWEEPS = 2
STEPS = 4
HALO = STEPS
ROWS = STEPS
LANES = 128
CHUNK = 16
LAG = 8

step_size = 0.07

NT = (((1,), (1,)), ((), ()))
NN = (((1,), (0,)), ((), ()))


def params(mib):
    return pltpu.CompilerParams(vmem_limit_bytes=mib * 1024 * 1024)


def cost(flops, nbytes):
    return pl.CostEstimate(flops=flops, bytes_accessed=nbytes, transcendentals=0)


def parts_of(x, count):
    out = []
    for _ in range(count - 1):
        part = x.astype(jnp.bfloat16)
        out.append(part)
        x = x - part.astype(jnp.float32)
    out.append(x.astype(jnp.bfloat16))
    return out


class Lagging:
    def __init__(self, depth):
        self.depth = depth
        self.waiting = []

    def add(self, store):
        self.waiting.append(store)
        if len(self.waiting) > self.depth:
            self.waiting.pop(0)()

    def finish(self):
        for store in self.waiting:
            store()
        self.waiting = []


def put(ref, index, value):
    return lambda: ref.__setitem__(index, value)


def emit_kernel(temp_ref, site_ref, mirror_ref, emitted_ref, copies_ref):
    nx, ny, _ = temp_ref.shape
    sheets = nx * ny // LANES
    per = LANES // ny
    lanes = lax.broadcasted_iota(jnp.int32, (LANES, LANES), 1)
    gathered = jnp.zeros((LANES, LANES), jnp.float32)
    for r in range(sheets):
        piece = temp_ref[per * r : per * r + per].reshape(LANES, LANES)
        if r:
            piece = pltpu.roll(piece, r, 1)
        gathered = jnp.where(lanes == r, piece, gathered)
    plane = gathered.T[:sheets]
    for half in range(site_ref.shape[0] // 8):
        rows = pl.ds(half * 8, 8)
        site = site_ref[rows, :]
        lane = site & (LANES - 1)
        sheet = site >> 7
        warmth = jnp.zeros(site.shape, jnp.float32)
        for r in range(sheets):
            line = jnp.broadcast_to(plane[r : r + 1, :], site.shape)
            picked = jnp.take_along_axis(line, lane, axis=1)
            warmth = jnp.where(sheet == r, picked, warmth)
        square = warmth * warmth
        emitted = (1.0 - mirror_ref[rows, :]) * (square * square)
        emitted_ref[rows, :] = emitted
        for d in range(copies_ref.shape[0]):
            copies_ref[d, rows, :] = emitted


def emit(temp, site, mirror, count):
    shape = mirror.shape
    nx, ny, _ = temp.shape
    patch = pl.BlockSpec(shape, lambda i: (0, 0))
    return pl.pallas_call(
        emit_kernel,
        grid=(1,),
        out_shape=(
            jax.ShapeDtypeStruct(shape, jnp.float32),
            jax.ShapeDtypeStruct((count,) + shape, jnp.float32),
        ),
        in_specs=[pl.BlockSpec((nx, ny, LANES), lambda i: (0, 0, 0)), patch, patch],
        out_specs=(patch, pl.BlockSpec((count,) + shape, lambda i: (0, 0, 0))),
        compiler_params=params(64),
        cost_estimate=cost(10_000, 900_000),
        name="emit",
    )(temp, site, mirror)


def tiles_kernel(
    live_ref, pairs_ref, lanes_ref, whole_ref, tiles_ref, out_ref, held, terms, sems
):
    slots = held.shape[0]
    live = live_ref[0]
    chunks = (live + CHUNK - 1) // CHUNK

    def chunk_copy(c):
        span = pl.ds(c * CHUNK, CHUNK)
        return pltpu.make_async_copy(tiles_ref.at[span], held.at[span], sems.at[c])

    @pl.loop(0, chunks)
    def _(c):
        chunk_copy(c).start()

    top = lax.broadcasted_iota(jnp.int32, (8, BLK), 0) == 0

    def split_row(block):
        row = jnp.broadcast_to(whole_ref[pl.ds(block, 1), :], (8, BLK))
        high = row.astype(jnp.bfloat16).astype(jnp.float32)
        return jnp.where(top, high, row - high)

    def vectors(a, b):
        stacked = jnp.concatenate([split_row(a), split_row(b)], axis=0)
        stacked = stacked.astype(jnp.bfloat16)
        return jnp.concatenate([stacked, stacked], axis=1)

    @pl.loop(0, chunks)
    def _(c):
        chunk_copy(c).wait()
        stores = Lagging(4 * CHUNK)
        for u in range(0, CHUNK, 2):
            t = c * CHUNK + u
            high_a, low_a = parts_of(held[t], 2)
            high_b, low_b = parts_of(held[t + 1], 2)
            both = jnp.concatenate(
                [
                    jnp.concatenate([high_a, high_b], axis=1),
                    jnp.concatenate([low_a, low_b], axis=1),
                ],
                axis=0,
            )
            second = lax.dot_general(
                vectors(pairs_ref[0, t], pairs_ref[0, t + 1]),
                both,
                NN,
                preferred_element_type=jnp.float32,
            )
            turned = jnp.concatenate(
                [
                    jnp.concatenate([high_a, low_a], axis=1),
                    jnp.concatenate([high_b, low_b], axis=1),
                ],
                axis=0,
            )
            first = lax.dot_general(
                vectors(pairs_ref[1, t], pairs_ref[1, t + 1]),
                turned,
                NT,
                preferred_element_type=jnp.float32,
            )
            for side, result in ((0, first), (1, second)):
                for v, (top_row, cols) in enumerate(((0, slice(0, BLK)), (8, slice(BLK, 2 * BLK)))):
                    row = result[top_row : top_row + 1, cols] + result[top_row + 1 : top_row + 2, cols]
                    stores.add(put(terms, (side, pl.ds(t + v, 1)), row))
        stores.finish()

    used = lax.broadcasted_iota(jnp.int32, (slots, BLK), 0) < live
    used_lane = lax.broadcasted_iota(jnp.int32, (1, slots), 1) < live
    blocks = out_ref.shape[0]
    group = min(blocks, 512)
    split = []
    for side in range(2):
        masked = jnp.where(used, terms[side], 0.0)
        split.append(jnp.concatenate(parts_of(masked, 2), axis=1))
    for base in range(0, blocks, group):
        rows = lax.broadcasted_iota(jnp.int32, (group, slots), 0) + base
        total = jnp.zeros((group, 2 * BLK), jnp.float32)
        for side in range(2):
            target = jnp.where(used_lane, lanes_ref[side : side + 1, :], -1)
            choose = jnp.where(rows == target, 1.0, 0.0).astype(jnp.bfloat16)
            total = total + jnp.dot(choose, split[side], preferred_element_type=jnp.float32)
        out_ref[base : base + group, :] = total[:, :BLK] + total[:, BLK:]


def tile_terms(whole, couples, live, tiles):
    slots = tiles.shape[0]
    smem = pl.BlockSpec(memory_space=pltpu.SMEM)
    vmem = pl.BlockSpec(memory_space=pltpu.VMEM)
    return pl.pallas_call(
        tiles_kernel,
        out_shape=jax.ShapeDtypeStruct(whole.shape, jnp.float32),
        in_specs=[smem, smem, vmem, vmem, pl.BlockSpec(memory_space=pl.ANY)],
        out_specs=vmem,
        scratch_shapes=[
            pltpu.VMEM(tiles.shape, jnp.float32),
            pltpu.VMEM((2, slots, BLK), jnp.float32),
            pltpu.SemaphoreType.DMA((slots // CHUNK,)),
        ],
        compiler_params=params(64),
        cost_estimate=cost(slots * BLK * BLK * 32, slots * BLK * BLK * 4),
        name="tiles",
    )(live, couples, couples, whole, tiles)


def sum_parts(parts_ref, rows):
    total = parts_ref[0, rows, :]
    for d in range(1, parts_ref.shape[0]):
        total = total + parts_ref[d, rows, :]
    return total


def middle_kernel(parts_ref, emitted_ref, mirror_ref, copies_ref):
    for half in range(emitted_ref.shape[0] // 8):
        rows = pl.ds(half * 8, 8)
        incident = sum_parts(parts_ref, rows)
        radiosity = emitted_ref[rows, :] + mirror_ref[rows, :] * incident
        for d in range(copies_ref.shape[0]):
            copies_ref[d, rows, :] = radiosity


def middle(parts, emitted, mirror):
    return pl.pallas_call(
        middle_kernel,
        out_shape=jax.ShapeDtypeStruct(parts.shape, jnp.float32),
        compiler_params=params(64),
        cost_estimate=cost(100_000, 600_000),
        name="middle",
    )(parts, emitted, mirror)


def last_kernel(scale, parts_ref, emitted_ref, mirror_ref, site_ref, rad_ref, source_ref):
    blocks = emitted_ref.shape[0]
    incident = sum_parts(parts_ref, slice(None))
    emitted = emitted_ref[...]
    mirror = mirror_ref[...]
    rad_ref[...] = emitted + mirror * incident
    absorbed = ((1.0 - mirror) * incident - emitted) * scale
    site = site_ref[...]
    lane = site & (LANES - 1)
    sheet = site >> 7
    sheets = source_ref.shape[1]
    sheet_iota = lax.broadcasted_iota(jnp.int32, (sheets, BLK), 0)
    lane_iota = lax.broadcasted_iota(jnp.int32, (LANES, BLK), 0)
    left = []
    right = []
    for b in range(blocks):
        here = jnp.where(sheet_iota == sheet[b : b + 1, :], absorbed[b : b + 1, :], 0.0)
        left.append(here)
        pick = jnp.where(lane_iota == lane[b : b + 1, :], 1.0, 0.0)
        right.append(pick.astype(jnp.bfloat16))
    left = jnp.concatenate(left, axis=1)
    right = jnp.concatenate(right, axis=1)
    source = jnp.zeros((sheets, LANES), jnp.float32)
    for part in parts_of(left, 3):
        source = source + lax.dot_general(part, right, NT, preferred_element_type=jnp.float32)
    for d in range(source_ref.shape[0]):
        source_ref[d] = source


def last(parts, emitted, mirror, site, cells, count):
    weight = cells / (mirror.shape[0] * BLK * 1.0)
    return pl.pallas_call(
        functools.partial(last_kernel, step_size * weight),
        out_shape=(
            jax.ShapeDtypeStruct(mirror.shape, jnp.float32),
            jax.ShapeDtypeStruct((count, cells // LANES, LANES), jnp.float32),
        ),
        compiler_params=params(64),
        cost_estimate=cost(10_000_000, 600_000),
        name="last",
    )(parts, emitted, mirror, site)


def pack_y_kernel(t0, k0, t7, k7, down_ref, up_ref):
    upper = lax.broadcasted_iota(jnp.int32, down_ref.shape[1:], 0) < ROWS
    for x in range(down_ref.shape[0]):
        down_ref[x] = jnp.where(upper, t0[x], pltpu.roll(k0[x], ROWS, 0))
        up_ref[x] = jnp.where(upper, pltpu.roll(t7[x], ROWS, 0), k7[x])


def pack_y(temp, cond):
    nx, ny, nz = temp.shape
    first = pl.BlockSpec((nx, 8, nz), lambda i: (0, 0, 0))
    final = pl.BlockSpec((nx, 8, nz), lambda i: (0, ny // 8 - 1, 0))
    shape = jax.ShapeDtypeStruct((nx, 8, nz), jnp.float32)
    return pl.pallas_call(
        pack_y_kernel,
        grid=(1,),
        out_shape=(shape, shape),
        in_specs=[first, first, final, final],
        out_specs=(first, first),
        compiler_params=params(64),
        cost_estimate=cost(0, 4 * nx * 8 * nz * 4),
        name="pack_y",
    )(temp, cond, temp, cond)


def pack_x_kernel(first, final, below0, above0, below1, above1, low_ref, high_ref):
    ny, nz = first.shape[1:]
    upper = lax.broadcasted_iota(jnp.int32, (8, nz), 0) < ROWS
    for send, temp, below, above in (
        (low_ref, first, below0, above0),
        (high_ref, final, below1, above1),
    ):
        for p in range(HALO):
            send[p, :ny] = temp[p]
            send[p, ny : ny + 8] = jnp.where(upper, above[p], pltpu.roll(below[p], ROWS, 0))
            send[p, ny + 8 :] = jnp.where(upper, pltpu.roll(above[p], ROWS, 0), below[p])


def pack_x(temp, below, above):
    nx, ny, nz = temp.shape

    def ends(rows):
        return (
            pl.BlockSpec((HALO, rows, nz), lambda i: (0, 0, 0)),
            pl.BlockSpec((HALO, rows, nz), lambda i: (nx // HALO - 1, 0, 0)),
        )

    first, final = ends(ny)
    first_rows, final_rows = ends(8)
    whole = pl.BlockSpec((HALO, ny + 16, nz), lambda i: (0, 0, 0))
    shape = jax.ShapeDtypeStruct((HALO, ny + 16, nz), jnp.float32)
    return pl.pallas_call(
        pack_x_kernel,
        grid=(1,),
        out_shape=(shape, shape),
        in_specs=[first, final, first_rows, first_rows, final_rows, final_rows],
        out_specs=(whole, whole),
        compiler_params=params(64),
        cost_estimate=cost(0, 4 * HALO * (ny + 16) * nz * 4),
        name="pack_x",
    )(temp, temp, below, above, below, above)


def coupling(a, b):
    return jnp.where(jnp.minimum(a, b) > 0.0, (0.5 * step_size) * (a + b), 0.0)


def neighbours():
    slab, pair = lax.axis_index("slab"), lax.axis_index("pair")
    return slab > 0, slab < lax.axis_size("slab") - 1, pair > 0, pair < lax.axis_size("pair") - 1


def lane_tiles(nz):
    return [slice(j * LANES, (j + 1) * LANES) for j in range(nz // LANES)]


def one_step(field, cond, begin, end, target, carried):
    wide, nz = field.shape[1:]
    tiles = wide // 8
    spans = lane_tiles(nz)
    count = len(spans)
    lane = lax.broadcasted_iota(jnp.int32, (8, LANES), 1)
    sub = lax.broadcasted_iota(jnp.int32, (8, LANES), 0)
    _, _, has_below, has_above = neighbours()
    keep_above = (sub < 7) | has_above
    keep_below = (sub < 7) | has_below

    carried[...] = (cond[begin - 1] + cond[begin]) * (field[begin] - field[begin - 1])

    def row_tile(ref, x, t):
        return [ref[x, 8 * t : 8 * t + 8, z] for z in spans]

    def first_rolled(ref, x):
        return [pltpu.roll(v, 7, 0) for v in row_tile(ref, x, 0)]

    def y_flux(t_now, k_now, t_next, k_next):
        return [
            (k_now[j] + k_next[j]) * (t_next[j] - t_now[j]) for j in range(count)
        ]

    def z_change(t_now, k_now):
        t_turned = [pltpu.roll(v, LANES - 1, 1) for v in t_now]
        k_turned = [pltpu.roll(v, LANES - 1, 1) for v in k_now]
        flux = []
        for j in range(count):
            t_deep = t_turned[j + 1] if j + 1 < count else 0.0
            k_deep = k_turned[j + 1] if j + 1 < count else k_now[j]
            t_deep = jnp.where(lane < LANES - 1, t_turned[j], t_deep)
            k_deep = jnp.where(lane < LANES - 1, k_turned[j], k_deep)
            flux.append((k_now[j] + k_deep) * (t_deep - t_now[j]))
        back = [pltpu.roll(f, 1, 1) for f in flux]
        out = []
        for j in range(count):
            low = back[j - 1] if j else (k_now[0] + k_now[0]) * t_now[0]
            out.append(flux[j] - jnp.where(lane > 0, back[j], low))
        return out

    @pl.loop(begin, end, step=2)
    def _(base):
        stores = Lagging(LAG)
        planes = (base, base + 1)
        low_y = []
        for x in planes:
            final = y_flux(
                row_tile(field, x, tiles - 1),
                row_tile(cond, x, tiles - 1),
                first_rolled(field, x),
                first_rolled(cond, x),
            )
            low_y.append([pltpu.roll(f, 1, 0) for f in final])
        t_now = [row_tile(field, x, 0) for x in planes]
        k_now = [row_tile(cond, x, 0) for x in planes]
        for t in range(tiles):
            rows = slice(8 * t, 8 * t + 8)
            if t + 1 < tiles:
                t_next = [row_tile(field, x, t + 1) for x in planes]
                k_next = [row_tile(cond, x, t + 1) for x in planes]
            else:
                t_next = [first_rolled(field, x) for x in planes]
                k_next = [first_rolled(cond, x) for x in planes]
            total = []
            for p in range(2):
                high_y = y_flux(t_now[p], k_now[p], t_next[p], k_next[p])
                change_z = z_change(t_now[p], k_now[p])
                total.append(
                    [
                        t_now[p][j] + (high_y[j] - low_y[p][j]) + change_z[j]
                        for j in range(count)
                    ]
                )
                low_y[p] = high_y
            for j, z in enumerate(spans):
                low_x = carried[rows, z]
                mid_x = (k_now[0][j] + k_now[1][j]) * (t_now[1][j] - t_now[0][j])
                high_x = (k_now[1][j] + cond[base + 2, rows, z]) * (
                    field[base + 2, rows, z] - t_now[1][j]
                )
                stores.add(put(carried, (rows, z), high_x))
                for p, change_x in enumerate((mid_x - low_x, high_x - mid_x)):
                    new = total[p][j] + change_x
                    if t:
                        new = jnp.where(keep_above if t <= ROWS else keep_below, new, 0.0)
                    stores.add(put(*target(base + p, t, z), new))
            t_now, k_now = t_next, k_next
        stores.finish()


def thin_planes(cond, ny, thin_ref):
    tall, _, wide, _ = cond.shape
    lane = lax.broadcasted_iota(jnp.int32, (wide, LANES), 1)
    y_lane = lax.broadcasted_iota(jnp.int32, (8, LANES), 1)
    for base in range(0, tall, 16):
        planes = min(16, tall - base)
        gathered = jnp.zeros((wide, LANES), jnp.float32)
        for g in range(planes):
            piece = cond[base + g, 0]
            if g:
                piece = pltpu.roll(piece, 8 * g, 1)
            gathered = jnp.where((lane >> 3) == g, piece, gathered)
        turned = jnp.concatenate(
            [gathered, jnp.zeros((LANES - wide, LANES), jnp.float32)], axis=0
        ).T
        for g in range(planes):
            rows = turned[8 * g : 8 * g + 8, :]
            moved = pltpu.roll(rows, LANES - wide, 1)
            thin_ref[base + g] = jnp.where(
                y_lane < ny + ROWS, rows, jnp.where(y_lane >= LANES - ROWS, moved, 0.0)
            )


def heat_kernel(
    t_ref, k_ref, k_low, k_high, t_low, t_high, below_ref, above_ref, out_ref, thin_ref,
    loaded, field, between, faces, carried, placed, sems,
):
    nx, ny, nz = t_ref.shape
    tall, wide = nx + 2 * HALO, ny + 2 * ROWS
    tiles = wide // 8
    raw_t, raw_k = loaded.at[0], loaded.at[1]
    spans = lane_tiles(nz)
    ends = (0, HALO + nx)

    def fetch(which, k, ref, source_row, planes, at, row, rows):
        return [
            pltpu.make_async_copy(
                ref.at[:, pl.ds(source_row, rows), pl.ds(z.start, LANES)],
                loaded.at[which, pl.ds(at, planes), j, pl.ds(row, rows)],
                sems.at[which, k, j],
            )
            for j, z in enumerate(spans)
        ]

    k_copies = fetch(1, 0, k_ref, 0, nx, HALO, 0, ny)
    t_copies = fetch(0, 0, t_ref, 0, nx, HALO, 0, ny)
    for k, (at, k_side, t_side) in enumerate(zip(ends, (k_low, k_high), (t_low, t_high))):
        k_copies += fetch(1, 1 + k, k_side, 0, HALO, at, 0, ny)
        k_copies += fetch(1, 3 + k, t_side, ny + 8, HALO, at, ny, 8)
        t_copies += fetch(0, 1 + k, t_side, 0, HALO, at, 0, ny + 8)
    for copy in k_copies + t_copies:
        copy.start()
    has_low, has_high, has_below, has_above = neighbours()
    upper = lax.broadcasted_iota(jnp.int32, (8, LANES), 0) < ROWS

    @pl.loop(0, nx)
    def _(x):
        for j, z in enumerate(spans):
            down, up = above_ref[x, :, z], below_ref[x, :, z]
            raw_t[HALO + x, j, ny:] = jnp.where(upper, down, pltpu.roll(up, ROWS, 0))
            raw_k[HALO + x, j, ny:] = jnp.where(upper, pltpu.roll(down, ROWS, 0), up)

    for copy in k_copies:
        copy.wait()

    thin_planes(raw_k, ny, thin_ref)

    @pl.when(jnp.logical_not(has_above & has_below))
    def _():
        missing = (upper & jnp.logical_not(has_above)) | (
            jnp.logical_not(upper) & jnp.logical_not(has_below)
        )

        @pl.loop(0, tall)
        def _(x):
            for j in range(len(spans)):
                edge = raw_k[x, j, ny:]
                last = jnp.broadcast_to(raw_k[x, j, ny - 1 : ny, :], edge.shape)
                first = jnp.broadcast_to(raw_k[x, j, 0:1, :], edge.shape)
                raw_k[x, j, ny:] = jnp.where(missing, jnp.where(upper, last, first), edge)

    @pl.when(jnp.logical_not(has_low))
    def _():
        raw_k[HALO - 1] = raw_k[HALO]

    @pl.when(jnp.logical_not(has_high))
    def _():
        raw_k[HALO + nx] = raw_k[HALO + nx - 1]

    def spread(which, target, scale):
        @pl.loop(0, tall)
        def _(x):
            for t in range(tiles):
                rows = pl.ds(t, 8, stride=tiles)
                for j, z in enumerate(spans):
                    value = loaded[which, x, j, rows, :]
                    target[x, 8 * t : 8 * t + 8, z] = value if scale is None else scale * value

    spread(1, faces, 0.5 * step_size)
    for copy in t_copies:
        copy.wait()
    spread(0, field, None)

    def inside(target):
        return lambda x, t, z: (target, (x, slice(8 * t, 8 * t + 8), z))

    def outside(x, t, z):
        return placed, (x - HALO, z.start // LANES, pl.ds(t, 8, stride=tiles))

    old, new = field, between
    for step in range(1, STEPS):
        one_step(old, faces, step, tall - step, inside(new), carried)
        for x, there in ((HALO - 1, has_low), (HALO + nx, has_high)):

            @pl.when(jnp.logical_not(there))
            def _():
                new[x] = jnp.zeros((wide, nz), jnp.float32)

        old, new = new, old
    one_step(old, faces, HALO, tall - HALO, outside, carried)

    @pl.loop(0, nx)
    def _(x):
        for j, z in enumerate(spans):
            out_ref[x, :, z] = placed[x, j, :ny, :]


def heat(temp, cond, k_low, k_high, t_low, t_high, below, above):
    nx, ny, nz = temp.shape
    tall, wide = nx + 2 * HALO, ny + 2 * ROWS
    hbm = pl.BlockSpec(memory_space=pl.ANY)
    vmem = pl.BlockSpec(memory_space=pltpu.VMEM)
    big = pltpu.VMEM((tall, wide, nz), jnp.float32)
    return pl.pallas_call(
        heat_kernel,
        out_shape=(
            jax.ShapeDtypeStruct(temp.shape, jnp.float32),
            jax.ShapeDtypeStruct((tall, 8, LANES), jnp.float32),
        ),
        in_specs=[hbm] * 6 + [vmem] * 2,
        scratch_shapes=[pltpu.VMEM((2, tall, nz // LANES, wide, LANES), jnp.float32)]
        + [big] * 3
        + [
            pltpu.VMEM((wide, nz), jnp.float32),
            pltpu.VMEM((nx, nz // LANES, wide, LANES), jnp.float32),
            pltpu.SemaphoreType.DMA((2, 5, nz // LANES)),
        ],
        compiler_params=params(64),
        cost_estimate=cost(tall * wide * nz * 100, 12 * nx * ny * nz * 4),
        name="heat",
    )(temp, cond, k_low, k_high, t_low, t_high, below, above)


def source_kernel(ny, all_ref, thin_ref, base_ref, out_ref):
    tall = thin_ref.shape[0]
    nx = tall - 2 * HALO
    sheets = all_ref.shape[1]
    sub = lax.broadcasted_iota(jnp.int32, (8, LANES), 0)
    y_lane = lax.broadcasted_iota(jnp.int32, (8, LANES), 1)

    slabs, pairs = lax.axis_size("slab"), lax.axis_size("pair")

    def sheet(down, across):
        slab = lax.axis_index("slab") + down
        pair = lax.axis_index("pair") + across
        inside = (slab >= 0) & (slab < slabs) & (pair >= 0) & (pair < pairs)
        found = all_ref[jnp.where(inside, slab * pairs + pair, 0)]
        return jnp.where(inside, found, 0.0)

    def rows_of(down):
        low, own, high = (sheet(down, across) for across in (-1, 0, 1))
        out = []
        for half in range(2):
            if half == 0:
                own_at, high_at, low_at = own, pltpu.roll(high, ny, 1), pltpu.roll(low, ny, 1)
            else:
                own_at, high_at, low_at = pltpu.roll(own, ny, 1), high, low
            out.append(
                jnp.where(
                    y_lane < ny,
                    own_at,
                    jnp.where(
                        y_lane < ny + HALO,
                        high_at,
                        jnp.where(y_lane >= LANES - HALO, low_at, 0.0),
                    ),
                )
            )
        return out

    lines = [rows_of(down) for down in (-1, 0, 1)]
    source = []
    for x in range(-HALO, nx + HALO):
        which, local = (x + nx) // nx, x % nx
        row = lines[which][local % 2][local // 2 : local // 2 + 1, :]
        source.append(jnp.where(sub == 0, jnp.broadcast_to(row, (8, LANES)), 0.0))

    cond = [thin_ref[x] for x in range(tall)]
    cx, cy, cz, centre = [], [], [], []
    for x in range(tall):
        here = cond[x]
        after = cond[min(x + 1, tall - 1)]
        before = cond[max(x - 1, 0)]
        y_after = pltpu.roll(here, LANES - 1, 1)
        y_before = pltpu.roll(here, 1, 1)
        z_after = jnp.where(sub == 7, 0.0, pltpu.roll(here, 7, 0))
        z_before = jnp.where(sub == 0, 0.0, pltpu.roll(here, 1, 0))
        cx.append(coupling(here, after))
        cy.append(coupling(here, y_after))
        cz.append(coupling(here, z_after))
        total = 6.0 * here
        for near in (after, before, y_after, y_before, z_after, z_before):
            total = total + jnp.where(near > 0.0, near, here)
        centre.append(1.0 - (0.5 * step_size) * total)

    added = source
    for step in range(1, STEPS):
        new = list(added)
        for x in range(step, tall - step):
            here = added[x]
            total = source[x] + centre[x] * here
            total = total + (cx[x] * added[x + 1] + cx[x - 1] * added[x - 1])
            total = total + cy[x] * pltpu.roll(here, LANES - 1, 1)
            total = total + pltpu.roll(cy[x] * here, 1, 1)
            total = total + cz[x] * pltpu.roll(here, 7, 0)
            new[x] = total + pltpu.roll(cz[x] * here, 1, 0)
        added = new

    lane = lax.broadcasted_iota(jnp.int32, (ny, LANES), 1)
    turned = jnp.concatenate(added[HALO : HALO + nx], axis=0).T[:ny]
    for x in range(nx):
        piece = turned if x == 0 else pltpu.roll(turned, LANES - 8 * x, 1)
        out_ref[x] = base_ref[x] + jnp.where(lane < STEPS, piece, 0.0)


def add_source(everything, thin, base):
    nx, ny, nz = base.shape
    block = pl.BlockSpec((nx, ny, LANES), lambda i: (0, 0, 0))
    return pl.pallas_call(
        functools.partial(source_kernel, ny),
        grid=(1,),
        out_shape=jax.ShapeDtypeStruct(base.shape, jnp.float32),
        in_specs=[
            pl.BlockSpec(everything.shape, lambda i: (0, 0, 0)),
            pl.BlockSpec(thin.shape, lambda i: (0, 0, 0)),
            block,
        ],
        out_specs=block,
        input_output_aliases={2: 0},
        compiler_params=params(64),
        cost_estimate=cost(1_000_000, 2 * nx * ny * LANES * 4),
        name="add_source",
    )(everything, thin, base)


def exchange(rows):
    return lax.all_to_all(rows, ("slab", "pair"), split_axis=0, concat_axis=0, tiled=True)


def together(*arrays):
    return lax.optimization_barrier(arrays)


def both_ways(low, high, axis):
    count = lax.axis_size(axis)
    forward = [(i, i + 1) for i in range(count - 1)]
    backward = [(target, source) for source, target in forward]
    from_low = lax.ppermute(high, axis, forward)
    from_high = lax.ppermute(low, axis, backward)
    return from_low, from_high


def shards(
    initial_warmth,
    heat_passing_coefficient,
    mirror_fraction,
    element_facing_site,
    tile_block_couples,
    active_slot_count,
    view_factor_blocks,
):
    nx, ny, _ = initial_warmth.shape
    slabs, pairs = lax.axis_size("slab"), lax.axis_size("pair")
    count = slabs * pairs
    blocks = mirror_fraction.shape[0]
    couples = tile_block_couples.T

    temp, cond = initial_warmth, heat_passing_coefficient
    emitted, copies = emit(temp, element_facing_site, mirror_fraction, count)
    temp, copies = together(temp, copies)

    def sweep_terms(whole):
        whole = whole.reshape(count * blocks, BLK)
        term = tile_terms(whole, couples, active_slot_count, view_factor_blocks)
        return term.reshape(count, blocks, BLK)

    whole = exchange(copies)
    cond, copies = together(cond, copies)
    send_low, send_high = cond[:HALO], cond[nx - HALO :]
    k_low, k_high = both_ways(send_low, send_high, "slab")
    whole = together(whole, send_low, send_high)[0]
    temp, cond, term = together(temp, cond, sweep_terms(whole))
    parts = exchange(term)
    below, above = both_ways(*pack_y(temp, cond), "pair")
    parts, below, above, k_low, k_high = together(parts, below, above, k_low, k_high)
    copies, below, above = together(middle(parts, emitted, mirror_fraction), below, above)
    whole = exchange(copies)
    send_low, send_high = pack_x(temp, below, above)
    t_low, t_high = both_ways(send_low, send_high, "slab")
    whole = together(whole, send_low, send_high)[0]
    parts = exchange(sweep_terms(whole))
    parts, t_low, t_high = together(parts, t_low, t_high)
    radiosity, source = last(parts, emitted, mirror_fraction, element_facing_site, nx * ny, count)
    everything = exchange(source)
    below, source = together(below, source)
    base, thin = heat(temp, cond, k_low, k_high, t_low, t_high, below, above)

    warmed_liner = add_source(everything, thin, base)
    return (radiosity, warmed_liner)


def solution(mesh):
    return jax.shard_map(
        shards,
        mesh=mesh,
        in_specs=(
            P("slab", "pair", None),
            P("slab", "pair", None),
            P(("slab", "pair"), None),
            P(("slab", "pair"), None),
            P(("slab", "pair"), None),
            P(("slab", "pair")),
            P(("slab", "pair"), None, None),
        ),
        out_specs=(P(("slab", "pair"), None), P("slab", "pair", None)),
        check_vma=False,
    )
```

```python
import functools

import jax
import jax.numpy as jnp
from jax import lax
from jax.experimental import pallas as pl
from jax.experimental.pallas import tpu as pltpu
from jax.sharding import PartitionSpec as P

BLK = 128
SWEEPS = 2
STEPS = 4
HALO = STEPS
ROWS = STEPS
LANES = 128
CHUNK = 16
LAG = 8

step_size = 0.07

NT = (((1,), (1,)), ((), ()))
NN = (((1,), (0,)), ((), ()))


def params(mib):
    return pltpu.CompilerParams(vmem_limit_bytes=mib * 1024 * 1024)


def cost(flops, nbytes):
    return pl.CostEstimate(flops=flops, bytes_accessed=nbytes, transcendentals=0)


def parts_of(x, count):
    out = []
    for _ in range(count - 1):
        part = x.astype(jnp.bfloat16)
        out.append(part)
        x = x - part.astype(jnp.float32)
    out.append(x.astype(jnp.bfloat16))
    return out


class Lagging:
    def __init__(self, depth):
        self.depth = depth
        self.waiting = []

    def add(self, store):
        self.waiting.append(store)
        if len(self.waiting) > self.depth:
            self.waiting.pop(0)()

    def finish(self):
        for store in self.waiting:
            store()
        self.waiting = []


def put(ref, index, value):
    return lambda: ref.__setitem__(index, value)


def emit_kernel(temp_ref, site_ref, mirror_ref, emitted_ref, copies_ref):
    nx, ny, _ = temp_ref.shape
    sheets = nx * ny // LANES
    per = LANES // ny
    lanes = lax.broadcasted_iota(jnp.int32, (LANES, LANES), 1)
    gathered = jnp.zeros((LANES, LANES), jnp.float32)
    for r in range(sheets):
        piece = temp_ref[per * r : per * r + per].reshape(LANES, LANES)
        if r:
            piece = pltpu.roll(piece, r, 1)
        gathered = jnp.where(lanes == r, piece, gathered)
    plane = gathered.T[:sheets]
    for half in range(site_ref.shape[0] // 8):
        rows = pl.ds(half * 8, 8)
        site = site_ref[rows, :]
        lane = site & (LANES - 1)
        sheet = site >> 7
        warmth = jnp.zeros(site.shape, jnp.float32)
        for r in range(sheets):
            line = jnp.broadcast_to(plane[r : r + 1, :], site.shape)
            picked = jnp.take_along_axis(line, lane, axis=1)
            warmth = jnp.where(sheet == r, picked, warmth)
        square = warmth * warmth
        emitted = (1.0 - mirror_ref[rows, :]) * (square * square)
        emitted_ref[rows, :] = emitted
        for d in range(copies_ref.shape[0]):
            copies_ref[d, rows, :] = emitted


def emit(temp, site, mirror, count):
    shape = mirror.shape
    nx, ny, _ = temp.shape
    patch = pl.BlockSpec(shape, lambda i: (0, 0))
    return pl.pallas_call(
        emit_kernel,
        grid=(1,),
        out_shape=(
            jax.ShapeDtypeStruct(shape, jnp.float32),
            jax.ShapeDtypeStruct((count,) + shape, jnp.float32),
        ),
        in_specs=[pl.BlockSpec((nx, ny, LANES), lambda i: (0, 0, 0)), patch, patch],
        out_specs=(patch, pl.BlockSpec((count,) + shape, lambda i: (0, 0, 0))),
        compiler_params=params(64),
        cost_estimate=cost(10_000, 900_000),
        name="emit",
    )(temp, site, mirror)


def tiles_kernel(
    live_ref, pairs_ref, lanes_ref, whole_ref, tiles_ref, out_ref, held, terms, sems
):
    slots = held.shape[0]
    live = live_ref[0]
    chunks = (live + CHUNK - 1) // CHUNK

    def chunk_copy(c):
        span = pl.ds(c * CHUNK, CHUNK)
        return pltpu.make_async_copy(tiles_ref.at[span], held.at[span], sems.at[c])

    @pl.loop(0, chunks)
    def _(c):
        chunk_copy(c).start()

    top = lax.broadcasted_iota(jnp.int32, (8, BLK), 0) == 0

    def split_row(block):
        row = jnp.broadcast_to(whole_ref[pl.ds(block, 1), :], (8, BLK))
        high = row.astype(jnp.bfloat16).astype(jnp.float32)
        return jnp.where(top, high, row - high)

    def vectors(a, b):
        stacked = jnp.concatenate([split_row(a), split_row(b)], axis=0)
        stacked = stacked.astype(jnp.bfloat16)
        return jnp.concatenate([stacked, stacked], axis=1)

    @pl.loop(0, chunks)
    def _(c):
        chunk_copy(c).wait()
        stores = Lagging(4 * CHUNK)
        for u in range(0, CHUNK, 2):
            t = c * CHUNK + u
            high_a, low_a = parts_of(held[t], 2)
            high_b, low_b = parts_of(held[t + 1], 2)
            both = jnp.concatenate(
                [
                    jnp.concatenate([high_a, high_b], axis=1),
                    jnp.concatenate([low_a, low_b], axis=1),
                ],
                axis=0,
            )
            second = lax.dot_general(
                vectors(pairs_ref[0, t], pairs_ref[0, t + 1]),
                both,
                NN,
                preferred_element_type=jnp.float32,
            )
            turned = jnp.concatenate(
                [
                    jnp.concatenate([high_a, low_a], axis=1),
                    jnp.concatenate([high_b, low_b], axis=1),
                ],
                axis=0,
            )
            first = lax.dot_general(
                vectors(pairs_ref[1, t], pairs_ref[1, t + 1]),
                turned,
                NT,
                preferred_element_type=jnp.float32,
            )
            for side, result in ((0, first), (1, second)):
                for v, (top_row, cols) in enumerate(((0, slice(0, BLK)), (8, slice(BLK, 2 * BLK)))):
                    row = result[top_row : top_row + 1, cols] + result[top_row + 1 : top_row + 2, cols]
                    stores.add(put(terms, (side, pl.ds(t + v, 1)), row))
        stores.finish()

    used = lax.broadcasted_iota(jnp.int32, (slots, BLK), 0) < live
    used_lane = lax.broadcasted_iota(jnp.int32, (1, slots), 1) < live
    blocks = out_ref.shape[0]
    group = min(blocks, 512)
    split = []
    for side in range(2):
        masked = jnp.where(used, terms[side], 0.0)
        split.append(jnp.concatenate(parts_of(masked, 2), axis=1))
    for base in range(0, blocks, group):
        rows = lax.broadcasted_iota(jnp.int32, (group, slots), 0) + base
        total = jnp.zeros((group, 2 * BLK), jnp.float32)
        for side in range(2):
            target = jnp.where(used_lane, lanes_ref[side : side + 1, :], -1)
            choose = jnp.where(rows == target, 1.0, 0.0).astype(jnp.bfloat16)
            total = total + jnp.dot(choose, split[side], preferred_element_type=jnp.float32)
        out_ref[base : base + group, :] = total[:, :BLK] + total[:, BLK:]


def tile_terms(whole, couples, live, tiles):
    slots = tiles.shape[0]
    smem = pl.BlockSpec(memory_space=pltpu.SMEM)
    vmem = pl.BlockSpec(memory_space=pltpu.VMEM)
    return pl.pallas_call(
        tiles_kernel,
        out_shape=jax.ShapeDtypeStruct(whole.shape, jnp.float32),
        in_specs=[smem, smem, vmem, vmem, pl.BlockSpec(memory_space=pl.ANY)],
        out_specs=vmem,
        scratch_shapes=[
            pltpu.VMEM(tiles.shape, jnp.float32),
            pltpu.VMEM((2, slots, BLK), jnp.float32),
            pltpu.SemaphoreType.DMA((slots // CHUNK,)),
        ],
        compiler_params=params(64),
        cost_estimate=cost(slots * BLK * BLK * 32, slots * BLK * BLK * 4),
        name="tiles",
    )(live, couples, couples, whole, tiles)


def sum_parts(parts_ref, rows):
    total = parts_ref[0, rows, :]
    for d in range(1, parts_ref.shape[0]):
        total = total + parts_ref[d, rows, :]
    return total


def middle_kernel(parts_ref, emitted_ref, mirror_ref, copies_ref):
    for half in range(emitted_ref.shape[0] // 8):
        rows = pl.ds(half * 8, 8)
        incident = sum_parts(parts_ref, rows)
        radiosity = emitted_ref[rows, :] + mirror_ref[rows, :] * incident
        for d in range(copies_ref.shape[0]):
            copies_ref[d, rows, :] = radiosity


def middle(parts, emitted, mirror):
    return pl.pallas_call(
        middle_kernel,
        out_shape=jax.ShapeDtypeStruct(parts.shape, jnp.float32),
        compiler_params=params(64),
        cost_estimate=cost(100_000, 600_000),
        name="middle",
    )(parts, emitted, mirror)


def last_kernel(scale, parts_ref, emitted_ref, mirror_ref, site_ref, rad_ref, source_ref):
    blocks = emitted_ref.shape[0]
    incident = sum_parts(parts_ref, slice(None))
    emitted = emitted_ref[...]
    mirror = mirror_ref[...]
    rad_ref[...] = emitted + mirror * incident
    absorbed = ((1.0 - mirror) * incident - emitted) * scale
    site = site_ref[...]
    lane = site & (LANES - 1)
    sheet = site >> 7
    sheets = source_ref.shape[1]
    sheet_iota = lax.broadcasted_iota(jnp.int32, (sheets, BLK), 0)
    lane_iota = lax.broadcasted_iota(jnp.int32, (LANES, BLK), 0)
    left = []
    right = []
    for b in range(blocks):
        here = jnp.where(sheet_iota == sheet[b : b + 1, :], absorbed[b : b + 1, :], 0.0)
        left.append(here)
        pick = jnp.where(lane_iota == lane[b : b + 1, :], 1.0, 0.0)
        right.append(pick.astype(jnp.bfloat16))
    left = jnp.concatenate(left, axis=1)
    right = jnp.concatenate(right, axis=1)
    source = jnp.zeros((sheets, LANES), jnp.float32)
    for part in parts_of(left, 3):
        source = source + lax.dot_general(part, right, NT, preferred_element_type=jnp.float32)
    for d in range(source_ref.shape[0]):
        source_ref[d] = source


def last(parts, emitted, mirror, site, cells, count):
    weight = cells / (mirror.shape[0] * BLK * 1.0)
    return pl.pallas_call(
        functools.partial(last_kernel, step_size * weight),
        out_shape=(
            jax.ShapeDtypeStruct(mirror.shape, jnp.float32),
            jax.ShapeDtypeStruct((count, cells // LANES, LANES), jnp.float32),
        ),
        compiler_params=params(64),
        cost_estimate=cost(10_000_000, 600_000),
        name="last",
    )(parts, emitted, mirror, site)


def pack_y_kernel(t0, k0, t7, k7, down_ref, up_ref):
    upper = lax.broadcasted_iota(jnp.int32, down_ref.shape[1:], 0) < ROWS
    for x in range(down_ref.shape[0]):
        down_ref[x] = jnp.where(upper, t0[x], pltpu.roll(k0[x], ROWS, 0))
        up_ref[x] = jnp.where(upper, pltpu.roll(t7[x], ROWS, 0), k7[x])


def pack_y(temp, cond):
    nx, ny, nz = temp.shape
    first = pl.BlockSpec((nx, 8, nz), lambda i: (0, 0, 0))
    final = pl.BlockSpec((nx, 8, nz), lambda i: (0, ny // 8 - 1, 0))
    shape = jax.ShapeDtypeStruct((nx, 8, nz), jnp.float32)
    return pl.pallas_call(
        pack_y_kernel,
        grid=(1,),
        out_shape=(shape, shape),
        in_specs=[first, first, final, final],
        out_specs=(first, first),
        compiler_params=params(64),
        cost_estimate=cost(0, 4 * nx * 8 * nz * 4),
        name="pack_y",
    )(temp, cond, temp, cond)


def pack_x_kernel(first, final, below0, above0, below1, above1, low_ref, high_ref):
    ny, nz = first.shape[1:]
    upper = lax.broadcasted_iota(jnp.int32, (8, nz), 0) < ROWS
    for send, temp, below, above in (
        (low_ref, first, below0, above0),
        (high_ref, final, below1, above1),
    ):
        for p in range(HALO):
            send[p, :ny] = temp[p]
            send[p, ny : ny + 8] = jnp.where(upper, above[p], pltpu.roll(below[p], ROWS, 0))
            send[p, ny + 8 :] = jnp.where(upper, pltpu.roll(above[p], ROWS, 0), below[p])


def pack_x(temp, below, above):
    nx, ny, nz = temp.shape

    def ends(rows):
        return (
            pl.BlockSpec((HALO, rows, nz), lambda i: (0, 0, 0)),
            pl.BlockSpec((HALO, rows, nz), lambda i: (nx // HALO - 1, 0, 0)),
        )

    first, final = ends(ny)
    first_rows, final_rows = ends(8)
    whole = pl.BlockSpec((HALO, ny + 16, nz), lambda i: (0, 0, 0))
    shape = jax.ShapeDtypeStruct((HALO, ny + 16, nz), jnp.float32)
    return pl.pallas_call(
        pack_x_kernel,
        grid=(1,),
        out_shape=(shape, shape),
        in_specs=[first, final, first_rows, first_rows, final_rows, final_rows],
        out_specs=(whole, whole),
        compiler_params=params(64),
        cost_estimate=cost(0, 4 * HALO * (ny + 16) * nz * 4),
        name="pack_x",
    )(temp, temp, below, above, below, above)


def coupling(a, b):
    return jnp.where(jnp.minimum(a, b) > 0.0, (0.5 * step_size) * (a + b), 0.0)


def neighbours():
    slab, pair = lax.axis_index("slab"), lax.axis_index("pair")
    return slab > 0, slab < lax.axis_size("slab") - 1, pair > 0, pair < lax.axis_size("pair") - 1


def lane_tiles(nz):
    return [slice(j * LANES, (j + 1) * LANES) for j in range(nz // LANES)]


def one_step(field, cond, gz, begin, end, target):
    wide, nz = field.shape[1:]
    tiles = wide // 8
    spans = lane_tiles(nz)
    count = len(spans)
    lane = lax.broadcasted_iota(jnp.int32, (8, LANES), 1)
    sub = lax.broadcasted_iota(jnp.int32, (8, LANES), 0)
    _, _, has_below, has_above = neighbours()
    keep_above = (sub < 7) | has_above
    keep_below = (sub < 7) | has_below

    def row_tile(ref, x, t):
        return [ref[x, 8 * t : 8 * t + 8, z] for z in spans]

    def first_rolled(ref, x):
        return [pltpu.roll(v, 7, 0) for v in row_tile(ref, x, 0)]

    def y_flux(t_now, k_now, t_next, k_next):
        return [
            (k_now[j] + k_next[j]) * (t_next[j] - t_now[j]) for j in range(count)
        ]

    def z_change(x, t, t_now, k_now):
        turned = [pltpu.roll(v, LANES - 1, 1) for v in t_now]
        flux = []
        for j, z in enumerate(spans):
            deep = turned[j + 1] if j + 1 < count else 0.0
            deep = jnp.where(lane < LANES - 1, turned[j], deep)
            flux.append(gz[x, 8 * t : 8 * t + 8, z] * (deep - t_now[j]))
        back = [pltpu.roll(f, 1, 1) for f in flux]
        out = []
        for j in range(count):
            low = back[j - 1] if j else (k_now[0] + k_now[0]) * t_now[0]
            out.append(flux[j] - jnp.where(lane > 0, back[j], low))
        return out

    @pl.loop(begin, end)
    def _(x):
        stores = Lagging(LAG)
        final = y_flux(
            row_tile(field, x, tiles - 1),
            row_tile(cond, x, tiles - 1),
            first_rolled(field, x),
            first_rolled(cond, x),
        )
        low_y = [pltpu.roll(f, 1, 0) for f in final]
        t_now, k_now = row_tile(field, x, 0), row_tile(cond, x, 0)
        for t in range(tiles):
            rows = slice(8 * t, 8 * t + 8)
            if t + 1 < tiles:
                t_next, k_next = row_tile(field, x, t + 1), row_tile(cond, x, t + 1)
            else:
                t_next, k_next = first_rolled(field, x), first_rolled(cond, x)
            high_y = y_flux(t_now, k_now, t_next, k_next)
            change_z = z_change(x, t, t_now, k_now)
            for j, z in enumerate(spans):
                now, here = t_now[j], k_now[j]
                high_x = (here + cond[x + 1, rows, z]) * (field[x + 1, rows, z] - now)
                low_x = (here + cond[x - 1, rows, z]) * (now - field[x - 1, rows, z])
                new = now + (high_x - low_x) + (high_y[j] - low_y[j]) + change_z[j]
                if t:
                    new = jnp.where(keep_above if t <= ROWS else keep_below, new, 0.0)
                stores.add(put(*target(x, t, z), new))
            low_y, t_now, k_now = high_y, t_next, k_next
        stores.finish()


def thin_planes(cond, ny, thin_ref):
    tall, _, wide, _ = cond.shape
    lane = lax.broadcasted_iota(jnp.int32, (wide, LANES), 1)
    y_lane = lax.broadcasted_iota(jnp.int32, (8, LANES), 1)
    for base in range(0, tall, 16):
        planes = min(16, tall - base)
        gathered = jnp.zeros((wide, LANES), jnp.float32)
        for g in range(planes):
            piece = cond[base + g, 0]
            if g:
                piece = pltpu.roll(piece, 8 * g, 1)
            gathered = jnp.where((lane >> 3) == g, piece, gathered)
        turned = jnp.concatenate(
            [gathered, jnp.zeros((LANES - wide, LANES), jnp.float32)], axis=0
        ).T
        for g in range(planes):
            rows = turned[8 * g : 8 * g + 8, :]
            moved = pltpu.roll(rows, LANES - wide, 1)
            thin_ref[base + g] = jnp.where(
                y_lane < ny + ROWS, rows, jnp.where(y_lane >= LANES - ROWS, moved, 0.0)
            )


def heat_kernel(
    t_ref, k_ref, k_low, k_high, t_low, t_high, below_ref, above_ref, out_ref, thin_ref,
    loaded, field, between, faces, gz, placed, sems,
):
    nx, ny, nz = t_ref.shape
    tall, wide = nx + 2 * HALO, ny + 2 * ROWS
    tiles = wide // 8
    raw_t, raw_k = loaded.at[0], loaded.at[1]
    spans = lane_tiles(nz)
    ends = (0, HALO + nx)

    def fetch(which, k, ref, source_row, planes, at, row, rows):
        return [
            pltpu.make_async_copy(
                ref.at[:, pl.ds(source_row, rows), pl.ds(z.start, LANES)],
                loaded.at[which, pl.ds(at, planes), j, pl.ds(row, rows)],
                sems.at[which, k, j],
            )
            for j, z in enumerate(spans)
        ]

    k_copies = fetch(1, 0, k_ref, 0, nx, HALO, 0, ny)
    t_copies = fetch(0, 0, t_ref, 0, nx, HALO, 0, ny)
    for k, (at, k_side, t_side) in enumerate(zip(ends, (k_low, k_high), (t_low, t_high))):
        k_copies += fetch(1, 1 + k, k_side, 0, HALO, at, 0, ny)
        k_copies += fetch(1, 3 + k, t_side, ny + 8, HALO, at, ny, 8)
        t_copies += fetch(0, 1 + k, t_side, 0, HALO, at, 0, ny + 8)
    for copy in k_copies + t_copies:
        copy.start()
    has_low, has_high, has_below, has_above = neighbours()
    upper = lax.broadcasted_iota(jnp.int32, (8, LANES), 0) < ROWS

    @pl.loop(0, nx)
    def _(x):
        for j, z in enumerate(spans):
            down, up = above_ref[x, :, z], below_ref[x, :, z]
            raw_t[HALO + x, j, ny:] = jnp.where(upper, down, pltpu.roll(up, ROWS, 0))
            raw_k[HALO + x, j, ny:] = jnp.where(upper, pltpu.roll(down, ROWS, 0), up)

    for copy in k_copies:
        copy.wait()

    thin_planes(raw_k, ny, thin_ref)

    @pl.when(jnp.logical_not(has_above & has_below))
    def _():
        missing = (upper & jnp.logical_not(has_above)) | (
            jnp.logical_not(upper) & jnp.logical_not(has_below)
        )

        @pl.loop(0, tall)
        def _(x):
            for j in range(len(spans)):
                edge = raw_k[x, j, ny:]
                last = jnp.broadcast_to(raw_k[x, j, ny - 1 : ny, :], edge.shape)
                first = jnp.broadcast_to(raw_k[x, j, 0:1, :], edge.shape)
                raw_k[x, j, ny:] = jnp.where(missing, jnp.where(upper, last, first), edge)

    @pl.when(jnp.logical_not(has_low))
    def _():
        raw_k[HALO - 1] = raw_k[HALO]

    @pl.when(jnp.logical_not(has_high))
    def _():
        raw_k[HALO + nx] = raw_k[HALO + nx - 1]

    lane = lax.broadcasted_iota(jnp.int32, (8, LANES), 1)

    @pl.loop(0, tall)
    def _(x):
        stores = Lagging(LAG)
        for t in range(tiles):
            rows = pl.ds(t, 8, stride=tiles)
            kept = slice(8 * t, 8 * t + 8)
            here = [(0.5 * step_size) * loaded[1, x, j, rows, :] for j in range(len(spans))]
            turned = [pltpu.roll(v, LANES - 1, 1) for v in here]
            for j, z in enumerate(spans):
                deep = turned[j + 1] if j + 1 < len(spans) else here[j]
                deep = jnp.where(lane < LANES - 1, turned[j], deep)
                stores.add(put(faces, (x, kept, z), here[j]))
                stores.add(put(gz, (x, kept, z), here[j] + deep))
        stores.finish()

    for copy in t_copies:
        copy.wait()

    @pl.loop(0, tall)
    def _(x):
        stores = Lagging(LAG)
        for t in range(tiles):
            rows = pl.ds(t, 8, stride=tiles)
            for j, z in enumerate(spans):
                stores.add(put(field, (x, slice(8 * t, 8 * t + 8), z), loaded[0, x, j, rows, :]))
        stores.finish()

    def inside(target):
        return lambda x, t, z: (target, (x, slice(8 * t, 8 * t + 8), z))

    def outside(x, t, z):
        return placed, (x - HALO, z.start // LANES, pl.ds(t, 8, stride=tiles))

    old, new = field, between
    for step in range(1, STEPS):
        one_step(old, faces, gz, step, tall - step, inside(new))
        for x, there in ((HALO - 1, has_low), (HALO + nx, has_high)):

            @pl.when(jnp.logical_not(there))
            def _():
                new[x] = jnp.zeros((wide, nz), jnp.float32)

        old, new = new, old
    one_step(old, faces, gz, HALO, tall - HALO, outside)

    @pl.loop(0, nx)
    def _(x):
        for j, z in enumerate(spans):
            out_ref[x, :, z] = placed[x, j, :ny, :]


def heat(temp, cond, k_low, k_high, t_low, t_high, below, above):
    nx, ny, nz = temp.shape
    tall, wide = nx + 2 * HALO, ny + 2 * ROWS
    hbm = pl.BlockSpec(memory_space=pl.ANY)
    vmem = pl.BlockSpec(memory_space=pltpu.VMEM)
    big = pltpu.VMEM((tall, wide, nz), jnp.float32)
    return pl.pallas_call(
        heat_kernel,
        out_shape=(
            jax.ShapeDtypeStruct(temp.shape, jnp.float32),
            jax.ShapeDtypeStruct((tall, 8, LANES), jnp.float32),
        ),
        in_specs=[hbm] * 6 + [vmem] * 2,
        scratch_shapes=[pltpu.VMEM((2, tall, nz // LANES, wide, LANES), jnp.float32)]
        + [big] * 4
        + [
            pltpu.VMEM((nx, nz // LANES, wide, LANES), jnp.float32),
            pltpu.SemaphoreType.DMA((2, 5, nz // LANES)),
        ],
        compiler_params=params(64),
        cost_estimate=cost(tall * wide * nz * 100, 12 * nx * ny * nz * 4),
        name="heat",
    )(temp, cond, k_low, k_high, t_low, t_high, below, above)


def source_kernel(ny, all_ref, thin_ref, base_ref, out_ref):
    tall = thin_ref.shape[0]
    nx = tall - 2 * HALO
    sheets = all_ref.shape[1]
    sub = lax.broadcasted_iota(jnp.int32, (8, LANES), 0)
    y_lane = lax.broadcasted_iota(jnp.int32, (8, LANES), 1)

    slabs, pairs = lax.axis_size("slab"), lax.axis_size("pair")

    def sheet(down, across):
        slab = lax.axis_index("slab") + down
        pair = lax.axis_index("pair") + across
        inside = (slab >= 0) & (slab < slabs) & (pair >= 0) & (pair < pairs)
        found = all_ref[jnp.where(inside, slab * pairs + pair, 0)]
        return jnp.where(inside, found, 0.0)

    def rows_of(down):
        low, own, high = (sheet(down, across) for across in (-1, 0, 1))
        out = []
        for half in range(2):
            if half == 0:
                own_at, high_at, low_at = own, pltpu.roll(high, ny, 1), pltpu.roll(low, ny, 1)
            else:
                own_at, high_at, low_at = pltpu.roll(own, ny, 1), high, low
            out.append(
                jnp.where(
                    y_lane < ny,
                    own_at,
                    jnp.where(
                        y_lane < ny + HALO,
                        high_at,
                        jnp.where(y_lane >= LANES - HALO, low_at, 0.0),
                    ),
                )
            )
        return out

    lines = [rows_of(down) for down in (-1, 0, 1)]
    source = []
    for x in range(-HALO, nx + HALO):
        which, local = (x + nx) // nx, x % nx
        row = lines[which][local % 2][local // 2 : local // 2 + 1, :]
        source.append(jnp.where(sub == 0, jnp.broadcast_to(row, (8, LANES)), 0.0))

    cond = [thin_ref[x] for x in range(tall)]
    cx, cy, cz, centre = [], [], [], []
    for x in range(tall):
        here = cond[x]
        after = cond[min(x + 1, tall - 1)]
        before = cond[max(x - 1, 0)]
        y_after = pltpu.roll(here, LANES - 1, 1)
        y_before = pltpu.roll(here, 1, 1)
        z_after = jnp.where(sub == 7, 0.0, pltpu.roll(here, 7, 0))
        z_before = jnp.where(sub == 0, 0.0, pltpu.roll(here, 1, 0))
        cx.append(coupling(here, after))
        cy.append(coupling(here, y_after))
        cz.append(coupling(here, z_after))
        total = 6.0 * here
        for near in (after, before, y_after, y_before, z_after, z_before):
            total = total + jnp.where(near > 0.0, near, here)
        centre.append(1.0 - (0.5 * step_size) * total)

    added = source
    for step in range(1, STEPS):
        new = list(added)
        for x in range(step, tall - step):
            here = added[x]
            total = source[x] + centre[x] * here
            total = total + (cx[x] * added[x + 1] + cx[x - 1] * added[x - 1])
            total = total + cy[x] * pltpu.roll(here, LANES - 1, 1)
            total = total + pltpu.roll(cy[x] * here, 1, 1)
            total = total + cz[x] * pltpu.roll(here, 7, 0)
            new[x] = total + pltpu.roll(cz[x] * here, 1, 0)
        added = new

    lane = lax.broadcasted_iota(jnp.int32, (ny, LANES), 1)
    turned = jnp.concatenate(added[HALO : HALO + nx], axis=0).T[:ny]
    for x in range(nx):
        piece = turned if x == 0 else pltpu.roll(turned, LANES - 8 * x, 1)
        out_ref[x] = base_ref[x] + jnp.where(lane < STEPS, piece, 0.0)


def add_source(everything, thin, base):
    nx, ny, nz = base.shape
    block = pl.BlockSpec((nx, ny, LANES), lambda i: (0, 0, 0))
    return pl.pallas_call(
        functools.partial(source_kernel, ny),
        grid=(1,),
        out_shape=jax.ShapeDtypeStruct(base.shape, jnp.float32),
        in_specs=[
            pl.BlockSpec(everything.shape, lambda i: (0, 0, 0)),
            pl.BlockSpec(thin.shape, lambda i: (0, 0, 0)),
            block,
        ],
        out_specs=block,
        input_output_aliases={2: 0},
        compiler_params=params(64),
        cost_estimate=cost(1_000_000, 2 * nx * ny * LANES * 4),
        name="add_source",
    )(everything, thin, base)


def exchange(rows):
    return lax.all_to_all(rows, ("slab", "pair"), split_axis=0, concat_axis=0, tiled=True)


def together(*arrays):
    return lax.optimization_barrier(arrays)


def both_ways(low, high, axis):
    count = lax.axis_size(axis)
    forward = [(i, i + 1) for i in range(count - 1)]
    backward = [(target, source) for source, target in forward]
    from_low = lax.ppermute(high, axis, forward)
    from_high = lax.ppermute(low, axis, backward)
    return from_low, from_high


def shards(
    initial_warmth,
    heat_passing_coefficient,
    mirror_fraction,
    element_facing_site,
    tile_block_couples,
    active_slot_count,
    view_factor_blocks,
):
    nx, ny, _ = initial_warmth.shape
    slabs, pairs = lax.axis_size("slab"), lax.axis_size("pair")
    count = slabs * pairs
    blocks = mirror_fraction.shape[0]
    couples = tile_block_couples.T

    temp, cond = initial_warmth, heat_passing_coefficient
    emitted, copies = emit(temp, element_facing_site, mirror_fraction, count)
    temp, copies = together(temp, copies)

    def sweep_terms(whole):
        whole = whole.reshape(count * blocks, BLK)
        term = tile_terms(whole, couples, active_slot_count, view_factor_blocks)
        return term.reshape(count, blocks, BLK)

    whole = exchange(copies)
    cond, copies = together(cond, copies)
    send_low, send_high = cond[:HALO], cond[nx - HALO :]
    k_low, k_high = both_ways(send_low, send_high, "slab")
    whole = together(whole, send_low, send_high)[0]
    temp, cond, term = together(temp, cond, sweep_terms(whole))
    parts = exchange(term)
    below, above = both_ways(*pack_y(temp, cond), "pair")
    parts, below, above, k_low, k_high = together(parts, below, above, k_low, k_high)
    copies, below, above = together(middle(parts, emitted, mirror_fraction), below, above)
    whole = exchange(copies)
    send_low, send_high = pack_x(temp, below, above)
    t_low, t_high = both_ways(send_low, send_high, "slab")
    whole = together(whole, send_low, send_high)[0]
    parts = exchange(sweep_terms(whole))
    parts, t_low, t_high = together(parts, t_low, t_high)
    radiosity, source = last(parts, emitted, mirror_fraction, element_facing_site, nx * ny, count)
    everything = exchange(source)
    below, source = together(below, source)
    base, thin = heat(temp, cond, k_low, k_high, t_low, t_high, below, above)

    warmed_liner = add_source(everything, thin, base)
    return (radiosity, warmed_liner)


def solution(mesh):
    return jax.shard_map(
        shards,
        mesh=mesh,
        in_specs=(
            P("slab", "pair", None),
            P("slab", "pair", None),
            P(("slab", "pair"), None),
            P(("slab", "pair"), None),
            P(("slab", "pair"), None),
            P(("slab", "pair")),
            P(("slab", "pair"), None, None),
        ),
        out_specs=(P(("slab", "pair"), None), P("slab", "pair", None)),
        check_vma=False,
    )
```

```python
import functools

import jax
import jax.numpy as jnp
from jax import lax
from jax.experimental import pallas as pl
from jax.experimental.pallas import tpu as pltpu
from jax.sharding import PartitionSpec as P

BLK = 128
SWEEPS = 2
STEPS = 4
HALO = STEPS
ROWS = STEPS
LANES = 128
CHUNK = 16
LAG = 8

step_size = 0.07

NT = (((1,), (1,)), ((), ()))
NN = (((1,), (0,)), ((), ()))


def params(mib):
    return pltpu.CompilerParams(vmem_limit_bytes=mib * 1024 * 1024)


def cost(flops, nbytes):
    return pl.CostEstimate(flops=flops, bytes_accessed=nbytes, transcendentals=0)


def parts_of(x, count):
    out = []
    for _ in range(count - 1):
        part = x.astype(jnp.bfloat16)
        out.append(part)
        x = x - part.astype(jnp.float32)
    out.append(x.astype(jnp.bfloat16))
    return out


class Lagging:
    def __init__(self, depth):
        self.depth = depth
        self.waiting = []

    def add(self, store):
        self.waiting.append(store)
        if len(self.waiting) > self.depth:
            self.waiting.pop(0)()

    def finish(self):
        for store in self.waiting:
            store()
        self.waiting = []


def put(ref, index, value):
    return lambda: ref.__setitem__(index, value)


def emit_kernel(temp_ref, site_ref, mirror_ref, emitted_ref, copies_ref):
    nx, ny, _ = temp_ref.shape
    sheets = nx * ny // LANES
    per = LANES // ny
    lanes = lax.broadcasted_iota(jnp.int32, (LANES, LANES), 1)
    gathered = jnp.zeros((LANES, LANES), jnp.float32)
    for r in range(sheets):
        piece = temp_ref[per * r : per * r + per].reshape(LANES, LANES)
        if r:
            piece = pltpu.roll(piece, r, 1)
        gathered = jnp.where(lanes == r, piece, gathered)
    plane = gathered.T[:sheets]
    for half in range(site_ref.shape[0] // 8):
        rows = pl.ds(half * 8, 8)
        site = site_ref[rows, :]
        lane = site & (LANES - 1)
        sheet = site >> 7
        warmth = jnp.zeros(site.shape, jnp.float32)
        for r in range(sheets):
            line = jnp.broadcast_to(plane[r : r + 1, :], site.shape)
            picked = jnp.take_along_axis(line, lane, axis=1)
            warmth = jnp.where(sheet == r, picked, warmth)
        square = warmth * warmth
        emitted = (1.0 - mirror_ref[rows, :]) * (square * square)
        emitted_ref[rows, :] = emitted
        for d in range(copies_ref.shape[0]):
            copies_ref[d, rows, :] = emitted


def emit(temp, site, mirror, count):
    shape = mirror.shape
    nx, ny, _ = temp.shape
    patch = pl.BlockSpec(shape, lambda i: (0, 0))
    return pl.pallas_call(
        emit_kernel,
        grid=(1,),
        out_shape=(
            jax.ShapeDtypeStruct(shape, jnp.float32),
            jax.ShapeDtypeStruct((count,) + shape, jnp.float32),
        ),
        in_specs=[pl.BlockSpec((nx, ny, LANES), lambda i: (0, 0, 0)), patch, patch],
        out_specs=(patch, pl.BlockSpec((count,) + shape, lambda i: (0, 0, 0))),
        compiler_params=params(64),
        cost_estimate=cost(10_000, 900_000),
        name="emit",
    )(temp, site, mirror)


def tiles_kernel(
    live_ref, pairs_ref, lanes_ref, whole_ref, tiles_ref, out_ref, held, terms, sems
):
    slots = held.shape[0]
    live = live_ref[0]
    chunks = (live + CHUNK - 1) // CHUNK

    def chunk_copy(c):
        span = pl.ds(c * CHUNK, CHUNK)
        return pltpu.make_async_copy(tiles_ref.at[span], held.at[span], sems.at[c])

    @pl.loop(0, chunks)
    def _(c):
        chunk_copy(c).start()

    top = lax.broadcasted_iota(jnp.int32, (8, BLK), 0) == 0

    def split_row(block):
        row = jnp.broadcast_to(whole_ref[pl.ds(block, 1), :], (8, BLK))
        high = row.astype(jnp.bfloat16).astype(jnp.float32)
        return jnp.where(top, high, row - high)

    def vectors(a, b):
        stacked = jnp.concatenate([split_row(a), split_row(b)], axis=0)
        stacked = stacked.astype(jnp.bfloat16)
        return jnp.concatenate([stacked, stacked], axis=1)

    @pl.loop(0, chunks)
    def _(c):
        chunk_copy(c).wait()
        stores = Lagging(4 * CHUNK)
        for u in range(0, CHUNK, 2):
            t = c * CHUNK + u
            high_a, low_a = parts_of(held[t], 2)
            high_b, low_b = parts_of(held[t + 1], 2)
            both = jnp.concatenate(
                [
                    jnp.concatenate([high_a, high_b], axis=1),
                    jnp.concatenate([low_a, low_b], axis=1),
                ],
                axis=0,
            )
            second = lax.dot_general(
                vectors(pairs_ref[0, t], pairs_ref[0, t + 1]),
                both,
                NN,
                preferred_element_type=jnp.float32,
            )
            turned = jnp.concatenate(
                [
                    jnp.concatenate([high_a, low_a], axis=1),
                    jnp.concatenate([high_b, low_b], axis=1),
                ],
                axis=0,
            )
            first = lax.dot_general(
                vectors(pairs_ref[1, t], pairs_ref[1, t + 1]),
                turned,
                NT,
                preferred_element_type=jnp.float32,
            )
            for side, result in ((0, first), (1, second)):
                for v, (top_row, cols) in enumerate(((0, slice(0, BLK)), (8, slice(BLK, 2 * BLK)))):
                    row = result[top_row : top_row + 1, cols] + result[top_row + 1 : top_row + 2, cols]
                    stores.add(put(terms, (side, pl.ds(t + v, 1)), row))
        stores.finish()

    used = lax.broadcasted_iota(jnp.int32, (slots, BLK), 0) < live
    used_lane = lax.broadcasted_iota(jnp.int32, (1, slots), 1) < live
    blocks = out_ref.shape[0]
    group = min(blocks, 512)
    split = []
    for side in range(2):
        masked = jnp.where(used, terms[side], 0.0)
        split.append(jnp.concatenate(parts_of(masked, 2), axis=1))
    for base in range(0, blocks, group):
        rows = lax.broadcasted_iota(jnp.int32, (group, slots), 0) + base
        total = jnp.zeros((group, 2 * BLK), jnp.float32)
        for side in range(2):
            target = jnp.where(used_lane, lanes_ref[side : side + 1, :], -1)
            choose = jnp.where(rows == target, 1.0, 0.0).astype(jnp.bfloat16)
            total = total + jnp.dot(choose, split[side], preferred_element_type=jnp.float32)
        out_ref[base : base + group, :] = total[:, :BLK] + total[:, BLK:]


def tile_terms(whole, couples, live, tiles):
    slots = tiles.shape[0]
    smem = pl.BlockSpec(memory_space=pltpu.SMEM)
    vmem = pl.BlockSpec(memory_space=pltpu.VMEM)
    return pl.pallas_call(
        tiles_kernel,
        out_shape=jax.ShapeDtypeStruct(whole.shape, jnp.float32),
        in_specs=[smem, smem, vmem, vmem, pl.BlockSpec(memory_space=pl.ANY)],
        out_specs=vmem,
        scratch_shapes=[
            pltpu.VMEM(tiles.shape, jnp.float32),
            pltpu.VMEM((2, slots, BLK), jnp.float32),
            pltpu.SemaphoreType.DMA((slots // CHUNK,)),
        ],
        compiler_params=params(64),
        cost_estimate=cost(slots * BLK * BLK * 32, slots * BLK * BLK * 4),
        name="tiles",
    )(live, couples, couples, whole, tiles)


def sum_parts(parts_ref, rows):
    total = parts_ref[0, rows, :]
    for d in range(1, parts_ref.shape[0]):
        total = total + parts_ref[d, rows, :]
    return total


def middle_kernel(parts_ref, emitted_ref, mirror_ref, copies_ref):
    for half in range(emitted_ref.shape[0] // 8):
        rows = pl.ds(half * 8, 8)
        incident = sum_parts(parts_ref, rows)
        radiosity = emitted_ref[rows, :] + mirror_ref[rows, :] * incident
        for d in range(copies_ref.shape[0]):
            copies_ref[d, rows, :] = radiosity


def middle(parts, emitted, mirror):
    return pl.pallas_call(
        middle_kernel,
        out_shape=jax.ShapeDtypeStruct(parts.shape, jnp.float32),
        compiler_params=params(64),
        cost_estimate=cost(100_000, 600_000),
        name="middle",
    )(parts, emitted, mirror)


def last_kernel(scale, parts_ref, emitted_ref, mirror_ref, site_ref, rad_ref, source_ref):
    blocks = emitted_ref.shape[0]
    incident = sum_parts(parts_ref, slice(None))
    emitted = emitted_ref[...]
    mirror = mirror_ref[...]
    rad_ref[...] = emitted + mirror * incident
    absorbed = ((1.0 - mirror) * incident - emitted) * scale
    site = site_ref[...]
    lane = site & (LANES - 1)
    sheet = site >> 7
    sheets = source_ref.shape[1]
    sheet_iota = lax.broadcasted_iota(jnp.int32, (sheets, BLK), 0)
    lane_iota = lax.broadcasted_iota(jnp.int32, (LANES, BLK), 0)
    left = []
    right = []
    for b in range(blocks):
        here = jnp.where(sheet_iota == sheet[b : b + 1, :], absorbed[b : b + 1, :], 0.0)
        left.append(here)
        pick = jnp.where(lane_iota == lane[b : b + 1, :], 1.0, 0.0)
        right.append(pick.astype(jnp.bfloat16))
    left = jnp.concatenate(left, axis=1)
    right = jnp.concatenate(right, axis=1)
    source = jnp.zeros((sheets, LANES), jnp.float32)
    for part in parts_of(left, 3):
        source = source + lax.dot_general(part, right, NT, preferred_element_type=jnp.float32)
    for d in range(source_ref.shape[0]):
        source_ref[d] = source


def last(parts, emitted, mirror, site, cells, count):
    weight = cells / (mirror.shape[0] * BLK * 1.0)
    return pl.pallas_call(
        functools.partial(last_kernel, step_size * weight),
        out_shape=(
            jax.ShapeDtypeStruct(mirror.shape, jnp.float32),
            jax.ShapeDtypeStruct((count, cells // LANES, LANES), jnp.float32),
        ),
        compiler_params=params(64),
        cost_estimate=cost(10_000_000, 600_000),
        name="last",
    )(parts, emitted, mirror, site)


def pack_y_kernel(t0, k0, t7, k7, down_ref, up_ref):
    upper = lax.broadcasted_iota(jnp.int32, down_ref.shape[1:], 0) < ROWS
    for x in range(down_ref.shape[0]):
        down_ref[x] = jnp.where(upper, t0[x], pltpu.roll(k0[x], ROWS, 0))
        up_ref[x] = jnp.where(upper, pltpu.roll(t7[x], ROWS, 0), k7[x])


def pack_y(temp, cond):
    nx, ny, nz = temp.shape
    first = pl.BlockSpec((nx, 8, nz), lambda i: (0, 0, 0))
    final = pl.BlockSpec((nx, 8, nz), lambda i: (0, ny // 8 - 1, 0))
    shape = jax.ShapeDtypeStruct((nx, 8, nz), jnp.float32)
    return pl.pallas_call(
        pack_y_kernel,
        grid=(1,),
        out_shape=(shape, shape),
        in_specs=[first, first, final, final],
        out_specs=(first, first),
        compiler_params=params(64),
        cost_estimate=cost(0, 4 * nx * 8 * nz * 4),
        name="pack_y",
    )(temp, cond, temp, cond)


def pack_x_kernel(first, final, below0, above0, below1, above1, low_ref, high_ref):
    ny, nz = first.shape[1:]
    upper = lax.broadcasted_iota(jnp.int32, (8, nz), 0) < ROWS
    for send, temp, below, above in (
        (low_ref, first, below0, above0),
        (high_ref, final, below1, above1),
    ):
        for p in range(HALO):
            send[p, :ny] = temp[p]
            send[p, ny : ny + 8] = jnp.where(upper, above[p], pltpu.roll(below[p], ROWS, 0))
            send[p, ny + 8 :] = jnp.where(upper, pltpu.roll(above[p], ROWS, 0), below[p])


def pack_x(temp, below, above):
    nx, ny, nz = temp.shape

    def ends(rows):
        return (
            pl.BlockSpec((HALO, rows, nz), lambda i: (0, 0, 0)),
            pl.BlockSpec((HALO, rows, nz), lambda i: (nx // HALO - 1, 0, 0)),
        )

    first, final = ends(ny)
    first_rows, final_rows = ends(8)
    whole = pl.BlockSpec((HALO, ny + 16, nz), lambda i: (0, 0, 0))
    shape = jax.ShapeDtypeStruct((HALO, ny + 16, nz), jnp.float32)
    return pl.pallas_call(
        pack_x_kernel,
        grid=(1,),
        out_shape=(shape, shape),
        in_specs=[first, final, first_rows, first_rows, final_rows, final_rows],
        out_specs=(whole, whole),
        compiler_params=params(64),
        cost_estimate=cost(0, 4 * HALO * (ny + 16) * nz * 4),
        name="pack_x",
    )(temp, temp, below, above, below, above)


def coupling(a, b):
    return jnp.where(jnp.minimum(a, b) > 0.0, (0.5 * step_size) * (a + b), 0.0)


def neighbours():
    slab, pair = lax.axis_index("slab"), lax.axis_index("pair")
    return slab > 0, slab < lax.axis_size("slab") - 1, pair > 0, pair < lax.axis_size("pair") - 1


def lane_tiles(nz):
    return [slice(j * LANES, (j + 1) * LANES) for j in range(nz // LANES)]


def one_step(field, cond, gz, begin, end, target):
    wide, nz = field.shape[1:]
    tiles = wide // 8
    spans = lane_tiles(nz)
    count = len(spans)
    lane = lax.broadcasted_iota(jnp.int32, (8, LANES), 1)
    sub = lax.broadcasted_iota(jnp.int32, (8, LANES), 0)
    _, _, has_below, has_above = neighbours()
    keep_above = (sub < 7) | has_above
    keep_below = (sub < 7) | has_below

    def row_tile(ref, x, t):
        return [ref[x, 8 * t : 8 * t + 8, z] for z in spans]

    def first_rolled(ref, x):
        return [pltpu.roll(v, 7, 0) for v in row_tile(ref, x, 0)]

    def y_flux(t_now, k_now, t_next, k_next):
        return [
            (k_now[j] + k_next[j]) * (t_next[j] - t_now[j]) for j in range(count)
        ]

    def z_change(x, t, t_now, k_now):
        turned = [pltpu.roll(v, LANES - 1, 1) for v in t_now]
        flux = []
        for j, z in enumerate(spans):
            deep = turned[j + 1] if j + 1 < count else 0.0
            deep = jnp.where(lane < LANES - 1, turned[j], deep)
            flux.append(gz[x, 8 * t : 8 * t + 8, z] * (deep - t_now[j]))
        back = [pltpu.roll(f, 1, 1) for f in flux]
        out = []
        for j in range(count):
            low = back[j - 1] if j else (k_now[0] + k_now[0]) * t_now[0]
            out.append(flux[j] - jnp.where(lane > 0, back[j], low))
        return out

    @pl.loop(begin, end)
    def _(x):
        stores = Lagging(LAG)
        final = y_flux(
            row_tile(field, x, tiles - 1),
            row_tile(cond, x, tiles - 1),
            first_rolled(field, x),
            first_rolled(cond, x),
        )
        low_y = [pltpu.roll(f, 1, 0) for f in final]
        t_now, k_now = row_tile(field, x, 0), row_tile(cond, x, 0)
        for t in range(tiles):
            rows = slice(8 * t, 8 * t + 8)
            if t + 1 < tiles:
                t_next, k_next = row_tile(field, x, t + 1), row_tile(cond, x, t + 1)
            else:
                t_next, k_next = first_rolled(field, x), first_rolled(cond, x)
            high_y = y_flux(t_now, k_now, t_next, k_next)
            change_z = z_change(x, t, t_now, k_now)
            for j, z in enumerate(spans):
                now, here = t_now[j], k_now[j]
                high_x = (here + cond[x + 1, rows, z]) * (field[x + 1, rows, z] - now)
                low_x = (here + cond[x - 1, rows, z]) * (now - field[x - 1, rows, z])
                new = now + (high_x - low_x) + (high_y[j] - low_y[j]) + change_z[j]
                if t:
                    new = jnp.where(keep_above if t <= ROWS else keep_below, new, 0.0)
                stores.add(put(*target(x, t, z), new))
            low_y, t_now, k_now = high_y, t_next, k_next
        stores.finish()


def thin_planes(cond, ny, store):
    tall, _, wide, _ = cond.shape
    lane = lax.broadcasted_iota(jnp.int32, (wide, LANES), 1)
    y_lane = lax.broadcasted_iota(jnp.int32, (8, LANES), 1)
    for base in range(0, tall, 16):
        planes = min(16, tall - base)
        gathered = jnp.zeros((wide, LANES), jnp.float32)
        for g in range(planes):
            piece = cond[base + g, 0]
            if g:
                piece = pltpu.roll(piece, 8 * g, 1)
            gathered = jnp.where((lane >> 3) == g, piece, gathered)
        turned = jnp.concatenate(
            [gathered, jnp.zeros((LANES - wide, LANES), jnp.float32)], axis=0
        ).T
        for g in range(planes):
            rows = turned[8 * g : 8 * g + 8, :]
            moved = pltpu.roll(rows, LANES - wide, 1)
            store(
                base + g,
                jnp.where(
                    y_lane < ny + ROWS, rows, jnp.where(y_lane >= LANES - ROWS, moved, 0.0)
                ),
            )


def mirror_rows(raw_k, ny):
    _, _, has_below, has_above = neighbours()
    upper = lax.broadcasted_iota(jnp.int32, (8, LANES), 0) < ROWS

    @pl.when(jnp.logical_not(has_above & has_below))
    def _():
        missing = (upper & jnp.logical_not(has_above)) | (
            jnp.logical_not(upper) & jnp.logical_not(has_below)
        )

        @pl.loop(0, raw_k.shape[0])
        def _(x):
            for j in range(raw_k.shape[1]):
                edge = raw_k[x, j, ny:]
                last = jnp.broadcast_to(raw_k[x, j, ny - 1 : ny, :], edge.shape)
                first = jnp.broadcast_to(raw_k[x, j, 0:1, :], edge.shape)
                raw_k[x, j, ny:] = jnp.where(missing, jnp.where(upper, last, first), edge)


def lay_out_k(loaded, place, faces, gz):
    planes, count, wide, _ = loaded.shape[1:]
    tiles = wide // 8
    spans = lane_tiles(count * LANES)
    lane = lax.broadcasted_iota(jnp.int32, (8, LANES), 1)

    @pl.loop(0, planes)
    def _(x):
        stores = Lagging(LAG)
        to = place(x)
        for t in range(tiles):
            rows = pl.ds(t, 8, stride=tiles)
            kept = slice(8 * t, 8 * t + 8)
            here = [(0.5 * step_size) * loaded[1, x, j, rows, :] for j in range(count)]
            turned = [pltpu.roll(v, LANES - 1, 1) for v in here]
            for j, z in enumerate(spans):
                deep = turned[j + 1] if j + 1 < count else here[j]
                deep = jnp.where(lane < LANES - 1, turned[j], deep)
                stores.add(put(faces, (to, kept, z), here[j]))
                stores.add(put(gz, (to, kept, z), here[j] + deep))
        stores.finish()


def lay_out_t(loaded, place, field):
    planes, count, wide, _ = loaded.shape[1:]
    tiles = wide // 8
    spans = lane_tiles(count * LANES)

    @pl.loop(0, planes)
    def _(x):
        stores = Lagging(LAG)
        to = place(x)
        for t in range(tiles):
            rows = pl.ds(t, 8, stride=tiles)
            for j, z in enumerate(spans):
                stores.add(put(field, (to, slice(8 * t, 8 * t + 8), z), loaded[0, x, j, rows, :]))
        stores.finish()


def fetch(loaded, which, ref, source_row, at, row, rows, sems):
    planes, count = ref.shape[0], loaded.shape[2]
    return [
        pltpu.make_async_copy(
            ref.at[:, pl.ds(source_row, rows), pl.ds(j * LANES, LANES)],
            loaded.at[which, pl.ds(at, planes), j, pl.ds(row, rows)],
            sems.at[j],
        )
        for j in range(count)
    ]


def own_planes_kernel(
    t_ref, k_ref, below_ref, above_ref, field, faces, gz, thin_ref, loaded, sems
):
    nx, ny, nz = t_ref.shape
    raw_t, raw_k = loaded.at[0], loaded.at[1]
    k_copies = fetch(loaded, 1, k_ref, 0, 0, 0, ny, sems.at[1])
    t_copies = fetch(loaded, 0, t_ref, 0, 0, 0, ny, sems.at[0])
    for copy in k_copies + t_copies:
        copy.start()
    upper = lax.broadcasted_iota(jnp.int32, (8, LANES), 0) < ROWS

    @pl.loop(0, nx)
    def _(x):
        for j, z in enumerate(lane_tiles(nz)):
            down, up = above_ref[x, :, z], below_ref[x, :, z]
            raw_t[x, j, ny:] = jnp.where(upper, down, pltpu.roll(up, ROWS, 0))
            raw_k[x, j, ny:] = jnp.where(upper, pltpu.roll(down, ROWS, 0), up)

    for copy in k_copies:
        copy.wait()
    thin_planes(raw_k, ny, lambda x, v: thin_ref.__setitem__(x, v))
    mirror_rows(raw_k, ny)
    lay_out_k(loaded, lambda x: x, faces, gz)
    for copy in t_copies:
        copy.wait()
    lay_out_t(loaded, lambda x: x, field)


def own_planes(temp, cond, below, above):
    nx, ny, nz = temp.shape
    wide = ny + 2 * ROWS
    hbm = pl.BlockSpec(memory_space=pl.ANY)
    vmem = pl.BlockSpec(memory_space=pltpu.VMEM)
    shape = jax.ShapeDtypeStruct((nx, wide, nz), jnp.float32)
    return pl.pallas_call(
        own_planes_kernel,
        out_shape=(shape, shape, shape, jax.ShapeDtypeStruct((nx, 8, LANES), jnp.float32)),
        in_specs=[hbm, hbm, vmem, vmem],
        scratch_shapes=[
            pltpu.VMEM((2, nx, nz // LANES, wide, LANES), jnp.float32),
            pltpu.SemaphoreType.DMA((2, nz // LANES)),
        ],
        compiler_params=params(64),
        cost_estimate=cost(nx * wide * nz * 10, 6 * nx * wide * nz * 4),
        name="own_planes",
    )(temp, cond, below, above)


def heat_kernel(
    own_field, own_faces, own_gz, own_thin, k_low, k_high, t_low, t_high, out_ref, thin_ref,
    loaded, field, between, faces, gz, placed, sems, own_sems,
):
    nx, wide, nz = own_field.shape
    ny = wide - 2 * ROWS
    tall = nx + 2 * HALO
    tiles = wide // 8
    spans = lane_tiles(nz)
    k_copies, t_copies = [], []
    for k, (k_side, t_side) in enumerate(((k_low, t_low), (k_high, t_high))):
        at = k * HALO
        k_copies += fetch(loaded, 1, k_side, 0, at, 0, ny, sems.at[3 * k])
        k_copies += fetch(loaded, 1, t_side, ny + 8, at, ny, 8, sems.at[3 * k + 1])
        t_copies += fetch(loaded, 0, t_side, 0, at, 0, ny + 8, sems.at[3 * k + 2])
    own = [
        pltpu.make_async_copy(ref, whole.at[pl.ds(HALO, nx)], own_sems.at[k])
        for k, (ref, whole) in enumerate(
            ((own_faces, faces), (own_gz, gz), (own_field, field))
        )
    ]
    for copy in k_copies + t_copies + own:
        copy.start()
    has_low, has_high, _, _ = neighbours()

    def place(x):
        return jnp.where(x < HALO, x, x + nx)

    def store_thin(x, value):
        thin_ref[x if x < HALO else x + nx] = value

    thin_ref[HALO : HALO + nx] = own_thin[...]
    raw_k = loaded.at[1]
    for copy in k_copies:
        copy.wait()
    thin_planes(raw_k, ny, store_thin)
    mirror_rows(raw_k, ny)
    lay_out_k(loaded, place, faces, gz)
    for copy in t_copies:
        copy.wait()
    lay_out_t(loaded, place, field)
    for copy in own:
        copy.wait()

    @pl.when(jnp.logical_not(has_low))
    def _():
        faces[HALO - 1] = faces[HALO]

    @pl.when(jnp.logical_not(has_high))
    def _():
        faces[HALO + nx] = faces[HALO + nx - 1]

    def inside(target):
        return lambda x, t, z: (target, (x, slice(8 * t, 8 * t + 8), z))

    def outside(x, t, z):
        return placed, (x - HALO, z.start // LANES, pl.ds(t, 8, stride=tiles))

    old, new = field, between
    for step in range(1, STEPS):
        one_step(old, faces, gz, step, tall - step, inside(new))
        for x, there in ((HALO - 1, has_low), (HALO + nx, has_high)):

            @pl.when(jnp.logical_not(there))
            def _():
                new[x] = jnp.zeros((wide, nz), jnp.float32)

        old, new = new, old
    one_step(old, faces, gz, HALO, tall - HALO, outside)

    @pl.loop(0, nx)
    def _(x):
        for j, z in enumerate(spans):
            out_ref[x, :, z] = placed[x, j, :ny, :]


def heat(own, k_low, k_high, t_low, t_high, shape):
    nx, ny, nz = shape
    tall, wide = nx + 2 * HALO, ny + 2 * ROWS
    hbm = pl.BlockSpec(memory_space=pl.ANY)
    vmem = pl.BlockSpec(memory_space=pltpu.VMEM)
    big = pltpu.VMEM((tall, wide, nz), jnp.float32)
    return pl.pallas_call(
        heat_kernel,
        out_shape=(
            jax.ShapeDtypeStruct(shape, jnp.float32),
            jax.ShapeDtypeStruct((tall, 8, LANES), jnp.float32),
        ),
        in_specs=[hbm] * 3 + [vmem] + [hbm] * 4,
        scratch_shapes=[
            pltpu.VMEM((2, 2 * HALO, nz // LANES, wide, LANES), jnp.float32),
            big,
            big,
            big,
            big,
            pltpu.VMEM((nx, nz // LANES, wide, LANES), jnp.float32),
            pltpu.SemaphoreType.DMA((6, nz // LANES)),
            pltpu.SemaphoreType.DMA((3,)),
        ],
        compiler_params=params(64),
        cost_estimate=cost(tall * wide * nz * 100, 12 * nx * ny * nz * 4),
        name="heat",
    )(*own, k_low, k_high, t_low, t_high)


def source_kernel(ny, all_ref, thin_ref, base_ref, out_ref):
    tall = thin_ref.shape[0]
    nx = tall - 2 * HALO
    sheets = all_ref.shape[1]
    sub = lax.broadcasted_iota(jnp.int32, (8, LANES), 0)
    y_lane = lax.broadcasted_iota(jnp.int32, (8, LANES), 1)

    slabs, pairs = lax.axis_size("slab"), lax.axis_size("pair")

    def sheet(down, across):
        slab = lax.axis_index("slab") + down
        pair = lax.axis_index("pair") + across
        inside = (slab >= 0) & (slab < slabs) & (pair >= 0) & (pair < pairs)
        found = all_ref[jnp.where(inside, slab * pairs + pair, 0)]
        return jnp.where(inside, found, 0.0)

    def rows_of(down):
        low, own, high = (sheet(down, across) for across in (-1, 0, 1))
        out = []
        for half in range(2):
            if half == 0:
                own_at, high_at, low_at = own, pltpu.roll(high, ny, 1), pltpu.roll(low, ny, 1)
            else:
                own_at, high_at, low_at = pltpu.roll(own, ny, 1), high, low
            out.append(
                jnp.where(
                    y_lane < ny,
                    own_at,
                    jnp.where(
                        y_lane < ny + HALO,
                        high_at,
                        jnp.where(y_lane >= LANES - HALO, low_at, 0.0),
                    ),
                )
            )
        return out

    lines = [rows_of(down) for down in (-1, 0, 1)]
    source = []
    for x in range(-HALO, nx + HALO):
        which, local = (x + nx) // nx, x % nx
        row = lines[which][local % 2][local // 2 : local // 2 + 1, :]
        source.append(jnp.where(sub == 0, jnp.broadcast_to(row, (8, LANES)), 0.0))

    cond = [thin_ref[x] for x in range(tall)]
    cx, cy, cz, centre = [], [], [], []
    for x in range(tall):
        here = cond[x]
        after = cond[min(x + 1, tall - 1)]
        before = cond[max(x - 1, 0)]
        y_after = pltpu.roll(here, LANES - 1, 1)
        y_before = pltpu.roll(here, 1, 1)
        z_after = jnp.where(sub == 7, 0.0, pltpu.roll(here, 7, 0))
        z_before = jnp.where(sub == 0, 0.0, pltpu.roll(here, 1, 0))
        cx.append(coupling(here, after))
        cy.append(coupling(here, y_after))
        cz.append(coupling(here, z_after))
        total = 6.0 * here
        for near in (after, before, y_after, y_before, z_after, z_before):
            total = total + jnp.where(near > 0.0, near, here)
        centre.append(1.0 - (0.5 * step_size) * total)

    added = source
    for step in range(1, STEPS):
        new = list(added)
        for x in range(step, tall - step):
            here = added[x]
            total = source[x] + centre[x] * here
            total = total + (cx[x] * added[x + 1] + cx[x - 1] * added[x - 1])
            total = total + cy[x] * pltpu.roll(here, LANES - 1, 1)
            total = total + pltpu.roll(cy[x] * here, 1, 1)
            total = total + cz[x] * pltpu.roll(here, 7, 0)
            new[x] = total + pltpu.roll(cz[x] * here, 1, 0)
        added = new

    lane = lax.broadcasted_iota(jnp.int32, (ny, LANES), 1)
    turned = jnp.concatenate(added[HALO : HALO + nx], axis=0).T[:ny]
    for x in range(nx):
        piece = turned if x == 0 else pltpu.roll(turned, LANES - 8 * x, 1)
        out_ref[x] = base_ref[x] + jnp.where(lane < STEPS, piece, 0.0)


def add_source(everything, thin, base):
    nx, ny, nz = base.shape
    block = pl.BlockSpec((nx, ny, LANES), lambda i: (0, 0, 0))
    return pl.pallas_call(
        functools.partial(source_kernel, ny),
        grid=(1,),
        out_shape=jax.ShapeDtypeStruct(base.shape, jnp.float32),
        in_specs=[
            pl.BlockSpec(everything.shape, lambda i: (0, 0, 0)),
            pl.BlockSpec(thin.shape, lambda i: (0, 0, 0)),
            block,
        ],
        out_specs=block,
        input_output_aliases={2: 0},
        compiler_params=params(64),
        cost_estimate=cost(1_000_000, 2 * nx * ny * LANES * 4),
        name="add_source",
    )(everything, thin, base)


def exchange(rows):
    return lax.all_to_all(rows, ("slab", "pair"), split_axis=0, concat_axis=0, tiled=True)


def together(*arrays):
    return lax.optimization_barrier(arrays)


def both_ways(low, high, axis):
    count = lax.axis_size(axis)
    forward = [(i, i + 1) for i in range(count - 1)]
    backward = [(target, source) for source, target in forward]
    from_low = lax.ppermute(high, axis, forward)
    from_high = lax.ppermute(low, axis, backward)
    return from_low, from_high


def shards(
    initial_warmth,
    heat_passing_coefficient,
    mirror_fraction,
    element_facing_site,
    tile_block_couples,
    active_slot_count,
    view_factor_blocks,
):
    nx, ny, _ = initial_warmth.shape
    slabs, pairs = lax.axis_size("slab"), lax.axis_size("pair")
    count = slabs * pairs
    blocks = mirror_fraction.shape[0]
    couples = tile_block_couples.T

    temp, cond = initial_warmth, heat_passing_coefficient
    emitted, copies = emit(temp, element_facing_site, mirror_fraction, count)
    temp, copies = together(temp, copies)

    def sweep_terms(whole):
        whole = whole.reshape(count * blocks, BLK)
        term = tile_terms(whole, couples, active_slot_count, view_factor_blocks)
        return term.reshape(count, blocks, BLK)

    whole = exchange(copies)
    cond, copies = together(cond, copies)
    send_low, send_high = cond[:HALO], cond[nx - HALO :]
    k_low, k_high = both_ways(send_low, send_high, "slab")
    whole = together(whole, send_low, send_high)[0]
    temp, cond, term = together(temp, cond, sweep_terms(whole))
    parts = exchange(term)
    below, above = both_ways(*pack_y(temp, cond), "pair")
    parts, below, above, k_low, k_high = together(parts, below, above, k_low, k_high)
    copies, below, above = together(middle(parts, emitted, mirror_fraction), below, above)
    whole = exchange(copies)
    send_low, send_high = pack_x(temp, below, above)
    t_low, t_high = both_ways(send_low, send_high, "slab")
    whole = together(whole, send_low, send_high)[0]
    temp, cond, term = together(temp, cond, sweep_terms(whole))
    parts = exchange(term)
    own = own_planes(temp, cond, below, above)
    parts, t_low, t_high, own = together(parts, t_low, t_high, own)
    radiosity, source = last(parts, emitted, mirror_fraction, element_facing_site, nx * ny, count)
    everything = exchange(source)
    own, source = together(own, source)
    base, thin = heat(own, k_low, k_high, t_low, t_high, temp.shape)

    warmed_liner = add_source(everything, thin, base)
    return (radiosity, warmed_liner)


def solution(mesh):
    return jax.shard_map(
        shards,
        mesh=mesh,
        in_specs=(
            P("slab", "pair", None),
            P("slab", "pair", None),
            P(("slab", "pair"), None),
            P(("slab", "pair"), None),
            P(("slab", "pair"), None),
            P(("slab", "pair")),
            P(("slab", "pair"), None, None),
        ),
        out_specs=(P(("slab", "pair"), None), P("slab", "pair", None)),
        check_vma=False,
    )
```

```python
import functools

import jax
import jax.numpy as jnp
from jax import lax
from jax.experimental import pallas as pl
from jax.experimental.pallas import tpu as pltpu
from jax.sharding import PartitionSpec as P

BLK = 128
SWEEPS = 2
STEPS = 4
HALO = STEPS
ROWS = STEPS
LANES = 128
CHUNK = 16
LAG = 8

step_size = 0.07

NT = (((1,), (1,)), ((), ()))
NN = (((1,), (0,)), ((), ()))


def params(mib):
    return pltpu.CompilerParams(vmem_limit_bytes=mib * 1024 * 1024)


def cost(flops, nbytes):
    return pl.CostEstimate(flops=flops, bytes_accessed=nbytes, transcendentals=0)


def parts_of(x, count):
    out = []
    for _ in range(count - 1):
        part = x.astype(jnp.bfloat16)
        out.append(part)
        x = x - part.astype(jnp.float32)
    out.append(x.astype(jnp.bfloat16))
    return out


class Lagging:
    def __init__(self, depth):
        self.depth = depth
        self.waiting = []

    def add(self, store):
        self.waiting.append(store)
        if len(self.waiting) > self.depth:
            self.waiting.pop(0)()

    def finish(self):
        for store in self.waiting:
            store()
        self.waiting = []


def put(ref, index, value):
    return lambda: ref.__setitem__(index, value)


def emit_kernel(temp_ref, site_ref, mirror_ref, emitted_ref, copies_ref):
    nx, ny, _ = temp_ref.shape
    sheets = nx * ny // LANES
    per = LANES // ny
    lanes = lax.broadcasted_iota(jnp.int32, (LANES, LANES), 1)
    gathered = jnp.zeros((LANES, LANES), jnp.float32)
    for r in range(sheets):
        piece = temp_ref[per * r : per * r + per].reshape(LANES, LANES)
        if r:
            piece = pltpu.roll(piece, r, 1)
        gathered = jnp.where(lanes == r, piece, gathered)
    plane = gathered.T[:sheets]
    for half in range(site_ref.shape[0] // 8):
        rows = pl.ds(half * 8, 8)
        site = site_ref[rows, :]
        lane = site & (LANES - 1)
        sheet = site >> 7
        warmth = jnp.zeros(site.shape, jnp.float32)
        for r in range(sheets):
            line = jnp.broadcast_to(plane[r : r + 1, :], site.shape)
            picked = jnp.take_along_axis(line, lane, axis=1)
            warmth = jnp.where(sheet == r, picked, warmth)
        square = warmth * warmth
        emitted = (1.0 - mirror_ref[rows, :]) * (square * square)
        emitted_ref[rows, :] = emitted
        for d in range(copies_ref.shape[0]):
            copies_ref[d, rows, :] = emitted


def emit(temp, site, mirror, count):
    shape = mirror.shape
    nx, ny, _ = temp.shape
    patch = pl.BlockSpec(shape, lambda i: (0, 0))
    return pl.pallas_call(
        emit_kernel,
        grid=(1,),
        out_shape=(
            jax.ShapeDtypeStruct(shape, jnp.float32),
            jax.ShapeDtypeStruct((count,) + shape, jnp.float32),
        ),
        in_specs=[pl.BlockSpec((nx, ny, LANES), lambda i: (0, 0, 0)), patch, patch],
        out_specs=(patch, pl.BlockSpec((count,) + shape, lambda i: (0, 0, 0))),
        compiler_params=params(64),
        cost_estimate=cost(10_000, 900_000),
        name="emit",
    )(temp, site, mirror)


def tiles_kernel(
    live_ref, pairs_ref, lanes_ref, whole_ref, tiles_ref, out_ref, held, terms, sems
):
    slots = held.shape[0]
    live = live_ref[0]
    chunks = (live + CHUNK - 1) // CHUNK

    def chunk_copy(c):
        span = pl.ds(c * CHUNK, CHUNK)
        return pltpu.make_async_copy(tiles_ref.at[span], held.at[span], sems.at[c])

    @pl.loop(0, chunks)
    def _(c):
        chunk_copy(c).start()

    top = lax.broadcasted_iota(jnp.int32, (8, BLK), 0) == 0

    def split_row(block):
        row = jnp.broadcast_to(whole_ref[pl.ds(block, 1), :], (8, BLK))
        high = row.astype(jnp.bfloat16).astype(jnp.float32)
        return jnp.where(top, high, row - high)

    def vectors(a, b):
        stacked = jnp.concatenate([split_row(a), split_row(b)], axis=0)
        stacked = stacked.astype(jnp.bfloat16)
        return jnp.concatenate([stacked, stacked], axis=1)

    @pl.loop(0, chunks)
    def _(c):
        chunk_copy(c).wait()
        stores = Lagging(4 * CHUNK)
        for u in range(0, CHUNK, 2):
            t = c * CHUNK + u
            high_a, low_a = parts_of(held[t], 2)
            high_b, low_b = parts_of(held[t + 1], 2)
            both = jnp.concatenate(
                [
                    jnp.concatenate([high_a, high_b], axis=1),
                    jnp.concatenate([low_a, low_b], axis=1),
                ],
                axis=0,
            )
            second = lax.dot_general(
                vectors(pairs_ref[0, t], pairs_ref[0, t + 1]),
                both,
                NN,
                preferred_element_type=jnp.float32,
            )
            turned = jnp.concatenate(
                [
                    jnp.concatenate([high_a, low_a], axis=1),
                    jnp.concatenate([high_b, low_b], axis=1),
                ],
                axis=0,
            )
            first = lax.dot_general(
                vectors(pairs_ref[1, t], pairs_ref[1, t + 1]),
                turned,
                NT,
                preferred_element_type=jnp.float32,
            )
            for side, result in ((0, first), (1, second)):
                for v, (top_row, cols) in enumerate(((0, slice(0, BLK)), (8, slice(BLK, 2 * BLK)))):
                    row = result[top_row : top_row + 1, cols] + result[top_row + 1 : top_row + 2, cols]
                    stores.add(put(terms, (side, pl.ds(t + v, 1)), row))
        stores.finish()

    used = lax.broadcasted_iota(jnp.int32, (slots, BLK), 0) < live
    used_lane = lax.broadcasted_iota(jnp.int32, (1, slots), 1) < live
    blocks = out_ref.shape[0]
    group = min(blocks, 512)
    split = []
    for side in range(2):
        masked = jnp.where(used, terms[side], 0.0)
        split.append(jnp.concatenate(parts_of(masked, 2), axis=1))
    for base in range(0, blocks, group):
        rows = lax.broadcasted_iota(jnp.int32, (group, slots), 0) + base
        total = jnp.zeros((group, 2 * BLK), jnp.float32)
        for side in range(2):
            target = jnp.where(used_lane, lanes_ref[side : side + 1, :], -1)
            choose = jnp.where(rows == target, 1.0, 0.0).astype(jnp.bfloat16)
            total = total + jnp.dot(choose, split[side], preferred_element_type=jnp.float32)
        out_ref[base : base + group, :] = total[:, :BLK] + total[:, BLK:]


def tile_terms(whole, couples, live, tiles):
    slots = tiles.shape[0]
    smem = pl.BlockSpec(memory_space=pltpu.SMEM)
    vmem = pl.BlockSpec(memory_space=pltpu.VMEM)
    return pl.pallas_call(
        tiles_kernel,
        out_shape=jax.ShapeDtypeStruct(whole.shape, jnp.float32),
        in_specs=[smem, smem, vmem, vmem, pl.BlockSpec(memory_space=pl.ANY)],
        out_specs=vmem,
        scratch_shapes=[
            pltpu.VMEM(tiles.shape, jnp.float32),
            pltpu.VMEM((2, slots, BLK), jnp.float32),
            pltpu.SemaphoreType.DMA((slots // CHUNK,)),
        ],
        compiler_params=params(64),
        cost_estimate=cost(slots * BLK * BLK * 32, slots * BLK * BLK * 4),
        name="tiles",
    )(live, couples, couples, whole, tiles)


def sum_parts(parts_ref, rows):
    total = parts_ref[0, rows, :]
    for d in range(1, parts_ref.shape[0]):
        total = total + parts_ref[d, rows, :]
    return total


def middle_kernel(parts_ref, emitted_ref, mirror_ref, copies_ref):
    for half in range(emitted_ref.shape[0] // 8):
        rows = pl.ds(half * 8, 8)
        incident = sum_parts(parts_ref, rows)
        radiosity = emitted_ref[rows, :] + mirror_ref[rows, :] * incident
        for d in range(copies_ref.shape[0]):
            copies_ref[d, rows, :] = radiosity


def middle(parts, emitted, mirror):
    return pl.pallas_call(
        middle_kernel,
        out_shape=jax.ShapeDtypeStruct(parts.shape, jnp.float32),
        compiler_params=params(64),
        cost_estimate=cost(100_000, 600_000),
        name="middle",
    )(parts, emitted, mirror)


def last_kernel(scale, parts_ref, emitted_ref, mirror_ref, site_ref, rad_ref, source_ref):
    blocks = emitted_ref.shape[0]
    incident = sum_parts(parts_ref, slice(None))
    emitted = emitted_ref[...]
    mirror = mirror_ref[...]
    rad_ref[...] = emitted + mirror * incident
    absorbed = ((1.0 - mirror) * incident - emitted) * scale
    site = site_ref[...]
    lane = site & (LANES - 1)
    sheet = site >> 7
    sheets = source_ref.shape[1]
    sheet_iota = lax.broadcasted_iota(jnp.int32, (sheets, BLK), 0)
    lane_iota = lax.broadcasted_iota(jnp.int32, (LANES, BLK), 0)
    left = []
    right = []
    for b in range(blocks):
        here = jnp.where(sheet_iota == sheet[b : b + 1, :], absorbed[b : b + 1, :], 0.0)
        left.append(here)
        pick = jnp.where(lane_iota == lane[b : b + 1, :], 1.0, 0.0)
        right.append(pick.astype(jnp.bfloat16))
    left = jnp.concatenate(left, axis=1)
    right = jnp.concatenate(right, axis=1)
    source = jnp.zeros((sheets, LANES), jnp.float32)
    for part in parts_of(left, 3):
        source = source + lax.dot_general(part, right, NT, preferred_element_type=jnp.float32)
    for d in range(source_ref.shape[0]):
        source_ref[d] = source


def last(parts, emitted, mirror, site, cells, count):
    weight = cells / (mirror.shape[0] * BLK * 1.0)
    return pl.pallas_call(
        functools.partial(last_kernel, step_size * weight),
        out_shape=(
            jax.ShapeDtypeStruct(mirror.shape, jnp.float32),
            jax.ShapeDtypeStruct((count, cells // LANES, LANES), jnp.float32),
        ),
        compiler_params=params(64),
        cost_estimate=cost(10_000_000, 600_000),
        name="last",
    )(parts, emitted, mirror, site)


def pack_y_kernel(t0, k0, t7, k7, down_ref, up_ref):
    upper = lax.broadcasted_iota(jnp.int32, down_ref.shape[1:], 0) < ROWS
    for x in range(down_ref.shape[0]):
        down_ref[x] = jnp.where(upper, t0[x], pltpu.roll(k0[x], ROWS, 0))
        up_ref[x] = jnp.where(upper, pltpu.roll(t7[x], ROWS, 0), k7[x])


def pack_y(temp, cond):
    nx, ny, nz = temp.shape
    first = pl.BlockSpec((nx, 8, nz), lambda i: (0, 0, 0))
    final = pl.BlockSpec((nx, 8, nz), lambda i: (0, ny // 8 - 1, 0))
    shape = jax.ShapeDtypeStruct((nx, 8, nz), jnp.float32)
    return pl.pallas_call(
        pack_y_kernel,
        grid=(1,),
        out_shape=(shape, shape),
        in_specs=[first, first, final, final],
        out_specs=(first, first),
        compiler_params=params(64),
        cost_estimate=cost(0, 4 * nx * 8 * nz * 4),
        name="pack_y",
    )(temp, cond, temp, cond)


def mixed_tile(t_tile, k_tile):
    row = lax.broadcasted_iota(jnp.int32, t_tile.shape, 0)
    of_k = jnp.where(row < 4, pltpu.roll(k_tile, 2, 0), pltpu.roll(k_tile, 6, 0))
    return jnp.where((row < 2) | (row >= 6), t_tile, of_k)


def unmixed(tile):
    row = lax.broadcasted_iota(jnp.int32, tile.shape, 0)
    outer = (row < 2) | (row >= 6)
    of_k = jnp.where(row < 4, pltpu.roll(tile, 6, 0), pltpu.roll(tile, 2, 0))
    return jnp.where(outer, tile, 0.0), jnp.where(outer, of_k, 0.0)


def pack_x_kernel(first, final, below0, above0, below1, above1, low_ref, high_ref):
    ny, nz = first.shape[1:]
    upper = lax.broadcasted_iota(jnp.int32, (8, nz), 0) < ROWS
    tail = HALO * ny
    for send, temp, below, above, order in (
        (low_ref, first, below0, above0, (0, 1, 2)),
        (high_ref, final, below1, above1, (HALO - 1, HALO - 2, HALO - 3)),
    ):
        for p in range(HALO):
            send[p * ny : (p + 1) * ny, :] = temp[p]
        for k, p in enumerate(order):
            t_tile = jnp.where(upper, above[p], pltpu.roll(below[p], ROWS, 0))
            k_tile = jnp.where(upper, pltpu.roll(above[p], ROWS, 0), below[p])
            if k == 0:
                send[tail : tail + 8, :] = t_tile
                send[tail + 8 : tail + 16, :] = k_tile
            else:
                at = tail + 8 + 8 * k
                send[at : at + 8, :] = mixed_tile(t_tile, k_tile)


def pack_x(temp, below, above):
    nx, ny, nz = temp.shape

    def ends(rows):
        return (
            pl.BlockSpec((HALO, rows, nz), lambda i: (0, 0, 0)),
            pl.BlockSpec((HALO, rows, nz), lambda i: (nx // HALO - 1, 0, 0)),
        )

    first, final = ends(ny)
    first_rows, final_rows = ends(8)
    rows = HALO * ny + 32
    whole = pl.BlockSpec((rows, nz), lambda i: (0, 0))
    shape = jax.ShapeDtypeStruct((rows, nz), jnp.float32)
    return pl.pallas_call(
        pack_x_kernel,
        grid=(1,),
        out_shape=(shape, shape),
        in_specs=[first, final, first_rows, first_rows, final_rows, final_rows],
        out_specs=(whole, whole),
        compiler_params=params(64),
        cost_estimate=cost(0, 4 * rows * nz * 4),
        name="pack_x",
    )(temp, temp, below, above, below, above)


def coupling(a, b):
    return jnp.where(jnp.minimum(a, b) > 0.0, (0.5 * step_size) * (a + b), 0.0)


def neighbours():
    slab, pair = lax.axis_index("slab"), lax.axis_index("pair")
    return slab > 0, slab < lax.axis_size("slab") - 1, pair > 0, pair < lax.axis_size("pair") - 1


def lane_tiles(nz):
    return [slice(j * LANES, (j + 1) * LANES) for j in range(nz // LANES)]


def one_step(field, cond, gz, begin, end, target):
    wide, nz = field.shape[1:]
    tiles = wide // 8
    spans = lane_tiles(nz)
    count = len(spans)
    lane = lax.broadcasted_iota(jnp.int32, (8, LANES), 1)
    sub = lax.broadcasted_iota(jnp.int32, (8, LANES), 0)
    _, _, has_below, has_above = neighbours()
    keep_above = (sub < 7) | has_above
    keep_below = (sub < 7) | has_below

    def row_tile(ref, x, t):
        return [ref[x, 8 * t : 8 * t + 8, z] for z in spans]

    def first_rolled(ref, x):
        return [pltpu.roll(v, 7, 0) for v in row_tile(ref, x, 0)]

    def y_flux(t_now, k_now, t_next, k_next):
        return [
            (k_now[j] + k_next[j]) * (t_next[j] - t_now[j]) for j in range(count)
        ]

    def z_change(x, t, t_now, k_now):
        turned = [pltpu.roll(v, LANES - 1, 1) for v in t_now]
        flux = []
        for j, z in enumerate(spans):
            deep = turned[j + 1] if j + 1 < count else 0.0
            deep = jnp.where(lane < LANES - 1, turned[j], deep)
            flux.append(gz[x, 8 * t : 8 * t + 8, z] * (deep - t_now[j]))
        back = [pltpu.roll(f, 1, 1) for f in flux]
        out = []
        for j in range(count):
            low = back[j - 1] if j else (k_now[0] + k_now[0]) * t_now[0]
            out.append(flux[j] - jnp.where(lane > 0, back[j], low))
        return out

    @pl.loop(begin, end)
    def _(x):
        stores = Lagging(LAG)
        final = y_flux(
            row_tile(field, x, tiles - 1),
            row_tile(cond, x, tiles - 1),
            first_rolled(field, x),
            first_rolled(cond, x),
        )
        low_y = [pltpu.roll(f, 1, 0) for f in final]
        t_now, k_now = row_tile(field, x, 0), row_tile(cond, x, 0)
        for t in range(tiles):
            rows = slice(8 * t, 8 * t + 8)
            if t + 1 < tiles:
                t_next, k_next = row_tile(field, x, t + 1), row_tile(cond, x, t + 1)
            else:
                t_next, k_next = first_rolled(field, x), first_rolled(cond, x)
            high_y = y_flux(t_now, k_now, t_next, k_next)
            change_z = z_change(x, t, t_now, k_now)
            for j, z in enumerate(spans):
                now, here = t_now[j], k_now[j]
                high_x = (here + cond[x + 1, rows, z]) * (field[x + 1, rows, z] - now)
                low_x = (here + cond[x - 1, rows, z]) * (now - field[x - 1, rows, z])
                new = now + (high_x - low_x) + (high_y[j] - low_y[j]) + change_z[j]
                if t:
                    new = jnp.where(keep_above if t <= ROWS else keep_below, new, 0.0)
                stores.add(put(*target(x, t, z), new))
            low_y, t_now, k_now = high_y, t_next, k_next
        stores.finish()


def thin_planes(cond, ny, store):
    tall, _, wide, _ = cond.shape
    lane = lax.broadcasted_iota(jnp.int32, (wide, LANES), 1)
    y_lane = lax.broadcasted_iota(jnp.int32, (8, LANES), 1)
    for base in range(0, tall, 16):
        planes = min(16, tall - base)
        gathered = jnp.zeros((wide, LANES), jnp.float32)
        for g in range(planes):
            piece = cond[base + g, 0]
            if g:
                piece = pltpu.roll(piece, 8 * g, 1)
            gathered = jnp.where((lane >> 3) == g, piece, gathered)
        turned = jnp.concatenate(
            [gathered, jnp.zeros((LANES - wide, LANES), jnp.float32)], axis=0
        ).T
        for g in range(planes):
            rows = turned[8 * g : 8 * g + 8, :]
            moved = pltpu.roll(rows, LANES - wide, 1)
            store(
                base + g,
                jnp.where(
                    y_lane < ny + ROWS, rows, jnp.where(y_lane >= LANES - ROWS, moved, 0.0)
                ),
            )


def mirror_rows(raw_k, ny):
    _, _, has_below, has_above = neighbours()
    upper = lax.broadcasted_iota(jnp.int32, (8, LANES), 0) < ROWS

    @pl.when(jnp.logical_not(has_above & has_below))
    def _():
        missing = (upper & jnp.logical_not(has_above)) | (
            jnp.logical_not(upper) & jnp.logical_not(has_below)
        )

        @pl.loop(0, raw_k.shape[0])
        def _(x):
            for j in range(raw_k.shape[1]):
                edge = raw_k[x, j, ny:]
                last = jnp.broadcast_to(raw_k[x, j, ny - 1 : ny, :], edge.shape)
                first = jnp.broadcast_to(raw_k[x, j, 0:1, :], edge.shape)
                raw_k[x, j, ny:] = jnp.where(missing, jnp.where(upper, last, first), edge)


def lay_out_k(loaded, place, faces, gz):
    planes, count, wide, _ = loaded.shape[1:]
    tiles = wide // 8
    spans = lane_tiles(count * LANES)
    lane = lax.broadcasted_iota(jnp.int32, (8, LANES), 1)

    @pl.loop(0, planes)
    def _(x):
        stores = Lagging(LAG)
        to = place(x)
        for t in range(tiles):
            rows = pl.ds(t, 8, stride=tiles)
            kept = slice(8 * t, 8 * t + 8)
            here = [(0.5 * step_size) * loaded[1, x, j, rows, :] for j in range(count)]
            turned = [pltpu.roll(v, LANES - 1, 1) for v in here]
            for j, z in enumerate(spans):
                deep = turned[j + 1] if j + 1 < count else here[j]
                deep = jnp.where(lane < LANES - 1, turned[j], deep)
                stores.add(put(faces, (to, kept, z), here[j]))
                stores.add(put(gz, (to, kept, z), here[j] + deep))
        stores.finish()


def lay_out_t(loaded, place, field):
    planes, count, wide, _ = loaded.shape[1:]
    tiles = wide // 8
    spans = lane_tiles(count * LANES)

    @pl.loop(0, planes)
    def _(x):
        stores = Lagging(LAG)
        to = place(x)
        for t in range(tiles):
            rows = pl.ds(t, 8, stride=tiles)
            for j, z in enumerate(spans):
                stores.add(put(field, (to, slice(8 * t, 8 * t + 8), z), loaded[0, x, j, rows, :]))
        stores.finish()


def fetch(loaded, which, ref, source_row, at, row, rows, sems):
    planes, count = ref.shape[0], loaded.shape[2]
    return [
        pltpu.make_async_copy(
            ref.at[:, pl.ds(source_row, rows), pl.ds(j * LANES, LANES)],
            loaded.at[which, pl.ds(at, planes), j, pl.ds(row, rows)],
            sems.at[j],
        )
        for j in range(count)
    ]


def own_planes_kernel(
    t_ref, k_ref, below_ref, above_ref, field, faces, gz, thin_ref, loaded, sems
):
    nx, ny, nz = t_ref.shape
    raw_t, raw_k = loaded.at[0], loaded.at[1]
    k_copies = fetch(loaded, 1, k_ref, 0, 0, 0, ny, sems.at[1])
    t_copies = fetch(loaded, 0, t_ref, 0, 0, 0, ny, sems.at[0])
    for copy in k_copies + t_copies:
        copy.start()
    upper = lax.broadcasted_iota(jnp.int32, (8, LANES), 0) < ROWS

    @pl.loop(0, nx)
    def _(x):
        for j, z in enumerate(lane_tiles(nz)):
            down, up = above_ref[x, :, z], below_ref[x, :, z]
            raw_t[x, j, ny:] = jnp.where(upper, down, pltpu.roll(up, ROWS, 0))
            raw_k[x, j, ny:] = jnp.where(upper, pltpu.roll(down, ROWS, 0), up)

    for copy in k_copies:
        copy.wait()
    thin_planes(raw_k, ny, lambda x, v: thin_ref.__setitem__(x, v))
    mirror_rows(raw_k, ny)
    lay_out_k(loaded, lambda x: x, faces, gz)
    for copy in t_copies:
        copy.wait()
    lay_out_t(loaded, lambda x: x, field)


def own_planes(temp, cond, below, above):
    nx, ny, nz = temp.shape
    wide = ny + 2 * ROWS
    hbm = pl.BlockSpec(memory_space=pl.ANY)
    vmem = pl.BlockSpec(memory_space=pltpu.VMEM)
    shape = jax.ShapeDtypeStruct((nx, wide, nz), jnp.float32)
    return pl.pallas_call(
        own_planes_kernel,
        out_shape=(shape, shape, shape, jax.ShapeDtypeStruct((nx, 8, LANES), jnp.float32)),
        in_specs=[hbm, hbm, vmem, vmem],
        scratch_shapes=[
            pltpu.VMEM((2, nx, nz // LANES, wide, LANES), jnp.float32),
            pltpu.SemaphoreType.DMA((2, nz // LANES)),
        ],
        compiler_params=params(64),
        cost_estimate=cost(nx * wide * nz * 10, 6 * nx * wide * nz * 4),
        name="own_planes",
    )(temp, cond, below, above)


def heat_kernel(
    own_field, own_faces, own_gz, own_thin, k_low, k_high, t_low, t_high, out_ref, thin_ref,
    loaded, corners, field, between, faces, gz, placed, sems, own_sems,
):
    nx, wide, nz = own_field.shape
    ny = wide - 2 * ROWS
    tall = nx + 2 * HALO
    tiles = wide // 8
    spans = lane_tiles(nz)
    k_copies, t_copies = [], []
    for k, (k_side, t_side) in enumerate(((k_low, t_low), (k_high, t_high))):
        at = k * HALO
        k_copies += fetch(loaded, 1, k_side, 0, at, 0, ny, sems.at[3 * k])
        k_copies.append(
            pltpu.make_async_copy(
                t_side.at[pl.ds(HALO * ny, 32)], corners.at[k], own_sems.at[3 + k]
            )
        )
        for p in range(HALO):
            t_copies += [
                pltpu.make_async_copy(
                    t_side.at[pl.ds(p * ny, ny), pl.ds(j * LANES, LANES)],
                    loaded.at[0, at + p, j, pl.ds(0, ny)],
                    sems.at[3 * (k + 1) - 1 + 6 * p, j],
                )
                for j in range(len(spans))
            ]
    own = [
        pltpu.make_async_copy(ref, whole.at[pl.ds(HALO, nx)], own_sems.at[k])
        for k, (ref, whole) in enumerate(
            ((own_faces, faces), (own_gz, gz), (own_field, field))
        )
    ]
    for copy in k_copies + t_copies + own:
        copy.start()
    has_low, has_high, _, _ = neighbours()

    def place(x):
        return jnp.where(x < HALO, x, x + nx)

    def store_thin(x, value):
        thin_ref[x if x < HALO else x + nx] = value

    thin_ref[HALO : HALO + nx] = own_thin[...]
    raw_t, raw_k = loaded.at[0], loaded.at[1]
    for copy in k_copies:
        copy.wait()
    for k, order in enumerate(
        ((HALO - 1, HALO - 2, HALO - 3, 0), (HALO, HALO + 1, HALO + 2, 2 * HALO - 1))
    ):
        for distance, p in enumerate(order):
            for j, z in enumerate(spans):
                if distance == 0:
                    t_tile, k_tile = corners[k, :8, z], corners[k, 8:16, z]
                elif distance + 1 < HALO:
                    t_tile, k_tile = unmixed(corners[k, 8 + 8 * distance : 16 + 8 * distance, z])
                else:
                    t_tile = k_tile = jnp.zeros((8, LANES), jnp.float32)
                raw_t[p, j, ny:] = t_tile
                raw_k[p, j, ny:] = k_tile
    thin_planes(raw_k, ny, store_thin)
    mirror_rows(raw_k, ny)
    lay_out_k(loaded, place, faces, gz)
    for copy in t_copies:
        copy.wait()
    lay_out_t(loaded, place, field)
    for copy in own:
        copy.wait()

    @pl.when(jnp.logical_not(has_low))
    def _():
        faces[HALO - 1] = faces[HALO]

    @pl.when(jnp.logical_not(has_high))
    def _():
        faces[HALO + nx] = faces[HALO + nx - 1]

    def inside(target):
        return lambda x, t, z: (target, (x, slice(8 * t, 8 * t + 8), z))

    def outside(x, t, z):
        return placed, (x - HALO, z.start // LANES, pl.ds(t, 8, stride=tiles))

    old, new = field, between
    for step in range(1, STEPS):
        one_step(old, faces, gz, step, tall - step, inside(new))
        for x, there in ((HALO - 1, has_low), (HALO + nx, has_high)):

            @pl.when(jnp.logical_not(there))
            def _():
                new[x] = jnp.zeros((wide, nz), jnp.float32)

        old, new = new, old
    one_step(old, faces, gz, HALO, tall - HALO, outside)

    @pl.loop(0, nx)
    def _(x):
        for j, z in enumerate(spans):
            out_ref[x, :, z] = placed[x, j, :ny, :]


def heat(own, k_low, k_high, t_low, t_high, shape):
    nx, ny, nz = shape
    tall, wide = nx + 2 * HALO, ny + 2 * ROWS
    hbm = pl.BlockSpec(memory_space=pl.ANY)
    vmem = pl.BlockSpec(memory_space=pltpu.VMEM)
    big = pltpu.VMEM((tall, wide, nz), jnp.float32)
    return pl.pallas_call(
        heat_kernel,
        out_shape=(
            jax.ShapeDtypeStruct(shape, jnp.float32),
            jax.ShapeDtypeStruct((tall, 8, LANES), jnp.float32),
        ),
        in_specs=[hbm] * 3 + [vmem] + [hbm] * 4,
        scratch_shapes=[
            pltpu.VMEM((2, 2 * HALO, nz // LANES, wide, LANES), jnp.float32),
            pltpu.VMEM((2, 32, nz), jnp.float32),
            big,
            big,
            big,
            big,
            pltpu.VMEM((nx, nz // LANES, wide, LANES), jnp.float32),
            pltpu.SemaphoreType.DMA((6 * HALO, nz // LANES)),
            pltpu.SemaphoreType.DMA((5,)),
        ],
        compiler_params=params(64),
        cost_estimate=cost(tall * wide * nz * 100, 12 * nx * ny * nz * 4),
        name="heat",
    )(*own, k_low, k_high, t_low, t_high)


def source_kernel(ny, all_ref, thin_ref, base_ref, out_ref):
    tall = thin_ref.shape[0]
    nx = tall - 2 * HALO
    sheets = all_ref.shape[1]
    sub = lax.broadcasted_iota(jnp.int32, (8, LANES), 0)
    y_lane = lax.broadcasted_iota(jnp.int32, (8, LANES), 1)

    slabs, pairs = lax.axis_size("slab"), lax.axis_size("pair")

    def sheet(down, across):
        slab = lax.axis_index("slab") + down
        pair = lax.axis_index("pair") + across
        inside = (slab >= 0) & (slab < slabs) & (pair >= 0) & (pair < pairs)
        found = all_ref[jnp.where(inside, slab * pairs + pair, 0)]
        return jnp.where(inside, found, 0.0)

    def rows_of(down):
        low, own, high = (sheet(down, across) for across in (-1, 0, 1))
        out = []
        for half in range(2):
            if half == 0:
                own_at, high_at, low_at = own, pltpu.roll(high, ny, 1), pltpu.roll(low, ny, 1)
            else:
                own_at, high_at, low_at = pltpu.roll(own, ny, 1), high, low
            out.append(
                jnp.where(
                    y_lane < ny,
                    own_at,
                    jnp.where(
                        y_lane < ny + HALO,
                        high_at,
                        jnp.where(y_lane >= LANES - HALO, low_at, 0.0),
                    ),
                )
            )
        return out

    lines = [rows_of(down) for down in (-1, 0, 1)]
    source = []
    for x in range(-HALO, nx + HALO):
        which, local = (x + nx) // nx, x % nx
        row = lines[which][local % 2][local // 2 : local // 2 + 1, :]
        source.append(jnp.where(sub == 0, jnp.broadcast_to(row, (8, LANES)), 0.0))

    cond = [thin_ref[x] for x in range(tall)]
    cx, cy, cz, centre = [], [], [], []
    for x in range(tall):
        here = cond[x]
        after = cond[min(x + 1, tall - 1)]
        before = cond[max(x - 1, 0)]
        y_after = pltpu.roll(here, LANES - 1, 1)
        y_before = pltpu.roll(here, 1, 1)
        z_after = jnp.where(sub == 7, 0.0, pltpu.roll(here, 7, 0))
        z_before = jnp.where(sub == 0, 0.0, pltpu.roll(here, 1, 0))
        cx.append(coupling(here, after))
        cy.append(coupling(here, y_after))
        cz.append(coupling(here, z_after))
        total = 6.0 * here
        for near in (after, before, y_after, y_before, z_after, z_before):
            total = total + jnp.where(near > 0.0, near, here)
        centre.append(1.0 - (0.5 * step_size) * total)

    added = source
    for step in range(1, STEPS):
        new = list(added)
        for x in range(step, tall - step):
            here = added[x]
            total = source[x] + centre[x] * here
            total = total + (cx[x] * added[x + 1] + cx[x - 1] * added[x - 1])
            total = total + cy[x] * pltpu.roll(here, LANES - 1, 1)
            total = total + pltpu.roll(cy[x] * here, 1, 1)
            total = total + cz[x] * pltpu.roll(here, 7, 0)
            new[x] = total + pltpu.roll(cz[x] * here, 1, 0)
        added = new

    lane = lax.broadcasted_iota(jnp.int32, (ny, LANES), 1)
    turned = jnp.concatenate(added[HALO : HALO + nx], axis=0).T[:ny]
    for x in range(nx):
        piece = turned if x == 0 else pltpu.roll(turned, LANES - 8 * x, 1)
        out_ref[x] = base_ref[x] + jnp.where(lane < STEPS, piece, 0.0)


def add_source(everything, thin, base):
    nx, ny, nz = base.shape
    block = pl.BlockSpec((nx, ny, LANES), lambda i: (0, 0, 0))
    return pl.pallas_call(
        functools.partial(source_kernel, ny),
        grid=(1,),
        out_shape=jax.ShapeDtypeStruct(base.shape, jnp.float32),
        in_specs=[
            pl.BlockSpec(everything.shape, lambda i: (0, 0, 0)),
            pl.BlockSpec(thin.shape, lambda i: (0, 0, 0)),
            block,
        ],
        out_specs=block,
        input_output_aliases={2: 0},
        compiler_params=params(64),
        cost_estimate=cost(1_000_000, 2 * nx * ny * LANES * 4),
        name="add_source",
    )(everything, thin, base)


def exchange(rows):
    return lax.all_to_all(rows, ("slab", "pair"), split_axis=0, concat_axis=0, tiled=True)


def together(*arrays):
    return lax.optimization_barrier(arrays)


def both_ways(low, high, axis):
    count = lax.axis_size(axis)
    forward = [(i, i + 1) for i in range(count - 1)]
    backward = [(target, source) for source, target in forward]
    from_low = lax.ppermute(high, axis, forward)
    from_high = lax.ppermute(low, axis, backward)
    return from_low, from_high


def shards(
    initial_warmth,
    heat_passing_coefficient,
    mirror_fraction,
    element_facing_site,
    tile_block_couples,
    active_slot_count,
    view_factor_blocks,
):
    nx, ny, _ = initial_warmth.shape
    slabs, pairs = lax.axis_size("slab"), lax.axis_size("pair")
    count = slabs * pairs
    blocks = mirror_fraction.shape[0]
    couples = tile_block_couples.T

    temp, cond = initial_warmth, heat_passing_coefficient
    emitted, copies = emit(temp, element_facing_site, mirror_fraction, count)
    temp, copies = together(temp, copies)

    def sweep_terms(whole):
        whole = whole.reshape(count * blocks, BLK)
        term = tile_terms(whole, couples, active_slot_count, view_factor_blocks)
        return term.reshape(count, blocks, BLK)

    whole = exchange(copies)
    cond, copies = together(cond, copies)
    send_low, send_high = cond[:HALO], cond[nx - HALO :]
    k_low, k_high = both_ways(send_low, send_high, "slab")
    whole = together(whole, send_low, send_high)[0]
    temp, cond, term = together(temp, cond, sweep_terms(whole))
    parts = exchange(term)
    below, above = both_ways(*pack_y(temp, cond), "pair")
    parts, below, above, k_low, k_high = together(parts, below, above, k_low, k_high)
    copies, below, above = together(middle(parts, emitted, mirror_fraction), below, above)
    whole = exchange(copies)
    send_low, send_high = pack_x(temp, below, above)
    t_low, t_high = both_ways(send_low, send_high, "slab")
    whole = together(whole, send_low, send_high)[0]
    temp, cond, term = together(temp, cond, sweep_terms(whole))
    parts = exchange(term)
    own = own_planes(temp, cond, below, above)
    parts, t_low, t_high, own = together(parts, t_low, t_high, own)
    radiosity, source = last(parts, emitted, mirror_fraction, element_facing_site, nx * ny, count)
    everything = exchange(source)
    own, source = together(own, source)
    base, thin = heat(own, k_low, k_high, t_low, t_high, temp.shape)

    warmed_liner = add_source(everything, thin, base)
    return (radiosity, warmed_liner)


def solution(mesh):
    return jax.shard_map(
        shards,
        mesh=mesh,
        in_specs=(
            P("slab", "pair", None),
            P("slab", "pair", None),
            P(("slab", "pair"), None),
            P(("slab", "pair"), None),
            P(("slab", "pair"), None),
            P(("slab", "pair")),
            P(("slab", "pair"), None, None),
        ),
        out_specs=(P(("slab", "pair"), None), P("slab", "pair", None)),
        check_vma=False,
    )
```

```python
import functools

import jax
import jax.numpy as jnp
from jax import lax
from jax.experimental import pallas as pl
from jax.experimental.pallas import tpu as pltpu
from jax.sharding import PartitionSpec as P

BLK = 128
SWEEPS = 2
STEPS = 4
HALO = STEPS
ROWS = STEPS
LANES = 128
CHUNK = 16
LAG = 8

step_size = 0.07

NT = (((1,), (1,)), ((), ()))
NN = (((1,), (0,)), ((), ()))


def params(mib):
    return pltpu.CompilerParams(vmem_limit_bytes=mib * 1024 * 1024)


def cost(flops, nbytes):
    return pl.CostEstimate(flops=flops, bytes_accessed=nbytes, transcendentals=0)


def parts_of(x, count):
    out = []
    for _ in range(count - 1):
        part = x.astype(jnp.bfloat16)
        out.append(part)
        x = x - part.astype(jnp.float32)
    out.append(x.astype(jnp.bfloat16))
    return out


class Lagging:
    def __init__(self, depth):
        self.depth = depth
        self.waiting = []

    def add(self, store):
        self.waiting.append(store)
        if len(self.waiting) > self.depth:
            self.waiting.pop(0)()

    def finish(self):
        for store in self.waiting:
            store()
        self.waiting = []


def put(ref, index, value):
    return lambda: ref.__setitem__(index, value)


def emit_kernel(temp_ref, site_ref, mirror_ref, emitted_ref, copies_ref):
    nx, ny, _ = temp_ref.shape
    sheets = nx * ny // LANES
    per = LANES // ny
    lanes = lax.broadcasted_iota(jnp.int32, (LANES, LANES), 1)
    gathered = jnp.zeros((LANES, LANES), jnp.float32)
    for r in range(sheets):
        piece = temp_ref[per * r : per * r + per].reshape(LANES, LANES)
        if r:
            piece = pltpu.roll(piece, r, 1)
        gathered = jnp.where(lanes == r, piece, gathered)
    plane = gathered.T[:sheets]
    for half in range(site_ref.shape[0] // 8):
        rows = pl.ds(half * 8, 8)
        site = site_ref[rows, :]
        lane = site & (LANES - 1)
        sheet = site >> 7
        warmth = jnp.zeros(site.shape, jnp.float32)
        for r in range(sheets):
            line = jnp.broadcast_to(plane[r : r + 1, :], site.shape)
            picked = jnp.take_along_axis(line, lane, axis=1)
            warmth = jnp.where(sheet == r, picked, warmth)
        square = warmth * warmth
        emitted = (1.0 - mirror_ref[rows, :]) * (square * square)
        emitted_ref[rows, :] = emitted
        for d in range(copies_ref.shape[0]):
            copies_ref[d, rows, :] = emitted


def emit(temp, site, mirror, count):
    shape = mirror.shape
    nx, ny, _ = temp.shape
    patch = pl.BlockSpec(shape, lambda i: (0, 0))
    return pl.pallas_call(
        emit_kernel,
        grid=(1,),
        out_shape=(
            jax.ShapeDtypeStruct(shape, jnp.float32),
            jax.ShapeDtypeStruct((count,) + shape, jnp.float32),
        ),
        in_specs=[pl.BlockSpec((nx, ny, LANES), lambda i: (0, 0, 0)), patch, patch],
        out_specs=(patch, pl.BlockSpec((count,) + shape, lambda i: (0, 0, 0))),
        compiler_params=params(64),
        cost_estimate=cost(10_000, 900_000),
        name="emit",
    )(temp, site, mirror)


def tiles_kernel(
    live_ref, pairs_ref, lanes_ref, whole_ref, tiles_ref, out_ref, held, terms, sems
):
    slots = held.shape[0]
    live = live_ref[0]
    chunks = (live + CHUNK - 1) // CHUNK

    def chunk_copy(c):
        span = pl.ds(c * CHUNK, CHUNK)
        return pltpu.make_async_copy(tiles_ref.at[span], held.at[span], sems.at[c])

    @pl.loop(0, chunks)
    def _(c):
        chunk_copy(c).start()

    top = lax.broadcasted_iota(jnp.int32, (8, BLK), 0) == 0

    def split_row(block):
        row = jnp.broadcast_to(whole_ref[pl.ds(block, 1), :], (8, BLK))
        high = row.astype(jnp.bfloat16).astype(jnp.float32)
        return jnp.where(top, high, row - high)

    def vectors(a, b):
        stacked = jnp.concatenate([split_row(a), split_row(b)], axis=0)
        stacked = stacked.astype(jnp.bfloat16)
        return jnp.concatenate([stacked, stacked], axis=1)

    @pl.loop(0, chunks)
    def _(c):
        chunk_copy(c).wait()
        stores = Lagging(4 * CHUNK)
        for u in range(0, CHUNK, 2):
            t = c * CHUNK + u
            high_a, low_a = parts_of(held[t], 2)
            high_b, low_b = parts_of(held[t + 1], 2)
            both = jnp.concatenate(
                [
                    jnp.concatenate([high_a, high_b], axis=1),
                    jnp.concatenate([low_a, low_b], axis=1),
                ],
                axis=0,
            )
            second = lax.dot_general(
                vectors(pairs_ref[0, t], pairs_ref[0, t + 1]),
                both,
                NN,
                preferred_element_type=jnp.float32,
            )
            turned = jnp.concatenate(
                [
                    jnp.concatenate([high_a, low_a], axis=1),
                    jnp.concatenate([high_b, low_b], axis=1),
                ],
                axis=0,
            )
            first = lax.dot_general(
                vectors(pairs_ref[1, t], pairs_ref[1, t + 1]),
                turned,
                NT,
                preferred_element_type=jnp.float32,
            )
            for side, result in ((0, first), (1, second)):
                for v, (top_row, cols) in enumerate(((0, slice(0, BLK)), (8, slice(BLK, 2 * BLK)))):
                    row = result[top_row : top_row + 1, cols] + result[top_row + 1 : top_row + 2, cols]
                    stores.add(put(terms, (side, pl.ds(t + v, 1)), row))
        stores.finish()

    used = lax.broadcasted_iota(jnp.int32, (slots, BLK), 0) < live
    used_lane = lax.broadcasted_iota(jnp.int32, (1, slots), 1) < live
    blocks = out_ref.shape[0]
    group = min(blocks, 512)
    split = []
    for side in range(2):
        masked = jnp.where(used, terms[side], 0.0)
        split.append(jnp.concatenate(parts_of(masked, 2), axis=1))
    for base in range(0, blocks, group):
        rows = lax.broadcasted_iota(jnp.int32, (group, slots), 0) + base
        total = jnp.zeros((group, 2 * BLK), jnp.float32)
        for side in range(2):
            target = jnp.where(used_lane, lanes_ref[side : side + 1, :], -1)
            choose = jnp.where(rows == target, 1.0, 0.0).astype(jnp.bfloat16)
            total = total + jnp.dot(choose, split[side], preferred_element_type=jnp.float32)
        out_ref[base : base + group, :] = total[:, :BLK] + total[:, BLK:]


def tile_terms(whole, couples, live, tiles):
    slots = tiles.shape[0]
    smem = pl.BlockSpec(memory_space=pltpu.SMEM)
    vmem = pl.BlockSpec(memory_space=pltpu.VMEM)
    return pl.pallas_call(
        tiles_kernel,
        out_shape=jax.ShapeDtypeStruct(whole.shape, jnp.float32),
        in_specs=[smem, smem, vmem, vmem, pl.BlockSpec(memory_space=pl.ANY)],
        out_specs=vmem,
        scratch_shapes=[
            pltpu.VMEM(tiles.shape, jnp.float32),
            pltpu.VMEM((2, slots, BLK), jnp.float32),
            pltpu.SemaphoreType.DMA((slots // CHUNK,)),
        ],
        compiler_params=params(64),
        cost_estimate=cost(slots * BLK * BLK * 32, slots * BLK * BLK * 4),
        name="tiles",
    )(live, couples, couples, whole, tiles)


def sum_parts(parts_ref, rows):
    total = parts_ref[0, rows, :]
    for d in range(1, parts_ref.shape[0]):
        total = total + parts_ref[d, rows, :]
    return total


def middle_kernel(parts_ref, emitted_ref, mirror_ref, copies_ref):
    for half in range(emitted_ref.shape[0] // 8):
        rows = pl.ds(half * 8, 8)
        incident = sum_parts(parts_ref, rows)
        radiosity = emitted_ref[rows, :] + mirror_ref[rows, :] * incident
        for d in range(copies_ref.shape[0]):
            copies_ref[d, rows, :] = radiosity


def middle(parts, emitted, mirror):
    return pl.pallas_call(
        middle_kernel,
        out_shape=jax.ShapeDtypeStruct(parts.shape, jnp.float32),
        compiler_params=params(64),
        cost_estimate=cost(100_000, 600_000),
        name="middle",
    )(parts, emitted, mirror)


def last_kernel(scale, parts_ref, emitted_ref, mirror_ref, site_ref, rad_ref, source_ref):
    blocks = emitted_ref.shape[0]
    incident = sum_parts(parts_ref, slice(None))
    emitted = emitted_ref[...]
    mirror = mirror_ref[...]
    rad_ref[...] = emitted + mirror * incident
    absorbed = ((1.0 - mirror) * incident - emitted) * scale
    site = site_ref[...]
    lane = site & (LANES - 1)
    sheet = site >> 7
    sheets = source_ref.shape[1]
    sheet_iota = lax.broadcasted_iota(jnp.int32, (sheets, BLK), 0)
    lane_iota = lax.broadcasted_iota(jnp.int32, (LANES, BLK), 0)
    left = []
    right = []
    for b in range(blocks):
        here = jnp.where(sheet_iota == sheet[b : b + 1, :], absorbed[b : b + 1, :], 0.0)
        left.append(here)
        pick = jnp.where(lane_iota == lane[b : b + 1, :], 1.0, 0.0)
        right.append(pick.astype(jnp.bfloat16))
    left = jnp.concatenate(left, axis=1)
    right = jnp.concatenate(right, axis=1)
    source = jnp.zeros((sheets, LANES), jnp.float32)
    for part in parts_of(left, 3):
        source = source + lax.dot_general(part, right, NT, preferred_element_type=jnp.float32)
    for d in range(source_ref.shape[0]):
        source_ref[d] = source


def last(parts, emitted, mirror, site, cells, count):
    weight = cells / (mirror.shape[0] * BLK * 1.0)
    return pl.pallas_call(
        functools.partial(last_kernel, step_size * weight),
        out_shape=(
            jax.ShapeDtypeStruct(mirror.shape, jnp.float32),
            jax.ShapeDtypeStruct((count, cells // LANES, LANES), jnp.float32),
        ),
        compiler_params=params(64),
        cost_estimate=cost(10_000_000, 600_000),
        name="last",
    )(parts, emitted, mirror, site)


def pack_y_kernel(t0, k0, t7, k7, down_ref, up_ref):
    upper = lax.broadcasted_iota(jnp.int32, down_ref.shape[1:], 0) < ROWS
    for x in range(down_ref.shape[0]):
        down_ref[x] = jnp.where(upper, t0[x], pltpu.roll(k0[x], ROWS, 0))
        up_ref[x] = jnp.where(upper, pltpu.roll(t7[x], ROWS, 0), k7[x])


def pack_y(temp, cond):
    nx, ny, nz = temp.shape
    first = pl.BlockSpec((nx, 8, nz), lambda i: (0, 0, 0))
    final = pl.BlockSpec((nx, 8, nz), lambda i: (0, ny // 8 - 1, 0))
    shape = jax.ShapeDtypeStruct((nx, 8, nz), jnp.float32)
    return pl.pallas_call(
        pack_y_kernel,
        grid=(1,),
        out_shape=(shape, shape),
        in_specs=[first, first, final, final],
        out_specs=(first, first),
        compiler_params=params(64),
        cost_estimate=cost(0, 4 * nx * 8 * nz * 4),
        name="pack_y",
    )(temp, cond, temp, cond)


def mixed_tile(t_tile, k_tile):
    row = lax.broadcasted_iota(jnp.int32, t_tile.shape, 0)
    of_k = jnp.where(row < 4, pltpu.roll(k_tile, 2, 0), pltpu.roll(k_tile, 6, 0))
    return jnp.where((row < 2) | (row >= 6), t_tile, of_k)


def unmixed(tile):
    row = lax.broadcasted_iota(jnp.int32, tile.shape, 0)
    outer = (row < 2) | (row >= 6)
    of_k = jnp.where(row < 4, pltpu.roll(tile, 6, 0), pltpu.roll(tile, 2, 0))
    return jnp.where(outer, tile, 0.0), jnp.where(outer, of_k, 0.0)


def pack_x_kernel(first, final, below0, above0, below1, above1, low_ref, high_ref):
    ny, nz = first.shape[1:]
    upper = lax.broadcasted_iota(jnp.int32, (8, nz), 0) < ROWS
    tail = HALO * ny
    for send, temp, below, above, order in (
        (low_ref, first, below0, above0, (0, 1, 2)),
        (high_ref, final, below1, above1, (HALO - 1, HALO - 2, HALO - 3)),
    ):
        for p in range(HALO):
            send[p * ny : (p + 1) * ny, :] = temp[p]
        for k, p in enumerate(order):
            t_tile = jnp.where(upper, above[p], pltpu.roll(below[p], ROWS, 0))
            k_tile = jnp.where(upper, pltpu.roll(above[p], ROWS, 0), below[p])
            if k == 0:
                send[tail : tail + 8, :] = t_tile
                send[tail + 8 : tail + 16, :] = k_tile
            else:
                at = tail + 8 + 8 * k
                send[at : at + 8, :] = mixed_tile(t_tile, k_tile)


def pack_x(temp, below, above):
    nx, ny, nz = temp.shape

    def ends(rows):
        return (
            pl.BlockSpec((HALO, rows, nz), lambda i: (0, 0, 0)),
            pl.BlockSpec((HALO, rows, nz), lambda i: (nx // HALO - 1, 0, 0)),
        )

    first, final = ends(ny)
    first_rows, final_rows = ends(8)
    rows = HALO * ny + 32
    whole = pl.BlockSpec((rows, nz), lambda i: (0, 0))
    shape = jax.ShapeDtypeStruct((rows, nz), jnp.float32)
    return pl.pallas_call(
        pack_x_kernel,
        grid=(1,),
        out_shape=(shape, shape),
        in_specs=[first, final, first_rows, first_rows, final_rows, final_rows],
        out_specs=(whole, whole),
        compiler_params=params(64),
        cost_estimate=cost(0, 4 * rows * nz * 4),
        name="pack_x",
    )(temp, temp, below, above, below, above)


def coupling(a, b):
    return jnp.where(jnp.minimum(a, b) > 0.0, (0.5 * step_size) * (a + b), 0.0)


def neighbours():
    slab, pair = lax.axis_index("slab"), lax.axis_index("pair")
    return slab > 0, slab < lax.axis_size("slab") - 1, pair > 0, pair < lax.axis_size("pair") - 1


def lane_tiles(nz):
    return [slice(j * LANES, (j + 1) * LANES) for j in range(nz // LANES)]


def one_step(field, cond, gz, begin, end, target):
    wide, nz = field.shape[1:]
    tiles = wide // 8
    spans = lane_tiles(nz)
    count = len(spans)
    lane = lax.broadcasted_iota(jnp.int32, (8, LANES), 1)
    sub = lax.broadcasted_iota(jnp.int32, (8, LANES), 0)
    _, _, has_below, has_above = neighbours()
    keep_above = (sub < 7) | has_above
    keep_below = (sub < 7) | has_below

    def row_tile(ref, x, t):
        return [ref[x, 8 * t : 8 * t + 8, z] for z in spans]

    def first_rolled(ref, x):
        return [pltpu.roll(v, 7, 0) for v in row_tile(ref, x, 0)]

    def y_flux(t_now, k_now, t_next, k_next):
        return [
            (k_now[j] + k_next[j]) * (t_next[j] - t_now[j]) for j in range(count)
        ]

    def z_change(x, t, t_now, k_now):
        turned = [pltpu.roll(v, LANES - 1, 1) for v in t_now]
        flux = []
        for j, z in enumerate(spans):
            deep = turned[j + 1] if j + 1 < count else 0.0
            deep = jnp.where(lane < LANES - 1, turned[j], deep)
            flux.append(gz[x, 8 * t : 8 * t + 8, z] * (deep - t_now[j]))
        back = [pltpu.roll(f, 1, 1) for f in flux]
        out = []
        for j in range(count):
            low = back[j - 1] if j else (k_now[0] + k_now[0]) * t_now[0]
            out.append(flux[j] - jnp.where(lane > 0, back[j], low))
        return out

    @pl.loop(begin, end)
    def _(x):
        stores = Lagging(LAG)
        final = y_flux(
            row_tile(field, x, tiles - 1),
            row_tile(cond, x, tiles - 1),
            first_rolled(field, x),
            first_rolled(cond, x),
        )
        low_y = [pltpu.roll(f, 1, 0) for f in final]
        t_now, k_now = row_tile(field, x, 0), row_tile(cond, x, 0)
        for t in range(tiles):
            rows = slice(8 * t, 8 * t + 8)
            if t + 1 < tiles:
                t_next, k_next = row_tile(field, x, t + 1), row_tile(cond, x, t + 1)
            else:
                t_next, k_next = first_rolled(field, x), first_rolled(cond, x)
            high_y = y_flux(t_now, k_now, t_next, k_next)
            change_z = z_change(x, t, t_now, k_now)
            for j, z in enumerate(spans):
                now, here = t_now[j], k_now[j]
                high_x = (here + cond[x + 1, rows, z]) * (field[x + 1, rows, z] - now)
                low_x = (here + cond[x - 1, rows, z]) * (now - field[x - 1, rows, z])
                new = now + (high_x - low_x) + (high_y[j] - low_y[j]) + change_z[j]
                if t:
                    new = jnp.where(keep_above if t <= ROWS else keep_below, new, 0.0)
                stores.add(put(*target(x, t, z), new))
            low_y, t_now, k_now = high_y, t_next, k_next
        stores.finish()


def thin_planes(cond, ny, store):
    tall, _, wide, _ = cond.shape
    lane = lax.broadcasted_iota(jnp.int32, (wide, LANES), 1)
    y_lane = lax.broadcasted_iota(jnp.int32, (8, LANES), 1)
    for base in range(0, tall, 16):
        planes = min(16, tall - base)
        gathered = jnp.zeros((wide, LANES), jnp.float32)
        for g in range(planes):
            piece = cond[base + g, 0]
            if g:
                piece = pltpu.roll(piece, 8 * g, 1)
            gathered = jnp.where((lane >> 3) == g, piece, gathered)
        turned = jnp.concatenate(
            [gathered, jnp.zeros((LANES - wide, LANES), jnp.float32)], axis=0
        ).T
        for g in range(planes):
            rows = turned[8 * g : 8 * g + 8, :]
            moved = pltpu.roll(rows, LANES - wide, 1)
            store(
                base + g,
                jnp.where(
                    y_lane < ny + ROWS, rows, jnp.where(y_lane >= LANES - ROWS, moved, 0.0)
                ),
            )


def mirror_rows(raw_k, ny):
    _, _, has_below, has_above = neighbours()
    upper = lax.broadcasted_iota(jnp.int32, (8, LANES), 0) < ROWS

    @pl.when(jnp.logical_not(has_above & has_below))
    def _():
        missing = (upper & jnp.logical_not(has_above)) | (
            jnp.logical_not(upper) & jnp.logical_not(has_below)
        )

        @pl.loop(0, raw_k.shape[0])
        def _(x):
            for j in range(raw_k.shape[1]):
                edge = raw_k[x, j, ny:]
                last = jnp.broadcast_to(raw_k[x, j, ny - 1 : ny, :], edge.shape)
                first = jnp.broadcast_to(raw_k[x, j, 0:1, :], edge.shape)
                raw_k[x, j, ny:] = jnp.where(missing, jnp.where(upper, last, first), edge)


def lay_out_k(loaded, place, faces, gz):
    planes, count, wide, _ = loaded.shape[1:]
    tiles = wide // 8
    spans = lane_tiles(count * LANES)
    lane = lax.broadcasted_iota(jnp.int32, (8, LANES), 1)

    @pl.loop(0, planes)
    def _(x):
        stores = Lagging(LAG)
        to = place(x)
        for t in range(tiles):
            rows = pl.ds(t, 8, stride=tiles)
            kept = slice(8 * t, 8 * t + 8)
            here = [(0.5 * step_size) * loaded[1, x, j, rows, :] for j in range(count)]
            turned = [pltpu.roll(v, LANES - 1, 1) for v in here]
            for j, z in enumerate(spans):
                deep = turned[j + 1] if j + 1 < count else here[j]
                deep = jnp.where(lane < LANES - 1, turned[j], deep)
                stores.add(put(faces, (to, kept, z), here[j]))
                stores.add(put(gz, (to, kept, z), here[j] + deep))
        stores.finish()


def lay_out_t(loaded, place, field):
    planes, count, wide, _ = loaded.shape[1:]
    tiles = wide // 8
    spans = lane_tiles(count * LANES)

    @pl.loop(0, planes)
    def _(x):
        stores = Lagging(LAG)
        to = place(x)
        for t in range(tiles):
            rows = pl.ds(t, 8, stride=tiles)
            for j, z in enumerate(spans):
                stores.add(put(field, (to, slice(8 * t, 8 * t + 8), z), loaded[0, x, j, rows, :]))
        stores.finish()


def fetch(loaded, which, ref, source_row, at, row, rows, sems):
    planes, count = ref.shape[0], loaded.shape[2]
    return [
        pltpu.make_async_copy(
            ref.at[:, pl.ds(source_row, rows), pl.ds(j * LANES, LANES)],
            loaded.at[which, pl.ds(at, planes), j, pl.ds(row, rows)],
            sems.at[j],
        )
        for j in range(count)
    ]


def own_planes_kernel(
    t_ref, k_ref, below_ref, above_ref, field, faces, gz, thin_ref, loaded, sems
):
    nx, ny, nz = t_ref.shape
    raw_t, raw_k = loaded.at[0], loaded.at[1]
    k_copies = fetch(loaded, 1, k_ref, 0, 0, 0, ny, sems.at[1])
    t_copies = fetch(loaded, 0, t_ref, 0, 0, 0, ny, sems.at[0])
    for copy in k_copies + t_copies:
        copy.start()
    upper = lax.broadcasted_iota(jnp.int32, (8, LANES), 0) < ROWS

    @pl.loop(0, nx)
    def _(x):
        for j, z in enumerate(lane_tiles(nz)):
            down, up = above_ref[x, :, z], below_ref[x, :, z]
            raw_t[x, j, ny:] = jnp.where(upper, down, pltpu.roll(up, ROWS, 0))
            raw_k[x, j, ny:] = jnp.where(upper, pltpu.roll(down, ROWS, 0), up)

    for copy in k_copies:
        copy.wait()
    thin_planes(raw_k, ny, lambda x, v: thin_ref.__setitem__(x, v))
    mirror_rows(raw_k, ny)
    lay_out_k(loaded, lambda x: x, faces, gz)
    for copy in t_copies:
        copy.wait()
    lay_out_t(loaded, lambda x: x, field)


def own_planes(temp, cond, below, above):
    nx, ny, nz = temp.shape
    wide = ny + 2 * ROWS
    hbm = pl.BlockSpec(memory_space=pl.ANY)
    vmem = pl.BlockSpec(memory_space=pltpu.VMEM)
    shape = jax.ShapeDtypeStruct((nx, wide, nz), jnp.float32)
    return pl.pallas_call(
        own_planes_kernel,
        out_shape=(shape, shape, shape, jax.ShapeDtypeStruct((nx, 8, LANES), jnp.float32)),
        in_specs=[hbm, hbm, vmem, vmem],
        scratch_shapes=[
            pltpu.VMEM((2, nx, nz // LANES, wide, LANES), jnp.float32),
            pltpu.SemaphoreType.DMA((2, nz // LANES)),
        ],
        compiler_params=params(64),
        cost_estimate=cost(nx * wide * nz * 10, 6 * nx * wide * nz * 4),
        name="own_planes",
    )(temp, cond, below, above)


def heat_kernel(
    own_field, own_faces, own_gz, own_thin, k_low, k_high, t_low, t_high, out_ref, thin_ref,
    loaded, corners, field, between, faces, gz, placed, sems, own_sems, out_sems,
):
    nx, wide, nz = own_field.shape
    ny = wide - 2 * ROWS
    tall = nx + 2 * HALO
    tiles = wide // 8
    spans = lane_tiles(nz)
    k_copies, t_copies = [], []
    for k, (k_side, t_side) in enumerate(((k_low, t_low), (k_high, t_high))):
        at = k * HALO
        k_copies += fetch(loaded, 1, k_side, 0, at, 0, ny, sems.at[3 * k])
        k_copies.append(
            pltpu.make_async_copy(
                t_side.at[pl.ds(HALO * ny, 32)], corners.at[k], own_sems.at[3 + k]
            )
        )
        for p in range(HALO):
            t_copies += [
                pltpu.make_async_copy(
                    t_side.at[pl.ds(p * ny, ny), pl.ds(j * LANES, LANES)],
                    loaded.at[0, at + p, j, pl.ds(0, ny)],
                    sems.at[3 * (k + 1) - 1 + 6 * p, j],
                )
                for j in range(len(spans))
            ]
    own = [
        pltpu.make_async_copy(ref, whole.at[pl.ds(HALO, nx)], own_sems.at[k])
        for k, (ref, whole) in enumerate(
            ((own_faces, faces), (own_gz, gz), (own_field, field))
        )
    ]
    for copy in k_copies + t_copies + own:
        copy.start()
    has_low, has_high, _, _ = neighbours()

    def place(x):
        return jnp.where(x < HALO, x, x + nx)

    def store_thin(x, value):
        thin_ref[x if x < HALO else x + nx] = value

    thin_ref[HALO : HALO + nx] = own_thin[...]
    raw_t, raw_k = loaded.at[0], loaded.at[1]
    for copy in k_copies:
        copy.wait()
    for k, order in enumerate(
        ((HALO - 1, HALO - 2, HALO - 3, 0), (HALO, HALO + 1, HALO + 2, 2 * HALO - 1))
    ):
        for distance, p in enumerate(order):
            for j, z in enumerate(spans):
                if distance == 0:
                    t_tile, k_tile = corners[k, :8, z], corners[k, 8:16, z]
                elif distance + 1 < HALO:
                    t_tile, k_tile = unmixed(corners[k, 8 + 8 * distance : 16 + 8 * distance, z])
                else:
                    t_tile = k_tile = jnp.zeros((8, LANES), jnp.float32)
                raw_t[p, j, ny:] = t_tile
                raw_k[p, j, ny:] = k_tile
    thin_planes(raw_k, ny, store_thin)
    mirror_rows(raw_k, ny)
    lay_out_k(loaded, place, faces, gz)
    for copy in t_copies:
        copy.wait()
    lay_out_t(loaded, place, field)
    for copy in own:
        copy.wait()

    @pl.when(jnp.logical_not(has_low))
    def _():
        faces[HALO - 1] = faces[HALO]

    @pl.when(jnp.logical_not(has_high))
    def _():
        faces[HALO + nx] = faces[HALO + nx - 1]

    def inside(target):
        return lambda x, t, z: (target, (x, slice(8 * t, 8 * t + 8), z))

    def outside(x, t, z):
        return placed, (x - HALO, z.start // LANES, pl.ds(t, 8, stride=tiles))

    old, new = field, between
    for step in range(1, STEPS):
        one_step(old, faces, gz, step, tall - step, inside(new))
        for x, there in ((HALO - 1, has_low), (HALO + nx, has_high)):

            @pl.when(jnp.logical_not(there))
            def _():
                new[x] = jnp.zeros((wide, nz), jnp.float32)

        old, new = new, old
    results = []
    for part, begin in enumerate((0, nx // 2)):
        planes = nx // 2
        one_step(old, faces, gz, HALO + begin, HALO + begin + planes, outside)
        for j in range(len(spans)):
            copy = pltpu.make_async_copy(
                placed.at[pl.ds(begin, planes), j, pl.ds(0, ny)],
                out_ref.at[pl.ds(begin, planes), :, pl.ds(j * LANES, LANES)],
                out_sems.at[part, j],
            )
            copy.start()
            results.append(copy)
    for copy in results:
        copy.wait()


def heat(own, k_low, k_high, t_low, t_high, shape):
    nx, ny, nz = shape
    tall, wide = nx + 2 * HALO, ny + 2 * ROWS
    hbm = pl.BlockSpec(memory_space=pl.ANY)
    vmem = pl.BlockSpec(memory_space=pltpu.VMEM)
    big = pltpu.VMEM((tall, wide, nz), jnp.float32)
    return pl.pallas_call(
        heat_kernel,
        out_shape=(
            jax.ShapeDtypeStruct(shape, jnp.float32),
            jax.ShapeDtypeStruct((tall, 8, LANES), jnp.float32),
        ),
        in_specs=[hbm] * 3 + [vmem] + [hbm] * 4,
        out_specs=(hbm, vmem),
        scratch_shapes=[
            pltpu.VMEM((2, 2 * HALO, nz // LANES, wide, LANES), jnp.float32),
            pltpu.VMEM((2, 32, nz), jnp.float32),
            big,
            big,
            big,
            big,
            pltpu.VMEM((nx, nz // LANES, wide, LANES), jnp.float32),
            pltpu.SemaphoreType.DMA((6 * HALO, nz // LANES)),
            pltpu.SemaphoreType.DMA((5,)),
            pltpu.SemaphoreType.DMA((2, nz // LANES)),
        ],
        compiler_params=params(64),
        cost_estimate=cost(tall * wide * nz * 100, 12 * nx * ny * nz * 4),
        name="heat",
    )(*own, k_low, k_high, t_low, t_high)


def source_kernel(ny, all_ref, thin_ref, base_ref, out_ref):
    tall = thin_ref.shape[0]
    nx = tall - 2 * HALO
    sheets = all_ref.shape[1]
    sub = lax.broadcasted_iota(jnp.int32, (8, LANES), 0)
    y_lane = lax.broadcasted_iota(jnp.int32, (8, LANES), 1)

    slabs, pairs = lax.axis_size("slab"), lax.axis_size("pair")

    def sheet(down, across):
        slab = lax.axis_index("slab") + down
        pair = lax.axis_index("pair") + across
        inside = (slab >= 0) & (slab < slabs) & (pair >= 0) & (pair < pairs)
        found = all_ref[jnp.where(inside, slab * pairs + pair, 0)]
        return jnp.where(inside, found, 0.0)

    def rows_of(down):
        low, own, high = (sheet(down, across) for across in (-1, 0, 1))
        out = []
        for half in range(2):
            if half == 0:
                own_at, high_at, low_at = own, pltpu.roll(high, ny, 1), pltpu.roll(low, ny, 1)
            else:
                own_at, high_at, low_at = pltpu.roll(own, ny, 1), high, low
            out.append(
                jnp.where(
                    y_lane < ny,
                    own_at,
                    jnp.where(
                        y_lane < ny + HALO,
                        high_at,
                        jnp.where(y_lane >= LANES - HALO, low_at, 0.0),
                    ),
                )
            )
        return out

    lines = [rows_of(down) for down in (-1, 0, 1)]
    source = []
    for x in range(-HALO, nx + HALO):
        which, local = (x + nx) // nx, x % nx
        row = lines[which][local % 2][local // 2 : local // 2 + 1, :]
        source.append(jnp.where(sub == 0, jnp.broadcast_to(row, (8, LANES)), 0.0))

    cond = [thin_ref[x] for x in range(tall)]
    cx, cy, cz, centre = [], [], [], []
    for x in range(tall):
        here = cond[x]
        after = cond[min(x + 1, tall - 1)]
        before = cond[max(x - 1, 0)]
        y_after = pltpu.roll(here, LANES - 1, 1)
        y_before = pltpu.roll(here, 1, 1)
        z_after = jnp.where(sub == 7, 0.0, pltpu.roll(here, 7, 0))
        z_before = jnp.where(sub == 0, 0.0, pltpu.roll(here, 1, 0))
        cx.append(coupling(here, after))
        cy.append(coupling(here, y_after))
        cz.append(coupling(here, z_after))
        total = 6.0 * here
        for near in (after, before, y_after, y_before, z_after, z_before):
            total = total + jnp.where(near > 0.0, near, here)
        centre.append(1.0 - (0.5 * step_size) * total)

    added = source
    for step in range(1, STEPS):
        new = list(added)
        for x in range(step, tall - step):
            here = added[x]
            total = source[x] + centre[x] * here
            total = total + (cx[x] * added[x + 1] + cx[x - 1] * added[x - 1])
            total = total + cy[x] * pltpu.roll(here, LANES - 1, 1)
            total = total + pltpu.roll(cy[x] * here, 1, 1)
            total = total + cz[x] * pltpu.roll(here, 7, 0)
            new[x] = total + pltpu.roll(cz[x] * here, 1, 0)
        added = new

    lane = lax.broadcasted_iota(jnp.int32, (ny, LANES), 1)
    turned = jnp.concatenate(added[HALO : HALO + nx], axis=0).T[:ny]
    for x in range(nx):
        piece = turned if x == 0 else pltpu.roll(turned, LANES - 8 * x, 1)
        out_ref[x] = base_ref[x] + jnp.where(lane < STEPS, piece, 0.0)


def add_source(everything, thin, base):
    nx, ny, nz = base.shape
    block = pl.BlockSpec((nx, ny, LANES), lambda i: (0, 0, 0))
    return pl.pallas_call(
        functools.partial(source_kernel, ny),
        grid=(1,),
        out_shape=jax.ShapeDtypeStruct(base.shape, jnp.float32),
        in_specs=[
            pl.BlockSpec(everything.shape, lambda i: (0, 0, 0)),
            pl.BlockSpec(thin.shape, lambda i: (0, 0, 0)),
            block,
        ],
        out_specs=block,
        input_output_aliases={2: 0},
        compiler_params=params(64),
        cost_estimate=cost(1_000_000, 2 * nx * ny * LANES * 4),
        name="add_source",
    )(everything, thin, base)


def exchange(rows):
    return lax.all_to_all(rows, ("slab", "pair"), split_axis=0, concat_axis=0, tiled=True)


def together(*arrays):
    return lax.optimization_barrier(arrays)


def both_ways(low, high, axis):
    count = lax.axis_size(axis)
    forward = [(i, i + 1) for i in range(count - 1)]
    backward = [(target, source) for source, target in forward]
    from_low = lax.ppermute(high, axis, forward)
    from_high = lax.ppermute(low, axis, backward)
    return from_low, from_high


def shards(
    initial_warmth,
    heat_passing_coefficient,
    mirror_fraction,
    element_facing_site,
    tile_block_couples,
    active_slot_count,
    view_factor_blocks,
):
    nx, ny, _ = initial_warmth.shape
    slabs, pairs = lax.axis_size("slab"), lax.axis_size("pair")
    count = slabs * pairs
    blocks = mirror_fraction.shape[0]
    couples = tile_block_couples.T

    temp, cond = initial_warmth, heat_passing_coefficient
    emitted, copies = emit(temp, element_facing_site, mirror_fraction, count)
    temp, copies = together(temp, copies)

    def sweep_terms(whole):
        whole = whole.reshape(count * blocks, BLK)
        term = tile_terms(whole, couples, active_slot_count, view_factor_blocks)
        return term.reshape(count, blocks, BLK)

    whole = exchange(copies)
    cond, copies = together(cond, copies)
    send_low, send_high = cond[:HALO], cond[nx - HALO :]
    k_low, k_high = both_ways(send_low, send_high, "slab")
    whole = together(whole, send_low, send_high)[0]
    temp, cond, term = together(temp, cond, sweep_terms(whole))
    parts = exchange(term)
    below, above = both_ways(*pack_y(temp, cond), "pair")
    parts, below, above, k_low, k_high = together(parts, below, above, k_low, k_high)
    copies, below, above = together(middle(parts, emitted, mirror_fraction), below, above)
    whole = exchange(copies)
    send_low, send_high = pack_x(temp, below, above)
    t_low, t_high = both_ways(send_low, send_high, "slab")
    whole = together(whole, send_low, send_high)[0]
    temp, cond, term = together(temp, cond, sweep_terms(whole))
    parts = exchange(term)
    own = own_planes(temp, cond, below, above)
    parts, t_low, t_high, own = together(parts, t_low, t_high, own)
    radiosity, source = last(parts, emitted, mirror_fraction, element_facing_site, nx * ny, count)
    everything = exchange(source)
    own, source = together(own, source)
    base, thin = heat(own, k_low, k_high, t_low, t_high, temp.shape)

    warmed_liner = add_source(everything, thin, base)
    return (radiosity, warmed_liner)


def solution(mesh):
    return jax.shard_map(
        shards,
        mesh=mesh,
        in_specs=(
            P("slab", "pair", None),
            P("slab", "pair", None),
            P(("slab", "pair"), None),
            P(("slab", "pair"), None),
            P(("slab", "pair"), None),
            P(("slab", "pair")),
            P(("slab", "pair"), None, None),
        ),
        out_specs=(P(("slab", "pair"), None), P("slab", "pair", None)),
        check_vma=False,
    )
```

```python
import functools

import jax
import jax.numpy as jnp
from jax import lax
from jax.experimental import pallas as pl
from jax.experimental.pallas import tpu as pltpu
from jax.sharding import PartitionSpec as P

BLK = 128
SWEEPS = 2
STEPS = 4
HALO = STEPS
ROWS = STEPS
LANES = 128
CHUNK = 16
LAG = 8

step_size = 0.07

NT = (((1,), (1,)), ((), ()))
NN = (((1,), (0,)), ((), ()))


def params(mib):
    return pltpu.CompilerParams(vmem_limit_bytes=mib * 1024 * 1024)


def cost(flops, nbytes):
    return pl.CostEstimate(flops=flops, bytes_accessed=nbytes, transcendentals=0)


def parts_of(x, count):
    out = []
    for _ in range(count - 1):
        part = x.astype(jnp.bfloat16)
        out.append(part)
        x = x - part.astype(jnp.float32)
    out.append(x.astype(jnp.bfloat16))
    return out


class Lagging:
    def __init__(self, depth):
        self.depth = depth
        self.waiting = []

    def add(self, store):
        self.waiting.append(store)
        if len(self.waiting) > self.depth:
            self.waiting.pop(0)()

    def finish(self):
        for store in self.waiting:
            store()
        self.waiting = []


def put(ref, index, value):
    return lambda: ref.__setitem__(index, value)


def emit_kernel(temp_ref, site_ref, mirror_ref, emitted_ref, copies_ref):
    nx, ny, _ = temp_ref.shape
    sheets = nx * ny // LANES
    per = LANES // ny
    lanes = lax.broadcasted_iota(jnp.int32, (LANES, LANES), 1)
    gathered = jnp.zeros((LANES, LANES), jnp.float32)
    for r in range(sheets):
        piece = temp_ref[per * r : per * r + per].reshape(LANES, LANES)
        if r:
            piece = pltpu.roll(piece, r, 1)
        gathered = jnp.where(lanes == r, piece, gathered)
    plane = gathered.T[:sheets]
    for half in range(site_ref.shape[0] // 8):
        rows = pl.ds(half * 8, 8)
        site = site_ref[rows, :]
        lane = site & (LANES - 1)
        sheet = site >> 7
        warmth = jnp.zeros(site.shape, jnp.float32)
        for r in range(sheets):
            line = jnp.broadcast_to(plane[r : r + 1, :], site.shape)
            picked = jnp.take_along_axis(line, lane, axis=1)
            warmth = jnp.where(sheet == r, picked, warmth)
        square = warmth * warmth
        emitted = (1.0 - mirror_ref[rows, :]) * (square * square)
        emitted_ref[rows, :] = emitted
        for d in range(copies_ref.shape[0]):
            copies_ref[d, rows, :] = emitted


def emit(temp, site, mirror, count):
    shape = mirror.shape
    nx, ny, _ = temp.shape
    patch = pl.BlockSpec(shape, lambda i: (0, 0))
    return pl.pallas_call(
        emit_kernel,
        grid=(1,),
        out_shape=(
            jax.ShapeDtypeStruct(shape, jnp.float32),
            jax.ShapeDtypeStruct((count,) + shape, jnp.float32),
        ),
        in_specs=[pl.BlockSpec((nx, ny, LANES), lambda i: (0, 0, 0)), patch, patch],
        out_specs=(patch, pl.BlockSpec((count,) + shape, lambda i: (0, 0, 0))),
        compiler_params=params(64),
        cost_estimate=cost(10_000, 900_000),
        name="emit",
    )(temp, site, mirror)


def tiles_kernel(
    live_ref, pairs_ref, lanes_ref, whole_ref, tiles_ref, out_ref, held, terms, sems
):
    slots = held.shape[0]
    live = live_ref[0]
    chunks = (live + CHUNK - 1) // CHUNK

    def chunk_copy(c):
        span = pl.ds(c * CHUNK, CHUNK)
        return pltpu.make_async_copy(tiles_ref.at[span], held.at[span], sems.at[c])

    @pl.loop(0, chunks)
    def _(c):
        chunk_copy(c).start()

    top = lax.broadcasted_iota(jnp.int32, (8, BLK), 0) == 0

    def split_row(block):
        row = jnp.broadcast_to(whole_ref[pl.ds(block, 1), :], (8, BLK))
        high = row.astype(jnp.bfloat16).astype(jnp.float32)
        return jnp.where(top, high, row - high)

    def vectors(a, b):
        stacked = jnp.concatenate([split_row(a), split_row(b)], axis=0)
        stacked = stacked.astype(jnp.bfloat16)
        return jnp.concatenate([stacked, stacked], axis=1)

    @pl.loop(0, chunks)
    def _(c):
        chunk_copy(c).wait()
        stores = Lagging(4 * CHUNK)
        for u in range(0, CHUNK, 2):
            t = c * CHUNK + u
            high_a, low_a = parts_of(held[t], 2)
            high_b, low_b = parts_of(held[t + 1], 2)
            both = jnp.concatenate(
                [
                    jnp.concatenate([high_a, high_b], axis=1),
                    jnp.concatenate([low_a, low_b], axis=1),
                ],
                axis=0,
            )
            second = lax.dot_general(
                vectors(pairs_ref[0, t], pairs_ref[0, t + 1]),
                both,
                NN,
                preferred_element_type=jnp.float32,
            )
            turned = jnp.concatenate(
                [
                    jnp.concatenate([high_a, low_a], axis=1),
                    jnp.concatenate([high_b, low_b], axis=1),
                ],
                axis=0,
            )
            first = lax.dot_general(
                vectors(pairs_ref[1, t], pairs_ref[1, t + 1]),
                turned,
                NT,
                preferred_element_type=jnp.float32,
            )
            for side, result in ((0, first), (1, second)):
                for v, (top_row, cols) in enumerate(((0, slice(0, BLK)), (8, slice(BLK, 2 * BLK)))):
                    row = result[top_row : top_row + 1, cols] + result[top_row + 1 : top_row + 2, cols]
                    stores.add(put(terms, (side, pl.ds(t + v, 1)), row))
        stores.finish()

    used = lax.broadcasted_iota(jnp.int32, (slots, BLK), 0) < live
    used_lane = lax.broadcasted_iota(jnp.int32, (1, slots), 1) < live
    blocks = out_ref.shape[0]
    group = min(blocks, 512)
    split = []
    for side in range(2):
        masked = jnp.where(used, terms[side], 0.0)
        split.append(jnp.concatenate(parts_of(masked, 2), axis=1))
    for base in range(0, blocks, group):
        rows = lax.broadcasted_iota(jnp.int32, (group, slots), 0) + base
        total = jnp.zeros((group, 2 * BLK), jnp.float32)
        for side in range(2):
            target = jnp.where(used_lane, lanes_ref[side : side + 1, :], -1)
            choose = jnp.where(rows == target, 1.0, 0.0).astype(jnp.bfloat16)
            total = total + jnp.dot(choose, split[side], preferred_element_type=jnp.float32)
        out_ref[base : base + group, :] = total[:, :BLK] + total[:, BLK:]


def tile_terms(whole, couples, live, tiles):
    slots = tiles.shape[0]
    smem = pl.BlockSpec(memory_space=pltpu.SMEM)
    vmem = pl.BlockSpec(memory_space=pltpu.VMEM)
    return pl.pallas_call(
        tiles_kernel,
        out_shape=jax.ShapeDtypeStruct(whole.shape, jnp.float32),
        in_specs=[smem, smem, vmem, vmem, pl.BlockSpec(memory_space=pl.ANY)],
        out_specs=vmem,
        scratch_shapes=[
            pltpu.VMEM(tiles.shape, jnp.float32),
            pltpu.VMEM((2, slots, BLK), jnp.float32),
            pltpu.SemaphoreType.DMA((slots // CHUNK,)),
        ],
        compiler_params=params(64),
        cost_estimate=cost(slots * BLK * BLK * 32, slots * BLK * BLK * 4),
        name="tiles",
    )(live, couples, couples, whole, tiles)


def sum_parts(parts_ref, rows):
    total = parts_ref[0, rows, :]
    for d in range(1, parts_ref.shape[0]):
        total = total + parts_ref[d, rows, :]
    return total


def middle_kernel(parts_ref, emitted_ref, mirror_ref, copies_ref):
    for half in range(emitted_ref.shape[0] // 8):
        rows = pl.ds(half * 8, 8)
        incident = sum_parts(parts_ref, rows)
        radiosity = emitted_ref[rows, :] + mirror_ref[rows, :] * incident
        for d in range(copies_ref.shape[0]):
            copies_ref[d, rows, :] = radiosity


def middle(parts, emitted, mirror):
    return pl.pallas_call(
        middle_kernel,
        out_shape=jax.ShapeDtypeStruct(parts.shape, jnp.float32),
        compiler_params=params(64),
        cost_estimate=cost(100_000, 600_000),
        name="middle",
    )(parts, emitted, mirror)


def last_kernel(scale, parts_ref, emitted_ref, mirror_ref, site_ref, rad_ref, source_ref):
    blocks = emitted_ref.shape[0]
    incident = sum_parts(parts_ref, slice(None))
    emitted = emitted_ref[...]
    mirror = mirror_ref[...]
    rad_ref[...] = emitted + mirror * incident
    absorbed = ((1.0 - mirror) * incident - emitted) * scale
    site = site_ref[...]
    lane = site & (LANES - 1)
    sheet = site >> 7
    sheets = source_ref.shape[1]
    sheet_iota = lax.broadcasted_iota(jnp.int32, (sheets, BLK), 0)
    lane_iota = lax.broadcasted_iota(jnp.int32, (LANES, BLK), 0)
    left = []
    right = []
    for b in range(blocks):
        here = jnp.where(sheet_iota == sheet[b : b + 1, :], absorbed[b : b + 1, :], 0.0)
        left.append(here)
        pick = jnp.where(lane_iota == lane[b : b + 1, :], 1.0, 0.0)
        right.append(pick.astype(jnp.bfloat16))
    left = jnp.concatenate(left, axis=1)
    right = jnp.concatenate(right, axis=1)
    source = jnp.zeros((sheets, LANES), jnp.float32)
    for part in parts_of(left, 3):
        source = source + lax.dot_general(part, right, NT, preferred_element_type=jnp.float32)
    for d in range(source_ref.shape[0]):
        source_ref[d] = source


def last(parts, emitted, mirror, site, cells, count):
    weight = cells / (mirror.shape[0] * BLK * 1.0)
    return pl.pallas_call(
        functools.partial(last_kernel, step_size * weight),
        out_shape=(
            jax.ShapeDtypeStruct(mirror.shape, jnp.float32),
            jax.ShapeDtypeStruct((count, cells // LANES, LANES), jnp.float32),
        ),
        compiler_params=params(64),
        cost_estimate=cost(10_000_000, 600_000),
        name="last",
    )(parts, emitted, mirror, site)


def pack_y_kernel(t0, k0, t7, k7, down_ref, up_ref):
    upper = lax.broadcasted_iota(jnp.int32, down_ref.shape[1:], 0) < ROWS
    for x in range(down_ref.shape[0]):
        down_ref[x] = jnp.where(upper, t0[x], pltpu.roll(k0[x], ROWS, 0))
        up_ref[x] = jnp.where(upper, pltpu.roll(t7[x], ROWS, 0), k7[x])


def pack_y(temp, cond):
    nx, ny, nz = temp.shape
    first = pl.BlockSpec((nx, 8, nz), lambda i: (0, 0, 0))
    final = pl.BlockSpec((nx, 8, nz), lambda i: (0, ny // 8 - 1, 0))
    shape = jax.ShapeDtypeStruct((nx, 8, nz), jnp.float32)
    return pl.pallas_call(
        pack_y_kernel,
        grid=(1,),
        out_shape=(shape, shape),
        in_specs=[first, first, final, final],
        out_specs=(first, first),
        compiler_params=params(64),
        cost_estimate=cost(0, 4 * nx * 8 * nz * 4),
        name="pack_y",
    )(temp, cond, temp, cond)


def mixed_tile(t_tile, k_tile):
    row = lax.broadcasted_iota(jnp.int32, t_tile.shape, 0)
    of_k = jnp.where(row < 4, pltpu.roll(k_tile, 2, 0), pltpu.roll(k_tile, 6, 0))
    return jnp.where((row < 2) | (row >= 6), t_tile, of_k)


def unmixed(tile):
    row = lax.broadcasted_iota(jnp.int32, tile.shape, 0)
    outer = (row < 2) | (row >= 6)
    of_k = jnp.where(row < 4, pltpu.roll(tile, 6, 0), pltpu.roll(tile, 2, 0))
    return jnp.where(outer, tile, 0.0), jnp.where(outer, of_k, 0.0)


def pack_x_kernel(first, final, below0, above0, below1, above1, low_ref, high_ref):
    ny, nz = first.shape[1:]
    upper = lax.broadcasted_iota(jnp.int32, (8, nz), 0) < ROWS
    tail = HALO * ny
    for send, temp, below, above, order in (
        (low_ref, first, below0, above0, (0, 1, 2)),
        (high_ref, final, below1, above1, (HALO - 1, HALO - 2, HALO - 3)),
    ):
        for p in range(HALO):
            send[p * ny : (p + 1) * ny, :] = temp[p]
        for k, p in enumerate(order):
            t_tile = jnp.where(upper, above[p], pltpu.roll(below[p], ROWS, 0))
            k_tile = jnp.where(upper, pltpu.roll(above[p], ROWS, 0), below[p])
            if k == 0:
                send[tail : tail + 8, :] = t_tile
                send[tail + 8 : tail + 16, :] = k_tile
            else:
                at = tail + 8 + 8 * k
                send[at : at + 8, :] = mixed_tile(t_tile, k_tile)


def pack_x(temp, below, above):
    nx, ny, nz = temp.shape

    def ends(rows):
        return (
            pl.BlockSpec((HALO, rows, nz), lambda i: (0, 0, 0)),
            pl.BlockSpec((HALO, rows, nz), lambda i: (nx // HALO - 1, 0, 0)),
        )

    first, final = ends(ny)
    first_rows, final_rows = ends(8)
    rows = HALO * ny + 32
    whole = pl.BlockSpec((rows, nz), lambda i: (0, 0))
    shape = jax.ShapeDtypeStruct((rows, nz), jnp.float32)
    return pl.pallas_call(
        pack_x_kernel,
        grid=(1,),
        out_shape=(shape, shape),
        in_specs=[first, final, first_rows, first_rows, final_rows, final_rows],
        out_specs=(whole, whole),
        compiler_params=params(64),
        cost_estimate=cost(0, 4 * rows * nz * 4),
        name="pack_x",
    )(temp, temp, below, above, below, above)


def coupling(a, b):
    return jnp.where(jnp.minimum(a, b) > 0.0, (0.5 * step_size) * (a + b), 0.0)


def neighbours():
    slab, pair = lax.axis_index("slab"), lax.axis_index("pair")
    return slab > 0, slab < lax.axis_size("slab") - 1, pair > 0, pair < lax.axis_size("pair") - 1


def lane_tiles(nz):
    return [slice(j * LANES, (j + 1) * LANES) for j in range(nz // LANES)]


def one_step(field, cond, gz, begin, end, target):
    wide, nz = field.shape[1:]
    tiles = wide // 8
    spans = lane_tiles(nz)
    count = len(spans)
    lane = lax.broadcasted_iota(jnp.int32, (8, LANES), 1)
    sub = lax.broadcasted_iota(jnp.int32, (8, LANES), 0)
    _, _, has_below, has_above = neighbours()
    keep_above = (sub < 7) | has_above
    keep_below = (sub < 7) | has_below

    def row_tile(ref, x, t):
        return [ref[x, 8 * t : 8 * t + 8, z] for z in spans]

    def first_rolled(ref, x):
        return [pltpu.roll(v, 7, 0) for v in row_tile(ref, x, 0)]

    def y_flux(t_now, k_now, t_next, k_next):
        return [
            (k_now[j] + k_next[j]) * (t_next[j] - t_now[j]) for j in range(count)
        ]

    def z_change(x, t, t_now, k_now):
        turned = [pltpu.roll(v, LANES - 1, 1) for v in t_now]
        flux = []
        for j, z in enumerate(spans):
            deep = turned[j + 1] if j + 1 < count else 0.0
            deep = jnp.where(lane < LANES - 1, turned[j], deep)
            flux.append(gz[x, 8 * t : 8 * t + 8, z] * (deep - t_now[j]))
        back = [pltpu.roll(f, 1, 1) for f in flux]
        out = []
        for j in range(count):
            low = back[j - 1] if j else (k_now[0] + k_now[0]) * t_now[0]
            out.append(flux[j] - jnp.where(lane > 0, back[j], low))
        return out

    @pl.loop(begin, end)
    def _(x):
        stores = Lagging(LAG)
        final = y_flux(
            row_tile(field, x, tiles - 1),
            row_tile(cond, x, tiles - 1),
            first_rolled(field, x),
            first_rolled(cond, x),
        )
        low_y = [pltpu.roll(f, 1, 0) for f in final]
        t_now, k_now = row_tile(field, x, 0), row_tile(cond, x, 0)
        for t in range(tiles):
            rows = slice(8 * t, 8 * t + 8)
            if t + 1 < tiles:
                t_next, k_next = row_tile(field, x, t + 1), row_tile(cond, x, t + 1)
            else:
                t_next, k_next = first_rolled(field, x), first_rolled(cond, x)
            high_y = y_flux(t_now, k_now, t_next, k_next)
            change_z = z_change(x, t, t_now, k_now)
            for j, z in enumerate(spans):
                now, here = t_now[j], k_now[j]
                high_x = (here + cond[x + 1, rows, z]) * (field[x + 1, rows, z] - now)
                low_x = (here + cond[x - 1, rows, z]) * (now - field[x - 1, rows, z])
                new = now + (high_x - low_x) + (high_y[j] - low_y[j]) + change_z[j]
                if t:
                    new = jnp.where(keep_above if t <= ROWS else keep_below, new, 0.0)
                stores.add(put(*target(x, t, z), new))
            low_y, t_now, k_now = high_y, t_next, k_next
        stores.finish()


def thin_planes(cond, ny, store):
    tall, _, wide, _ = cond.shape
    lane = lax.broadcasted_iota(jnp.int32, (wide, LANES), 1)
    y_lane = lax.broadcasted_iota(jnp.int32, (8, LANES), 1)
    for base in range(0, tall, 16):
        planes = min(16, tall - base)
        gathered = jnp.zeros((wide, LANES), jnp.float32)
        for g in range(planes):
            piece = cond[base + g, 0]
            if g:
                piece = pltpu.roll(piece, 8 * g, 1)
            gathered = jnp.where((lane >> 3) == g, piece, gathered)
        turned = jnp.concatenate(
            [gathered, jnp.zeros((LANES - wide, LANES), jnp.float32)], axis=0
        ).T
        for g in range(planes):
            rows = turned[8 * g : 8 * g + 8, :]
            moved = pltpu.roll(rows, LANES - wide, 1)
            store(
                base + g,
                jnp.where(
                    y_lane < ny + ROWS, rows, jnp.where(y_lane >= LANES - ROWS, moved, 0.0)
                ),
            )


def mirror_rows(raw_k, ny):
    _, _, has_below, has_above = neighbours()
    upper = lax.broadcasted_iota(jnp.int32, (8, LANES), 0) < ROWS

    @pl.when(jnp.logical_not(has_above & has_below))
    def _():
        missing = (upper & jnp.logical_not(has_above)) | (
            jnp.logical_not(upper) & jnp.logical_not(has_below)
        )

        @pl.loop(0, raw_k.shape[0])
        def _(x):
            for j in range(raw_k.shape[1]):
                edge = raw_k[x, j, ny:]
                last = jnp.broadcast_to(raw_k[x, j, ny - 1 : ny, :], edge.shape)
                first = jnp.broadcast_to(raw_k[x, j, 0:1, :], edge.shape)
                raw_k[x, j, ny:] = jnp.where(missing, jnp.where(upper, last, first), edge)


def lay_out_k(loaded, place, faces, gz):
    planes, count, wide, _ = loaded.shape[1:]
    tiles = wide // 8
    spans = lane_tiles(count * LANES)
    lane = lax.broadcasted_iota(jnp.int32, (8, LANES), 1)

    @pl.loop(0, planes)
    def _(x):
        stores = Lagging(LAG)
        to = place(x)
        for t in range(tiles):
            rows = pl.ds(t, 8, stride=tiles)
            kept = slice(8 * t, 8 * t + 8)
            here = [(0.5 * step_size) * loaded[1, x, j, rows, :] for j in range(count)]
            turned = [pltpu.roll(v, LANES - 1, 1) for v in here]
            for j, z in enumerate(spans):
                deep = turned[j + 1] if j + 1 < count else here[j]
                deep = jnp.where(lane < LANES - 1, turned[j], deep)
                stores.add(put(faces, (to, kept, z), here[j]))
                stores.add(put(gz, (to, kept, z), here[j] + deep))
        stores.finish()


def lay_out_t(loaded, place, field):
    planes, count, wide, _ = loaded.shape[1:]
    tiles = wide // 8
    spans = lane_tiles(count * LANES)

    @pl.loop(0, planes)
    def _(x):
        stores = Lagging(LAG)
        to = place(x)
        for t in range(tiles):
            rows = pl.ds(t, 8, stride=tiles)
            for j, z in enumerate(spans):
                stores.add(put(field, (to, slice(8 * t, 8 * t + 8), z), loaded[0, x, j, rows, :]))
        stores.finish()


def fetch(loaded, which, ref, source_row, at, row, rows, sems):
    planes, count = ref.shape[0], loaded.shape[2]
    return [
        pltpu.make_async_copy(
            ref.at[:, pl.ds(source_row, rows), pl.ds(j * LANES, LANES)],
            loaded.at[which, pl.ds(at, planes), j, pl.ds(row, rows)],
            sems.at[j],
        )
        for j in range(count)
    ]


def own_planes_kernel(
    t_ref, k_ref, below_ref, above_ref, field, faces, gz, thin_ref, loaded, sems
):
    nx, ny, nz = t_ref.shape
    raw_t, raw_k = loaded.at[0], loaded.at[1]
    k_copies = fetch(loaded, 1, k_ref, 0, 0, 0, ny, sems.at[1])
    t_copies = fetch(loaded, 0, t_ref, 0, 0, 0, ny, sems.at[0])
    for copy in k_copies + t_copies:
        copy.start()
    upper = lax.broadcasted_iota(jnp.int32, (8, LANES), 0) < ROWS

    @pl.loop(0, nx)
    def _(x):
        for j, z in enumerate(lane_tiles(nz)):
            down, up = above_ref[x, :, z], below_ref[x, :, z]
            raw_t[x, j, ny:] = jnp.where(upper, down, pltpu.roll(up, ROWS, 0))
            raw_k[x, j, ny:] = jnp.where(upper, pltpu.roll(down, ROWS, 0), up)

    for copy in k_copies:
        copy.wait()
    thin_planes(raw_k, ny, lambda x, v: thin_ref.__setitem__(x, v))
    mirror_rows(raw_k, ny)
    lay_out_k(loaded, lambda x: x, faces, gz)
    for copy in t_copies:
        copy.wait()
    lay_out_t(loaded, lambda x: x, field)


def own_planes(temp, cond, below, above):
    nx, ny, nz = temp.shape
    wide = ny + 2 * ROWS
    hbm = pl.BlockSpec(memory_space=pl.ANY)
    vmem = pl.BlockSpec(memory_space=pltpu.VMEM)
    shape = jax.ShapeDtypeStruct((nx, wide, nz), jnp.float32)
    return pl.pallas_call(
        own_planes_kernel,
        out_shape=(shape, shape, shape, jax.ShapeDtypeStruct((nx, 8, LANES), jnp.float32)),
        in_specs=[hbm, hbm, vmem, vmem],
        scratch_shapes=[
            pltpu.VMEM((2, nx, nz // LANES, wide, LANES), jnp.float32),
            pltpu.SemaphoreType.DMA((2, nz // LANES)),
        ],
        compiler_params=params(64),
        cost_estimate=cost(nx * wide * nz * 10, 6 * nx * wide * nz * 4),
        name="own_planes",
    )(temp, cond, below, above)


def heat_kernel(
    own_field, own_faces, own_gz, own_thin, k_low, k_high, t_low, t_high, out_ref, thin_ref,
    loaded, corners, fields, faces, gz, placed, sems, own_sems,
):
    nx, wide, nz = own_field.shape
    field = fields.at[0]
    ny = wide - 2 * ROWS
    tall = nx + 2 * HALO
    tiles = wide // 8
    spans = lane_tiles(nz)
    k_copies, t_copies = [], []
    for k, (k_side, t_side) in enumerate(((k_low, t_low), (k_high, t_high))):
        at = k * HALO
        k_copies += fetch(loaded, 1, k_side, 0, at, 0, ny, sems.at[3 * k])
        k_copies.append(
            pltpu.make_async_copy(
                t_side.at[pl.ds(HALO * ny, 32)], corners.at[k], own_sems.at[3 + k]
            )
        )
        for p in range(HALO):
            t_copies += [
                pltpu.make_async_copy(
                    t_side.at[pl.ds(p * ny, ny), pl.ds(j * LANES, LANES)],
                    loaded.at[0, at + p, j, pl.ds(0, ny)],
                    sems.at[3 * (k + 1) - 1 + 6 * p, j],
                )
                for j in range(len(spans))
            ]
    own = [
        pltpu.make_async_copy(ref, whole.at[pl.ds(HALO, nx)], own_sems.at[k])
        for k, (ref, whole) in enumerate(
            ((own_faces, faces), (own_gz, gz), (own_field, field))
        )
    ]
    for copy in k_copies + t_copies + own:
        copy.start()
    has_low, has_high, _, _ = neighbours()

    def place(x):
        return jnp.where(x < HALO, x, x + nx)

    def store_thin(x, value):
        thin_ref[x if x < HALO else x + nx] = value

    thin_ref[HALO : HALO + nx] = own_thin[...]
    raw_t, raw_k = loaded.at[0], loaded.at[1]
    for copy in k_copies:
        copy.wait()
    for k, order in enumerate(
        ((HALO - 1, HALO - 2, HALO - 3, 0), (HALO, HALO + 1, HALO + 2, 2 * HALO - 1))
    ):
        for distance, p in enumerate(order):
            for j, z in enumerate(spans):
                if distance == 0:
                    t_tile, k_tile = corners[k, :8, z], corners[k, 8:16, z]
                elif distance + 1 < HALO:
                    t_tile, k_tile = unmixed(corners[k, 8 + 8 * distance : 16 + 8 * distance, z])
                else:
                    t_tile = k_tile = jnp.zeros((8, LANES), jnp.float32)
                raw_t[p, j, ny:] = t_tile
                raw_k[p, j, ny:] = k_tile
    thin_planes(raw_k, ny, store_thin)
    mirror_rows(raw_k, ny)
    lay_out_k(loaded, place, faces, gz)
    for copy in t_copies:
        copy.wait()
    lay_out_t(loaded, place, field)
    for copy in own:
        copy.wait()

    @pl.when(jnp.logical_not(has_low))
    def _():
        faces[HALO - 1] = faces[HALO]

    @pl.when(jnp.logical_not(has_high))
    def _():
        faces[HALO + nx] = faces[HALO + nx - 1]

    def outside(x, t, z):
        return placed, (x - HALO, z.start // LANES, pl.ds(t, 8, stride=tiles))

    @pl.loop(1, STEPS)
    def _(step):
        old, new = (step - 1) & 1, step & 1

        def inside(x, t, z):
            return fields, (new, x, slice(8 * t, 8 * t + 8), z)

        one_step(fields.at[old], faces, gz, step, tall - step, inside)
        for x, there in ((HALO - 1, has_low), (HALO + nx, has_high)):

            @pl.when(jnp.logical_not(there))
            def _():
                fields[new, x] = jnp.zeros((wide, nz), jnp.float32)

    old = fields.at[(STEPS - 1) & 1]
    one_step(old, faces, gz, HALO, tall - HALO, outside)

    @pl.loop(0, nx)
    def _(x):
        for j, z in enumerate(spans):
            out_ref[x, :, z] = placed[x, j, :ny, :]


def heat(own, k_low, k_high, t_low, t_high, shape):
    nx, ny, nz = shape
    tall, wide = nx + 2 * HALO, ny + 2 * ROWS
    hbm = pl.BlockSpec(memory_space=pl.ANY)
    vmem = pl.BlockSpec(memory_space=pltpu.VMEM)
    big = pltpu.VMEM((tall, wide, nz), jnp.float32)
    return pl.pallas_call(
        heat_kernel,
        out_shape=(
            jax.ShapeDtypeStruct(shape, jnp.float32),
            jax.ShapeDtypeStruct((tall, 8, LANES), jnp.float32),
        ),
        in_specs=[hbm] * 3 + [vmem] + [hbm] * 4,
        scratch_shapes=[
            pltpu.VMEM((2, 2 * HALO, nz // LANES, wide, LANES), jnp.float32),
            pltpu.VMEM((2, 32, nz), jnp.float32),
            pltpu.VMEM((2, tall, wide, nz), jnp.float32),
            big,
            big,
            pltpu.VMEM((nx, nz // LANES, wide, LANES), jnp.float32),
            pltpu.SemaphoreType.DMA((6 * HALO, nz // LANES)),
            pltpu.SemaphoreType.DMA((5,)),
        ],
        compiler_params=params(64),
        cost_estimate=cost(tall * wide * nz * 100, 12 * nx * ny * nz * 4),
        name="heat",
    )(*own, k_low, k_high, t_low, t_high)


def source_kernel(ny, all_ref, thin_ref, base_ref, out_ref):
    tall = thin_ref.shape[0]
    nx = tall - 2 * HALO
    sheets = all_ref.shape[1]
    sub = lax.broadcasted_iota(jnp.int32, (8, LANES), 0)
    y_lane = lax.broadcasted_iota(jnp.int32, (8, LANES), 1)

    slabs, pairs = lax.axis_size("slab"), lax.axis_size("pair")

    def sheet(down, across):
        slab = lax.axis_index("slab") + down
        pair = lax.axis_index("pair") + across
        inside = (slab >= 0) & (slab < slabs) & (pair >= 0) & (pair < pairs)
        found = all_ref[jnp.where(inside, slab * pairs + pair, 0)]
        return jnp.where(inside, found, 0.0)

    def rows_of(down):
        low, own, high = (sheet(down, across) for across in (-1, 0, 1))
        out = []
        for half in range(2):
            if half == 0:
                own_at, high_at, low_at = own, pltpu.roll(high, ny, 1), pltpu.roll(low, ny, 1)
            else:
                own_at, high_at, low_at = pltpu.roll(own, ny, 1), high, low
            out.append(
                jnp.where(
                    y_lane < ny,
                    own_at,
                    jnp.where(
                        y_lane < ny + HALO,
                        high_at,
                        jnp.where(y_lane >= LANES - HALO, low_at, 0.0),
                    ),
                )
            )
        return out

    lines = [rows_of(down) for down in (-1, 0, 1)]
    source = []
    for x in range(-HALO, nx + HALO):
        which, local = (x + nx) // nx, x % nx
        row = lines[which][local % 2][local // 2 : local // 2 + 1, :]
        source.append(jnp.where(sub == 0, jnp.broadcast_to(row, (8, LANES)), 0.0))

    cond = [thin_ref[x] for x in range(tall)]
    cx, cy, cz, centre = [], [], [], []
    for x in range(tall):
        here = cond[x]
        after = cond[min(x + 1, tall - 1)]
        before = cond[max(x - 1, 0)]
        y_after = pltpu.roll(here, LANES - 1, 1)
        y_before = pltpu.roll(here, 1, 1)
        z_after = jnp.where(sub == 7, 0.0, pltpu.roll(here, 7, 0))
        z_before = jnp.where(sub == 0, 0.0, pltpu.roll(here, 1, 0))
        cx.append(coupling(here, after))
        cy.append(coupling(here, y_after))
        cz.append(coupling(here, z_after))
        total = 6.0 * here
        for near in (after, before, y_after, y_before, z_after, z_before):
            total = total + jnp.where(near > 0.0, near, here)
        centre.append(1.0 - (0.5 * step_size) * total)

    added = source
    for step in range(1, STEPS):
        new = list(added)
        for x in range(step, tall - step):
            here = added[x]
            total = source[x] + centre[x] * here
            total = total + (cx[x] * added[x + 1] + cx[x - 1] * added[x - 1])
            total = total + cy[x] * pltpu.roll(here, LANES - 1, 1)
            total = total + pltpu.roll(cy[x] * here, 1, 1)
            total = total + cz[x] * pltpu.roll(here, 7, 0)
            new[x] = total + pltpu.roll(cz[x] * here, 1, 0)
        added = new

    lane = lax.broadcasted_iota(jnp.int32, (ny, LANES), 1)
    turned = jnp.concatenate(added[HALO : HALO + nx], axis=0).T[:ny]
    for x in range(nx):
        piece = turned if x == 0 else pltpu.roll(turned, LANES - 8 * x, 1)
        out_ref[x] = base_ref[x] + jnp.where(lane < STEPS, piece, 0.0)


def add_source(everything, thin, base):
    nx, ny, nz = base.shape
    block = pl.BlockSpec((nx, ny, LANES), lambda i: (0, 0, 0))
    return pl.pallas_call(
        functools.partial(source_kernel, ny),
        grid=(1,),
        out_shape=jax.ShapeDtypeStruct(base.shape, jnp.float32),
        in_specs=[
            pl.BlockSpec(everything.shape, lambda i: (0, 0, 0)),
            pl.BlockSpec(thin.shape, lambda i: (0, 0, 0)),
            block,
        ],
        out_specs=block,
        input_output_aliases={2: 0},
        compiler_params=params(64),
        cost_estimate=cost(1_000_000, 2 * nx * ny * LANES * 4),
        name="add_source",
    )(everything, thin, base)


def exchange(rows):
    return lax.all_to_all(rows, ("slab", "pair"), split_axis=0, concat_axis=0, tiled=True)


def together(*arrays):
    return lax.optimization_barrier(arrays)


def both_ways(low, high, axis):
    count = lax.axis_size(axis)
    forward = [(i, i + 1) for i in range(count - 1)]
    backward = [(target, source) for source, target in forward]
    from_low = lax.ppermute(high, axis, forward)
    from_high = lax.ppermute(low, axis, backward)
    return from_low, from_high


def shards(
    initial_warmth,
    heat_passing_coefficient,
    mirror_fraction,
    element_facing_site,
    tile_block_couples,
    active_slot_count,
    view_factor_blocks,
):
    nx, ny, _ = initial_warmth.shape
    slabs, pairs = lax.axis_size("slab"), lax.axis_size("pair")
    count = slabs * pairs
    blocks = mirror_fraction.shape[0]
    couples = tile_block_couples.T

    temp, cond = initial_warmth, heat_passing_coefficient
    emitted, copies = emit(temp, element_facing_site, mirror_fraction, count)
    temp, copies = together(temp, copies)

    def sweep_terms(whole):
        whole = whole.reshape(count * blocks, BLK)
        term = tile_terms(whole, couples, active_slot_count, view_factor_blocks)
        return term.reshape(count, blocks, BLK)

    whole = exchange(copies)
    cond, copies = together(cond, copies)
    send_low, send_high = cond[:HALO], cond[nx - HALO :]
    k_low, k_high = both_ways(send_low, send_high, "slab")
    whole = together(whole, send_low, send_high)[0]
    temp, cond, term = together(temp, cond, sweep_terms(whole))
    parts = exchange(term)
    below, above = both_ways(*pack_y(temp, cond), "pair")
    parts, below, above, k_low, k_high = together(parts, below, above, k_low, k_high)
    copies, below, above = together(middle(parts, emitted, mirror_fraction), below, above)
    whole = exchange(copies)
    send_low, send_high = pack_x(temp, below, above)
    t_low, t_high = both_ways(send_low, send_high, "slab")
    whole = together(whole, send_low, send_high)[0]
    temp, cond, term = together(temp, cond, sweep_terms(whole))
    parts = exchange(term)
    own = own_planes(temp, cond, below, above)
    parts, t_low, t_high, own = together(parts, t_low, t_high, own)
    radiosity, source = last(parts, emitted, mirror_fraction, element_facing_site, nx * ny, count)
    everything = exchange(source)
    own, source = together(own, source)
    base, thin = heat(own, k_low, k_high, t_low, t_high, temp.shape)

    warmed_liner = add_source(everything, thin, base)
    return (radiosity, warmed_liner)


def solution(mesh):
    return jax.shard_map(
        shards,
        mesh=mesh,
        in_specs=(
            P("slab", "pair", None),
            P("slab", "pair", None),
            P(("slab", "pair"), None),
            P(("slab", "pair"), None),
            P(("slab", "pair"), None),
            P(("slab", "pair")),
            P(("slab", "pair"), None, None),
        ),
        out_specs=(P(("slab", "pair"), None), P("slab", "pair", None)),
        check_vma=False,
    )
```

```python
import functools

import jax
import jax.numpy as jnp
from jax import lax
from jax.experimental import pallas as pl
from jax.experimental.pallas import tpu as pltpu
from jax.sharding import PartitionSpec as P

BLK = 128
SWEEPS = 2
STEPS = 4
HALO = STEPS
ROWS = STEPS
LANES = 128
CHUNK = 16
LAG = 0

step_size = 0.07

NT = (((1,), (1,)), ((), ()))
NN = (((1,), (0,)), ((), ()))


def params(mib):
    return pltpu.CompilerParams(vmem_limit_bytes=mib * 1024 * 1024)


def cost(flops, nbytes):
    return pl.CostEstimate(flops=flops, bytes_accessed=nbytes, transcendentals=0)


def parts_of(x, count):
    out = []
    for _ in range(count - 1):
        part = x.astype(jnp.bfloat16)
        out.append(part)
        x = x - part.astype(jnp.float32)
    out.append(x.astype(jnp.bfloat16))
    return out


class Lagging:
    def __init__(self, depth):
        self.depth = depth
        self.waiting = []

    def add(self, store):
        self.waiting.append(store)
        if len(self.waiting) > self.depth:
            self.waiting.pop(0)()

    def finish(self):
        for store in self.waiting:
            store()
        self.waiting = []


def put(ref, index, value):
    return lambda: ref.__setitem__(index, value)


def emit_kernel(temp_ref, site_ref, mirror_ref, emitted_ref, copies_ref):
    nx, ny, _ = temp_ref.shape
    sheets = nx * ny // LANES
    per = LANES // ny
    lanes = lax.broadcasted_iota(jnp.int32, (LANES, LANES), 1)
    gathered = jnp.zeros((LANES, LANES), jnp.float32)
    for r in range(sheets):
        piece = temp_ref[per * r : per * r + per].reshape(LANES, LANES)
        if r:
            piece = pltpu.roll(piece, r, 1)
        gathered = jnp.where(lanes == r, piece, gathered)
    plane = gathered.T[:sheets]
    for half in range(site_ref.shape[0] // 8):
        rows = pl.ds(half * 8, 8)
        site = site_ref[rows, :]
        lane = site & (LANES - 1)
        sheet = site >> 7
        warmth = jnp.zeros(site.shape, jnp.float32)
        for r in range(sheets):
            line = jnp.broadcast_to(plane[r : r + 1, :], site.shape)
            picked = jnp.take_along_axis(line, lane, axis=1)
            warmth = jnp.where(sheet == r, picked, warmth)
        square = warmth * warmth
        emitted = (1.0 - mirror_ref[rows, :]) * (square * square)
        emitted_ref[rows, :] = emitted
        for d in range(copies_ref.shape[0]):
            copies_ref[d, rows, :] = emitted


def emit(temp, site, mirror, count):
    shape = mirror.shape
    nx, ny, _ = temp.shape
    patch = pl.BlockSpec(shape, lambda i: (0, 0))
    return pl.pallas_call(
        emit_kernel,
        grid=(1,),
        out_shape=(
            jax.ShapeDtypeStruct(shape, jnp.float32),
            jax.ShapeDtypeStruct((count,) + shape, jnp.float32),
        ),
        in_specs=[pl.BlockSpec((nx, ny, LANES), lambda i: (0, 0, 0)), patch, patch],
        out_specs=(patch, pl.BlockSpec((count,) + shape, lambda i: (0, 0, 0))),
        compiler_params=params(64),
        cost_estimate=cost(10_000, 900_000),
        name="emit",
    )(temp, site, mirror)


def tiles_kernel(
    live_ref, pairs_ref, lanes_ref, whole_ref, tiles_ref, out_ref, held, terms, sems
):
    slots = held.shape[0]
    live = live_ref[0]
    chunks = (live + CHUNK - 1) // CHUNK

    def chunk_copy(c):
        span = pl.ds(c * CHUNK, CHUNK)
        return pltpu.make_async_copy(tiles_ref.at[span], held.at[span], sems.at[c])

    @pl.loop(0, chunks)
    def _(c):
        chunk_copy(c).start()

    top = lax.broadcasted_iota(jnp.int32, (8, BLK), 0) == 0

    def split_row(block):
        row = jnp.broadcast_to(whole_ref[pl.ds(block, 1), :], (8, BLK))
        high = row.astype(jnp.bfloat16).astype(jnp.float32)
        return jnp.where(top, high, row - high)

    def vectors(a, b):
        stacked = jnp.concatenate([split_row(a), split_row(b)], axis=0)
        stacked = stacked.astype(jnp.bfloat16)
        return jnp.concatenate([stacked, stacked], axis=1)

    @pl.loop(0, chunks)
    def _(c):
        chunk_copy(c).wait()
        stores = Lagging(4 * CHUNK)
        for u in range(0, CHUNK, 2):
            t = c * CHUNK + u
            high_a, low_a = parts_of(held[t], 2)
            high_b, low_b = parts_of(held[t + 1], 2)
            both = jnp.concatenate(
                [
                    jnp.concatenate([high_a, high_b], axis=1),
                    jnp.concatenate([low_a, low_b], axis=1),
                ],
                axis=0,
            )
            second = lax.dot_general(
                vectors(pairs_ref[0, t], pairs_ref[0, t + 1]),
                both,
                NN,
                preferred_element_type=jnp.float32,
            )
            turned = jnp.concatenate(
                [
                    jnp.concatenate([high_a, low_a], axis=1),
                    jnp.concatenate([high_b, low_b], axis=1),
                ],
                axis=0,
            )
            first = lax.dot_general(
                vectors(pairs_ref[1, t], pairs_ref[1, t + 1]),
                turned,
                NT,
                preferred_element_type=jnp.float32,
            )
            for side, result in ((0, first), (1, second)):
                for v, (top_row, cols) in enumerate(((0, slice(0, BLK)), (8, slice(BLK, 2 * BLK)))):
                    row = result[top_row : top_row + 1, cols] + result[top_row + 1 : top_row + 2, cols]
                    stores.add(put(terms, (side, pl.ds(t + v, 1)), row))
        stores.finish()

    used = lax.broadcasted_iota(jnp.int32, (slots, BLK), 0) < live
    used_lane = lax.broadcasted_iota(jnp.int32, (1, slots), 1) < live
    blocks = out_ref.shape[0]
    group = min(blocks, 512)
    split = []
    for side in range(2):
        masked = jnp.where(used, terms[side], 0.0)
        split.append(jnp.concatenate(parts_of(masked, 2), axis=1))
    for base in range(0, blocks, group):
        rows = lax.broadcasted_iota(jnp.int32, (group, slots), 0) + base
        total = jnp.zeros((group, 2 * BLK), jnp.float32)
        for side in range(2):
            target = jnp.where(used_lane, lanes_ref[side : side + 1, :], -1)
            choose = jnp.where(rows == target, 1.0, 0.0).astype(jnp.bfloat16)
            total = total + jnp.dot(choose, split[side], preferred_element_type=jnp.float32)
        out_ref[base : base + group, :] = total[:, :BLK] + total[:, BLK:]


def tile_terms(whole, couples, live, tiles):
    slots = tiles.shape[0]
    smem = pl.BlockSpec(memory_space=pltpu.SMEM)
    vmem = pl.BlockSpec(memory_space=pltpu.VMEM)
    return pl.pallas_call(
        tiles_kernel,
        out_shape=jax.ShapeDtypeStruct(whole.shape, jnp.float32),
        in_specs=[smem, smem, vmem, vmem, pl.BlockSpec(memory_space=pl.ANY)],
        out_specs=vmem,
        scratch_shapes=[
            pltpu.VMEM(tiles.shape, jnp.float32),
            pltpu.VMEM((2, slots, BLK), jnp.float32),
            pltpu.SemaphoreType.DMA((slots // CHUNK,)),
        ],
        compiler_params=params(64),
        cost_estimate=cost(slots * BLK * BLK * 32, slots * BLK * BLK * 4),
        name="tiles",
    )(live, couples, couples, whole, tiles)


def sum_parts(parts_ref, rows):
    total = parts_ref[0, rows, :]
    for d in range(1, parts_ref.shape[0]):
        total = total + parts_ref[d, rows, :]
    return total


def middle_kernel(parts_ref, emitted_ref, mirror_ref, copies_ref):
    for half in range(emitted_ref.shape[0] // 8):
        rows = pl.ds(half * 8, 8)
        incident = sum_parts(parts_ref, rows)
        radiosity = emitted_ref[rows, :] + mirror_ref[rows, :] * incident
        for d in range(copies_ref.shape[0]):
            copies_ref[d, rows, :] = radiosity


def middle(parts, emitted, mirror):
    return pl.pallas_call(
        middle_kernel,
        out_shape=jax.ShapeDtypeStruct(parts.shape, jnp.float32),
        compiler_params=params(64),
        cost_estimate=cost(100_000, 600_000),
        name="middle",
    )(parts, emitted, mirror)


def last_kernel(scale, parts_ref, emitted_ref, mirror_ref, site_ref, rad_ref, source_ref):
    blocks = emitted_ref.shape[0]
    incident = sum_parts(parts_ref, slice(None))
    emitted = emitted_ref[...]
    mirror = mirror_ref[...]
    rad_ref[...] = emitted + mirror * incident
    absorbed = ((1.0 - mirror) * incident - emitted) * scale
    site = site_ref[...]
    lane = site & (LANES - 1)
    sheet = site >> 7
    sheets = source_ref.shape[1]
    sheet_iota = lax.broadcasted_iota(jnp.int32, (sheets, BLK), 0)
    lane_iota = lax.broadcasted_iota(jnp.int32, (LANES, BLK), 0)
    left = []
    right = []
    for b in range(blocks):
        here = jnp.where(sheet_iota == sheet[b : b + 1, :], absorbed[b : b + 1, :], 0.0)
        left.append(here)
        pick = jnp.where(lane_iota == lane[b : b + 1, :], 1.0, 0.0)
        right.append(pick.astype(jnp.bfloat16))
    left = jnp.concatenate(left, axis=1)
    right = jnp.concatenate(right, axis=1)
    source = jnp.zeros((sheets, LANES), jnp.float32)
    for part in parts_of(left, 3):
        source = source + lax.dot_general(part, right, NT, preferred_element_type=jnp.float32)
    for d in range(source_ref.shape[0]):
        source_ref[d] = source


def last(parts, emitted, mirror, site, cells, count):
    weight = cells / (mirror.shape[0] * BLK * 1.0)
    return pl.pallas_call(
        functools.partial(last_kernel, step_size * weight),
        out_shape=(
            jax.ShapeDtypeStruct(mirror.shape, jnp.float32),
            jax.ShapeDtypeStruct((count, cells // LANES, LANES), jnp.float32),
        ),
        compiler_params=params(64),
        cost_estimate=cost(10_000_000, 600_000),
        name="last",
    )(parts, emitted, mirror, site)


def pack_y_kernel(t0, k0, t7, k7, down_ref, up_ref):
    upper = lax.broadcasted_iota(jnp.int32, down_ref.shape[1:], 0) < ROWS
    for x in range(down_ref.shape[0]):
        down_ref[x] = jnp.where(upper, t0[x], pltpu.roll(k0[x], ROWS, 0))
        up_ref[x] = jnp.where(upper, pltpu.roll(t7[x], ROWS, 0), k7[x])


def pack_y(temp, cond):
    nx, ny, nz = temp.shape
    first = pl.BlockSpec((nx, 8, nz), lambda i: (0, 0, 0))
    final = pl.BlockSpec((nx, 8, nz), lambda i: (0, ny // 8 - 1, 0))
    shape = jax.ShapeDtypeStruct((nx, 8, nz), jnp.float32)
    return pl.pallas_call(
        pack_y_kernel,
        grid=(1,),
        out_shape=(shape, shape),
        in_specs=[first, first, final, final],
        out_specs=(first, first),
        compiler_params=params(64),
        cost_estimate=cost(0, 4 * nx * 8 * nz * 4),
        name="pack_y",
    )(temp, cond, temp, cond)


def mixed_tile(t_tile, k_tile):
    row = lax.broadcasted_iota(jnp.int32, t_tile.shape, 0)
    of_k = jnp.where(row < 4, pltpu.roll(k_tile, 2, 0), pltpu.roll(k_tile, 6, 0))
    return jnp.where((row < 2) | (row >= 6), t_tile, of_k)


def unmixed(tile):
    row = lax.broadcasted_iota(jnp.int32, tile.shape, 0)
    outer = (row < 2) | (row >= 6)
    of_k = jnp.where(row < 4, pltpu.roll(tile, 6, 0), pltpu.roll(tile, 2, 0))
    return jnp.where(outer, tile, 0.0), jnp.where(outer, of_k, 0.0)


def pack_x_kernel(first, final, below0, above0, below1, above1, low_ref, high_ref):
    ny, nz = first.shape[1:]
    upper = lax.broadcasted_iota(jnp.int32, (8, nz), 0) < ROWS
    tail = HALO * ny
    for send, temp, below, above, order in (
        (low_ref, first, below0, above0, (0, 1, 2)),
        (high_ref, final, below1, above1, (HALO - 1, HALO - 2, HALO - 3)),
    ):
        for p in range(HALO):
            send[p * ny : (p + 1) * ny, :] = temp[p]
        for k, p in enumerate(order):
            t_tile = jnp.where(upper, above[p], pltpu.roll(below[p], ROWS, 0))
            k_tile = jnp.where(upper, pltpu.roll(above[p], ROWS, 0), below[p])
            if k == 0:
                send[tail : tail + 8, :] = t_tile
                send[tail + 8 : tail + 16, :] = k_tile
            else:
                at = tail + 8 + 8 * k
                send[at : at + 8, :] = mixed_tile(t_tile, k_tile)


def pack_x(temp, below, above):
    nx, ny, nz = temp.shape

    def ends(rows):
        return (
            pl.BlockSpec((HALO, rows, nz), lambda i: (0, 0, 0)),
            pl.BlockSpec((HALO, rows, nz), lambda i: (nx // HALO - 1, 0, 0)),
        )

    first, final = ends(ny)
    first_rows, final_rows = ends(8)
    rows = HALO * ny + 32
    whole = pl.BlockSpec((rows, nz), lambda i: (0, 0))
    shape = jax.ShapeDtypeStruct((rows, nz), jnp.float32)
    return pl.pallas_call(
        pack_x_kernel,
        grid=(1,),
        out_shape=(shape, shape),
        in_specs=[first, final, first_rows, first_rows, final_rows, final_rows],
        out_specs=(whole, whole),
        compiler_params=params(64),
        cost_estimate=cost(0, 4 * rows * nz * 4),
        name="pack_x",
    )(temp, temp, below, above, below, above)


def coupling(a, b):
    return jnp.where(jnp.minimum(a, b) > 0.0, (0.5 * step_size) * (a + b), 0.0)


def neighbours():
    slab, pair = lax.axis_index("slab"), lax.axis_index("pair")
    return slab > 0, slab < lax.axis_size("slab") - 1, pair > 0, pair < lax.axis_size("pair") - 1


def lane_tiles(nz):
    return [slice(j * LANES, (j + 1) * LANES) for j in range(nz // LANES)]


def one_step(field, cond, gz, begin, end, target):
    wide, nz = field.shape[1:]
    tiles = wide // 8
    spans = lane_tiles(nz)
    count = len(spans)
    lane = lax.broadcasted_iota(jnp.int32, (8, LANES), 1)
    sub = lax.broadcasted_iota(jnp.int32, (8, LANES), 0)
    _, _, has_below, has_above = neighbours()
    keep_above = (sub < 7) | has_above
    keep_below = (sub < 7) | has_below

    def row_tile(ref, x, t):
        return [ref[x, 8 * t : 8 * t + 8, z] for z in spans]

    def first_rolled(ref, x):
        return [pltpu.roll(v, 7, 0) for v in row_tile(ref, x, 0)]

    def y_flux(t_now, k_now, t_next, k_next):
        return [
            (k_now[j] + k_next[j]) * (t_next[j] - t_now[j]) for j in range(count)
        ]

    def z_change(x, t, t_now, k_now):
        turned = [pltpu.roll(v, LANES - 1, 1) for v in t_now]
        flux = []
        for j, z in enumerate(spans):
            deep = turned[j + 1] if j + 1 < count else 0.0
            deep = jnp.where(lane < LANES - 1, turned[j], deep)
            flux.append(gz[x, 8 * t : 8 * t + 8, z] * (deep - t_now[j]))
        back = [pltpu.roll(f, 1, 1) for f in flux]
        out = []
        for j in range(count):
            low = back[j - 1] if j else (k_now[0] + k_now[0]) * t_now[0]
            out.append(flux[j] - jnp.where(lane > 0, back[j], low))
        return out

    @pl.loop(begin, end)
    def _(x):
        stores = Lagging(LAG)
        final = y_flux(
            row_tile(field, x, tiles - 1),
            row_tile(cond, x, tiles - 1),
            first_rolled(field, x),
            first_rolled(cond, x),
        )
        low_y = [pltpu.roll(f, 1, 0) for f in final]
        t_now, k_now = row_tile(field, x, 0), row_tile(cond, x, 0)
        for t in range(tiles):
            rows = slice(8 * t, 8 * t + 8)
            if t + 1 < tiles:
                t_next, k_next = row_tile(field, x, t + 1), row_tile(cond, x, t + 1)
            else:
                t_next, k_next = first_rolled(field, x), first_rolled(cond, x)
            high_y = y_flux(t_now, k_now, t_next, k_next)
            change_z = z_change(x, t, t_now, k_now)
            for j, z in enumerate(spans):
                now, here = t_now[j], k_now[j]
                high_x = (here + cond[x + 1, rows, z]) * (field[x + 1, rows, z] - now)
                low_x = (here + cond[x - 1, rows, z]) * (now - field[x - 1, rows, z])
                new = now + (high_x - low_x) + (high_y[j] - low_y[j]) + change_z[j]
                if t:
                    new = jnp.where(keep_above if t <= ROWS else keep_below, new, 0.0)
                stores.add(put(*target(x, t, z), new))
            low_y, t_now, k_now = high_y, t_next, k_next
        stores.finish()


def thin_planes(cond, ny, store):
    tall, _, wide, _ = cond.shape
    lane = lax.broadcasted_iota(jnp.int32, (wide, LANES), 1)
    y_lane = lax.broadcasted_iota(jnp.int32, (8, LANES), 1)
    for base in range(0, tall, 16):
        planes = min(16, tall - base)
        gathered = jnp.zeros((wide, LANES), jnp.float32)
        for g in range(planes):
            piece = cond[base + g, 0]
            if g:
                piece = pltpu.roll(piece, 8 * g, 1)
            gathered = jnp.where((lane >> 3) == g, piece, gathered)
        turned = jnp.concatenate(
            [gathered, jnp.zeros((LANES - wide, LANES), jnp.float32)], axis=0
        ).T
        for g in range(planes):
            rows = turned[8 * g : 8 * g + 8, :]
            moved = pltpu.roll(rows, LANES - wide, 1)
            store(
                base + g,
                jnp.where(
                    y_lane < ny + ROWS, rows, jnp.where(y_lane >= LANES - ROWS, moved, 0.0)
                ),
            )


def mirror_rows(raw_k, ny):
    _, _, has_below, has_above = neighbours()
    upper = lax.broadcasted_iota(jnp.int32, (8, LANES), 0) < ROWS

    @pl.when(jnp.logical_not(has_above & has_below))
    def _():
        missing = (upper & jnp.logical_not(has_above)) | (
            jnp.logical_not(upper) & jnp.logical_not(has_below)
        )

        @pl.loop(0, raw_k.shape[0])
        def _(x):
            for j in range(raw_k.shape[1]):
                edge = raw_k[x, j, ny:]
                last = jnp.broadcast_to(raw_k[x, j, ny - 1 : ny, :], edge.shape)
                first = jnp.broadcast_to(raw_k[x, j, 0:1, :], edge.shape)
                raw_k[x, j, ny:] = jnp.where(missing, jnp.where(upper, last, first), edge)


def lay_out_k(loaded, place, faces, gz):
    planes, count, wide, _ = loaded.shape[1:]
    tiles = wide // 8
    spans = lane_tiles(count * LANES)
    lane = lax.broadcasted_iota(jnp.int32, (8, LANES), 1)

    @pl.loop(0, planes)
    def _(x):
        stores = Lagging(LAG)
        to = place(x)
        for t in range(tiles):
            rows = pl.ds(t, 8, stride=tiles)
            kept = slice(8 * t, 8 * t + 8)
            here = [(0.5 * step_size) * loaded[1, x, j, rows, :] for j in range(count)]
            turned = [pltpu.roll(v, LANES - 1, 1) for v in here]
            for j, z in enumerate(spans):
                deep = turned[j + 1] if j + 1 < count else here[j]
                deep = jnp.where(lane < LANES - 1, turned[j], deep)
                stores.add(put(faces, (to, kept, z), here[j]))
                stores.add(put(gz, (to, kept, z), here[j] + deep))
        stores.finish()


def lay_out_t(loaded, place, field):
    planes, count, wide, _ = loaded.shape[1:]
    tiles = wide // 8
    spans = lane_tiles(count * LANES)

    @pl.loop(0, planes)
    def _(x):
        stores = Lagging(LAG)
        to = place(x)
        for t in range(tiles):
            rows = pl.ds(t, 8, stride=tiles)
            for j, z in enumerate(spans):
                stores.add(put(field, (to, slice(8 * t, 8 * t + 8), z), loaded[0, x, j, rows, :]))
        stores.finish()


def fetch(loaded, which, ref, source_row, at, row, rows, sems):
    planes, count = ref.shape[0], loaded.shape[2]
    return [
        pltpu.make_async_copy(
            ref.at[:, pl.ds(source_row, rows), pl.ds(j * LANES, LANES)],
            loaded.at[which, pl.ds(at, planes), j, pl.ds(row, rows)],
            sems.at[j],
        )
        for j in range(count)
    ]


def own_planes_kernel(
    t_ref, k_ref, below_ref, above_ref, field, faces, gz, thin_ref, loaded, sems
):
    nx, ny, nz = t_ref.shape
    raw_t, raw_k = loaded.at[0], loaded.at[1]
    k_copies = fetch(loaded, 1, k_ref, 0, 0, 0, ny, sems.at[1])
    t_copies = fetch(loaded, 0, t_ref, 0, 0, 0, ny, sems.at[0])
    for copy in k_copies + t_copies:
        copy.start()
    upper = lax.broadcasted_iota(jnp.int32, (8, LANES), 0) < ROWS

    @pl.loop(0, nx)
    def _(x):
        for j, z in enumerate(lane_tiles(nz)):
            down, up = above_ref[x, :, z], below_ref[x, :, z]
            raw_t[x, j, ny:] = jnp.where(upper, down, pltpu.roll(up, ROWS, 0))
            raw_k[x, j, ny:] = jnp.where(upper, pltpu.roll(down, ROWS, 0), up)

    for copy in k_copies:
        copy.wait()
    thin_planes(raw_k, ny, lambda x, v: thin_ref.__setitem__(x, v))
    mirror_rows(raw_k, ny)
    lay_out_k(loaded, lambda x: x, faces, gz)
    for copy in t_copies:
        copy.wait()
    lay_out_t(loaded, lambda x: x, field)


def own_planes(temp, cond, below, above):
    nx, ny, nz = temp.shape
    wide = ny + 2 * ROWS
    hbm = pl.BlockSpec(memory_space=pl.ANY)
    vmem = pl.BlockSpec(memory_space=pltpu.VMEM)
    shape = jax.ShapeDtypeStruct((nx, wide, nz), jnp.float32)
    return pl.pallas_call(
        own_planes_kernel,
        out_shape=(shape, shape, shape, jax.ShapeDtypeStruct((nx, 8, LANES), jnp.float32)),
        in_specs=[hbm, hbm, vmem, vmem],
        scratch_shapes=[
            pltpu.VMEM((2, nx, nz // LANES, wide, LANES), jnp.float32),
            pltpu.SemaphoreType.DMA((2, nz // LANES)),
        ],
        compiler_params=params(64),
        cost_estimate=cost(nx * wide * nz * 10, 6 * nx * wide * nz * 4),
        name="own_planes",
    )(temp, cond, below, above)


def heat_kernel(
    own_field, own_faces, own_gz, own_thin, k_low, k_high, t_low, t_high, out_ref, thin_ref,
    loaded, corners, field, between, faces, gz, placed, sems, own_sems,
):
    nx, wide, nz = own_field.shape
    ny = wide - 2 * ROWS
    tall = nx + 2 * HALO
    tiles = wide // 8
    spans = lane_tiles(nz)
    k_copies, t_copies = [], []
    for k, (k_side, t_side) in enumerate(((k_low, t_low), (k_high, t_high))):
        at = k * HALO
        k_copies += fetch(loaded, 1, k_side, 0, at, 0, ny, sems.at[3 * k])
        k_copies.append(
            pltpu.make_async_copy(
                t_side.at[pl.ds(HALO * ny, 32)], corners.at[k], own_sems.at[3 + k]
            )
        )
        for p in range(HALO):
            t_copies += [
                pltpu.make_async_copy(
                    t_side.at[pl.ds(p * ny, ny), pl.ds(j * LANES, LANES)],
                    loaded.at[0, at + p, j, pl.ds(0, ny)],
                    sems.at[3 * (k + 1) - 1 + 6 * p, j],
                )
                for j in range(len(spans))
            ]
    own = [
        pltpu.make_async_copy(ref, whole.at[pl.ds(HALO, nx)], own_sems.at[k])
        for k, (ref, whole) in enumerate(
            ((own_faces, faces), (own_gz, gz), (own_field, field))
        )
    ]
    for copy in k_copies + t_copies + own:
        copy.start()
    has_low, has_high, _, _ = neighbours()

    def place(x):
        return jnp.where(x < HALO, x, x + nx)

    def store_thin(x, value):
        thin_ref[x if x < HALO else x + nx] = value

    thin_ref[HALO : HALO + nx] = own_thin[...]
    raw_t, raw_k = loaded.at[0], loaded.at[1]
    for copy in k_copies:
        copy.wait()
    for k, order in enumerate(
        ((HALO - 1, HALO - 2, HALO - 3, 0), (HALO, HALO + 1, HALO + 2, 2 * HALO - 1))
    ):
        for distance, p in enumerate(order):
            for j, z in enumerate(spans):
                if distance == 0:
                    t_tile, k_tile = corners[k, :8, z], corners[k, 8:16, z]
                elif distance + 1 < HALO:
                    t_tile, k_tile = unmixed(corners[k, 8 + 8 * distance : 16 + 8 * distance, z])
                else:
                    t_tile = k_tile = jnp.zeros((8, LANES), jnp.float32)
                raw_t[p, j, ny:] = t_tile
                raw_k[p, j, ny:] = k_tile
    thin_planes(raw_k, ny, store_thin)
    mirror_rows(raw_k, ny)
    lay_out_k(loaded, place, faces, gz)
    for copy in t_copies:
        copy.wait()
    lay_out_t(loaded, place, field)
    for copy in own:
        copy.wait()

    @pl.when(jnp.logical_not(has_low))
    def _():
        faces[HALO - 1] = faces[HALO]

    @pl.when(jnp.logical_not(has_high))
    def _():
        faces[HALO + nx] = faces[HALO + nx - 1]

    def inside(target):
        return lambda x, t, z: (target, (x, slice(8 * t, 8 * t + 8), z))

    def outside(x, t, z):
        return placed, (x - HALO, z.start // LANES, pl.ds(t, 8, stride=tiles))

    old, new = field, between
    for step in range(1, STEPS):
        one_step(old, faces, gz, step, tall - step, inside(new))
        for x, there in ((HALO - 1, has_low), (HALO + nx, has_high)):

            @pl.when(jnp.logical_not(there))
            def _():
                new[x] = jnp.zeros((wide, nz), jnp.float32)

        old, new = new, old
    one_step(old, faces, gz, HALO, tall - HALO, outside)

    @pl.loop(0, nx)
    def _(x):
        for j, z in enumerate(spans):
            out_ref[x, :, z] = placed[x, j, :ny, :]


def heat(own, k_low, k_high, t_low, t_high, shape):
    nx, ny, nz = shape
    tall, wide = nx + 2 * HALO, ny + 2 * ROWS
    hbm = pl.BlockSpec(memory_space=pl.ANY)
    vmem = pl.BlockSpec(memory_space=pltpu.VMEM)
    big = pltpu.VMEM((tall, wide, nz), jnp.float32)
    return pl.pallas_call(
        heat_kernel,
        out_shape=(
            jax.ShapeDtypeStruct(shape, jnp.float32),
            jax.ShapeDtypeStruct((tall, 8, LANES), jnp.float32),
        ),
        in_specs=[hbm] * 3 + [vmem] + [hbm] * 4,
        scratch_shapes=[
            pltpu.VMEM((2, 2 * HALO, nz // LANES, wide, LANES), jnp.float32),
            pltpu.VMEM((2, 32, nz), jnp.float32),
            big,
            big,
            big,
            big,
            pltpu.VMEM((nx, nz // LANES, wide, LANES), jnp.float32),
            pltpu.SemaphoreType.DMA((6 * HALO, nz // LANES)),
            pltpu.SemaphoreType.DMA((5,)),
        ],
        compiler_params=params(64),
        cost_estimate=cost(tall * wide * nz * 100, 12 * nx * ny * nz * 4),
        name="heat",
    )(*own, k_low, k_high, t_low, t_high)


def source_kernel(ny, all_ref, thin_ref, base_ref, out_ref):
    tall = thin_ref.shape[0]
    nx = tall - 2 * HALO
    sheets = all_ref.shape[1]
    sub = lax.broadcasted_iota(jnp.int32, (8, LANES), 0)
    y_lane = lax.broadcasted_iota(jnp.int32, (8, LANES), 1)

    slabs, pairs = lax.axis_size("slab"), lax.axis_size("pair")

    def sheet(down, across):
        slab = lax.axis_index("slab") + down
        pair = lax.axis_index("pair") + across
        inside = (slab >= 0) & (slab < slabs) & (pair >= 0) & (pair < pairs)
        found = all_ref[jnp.where(inside, slab * pairs + pair, 0)]
        return jnp.where(inside, found, 0.0)

    def rows_of(down):
        low, own, high = (sheet(down, across) for across in (-1, 0, 1))
        out = []
        for half in range(2):
            if half == 0:
                own_at, high_at, low_at = own, pltpu.roll(high, ny, 1), pltpu.roll(low, ny, 1)
            else:
                own_at, high_at, low_at = pltpu.roll(own, ny, 1), high, low
            out.append(
                jnp.where(
                    y_lane < ny,
                    own_at,
                    jnp.where(
                        y_lane < ny + HALO,
                        high_at,
                        jnp.where(y_lane >= LANES - HALO, low_at, 0.0),
                    ),
                )
            )
        return out

    lines = [rows_of(down) for down in (-1, 0, 1)]
    source = []
    for x in range(-HALO, nx + HALO):
        which, local = (x + nx) // nx, x % nx
        row = lines[which][local % 2][local // 2 : local // 2 + 1, :]
        source.append(jnp.where(sub == 0, jnp.broadcast_to(row, (8, LANES)), 0.0))

    cond = [thin_ref[x] for x in range(tall)]
    cx, cy, cz, centre = [], [], [], []
    for x in range(tall):
        here = cond[x]
        after = cond[min(x + 1, tall - 1)]
        before = cond[max(x - 1, 0)]
        y_after = pltpu.roll(here, LANES - 1, 1)
        y_before = pltpu.roll(here, 1, 1)
        z_after = jnp.where(sub == 7, 0.0, pltpu.roll(here, 7, 0))
        z_before = jnp.where(sub == 0, 0.0, pltpu.roll(here, 1, 0))
        cx.append(coupling(here, after))
        cy.append(coupling(here, y_after))
        cz.append(coupling(here, z_after))
        total = 6.0 * here
        for near in (after, before, y_after, y_before, z_after, z_before):
            total = total + jnp.where(near > 0.0, near, here)
        centre.append(1.0 - (0.5 * step_size) * total)

    added = source
    for step in range(1, STEPS):
        new = list(added)
        for x in range(step, tall - step):
            here = added[x]
            total = source[x] + centre[x] * here
            total = total + (cx[x] * added[x + 1] + cx[x - 1] * added[x - 1])
            total = total + cy[x] * pltpu.roll(here, LANES - 1, 1)
            total = total + pltpu.roll(cy[x] * here, 1, 1)
            total = total + cz[x] * pltpu.roll(here, 7, 0)
            new[x] = total + pltpu.roll(cz[x] * here, 1, 0)
        added = new

    lane = lax.broadcasted_iota(jnp.int32, (ny, LANES), 1)
    turned = jnp.concatenate(added[HALO : HALO + nx], axis=0).T[:ny]
    for x in range(nx):
        piece = turned if x == 0 else pltpu.roll(turned, LANES - 8 * x, 1)
        out_ref[x] = base_ref[x] + jnp.where(lane < STEPS, piece, 0.0)


def add_source(everything, thin, base):
    nx, ny, nz = base.shape
    block = pl.BlockSpec((nx, ny, LANES), lambda i: (0, 0, 0))
    return pl.pallas_call(
        functools.partial(source_kernel, ny),
        grid=(1,),
        out_shape=jax.ShapeDtypeStruct(base.shape, jnp.float32),
        in_specs=[
            pl.BlockSpec(everything.shape, lambda i: (0, 0, 0)),
            pl.BlockSpec(thin.shape, lambda i: (0, 0, 0)),
            block,
        ],
        out_specs=block,
        input_output_aliases={2: 0},
        compiler_params=params(64),
        cost_estimate=cost(1_000_000, 2 * nx * ny * LANES * 4),
        name="add_source",
    )(everything, thin, base)


def exchange(rows):
    return lax.all_to_all(rows, ("slab", "pair"), split_axis=0, concat_axis=0, tiled=True)


def together(*arrays):
    return lax.optimization_barrier(arrays)


def both_ways(low, high, axis):
    count = lax.axis_size(axis)
    forward = [(i, i + 1) for i in range(count - 1)]
    backward = [(target, source) for source, target in forward]
    from_low = lax.ppermute(high, axis, forward)
    from_high = lax.ppermute(low, axis, backward)
    return from_low, from_high


def shards(
    initial_warmth,
    heat_passing_coefficient,
    mirror_fraction,
    element_facing_site,
    tile_block_couples,
    active_slot_count,
    view_factor_blocks,
):
    nx, ny, _ = initial_warmth.shape
    slabs, pairs = lax.axis_size("slab"), lax.axis_size("pair")
    count = slabs * pairs
    blocks = mirror_fraction.shape[0]
    couples = tile_block_couples.T

    temp, cond = initial_warmth, heat_passing_coefficient
    emitted, copies = emit(temp, element_facing_site, mirror_fraction, count)
    temp, copies = together(temp, copies)

    def sweep_terms(whole):
        whole = whole.reshape(count * blocks, BLK)
        term = tile_terms(whole, couples, active_slot_count, view_factor_blocks)
        return term.reshape(count, blocks, BLK)

    whole = exchange(copies)
    cond, copies = together(cond, copies)
    send_low, send_high = cond[:HALO], cond[nx - HALO :]
    k_low, k_high = both_ways(send_low, send_high, "slab")
    whole = together(whole, send_low, send_high)[0]
    temp, cond, term = together(temp, cond, sweep_terms(whole))
    parts = exchange(term)
    below, above = both_ways(*pack_y(temp, cond), "pair")
    parts, below, above, k_low, k_high = together(parts, below, above, k_low, k_high)
    copies, below, above = together(middle(parts, emitted, mirror_fraction), below, above)
    whole = exchange(copies)
    send_low, send_high = pack_x(temp, below, above)
    t_low, t_high = both_ways(send_low, send_high, "slab")
    whole = together(whole, send_low, send_high)[0]
    temp, cond, term = together(temp, cond, sweep_terms(whole))
    parts = exchange(term)
    own = own_planes(temp, cond, below, above)
    parts, t_low, t_high, own = together(parts, t_low, t_high, own)
    radiosity, source = last(parts, emitted, mirror_fraction, element_facing_site, nx * ny, count)
    everything = exchange(source)
    own, source = together(own, source)
    base, thin = heat(own, k_low, k_high, t_low, t_high, temp.shape)

    warmed_liner = add_source(everything, thin, base)
    return (radiosity, warmed_liner)


def solution(mesh):
    return jax.shard_map(
        shards,
        mesh=mesh,
        in_specs=(
            P("slab", "pair", None),
            P("slab", "pair", None),
            P(("slab", "pair"), None),
            P(("slab", "pair"), None),
            P(("slab", "pair"), None),
            P(("slab", "pair")),
            P(("slab", "pair"), None, None),
        ),
        out_specs=(P(("slab", "pair"), None), P("slab", "pair", None)),
        check_vma=False,
    )
```

```python
import functools

import jax
import jax.numpy as jnp
from jax import lax
from jax.experimental import pallas as pl
from jax.experimental.pallas import tpu as pltpu
from jax.sharding import PartitionSpec as P

BLK = 128
SWEEPS = 2
STEPS = 4
HALO = STEPS
ROWS = STEPS
LANES = 128
CHUNK = 16
LAG = 0

step_size = 0.07

NT = (((1,), (1,)), ((), ()))
NN = (((1,), (0,)), ((), ()))


def params(mib):
    return pltpu.CompilerParams(vmem_limit_bytes=mib * 1024 * 1024)


def cost(flops, nbytes):
    return pl.CostEstimate(flops=flops, bytes_accessed=nbytes, transcendentals=0)


def parts_of(x, count):
    out = []
    for _ in range(count - 1):
        part = x.astype(jnp.bfloat16)
        out.append(part)
        x = x - part.astype(jnp.float32)
    out.append(x.astype(jnp.bfloat16))
    return out


class Lagging:
    def __init__(self, depth):
        self.depth = depth
        self.waiting = []

    def add(self, store):
        self.waiting.append(store)
        if len(self.waiting) > self.depth:
            self.waiting.pop(0)()

    def finish(self):
        for store in self.waiting:
            store()
        self.waiting = []


def put(ref, index, value):
    return lambda: ref.__setitem__(index, value)


def emit_kernel(temp_ref, site_ref, mirror_ref, emitted_ref, copies_ref):
    nx, ny, _ = temp_ref.shape
    sheets = nx * ny // LANES
    per = LANES // ny
    lanes = lax.broadcasted_iota(jnp.int32, (LANES, LANES), 1)
    gathered = jnp.zeros((LANES, LANES), jnp.float32)
    for r in range(sheets):
        piece = temp_ref[per * r : per * r + per].reshape(LANES, LANES)
        if r:
            piece = pltpu.roll(piece, r, 1)
        gathered = jnp.where(lanes == r, piece, gathered)
    plane = gathered.T[:sheets]
    for half in range(site_ref.shape[0] // 8):
        rows = pl.ds(half * 8, 8)
        site = site_ref[rows, :]
        lane = site & (LANES - 1)
        sheet = site >> 7
        warmth = jnp.zeros(site.shape, jnp.float32)
        for r in range(sheets):
            line = jnp.broadcast_to(plane[r : r + 1, :], site.shape)
            picked = jnp.take_along_axis(line, lane, axis=1)
            warmth = jnp.where(sheet == r, picked, warmth)
        square = warmth * warmth
        emitted = (1.0 - mirror_ref[rows, :]) * (square * square)
        emitted_ref[rows, :] = emitted
        for d in range(copies_ref.shape[0]):
            copies_ref[d, rows, :] = emitted


def emit(temp, site, mirror, count):
    shape = mirror.shape
    nx, ny, _ = temp.shape
    patch = pl.BlockSpec(shape, lambda i: (0, 0))
    return pl.pallas_call(
        emit_kernel,
        grid=(1,),
        out_shape=(
            jax.ShapeDtypeStruct(shape, jnp.float32),
            jax.ShapeDtypeStruct((count,) + shape, jnp.float32),
        ),
        in_specs=[pl.BlockSpec((nx, ny, LANES), lambda i: (0, 0, 0)), patch, patch],
        out_specs=(patch, pl.BlockSpec((count,) + shape, lambda i: (0, 0, 0))),
        compiler_params=params(64),
        cost_estimate=cost(10_000, 900_000),
        name="emit",
    )(temp, site, mirror)


def tiles_kernel(
    live_ref, pairs_ref, lanes_ref, whole_ref, tiles_ref, out_ref, held, terms, sems
):
    slots = held.shape[0]
    live = live_ref[0]
    chunks = (live + CHUNK - 1) // CHUNK

    def chunk_copy(c):
        span = pl.ds(c * CHUNK, CHUNK)
        return pltpu.make_async_copy(tiles_ref.at[span], held.at[span], sems.at[c])

    @pl.loop(0, chunks)
    def _(c):
        chunk_copy(c).start()

    top = lax.broadcasted_iota(jnp.int32, (8, BLK), 0) == 0

    def split_row(block):
        row = jnp.broadcast_to(whole_ref[pl.ds(block, 1), :], (8, BLK))
        high = row.astype(jnp.bfloat16).astype(jnp.float32)
        return jnp.where(top, high, row - high)

    def vectors(a, b):
        stacked = jnp.concatenate([split_row(a), split_row(b)], axis=0)
        stacked = stacked.astype(jnp.bfloat16)
        return jnp.concatenate([stacked, stacked], axis=1)

    @pl.loop(0, chunks)
    def _(c):
        chunk_copy(c).wait()
        stores = Lagging(4 * CHUNK)
        for u in range(0, CHUNK, 2):
            t = c * CHUNK + u
            high_a, low_a = parts_of(held[t], 2)
            high_b, low_b = parts_of(held[t + 1], 2)
            both = jnp.concatenate(
                [
                    jnp.concatenate([high_a, high_b], axis=1),
                    jnp.concatenate([low_a, low_b], axis=1),
                ],
                axis=0,
            )
            second = lax.dot_general(
                vectors(pairs_ref[0, t], pairs_ref[0, t + 1]),
                both,
                NN,
                preferred_element_type=jnp.float32,
            )
            turned = jnp.concatenate(
                [
                    jnp.concatenate([high_a, low_a], axis=1),
                    jnp.concatenate([high_b, low_b], axis=1),
                ],
                axis=0,
            )
            first = lax.dot_general(
                vectors(pairs_ref[1, t], pairs_ref[1, t + 1]),
                turned,
                NT,
                preferred_element_type=jnp.float32,
            )
            for side, result in ((0, first), (1, second)):
                for v, (top_row, cols) in enumerate(((0, slice(0, BLK)), (8, slice(BLK, 2 * BLK)))):
                    row = result[top_row : top_row + 1, cols] + result[top_row + 1 : top_row + 2, cols]
                    stores.add(put(terms, (side, pl.ds(t + v, 1)), row))
        stores.finish()

    used = lax.broadcasted_iota(jnp.int32, (slots, BLK), 0) < live
    used_lane = lax.broadcasted_iota(jnp.int32, (1, slots), 1) < live
    blocks = out_ref.shape[0]
    group = min(blocks, 512)
    split = []
    for side in range(2):
        masked = jnp.where(used, terms[side], 0.0)
        split.append(jnp.concatenate(parts_of(masked, 2), axis=1))
    for base in range(0, blocks, group):
        rows = lax.broadcasted_iota(jnp.int32, (group, slots), 0) + base
        total = jnp.zeros((group, 2 * BLK), jnp.float32)
        for side in range(2):
            target = jnp.where(used_lane, lanes_ref[side : side + 1, :], -1)
            choose = jnp.where(rows == target, 1.0, 0.0).astype(jnp.bfloat16)
            total = total + jnp.dot(choose, split[side], preferred_element_type=jnp.float32)
        out_ref[base : base + group, :] = total[:, :BLK] + total[:, BLK:]


def tile_terms(whole, couples, live, tiles):
    slots = tiles.shape[0]
    smem = pl.BlockSpec(memory_space=pltpu.SMEM)
    vmem = pl.BlockSpec(memory_space=pltpu.VMEM)
    return pl.pallas_call(
        tiles_kernel,
        out_shape=jax.ShapeDtypeStruct(whole.shape, jnp.float32),
        in_specs=[smem, smem, vmem, vmem, pl.BlockSpec(memory_space=pl.ANY)],
        out_specs=vmem,
        scratch_shapes=[
            pltpu.VMEM(tiles.shape, jnp.float32),
            pltpu.VMEM((2, slots, BLK), jnp.float32),
            pltpu.SemaphoreType.DMA((slots // CHUNK,)),
        ],
        compiler_params=params(64),
        cost_estimate=cost(slots * BLK * BLK * 32, slots * BLK * BLK * 4),
        name="tiles",
    )(live, couples, couples, whole, tiles)


def sum_parts(parts_ref, rows):
    total = parts_ref[0, rows, :]
    for d in range(1, parts_ref.shape[0]):
        total = total + parts_ref[d, rows, :]
    return total


def middle_kernel(parts_ref, emitted_ref, mirror_ref, copies_ref):
    for half in range(emitted_ref.shape[0] // 8):
        rows = pl.ds(half * 8, 8)
        incident = sum_parts(parts_ref, rows)
        radiosity = emitted_ref[rows, :] + mirror_ref[rows, :] * incident
        for d in range(copies_ref.shape[0]):
            copies_ref[d, rows, :] = radiosity


def middle(parts, emitted, mirror):
    return pl.pallas_call(
        middle_kernel,
        out_shape=jax.ShapeDtypeStruct(parts.shape, jnp.float32),
        compiler_params=params(64),
        cost_estimate=cost(100_000, 600_000),
        name="middle",
    )(parts, emitted, mirror)


def last_kernel(scale, parts_ref, emitted_ref, mirror_ref, site_ref, rad_ref, source_ref):
    blocks = emitted_ref.shape[0]
    incident = sum_parts(parts_ref, slice(None))
    emitted = emitted_ref[...]
    mirror = mirror_ref[...]
    rad_ref[...] = emitted + mirror * incident
    absorbed = ((1.0 - mirror) * incident - emitted) * scale
    site = site_ref[...]
    lane = site & (LANES - 1)
    sheet = site >> 7
    sheets = source_ref.shape[1]
    sheet_iota = lax.broadcasted_iota(jnp.int32, (sheets, BLK), 0)
    lane_iota = lax.broadcasted_iota(jnp.int32, (LANES, BLK), 0)
    left = []
    right = []
    for b in range(blocks):
        here = jnp.where(sheet_iota == sheet[b : b + 1, :], absorbed[b : b + 1, :], 0.0)
        left.append(here)
        pick = jnp.where(lane_iota == lane[b : b + 1, :], 1.0, 0.0)
        right.append(pick.astype(jnp.bfloat16))
    left = jnp.concatenate(left, axis=1)
    right = jnp.concatenate(right, axis=1)
    source = jnp.zeros((sheets, LANES), jnp.float32)
    for part in parts_of(left, 3):
        source = source + lax.dot_general(part, right, NT, preferred_element_type=jnp.float32)
    for d in range(source_ref.shape[0]):
        source_ref[d] = source


def last(parts, emitted, mirror, site, cells, count):
    weight = cells / (mirror.shape[0] * BLK * 1.0)
    return pl.pallas_call(
        functools.partial(last_kernel, step_size * weight),
        out_shape=(
            jax.ShapeDtypeStruct(mirror.shape, jnp.float32),
            jax.ShapeDtypeStruct((count, cells // LANES, LANES), jnp.float32),
        ),
        compiler_params=params(64),
        cost_estimate=cost(10_000_000, 600_000),
        name="last",
    )(parts, emitted, mirror, site)


def pack_y_kernel(t0, k0, t7, k7, down_ref, up_ref):
    upper = lax.broadcasted_iota(jnp.int32, down_ref.shape[1:], 0) < ROWS
    for x in range(down_ref.shape[0]):
        down_ref[x] = jnp.where(upper, t0[x], pltpu.roll(k0[x], ROWS, 0))
        up_ref[x] = jnp.where(upper, pltpu.roll(t7[x], ROWS, 0), k7[x])


def pack_y(temp, cond):
    nx, ny, nz = temp.shape
    first = pl.BlockSpec((nx, 8, nz), lambda i: (0, 0, 0))
    final = pl.BlockSpec((nx, 8, nz), lambda i: (0, ny // 8 - 1, 0))
    shape = jax.ShapeDtypeStruct((nx, 8, nz), jnp.float32)
    return pl.pallas_call(
        pack_y_kernel,
        grid=(1,),
        out_shape=(shape, shape),
        in_specs=[first, first, final, final],
        out_specs=(first, first),
        compiler_params=params(64),
        cost_estimate=cost(0, 4 * nx * 8 * nz * 4),
        name="pack_y",
    )(temp, cond, temp, cond)


def mixed_tile(t_tile, k_tile):
    row = lax.broadcasted_iota(jnp.int32, t_tile.shape, 0)
    of_k = jnp.where(row < 4, pltpu.roll(k_tile, 2, 0), pltpu.roll(k_tile, 6, 0))
    return jnp.where((row < 2) | (row >= 6), t_tile, of_k)


def unmixed(tile):
    row = lax.broadcasted_iota(jnp.int32, tile.shape, 0)
    outer = (row < 2) | (row >= 6)
    of_k = jnp.where(row < 4, pltpu.roll(tile, 6, 0), pltpu.roll(tile, 2, 0))
    return jnp.where(outer, tile, 0.0), jnp.where(outer, of_k, 0.0)


def pack_x_kernel(first, final, below0, above0, below1, above1, low_ref, high_ref):
    ny, nz = first.shape[1:]
    upper = lax.broadcasted_iota(jnp.int32, (8, nz), 0) < ROWS
    tail = HALO * ny
    for send, temp, below, above, order in (
        (low_ref, first, below0, above0, (0, 1, 2)),
        (high_ref, final, below1, above1, (HALO - 1, HALO - 2, HALO - 3)),
    ):
        for p in range(HALO):
            send[p * ny : (p + 1) * ny, :] = temp[p]
        for k, p in enumerate(order):
            t_tile = jnp.where(upper, above[p], pltpu.roll(below[p], ROWS, 0))
            k_tile = jnp.where(upper, pltpu.roll(above[p], ROWS, 0), below[p])
            if k == 0:
                send[tail : tail + 8, :] = t_tile
                send[tail + 8 : tail + 16, :] = k_tile
            else:
                at = tail + 8 + 8 * k
                send[at : at + 8, :] = mixed_tile(t_tile, k_tile)


def pack_x(temp, below, above):
    nx, ny, nz = temp.shape

    def ends(rows):
        return (
            pl.BlockSpec((HALO, rows, nz), lambda i: (0, 0, 0)),
            pl.BlockSpec((HALO, rows, nz), lambda i: (nx // HALO - 1, 0, 0)),
        )

    first, final = ends(ny)
    first_rows, final_rows = ends(8)
    rows = HALO * ny + 32
    whole = pl.BlockSpec((rows, nz), lambda i: (0, 0))
    shape = jax.ShapeDtypeStruct((rows, nz), jnp.float32)
    return pl.pallas_call(
        pack_x_kernel,
        grid=(1,),
        out_shape=(shape, shape),
        in_specs=[first, final, first_rows, first_rows, final_rows, final_rows],
        out_specs=(whole, whole),
        compiler_params=params(64),
        cost_estimate=cost(0, 4 * rows * nz * 4),
        name="pack_x",
    )(temp, temp, below, above, below, above)


def coupling(a, b):
    return jnp.where(jnp.minimum(a, b) > 0.0, (0.5 * step_size) * (a + b), 0.0)


def neighbours():
    slab, pair = lax.axis_index("slab"), lax.axis_index("pair")
    return slab > 0, slab < lax.axis_size("slab") - 1, pair > 0, pair < lax.axis_size("pair") - 1


def lane_tiles(nz):
    return [slice(j * LANES, (j + 1) * LANES) for j in range(nz // LANES)]


def one_step(field, cond, gz, begin, end, target):
    wide, nz = field.shape[1:]
    tiles = wide // 8
    spans = lane_tiles(nz)
    count = len(spans)
    lane = lax.broadcasted_iota(jnp.int32, (8, LANES), 1)
    sub = lax.broadcasted_iota(jnp.int32, (8, LANES), 0)
    _, _, has_below, has_above = neighbours()
    keep_above = (sub < 7) | has_above
    keep_below = (sub < 7) | has_below

    def row_tile(ref, x, t):
        return [ref[x, 8 * t : 8 * t + 8, z] for z in spans]

    def first_rolled(ref, x):
        return [pltpu.roll(v, 7, 0) for v in row_tile(ref, x, 0)]

    def y_flux(t_now, k_now, t_next, k_next):
        return [
            (k_now[j] + k_next[j]) * (t_next[j] - t_now[j]) for j in range(count)
        ]

    def z_change(x, t, t_now, k_now):
        turned = [pltpu.roll(v, LANES - 1, 1) for v in t_now]
        flux = []
        for j, z in enumerate(spans):
            deep = turned[j + 1] if j + 1 < count else 0.0
            deep = jnp.where(lane < LANES - 1, turned[j], deep)
            flux.append(gz[x, 8 * t : 8 * t + 8, z] * (deep - t_now[j]))
        back = [pltpu.roll(f, 1, 1) for f in flux]
        out = []
        for j in range(count):
            low = back[j - 1] if j else (k_now[0] + k_now[0]) * t_now[0]
            out.append(flux[j] - jnp.where(lane > 0, back[j], low))
        return out

    @pl.loop(begin, end)
    def _(x):
        stores = Lagging(LAG)
        final = y_flux(
            row_tile(field, x, tiles - 1),
            row_tile(cond, x, tiles - 1),
            first_rolled(field, x),
            first_rolled(cond, x),
        )
        low_y = [pltpu.roll(f, 1, 0) for f in final]
        t_now, k_now = row_tile(field, x, 0), row_tile(cond, x, 0)
        for t in range(tiles):
            rows = slice(8 * t, 8 * t + 8)
            if t + 1 < tiles:
                t_next, k_next = row_tile(field, x, t + 1), row_tile(cond, x, t + 1)
            else:
                t_next, k_next = first_rolled(field, x), first_rolled(cond, x)
            high_y = y_flux(t_now, k_now, t_next, k_next)
            change_z = z_change(x, t, t_now, k_now)
            for j, z in enumerate(spans):
                now, here = t_now[j], k_now[j]
                high_x = (here + cond[x + 1, rows, z]) * (field[x + 1, rows, z] - now)
                low_x = (here + cond[x - 1, rows, z]) * (now - field[x - 1, rows, z])
                new = now + (high_x - low_x) + (high_y[j] - low_y[j]) + change_z[j]
                if t:
                    new = jnp.where(keep_above if t <= ROWS else keep_below, new, 0.0)
                stores.add(put(*target(x, t, z), new))
            low_y, t_now, k_now = high_y, t_next, k_next
        stores.finish()


def thin_planes(cond, ny, store):
    tall, _, wide, _ = cond.shape
    lane = lax.broadcasted_iota(jnp.int32, (wide, LANES), 1)
    y_lane = lax.broadcasted_iota(jnp.int32, (8, LANES), 1)
    for base in range(0, tall, 16):
        planes = min(16, tall - base)
        gathered = jnp.zeros((wide, LANES), jnp.float32)
        for g in range(planes):
            piece = cond[base + g, 0]
            if g:
                piece = pltpu.roll(piece, 8 * g, 1)
            gathered = jnp.where((lane >> 3) == g, piece, gathered)
        turned = jnp.concatenate(
            [gathered, jnp.zeros((LANES - wide, LANES), jnp.float32)], axis=0
        ).T
        for g in range(planes):
            rows = turned[8 * g : 8 * g + 8, :]
            moved = pltpu.roll(rows, LANES - wide, 1)
            store(
                base + g,
                jnp.where(
                    y_lane < ny + ROWS, rows, jnp.where(y_lane >= LANES - ROWS, moved, 0.0)
                ),
            )


def mirror_rows(raw_k, ny):
    _, _, has_below, has_above = neighbours()
    upper = lax.broadcasted_iota(jnp.int32, (8, LANES), 0) < ROWS

    @pl.when(jnp.logical_not(has_above & has_below))
    def _():
        missing = (upper & jnp.logical_not(has_above)) | (
            jnp.logical_not(upper) & jnp.logical_not(has_below)
        )

        @pl.loop(0, raw_k.shape[0])
        def _(x):
            for j in range(raw_k.shape[1]):
                edge = raw_k[x, j, ny:]
                last = jnp.broadcast_to(raw_k[x, j, ny - 1 : ny, :], edge.shape)
                first = jnp.broadcast_to(raw_k[x, j, 0:1, :], edge.shape)
                raw_k[x, j, ny:] = jnp.where(missing, jnp.where(upper, last, first), edge)


def lay_out_k(loaded, place, faces, gz):
    planes, count, wide, _ = loaded.shape[1:]
    tiles = wide // 8
    spans = lane_tiles(count * LANES)
    lane = lax.broadcasted_iota(jnp.int32, (8, LANES), 1)

    @pl.loop(0, planes)
    def _(x):
        stores = Lagging(LAG)
        to = place(x)
        for t in range(tiles):
            rows = pl.ds(t, 8, stride=tiles)
            kept = slice(8 * t, 8 * t + 8)
            here = [(0.5 * step_size) * loaded[1, x, j, rows, :] for j in range(count)]
            turned = [pltpu.roll(v, LANES - 1, 1) for v in here]
            for j, z in enumerate(spans):
                deep = turned[j + 1] if j + 1 < count else here[j]
                deep = jnp.where(lane < LANES - 1, turned[j], deep)
                stores.add(put(faces, (to, kept, z), here[j]))
                stores.add(put(gz, (to, kept, z), here[j] + deep))
        stores.finish()


def lay_out_t(loaded, place, field):
    planes, count, wide, _ = loaded.shape[1:]
    tiles = wide // 8
    spans = lane_tiles(count * LANES)

    @pl.loop(0, planes)
    def _(x):
        stores = Lagging(LAG)
        to = place(x)
        for t in range(tiles):
            rows = pl.ds(t, 8, stride=tiles)
            for j, z in enumerate(spans):
                stores.add(put(field, (to, slice(8 * t, 8 * t + 8), z), loaded[0, x, j, rows, :]))
        stores.finish()


def fetch(loaded, which, ref, source_row, at, row, rows, sems):
    planes, count = ref.shape[0], loaded.shape[2]
    return [
        pltpu.make_async_copy(
            ref.at[:, pl.ds(source_row, rows), pl.ds(j * LANES, LANES)],
            loaded.at[which, pl.ds(at, planes), j, pl.ds(row, rows)],
            sems.at[j],
        )
        for j in range(count)
    ]


def own_planes_kernel(
    t_ref, k_ref, below_ref, above_ref, field, faces, gz, thin_ref, loaded, sems
):
    nx, ny, nz = t_ref.shape
    raw_t, raw_k = loaded.at[0], loaded.at[1]
    k_copies = fetch(loaded, 1, k_ref, 0, 0, 0, ny, sems.at[1])
    t_copies = fetch(loaded, 0, t_ref, 0, 0, 0, ny, sems.at[0])
    for copy in k_copies + t_copies:
        copy.start()
    upper = lax.broadcasted_iota(jnp.int32, (8, LANES), 0) < ROWS

    @pl.loop(0, nx)
    def _(x):
        for j, z in enumerate(lane_tiles(nz)):
            down, up = above_ref[x, :, z], below_ref[x, :, z]
            raw_t[x, j, ny:] = jnp.where(upper, down, pltpu.roll(up, ROWS, 0))
            raw_k[x, j, ny:] = jnp.where(upper, pltpu.roll(down, ROWS, 0), up)

    for copy in k_copies:
        copy.wait()
    thin_planes(raw_k, ny, lambda x, v: thin_ref.__setitem__(x, v))
    mirror_rows(raw_k, ny)
    lay_out_k(loaded, lambda x: x, faces, gz)
    for copy in t_copies:
        copy.wait()
    lay_out_t(loaded, lambda x: x, field)


def own_planes(temp, cond, below, above):
    nx, ny, nz = temp.shape
    wide = ny + 2 * ROWS
    hbm = pl.BlockSpec(memory_space=pl.ANY)
    vmem = pl.BlockSpec(memory_space=pltpu.VMEM)
    shape = jax.ShapeDtypeStruct((nx, wide, nz), jnp.float32)
    return pl.pallas_call(
        own_planes_kernel,
        out_shape=(shape, shape, shape, jax.ShapeDtypeStruct((nx, 8, LANES), jnp.float32)),
        in_specs=[hbm, hbm, vmem, vmem],
        scratch_shapes=[
            pltpu.VMEM((2, nx, nz // LANES, wide, LANES), jnp.float32),
            pltpu.SemaphoreType.DMA((2, nz // LANES)),
        ],
        compiler_params=params(64),
        cost_estimate=cost(nx * wide * nz * 10, 6 * nx * wide * nz * 4),
        name="own_planes",
    )(temp, cond, below, above)


def heat_kernel(
    own_field, own_faces, own_gz, own_thin, k_low, k_high, t_low, t_high, out_ref, thin_ref,
    loaded, corners, field, between, faces, gz, placed, sems, own_sems, out_sems,
):
    nx, wide, nz = own_field.shape
    ny = wide - 2 * ROWS
    tall = nx + 2 * HALO
    tiles = wide // 8
    spans = lane_tiles(nz)
    k_copies, t_copies = [], []
    for k, (k_side, t_side) in enumerate(((k_low, t_low), (k_high, t_high))):
        at = k * HALO
        k_copies += fetch(loaded, 1, k_side, 0, at, 0, ny, sems.at[3 * k])
        k_copies.append(
            pltpu.make_async_copy(
                t_side.at[pl.ds(HALO * ny, 32)], corners.at[k], own_sems.at[3 + k]
            )
        )
        for p in range(HALO):
            t_copies += [
                pltpu.make_async_copy(
                    t_side.at[pl.ds(p * ny, ny), pl.ds(j * LANES, LANES)],
                    loaded.at[0, at + p, j, pl.ds(0, ny)],
                    sems.at[3 * (k + 1) - 1 + 6 * p, j],
                )
                for j in range(len(spans))
            ]
    own = [
        pltpu.make_async_copy(ref, whole.at[pl.ds(HALO, nx)], own_sems.at[k])
        for k, (ref, whole) in enumerate(
            ((own_faces, faces), (own_gz, gz), (own_field, field))
        )
    ]
    for copy in k_copies + t_copies + own:
        copy.start()
    has_low, has_high, _, _ = neighbours()

    def place(x):
        return jnp.where(x < HALO, x, x + nx)

    def store_thin(x, value):
        thin_ref[x if x < HALO else x + nx] = value

    thin_ref[HALO : HALO + nx] = own_thin[...]
    raw_t, raw_k = loaded.at[0], loaded.at[1]
    for copy in k_copies:
        copy.wait()
    for k, order in enumerate(
        ((HALO - 1, HALO - 2, HALO - 3, 0), (HALO, HALO + 1, HALO + 2, 2 * HALO - 1))
    ):
        for distance, p in enumerate(order):
            for j, z in enumerate(spans):
                if distance == 0:
                    t_tile, k_tile = corners[k, :8, z], corners[k, 8:16, z]
                elif distance + 1 < HALO:
                    t_tile, k_tile = unmixed(corners[k, 8 + 8 * distance : 16 + 8 * distance, z])
                else:
                    t_tile = k_tile = jnp.zeros((8, LANES), jnp.float32)
                raw_t[p, j, ny:] = t_tile
                raw_k[p, j, ny:] = k_tile
    thin_planes(raw_k, ny, store_thin)
    mirror_rows(raw_k, ny)
    lay_out_k(loaded, place, faces, gz)
    for copy in t_copies:
        copy.wait()
    lay_out_t(loaded, place, field)
    for copy in own:
        copy.wait()

    @pl.when(jnp.logical_not(has_low))
    def _():
        faces[HALO - 1] = faces[HALO]

    @pl.when(jnp.logical_not(has_high))
    def _():
        faces[HALO + nx] = faces[HALO + nx - 1]

    def inside(target):
        return lambda x, t, z: (target, (x, slice(8 * t, 8 * t + 8), z))

    def outside(x, t, z):
        return placed, (x - HALO, z.start // LANES, pl.ds(t, 8, stride=tiles))

    old, new = field, between
    for step in range(1, STEPS):
        one_step(old, faces, gz, step, tall - step, inside(new))
        for x, there in ((HALO - 1, has_low), (HALO + nx, has_high)):

            @pl.when(jnp.logical_not(there))
            def _():
                new[x] = jnp.zeros((wide, nz), jnp.float32)

        old, new = new, old
    one_step(old, faces, gz, HALO, tall - HALO, outside)

    results = [
        pltpu.make_async_copy(
            placed.at[:, j, pl.ds(0, ny)],
            out_ref.at[:, :, pl.ds(j * LANES, LANES)],
            out_sems.at[j],
        )
        for j in range(len(spans))
    ]
    for copy in results:
        copy.start()
    for copy in results:
        copy.wait()


def heat(own, k_low, k_high, t_low, t_high, shape):
    nx, ny, nz = shape
    tall, wide = nx + 2 * HALO, ny + 2 * ROWS
    hbm = pl.BlockSpec(memory_space=pl.ANY)
    vmem = pl.BlockSpec(memory_space=pltpu.VMEM)
    big = pltpu.VMEM((tall, wide, nz), jnp.float32)
    return pl.pallas_call(
        heat_kernel,
        out_shape=(
            jax.ShapeDtypeStruct(shape, jnp.float32),
            jax.ShapeDtypeStruct((tall, 8, LANES), jnp.float32),
        ),
        in_specs=[hbm] * 3 + [vmem] + [hbm] * 4,
        out_specs=(hbm, vmem),
        scratch_shapes=[
            pltpu.VMEM((2, 2 * HALO, nz // LANES, wide, LANES), jnp.float32),
            pltpu.VMEM((2, 32, nz), jnp.float32),
            big,
            big,
            big,
            big,
            pltpu.VMEM((nx, nz // LANES, wide, LANES), jnp.float32),
            pltpu.SemaphoreType.DMA((6 * HALO, nz // LANES)),
            pltpu.SemaphoreType.DMA((5,)),
            pltpu.SemaphoreType.DMA((nz // LANES,)),
        ],
        compiler_params=params(64),
        cost_estimate=cost(tall * wide * nz * 100, 12 * nx * ny * nz * 4),
        name="heat",
    )(*own, k_low, k_high, t_low, t_high)


def source_kernel(ny, all_ref, thin_ref, base_ref, out_ref):
    tall = thin_ref.shape[0]
    nx = tall - 2 * HALO
    sheets = all_ref.shape[1]
    sub = lax.broadcasted_iota(jnp.int32, (8, LANES), 0)
    y_lane = lax.broadcasted_iota(jnp.int32, (8, LANES), 1)

    slabs, pairs = lax.axis_size("slab"), lax.axis_size("pair")

    def sheet(down, across):
        slab = lax.axis_index("slab") + down
        pair = lax.axis_index("pair") + across
        inside = (slab >= 0) & (slab < slabs) & (pair >= 0) & (pair < pairs)
        found = all_ref[jnp.where(inside, slab * pairs + pair, 0)]
        return jnp.where(inside, found, 0.0)

    def rows_of(down):
        low, own, high = (sheet(down, across) for across in (-1, 0, 1))
        out = []
        for half in range(2):
            if half == 0:
                own_at, high_at, low_at = own, pltpu.roll(high, ny, 1), pltpu.roll(low, ny, 1)
            else:
                own_at, high_at, low_at = pltpu.roll(own, ny, 1), high, low
            out.append(
                jnp.where(
                    y_lane < ny,
                    own_at,
                    jnp.where(
                        y_lane < ny + HALO,
                        high_at,
                        jnp.where(y_lane >= LANES - HALO, low_at, 0.0),
                    ),
                )
            )
        return out

    lines = [rows_of(down) for down in (-1, 0, 1)]
    source = []
    for x in range(-HALO, nx + HALO):
        which, local = (x + nx) // nx, x % nx
        row = lines[which][local % 2][local // 2 : local // 2 + 1, :]
        source.append(jnp.where(sub == 0, jnp.broadcast_to(row, (8, LANES)), 0.0))

    cond = [thin_ref[x] for x in range(tall)]
    cx, cy, cz, centre = [], [], [], []
    for x in range(tall):
        here = cond[x]
        after = cond[min(x + 1, tall - 1)]
        before = cond[max(x - 1, 0)]
        y_after = pltpu.roll(here, LANES - 1, 1)
        y_before = pltpu.roll(here, 1, 1)
        z_after = jnp.where(sub == 7, 0.0, pltpu.roll(here, 7, 0))
        z_before = jnp.where(sub == 0, 0.0, pltpu.roll(here, 1, 0))
        cx.append(coupling(here, after))
        cy.append(coupling(here, y_after))
        cz.append(coupling(here, z_after))
        total = 6.0 * here
        for near in (after, before, y_after, y_before, z_after, z_before):
            total = total + jnp.where(near > 0.0, near, here)
        centre.append(1.0 - (0.5 * step_size) * total)

    added = source
    for step in range(1, STEPS):
        new = list(added)
        for x in range(step, tall - step):
            here = added[x]
            total = source[x] + centre[x] * here
            total = total + (cx[x] * added[x + 1] + cx[x - 1] * added[x - 1])
            total = total + cy[x] * pltpu.roll(here, LANES - 1, 1)
            total = total + pltpu.roll(cy[x] * here, 1, 1)
            total = total + cz[x] * pltpu.roll(here, 7, 0)
            new[x] = total + pltpu.roll(cz[x] * here, 1, 0)
        added = new

    lane = lax.broadcasted_iota(jnp.int32, (ny, LANES), 1)
    turned = jnp.concatenate(added[HALO : HALO + nx], axis=0).T[:ny]
    for x in range(nx):
        piece = turned if x == 0 else pltpu.roll(turned, LANES - 8 * x, 1)
        out_ref[x] = base_ref[x] + jnp.where(lane < STEPS, piece, 0.0)


def add_source(everything, thin, base):
    nx, ny, nz = base.shape
    block = pl.BlockSpec((nx, ny, LANES), lambda i: (0, 0, 0))
    return pl.pallas_call(
        functools.partial(source_kernel, ny),
        grid=(1,),
        out_shape=jax.ShapeDtypeStruct(base.shape, jnp.float32),
        in_specs=[
            pl.BlockSpec(everything.shape, lambda i: (0, 0, 0)),
            pl.BlockSpec(thin.shape, lambda i: (0, 0, 0)),
            block,
        ],
        out_specs=block,
        input_output_aliases={2: 0},
        compiler_params=params(64),
        cost_estimate=cost(1_000_000, 2 * nx * ny * LANES * 4),
        name="add_source",
    )(everything, thin, base)


def exchange(rows):
    return lax.all_to_all(rows, ("slab", "pair"), split_axis=0, concat_axis=0, tiled=True)


def together(*arrays):
    return lax.optimization_barrier(arrays)


def both_ways(low, high, axis):
    count = lax.axis_size(axis)
    forward = [(i, i + 1) for i in range(count - 1)]
    backward = [(target, source) for source, target in forward]
    from_low = lax.ppermute(high, axis, forward)
    from_high = lax.ppermute(low, axis, backward)
    return from_low, from_high


def shards(
    initial_warmth,
    heat_passing_coefficient,
    mirror_fraction,
    element_facing_site,
    tile_block_couples,
    active_slot_count,
    view_factor_blocks,
):
    nx, ny, _ = initial_warmth.shape
    slabs, pairs = lax.axis_size("slab"), lax.axis_size("pair")
    count = slabs * pairs
    blocks = mirror_fraction.shape[0]
    couples = tile_block_couples.T

    temp, cond = initial_warmth, heat_passing_coefficient
    emitted, copies = emit(temp, element_facing_site, mirror_fraction, count)
    temp, copies = together(temp, copies)

    def sweep_terms(whole):
        whole = whole.reshape(count * blocks, BLK)
        term = tile_terms(whole, couples, active_slot_count, view_factor_blocks)
        return term.reshape(count, blocks, BLK)

    whole = exchange(copies)
    cond, copies = together(cond, copies)
    send_low, send_high = cond[:HALO], cond[nx - HALO :]
    k_low, k_high = both_ways(send_low, send_high, "slab")
    whole = together(whole, send_low, send_high)[0]
    temp, cond, term = together(temp, cond, sweep_terms(whole))
    parts = exchange(term)
    below, above = both_ways(*pack_y(temp, cond), "pair")
    parts, below, above, k_low, k_high = together(parts, below, above, k_low, k_high)
    copies, below, above = together(middle(parts, emitted, mirror_fraction), below, above)
    whole = exchange(copies)
    send_low, send_high = pack_x(temp, below, above)
    t_low, t_high = both_ways(send_low, send_high, "slab")
    whole = together(whole, send_low, send_high)[0]
    temp, cond, term = together(temp, cond, sweep_terms(whole))
    parts = exchange(term)
    own = own_planes(temp, cond, below, above)
    parts, t_low, t_high, own = together(parts, t_low, t_high, own)
    radiosity, source = last(parts, emitted, mirror_fraction, element_facing_site, nx * ny, count)
    everything = exchange(source)
    own, source = together(own, source)
    base, thin = heat(own, k_low, k_high, t_low, t_high, temp.shape)

    warmed_liner = add_source(everything, thin, base)
    return (radiosity, warmed_liner)


def solution(mesh):
    return jax.shard_map(
        shards,
        mesh=mesh,
        in_specs=(
            P("slab", "pair", None),
            P("slab", "pair", None),
            P(("slab", "pair"), None),
            P(("slab", "pair"), None),
            P(("slab", "pair"), None),
            P(("slab", "pair")),
            P(("slab", "pair"), None, None),
        ),
        out_specs=(P(("slab", "pair"), None), P("slab", "pair", None)),
        check_vma=False,
    )
```
